32 devices in a mesh: grp: 4 (over y, x), seq: 8 (over z, core).
Axes of the slice: x: 2, y: 2, z: 4, core: 2. Of those that a mesh axis runs over, the one named last changes fastest.
Arguments:
- tokens: bfloat16 [2, 4, 512, 2048], P(None, 'grp', 'seq'), may hold values from -6 to 6
- cotangent: bfloat16 [2, 4, 512, 2048], P(None, 'grp', 'seq'), may hold values from -6 to 6
- lengths: int32 [2, 4], P(None, 'grp'), may hold values from 64 to 512, as said below
- decay_rate: float32 [16], replicated, may hold values from 0 to 1, as said below
- w_query: bfloat16 [2048, 2048], P('seq', 'grp'), may hold values from -0.125 to 0.125
- w_key: bfloat16 [2048, 2048], P('seq', 'grp'), may hold values from -0.125 to 0.125
- w_value: bfloat16 [2048, 2048], P('seq', 'grp'), may hold values from -0.125 to 0.125
- w_gate: bfloat16 [2048, 2048], P('seq', 'grp'), may hold values from -0.125 to 0.125
- w_out: bfloat16 [2048, 2048], P('seq', 'grp'), may hold values from -0.125 to 0.125
- w_first: bfloat16 [2048, 5632], P('seq', 'grp'), may hold values from -0.125 to 0.125
- w_second: bfloat16 [2048, 5632], P('seq', 'grp'), may hold values from -0.125 to 0.125
- w_third: bfloat16 [5632, 2048], P('seq', 'grp'), may hold values from -0.078125 to 0.078125
Outputs:
- layer_out: bfloat16 [2, 4, 512, 2048], P(None, 'grp', 'seq')
- grad_tokens: float32 [2, 4, 512, 2048], P(None, 'grp', 'seq')
- grad_query: float32 [2048, 2048], P('seq', 'grp')
- grad_key: float32 [2048, 2048], P('seq', 'grp')
- grad_value: float32 [2048, 2048], P('seq', 'grp')
- grad_gate: float32 [2048, 2048], P('seq', 'grp')
- grad_out: float32 [2048, 2048], P('seq', 'grp')
- grad_first: float32 [2048, 5632], P('seq', 'grp')
- grad_second: float32 [2048, 5632], P('seq', 'grp')
- grad_third: float32 [5632, 2048], P('seq', 'grp')
The draws below stay inside these ranges and needn't reach their ends.
Inputs may be any that keep to these rules, and one draw needn't show every extreme that they name: `lengths`: every length lies between 64 and 512; some sequence fills all 512 slots and some has exactly 64. `decay_rate`: each rate is positive and under one.
All inputs are finite; a program needn't handle non-finite values.
Results may differ from the reference program's by a relative error of at most 0.012.
Values may be sent and summed in bfloat16 or wider, within the bound.
A program may use at most 640 MiB of HBM per device.

```python
import jax
import jax.numpy as jnp
from jax import lax

D = 2048
HEADS = 16
HEAD_DIM = 128
FF = 5632
TOK_MB = 64
MB = 2
SLOT = 512
MINLEN = 64
GROUPS = 4


def draw_lengths(key, part):
    first, second = jax.random.split(jax.random.fold_in(key, 11))
    count = MB * GROUPS
    values = jax.random.randint(first, (count,), MINLEN, SLOT + 1).astype(jnp.int32)
    order = jax.random.permutation(second, count)
    values = values.at[order[0]].set(SLOT).at[order[1]].set(MINLEN)
    return values.reshape(MB, GROUPS).astype(jnp.int32)


def draw_decay_rate(key, part):
    first, second, third = jax.random.split(jax.random.fold_in(key, 23), 3)
    order = jax.random.permutation(first, HEADS)
    slow_count = HEADS // 2
    slow = jax.random.uniform(second, (HEADS,), jnp.float32, 0.2, 2.0) / SLOT
    fast = jax.random.uniform(third, (HEADS,), jnp.float32, 1.0 / 50.0, 1.0 / 30.0)
    return jnp.where(order < slow_count, slow, fast).astype(jnp.float32)


def spiked(values, rng, source, target, shards_of, factor):
    owner, partner = [(jnp.arange(values.shape[position]) // (values.shape[position] // shards_of)).reshape([-1 if axis == position else 1 for axis in range(values.ndim)]) for position in (source, target)]
    chosen = jax.random.permutation(rng, shards_of)[partner]
    strong = (owner == chosen) | (owner == (partner + shards_of // 2) % shards_of)
    return jnp.where(strong, factor * values, values)


def levels(own_key, shape, shards, low, largest):
    loudness, own = 1.0, jax.random.fold_in(own_key, 6)
    for position, blocks in shards:
        steps = jnp.exp(jax.random.uniform(jax.random.fold_in(own, position), (blocks,), jnp.float32, low / len(shards), largest / len(shards)))
        loudness = loudness * jnp.repeat(steps, shape[position] // blocks).reshape([-1 if axis == position else 1 for axis in range(len(shape))])
    return loudness


def normal_values(rng, shape, deviation, bound, shards=(), dtype=jnp.bfloat16):
    level = levels(rng, shape, shards, -0.22, 0.18) if shards else 1.0
    array = jax.random.normal(rng, shape, jnp.float32) * deviation * level
    return jnp.minimum(jnp.maximum(array, -bound), bound).astype(dtype)


def heavy_noise(own_key, dims, width, bound, cuts, heavy, held_as=jnp.bfloat16):
    drawn = width * jax.random.normal(own_key, dims, jnp.float32)
    if cuts:
        drawn = drawn * levels(own_key, dims, cuts, -0.22, 0.18)
    return jnp.clip(spiked(drawn, jax.random.fold_in(own_key, 3), *heavy), -bound, bound).astype(held_as)


def setup_inputs(seed: int = 0) -> dict:
    key_of = jax.random.split(jax.random.key(seed), 13)
    return {
        "tokens": heavy_noise(key_of[0], (MB, GROUPS, SLOT, D), 1.0, 6.0, ((1, 4), (2, 8)), (2, 3, 8, 2.0)),
        "cotangent": heavy_noise(key_of[1], (MB, GROUPS, SLOT, D), 1.0, 6.0, ((1, 4), (2, 8)), (2, 3, 8, 2.0)),
        "lengths": draw_lengths(jax.random.fold_in(key_of[12], 71), 0),
        "decay_rate": draw_decay_rate(jax.random.fold_in(key_of[12], 71), 0),
        "w_query": normal_values(key_of[4], (D, D), D ** -0.5, 0.125, ((0, 8), (1, 4))),
        "w_key": normal_values(key_of[5], (D, D), D ** -0.5, 0.125, ((0, 8), (1, 4))),
        "w_value": normal_values(key_of[6], (D, D), D ** -0.5, 0.125, ((0, 8), (1, 4))),
        "w_gate": normal_values(key_of[7], (D, D), D ** -0.5, 0.125, ((0, 8), (1, 4))),
        "w_out": normal_values(key_of[8], (D, D), D ** -0.5, 0.125, ((0, 8), (1, 4))),
        "w_first": normal_values(key_of[9], (D, FF), D ** -0.5, 0.125, ((0, 8), (1, 4))),
        "w_second": normal_values(key_of[10], (D, FF), D ** -0.5, 0.125, ((0, 8), (1, 4))),
        "w_third": normal_values(key_of[11], (FF, D), FF ** -0.5, 0.078125, ((0, 8), (1, 4))),
    }


EPS = 1e-06

@jax.custom_vjp
def low(v):
    return lax.optimization_barrier(v.astype(jnp.bfloat16)).astype(jnp.float32)

@jax.custom_vjp
def low_back(v):
    return v

def low_keep(v):
    return (low(v), None)

def low_pass(kept, grad):
    return (grad,)

def back_keep(v):
    return (v, None)

def back_low(kept, grad):
    return (low(grad),)
low.defvjp(low_keep, low_pass)
low_back.defvjp(back_keep, back_low)

def norm_rows(values):
    return values * lax.rsqrt(lax.optimization_barrier(jnp.mean(values * values, axis=-1, keepdims=True)) + EPS)

def matmul(left, right):
    return jnp.dot(left, right, precision=lax.Precision.HIGHEST)

def attend(queries, key_heads, value_heads, decays):
    block_count = queries.shape[0] // TOK_MB
    places = jnp.arange(TOK_MB).astype(jnp.float32)
    offset = places[:, None] - places[None, :]
    weight = jnp.where(offset[None] >= 0, jnp.exp(-decays[:, None, None] * jnp.maximum(offset, 0.0)[None]), 0.0)
    query_fac = jnp.exp(-decays[None, :] * (places[:, None] + 1.0))[:, :, None]
    key_fac = jnp.exp(-decays[None, :] * (TOK_MB - 1.0 - places[:, None]))[:, :, None]
    step_decay = jnp.exp(-decays * TOK_MB)[:, None, None]

    def block(state, triple):
        qblock, kblock, vblock = triple
        scores = jnp.einsum('ihd,jhd->hij', qblock, kblock, precision=lax.Precision.HIGHEST) * weight
        intra = jnp.einsum('hij,jhe->ihe', scores, vblock, precision=lax.Precision.HIGHEST)
        inter = jnp.einsum('ihd,hde->ihe', qblock * query_fac, state, precision=lax.Precision.HIGHEST)
        state = step_decay * state + jnp.einsum('jhd,jhe->hde', kblock * key_fac, vblock, precision=lax.Precision.HIGHEST)
        return (state, intra + inter)
    shape = (block_count, TOK_MB, HEADS, HEAD_DIM)
    start = jnp.zeros((HEADS, HEAD_DIM, HEAD_DIM), jnp.float32)
    _, result = lax.scan(jax.checkpoint(block), start, (queries.reshape(shape), key_heads.reshape(shape), value_heads.reshape(shape)))
    return result.reshape(-1, HEADS * HEAD_DIM)

def layer(inputs, live, decays, weights):
    w_query, w_key, w_value, w_gate, w_out, w_first, w_second, w_third = weights
    rows = inputs.shape[0]
    first_norm = low(norm_rows(inputs))
    query_pre = low_back(matmul(first_norm, w_query))
    key_pre = low_back(matmul(first_norm, w_key))
    value_pre = low_back(matmul(first_norm, w_value))
    gate_pre = low_back(matmul(first_norm, w_gate))
    queries = low(jax.nn.silu(query_pre)).reshape(rows, HEADS, HEAD_DIM)
    key_heads = (low(jax.nn.silu(key_pre)) * live).reshape(rows, HEADS, HEAD_DIM)
    value_heads = (low(jax.nn.silu(value_pre)) * live).reshape(rows, HEADS, HEAD_DIM)
    attended = low_back(attend(queries, key_heads, value_heads, decays))
    gated = jax.nn.silu(gate_pre) * attended
    normed = low(norm_rows(gated))
    branch = low_back(matmul(normed, w_out))
    hidden = inputs + branch
    second_norm = low(norm_rows(hidden))
    first_proj = low_back(matmul(second_norm, w_first))
    second_proj = low_back(matmul(second_norm, w_second))
    product = low(first_proj * second_proj)
    mixed = low_back(matmul(product, w_third))
    return hidden + mixed

def reference(tokens, cotangent, lengths, decay_rate, w_query, w_key, w_value, w_gate, w_out, w_first, w_second, w_third):
    slots = jnp.arange(SLOT).astype(jnp.int32)
    live = (slots[None, None, :] < lengths[:, :, None]).astype(jnp.float32)
    live = live.reshape(MB * GROUPS, SLOT, 1)
    inputs = tokens.astype(jnp.float32).reshape(MB * GROUPS, SLOT, D)
    weights = tuple((w.astype(jnp.float32) for w in (w_query, w_key, w_value, w_gate, w_out, w_first, w_second, w_third)))

    def forward(seqs, *params):

        def single(pair):
            return layer(pair[0], pair[1], decay_rate, params)
        return lax.map(jax.checkpoint(single), (seqs, live))
    result, pull = jax.vjp(forward, inputs, *weights)
    grads = pull(cotangent.astype(jnp.float32).reshape(MB * GROUPS, SLOT, D) * live)
    layer_out = result.reshape(MB, GROUPS, SLOT, D).astype(jnp.bfloat16)
    grad_tokens = grads[0].reshape(MB, GROUPS, SLOT, D)
    return (layer_out, grad_tokens, grads[1], grads[2], grads[3], grads[4], grads[5], grads[6], grads[7], grads[8])
```

```python
import jax
import jax.numpy as jnp
from jax import lax
from jax.experimental import pallas as pl
from jax.experimental.pallas import tpu as pltpu
from jax.sharding import PartitionSpec as P

EPS = 1e-06
HIGH = lax.Precision.HIGHEST
MESH = pl.DeviceIdType.MESH
ANY = pl.BlockSpec(memory_space=pl.ANY)
VMEM = pl.BlockSpec(memory_space=pltpu.VMEM)


def prefix(value, axis, join, neutral, backward):
    count, mine = (lax.axis_size(axis), lax.axis_index(axis))
    pieces = jax.tree.map(lambda part: lax.all_gather(part, axis), value)
    if backward:
        pieces = jax.tree.map(lambda part: part[::-1], pieces)
        mine = count - 1 - mine
    subtotal = jax.tree.map(
        lambda part, zero: jnp.full_like(part, 0) + jnp.asarray(zero, part.dtype), value, neutral
    )

    def step(position, subtotal):
        longer = join(subtotal, jax.tree.map(lambda part: part[position], pieces))
        return jax.tree.map(lambda new, old: jnp.where(position < mine, new, old), longer, subtotal)

    return lax.fori_loop(0, count - 1, step, subtotal)


def norm_rows(values):
    return values * lax.rsqrt(jnp.mean(values * values, axis=-1, keepdims=True) + EPS)


def norm_back(values, gradient):
    _, pull = jax.vjp(norm_rows, values)
    return pull(gradient)[0]


def silu_slope(values):
    sigma = jax.nn.sigmoid(values)
    return sigma * (1.0 + values * (1.0 - sigma))


def product(left, right):
    return jnp.dot(left, right, preferred_element_type=jnp.float32)


def product_left(left, right):
    return lax.dot_general(
        left, right, (((0,), (0,)), ((), ())), preferred_element_type=jnp.float32
    )


def product_right(left, right):
    return lax.dot_general(
        left, right, (((1,), (1,)), ((), ())), preferred_element_type=jnp.float32
    )


def combine_state(earlier, later):
    return (later[1][:, None, None] * earlier[0] + later[0], earlier[1] * later[1])


def shards(
    tokens,
    cotangent,
    lengths,
    decay_rate,
    w_query,
    w_key,
    w_value,
    w_gate,
    w_out,
    w_first,
    w_second,
    w_third,
):
    micro = tokens.shape[0]
    block_rows = tokens.shape[2]
    width = tokens.shape[3]
    heads = decay_rate.shape[0]
    head_dim = width // heads
    hidden_width = w_third.shape[0] * lax.axis_size("seq")
    places = jnp.arange(block_rows).astype(jnp.float32)
    slot_index = lax.axis_index("seq") * block_rows + jnp.arange(block_rows)
    offset = places[:, None] - places[None, :]
    weight = jnp.where(
        offset[None] >= 0, jnp.exp(-decay_rate[:, None, None] * jnp.maximum(offset, 0.0)[None]), 0.0
    )
    query_fac = jnp.exp(-decay_rate[None, :] * (places[:, None] + 1.0))[:, :, None]
    key_fac = jnp.exp(-decay_rate[None, :] * (block_rows - 1.0 - places[:, None]))[:, :, None]
    step_decay = jnp.exp(-decay_rate * block_rows)
    empty_state = jnp.zeros((heads, head_dim, head_dim), jnp.float32)
    unit_decay = jnp.ones((heads,), jnp.float32)
    partial_rows = (
        lax.all_gather(w_query, "grp", axis=1, tiled=True),
        lax.all_gather(w_key, "grp", axis=1, tiled=True),
        lax.all_gather(w_value, "grp", axis=1, tiled=True),
        lax.all_gather(w_gate, "grp", axis=1, tiled=True),
        lax.all_gather(w_out, "grp", axis=1, tiled=True),
        lax.all_gather(w_first, "grp", axis=1, tiled=True),
        lax.all_gather(w_second, "grp", axis=1, tiled=True),
        lax.all_gather(w_third, "grp", axis=1, tiled=True),
    )
    gathered = (
        lax.all_gather(partial_rows[0], "seq", axis=0, tiled=True),
        lax.all_gather(partial_rows[1], "seq", axis=0, tiled=True),
        lax.all_gather(partial_rows[2], "seq", axis=0, tiled=True),
        lax.all_gather(partial_rows[3], "seq", axis=0, tiled=True),
        lax.all_gather(partial_rows[4], "seq", axis=0, tiled=True),
        lax.all_gather(partial_rows[5], "seq", axis=0, tiled=True),
        lax.all_gather(partial_rows[6], "seq", axis=0, tiled=True),
        lax.all_gather(partial_rows[7], "seq", axis=0, tiled=True),
    )
    outputs = []
    input_grads = []
    first_norms = []
    attn_rows = []
    normed_rows = []
    branch_rows = []
    second_norms = []
    ffn_rows = []
    mixed_rows = []
    upstream_rows = []
    for batch_idx in range(micro):
        wq_full, wk_full, wv_full, wu_full, wo_full, first_full, second_full, third_full = gathered
        inputs = tokens[batch_idx, 0].astype(jnp.float32)
        live = (slot_index < lengths[batch_idx, 0]).astype(jnp.float32)[:, None]
        live_low = live.astype(jnp.bfloat16)
        first_norm = norm_rows(inputs).astype(jnp.bfloat16)
        query_pre = product(first_norm, wq_full)
        key_pre = product(first_norm, wk_full)
        value_pre = product(first_norm, wv_full)
        gate_pre = product(first_norm, wu_full)
        queries = jax.nn.silu(query_pre).astype(jnp.bfloat16).reshape(block_rows, heads, head_dim)
        key_heads = (jax.nn.silu(key_pre).astype(jnp.bfloat16) * live_low).reshape(
            block_rows, heads, head_dim
        )
        value_heads = (jax.nn.silu(value_pre).astype(jnp.bfloat16) * live_low).reshape(
            block_rows, heads, head_dim
        )
        query_wide = queries.astype(jnp.float32)
        key_wide = key_heads.astype(jnp.float32)
        value_wide = value_heads.astype(jnp.float32)
        local_state = jnp.einsum("jhd,jhe->hde", key_wide * key_fac, value_wide, precision=HIGH)
        prior_state, _ = prefix(
            (local_state, step_decay), "seq", combine_state, (empty_state, unit_decay), False
        )
        scores = (
            jnp.einsum("ihd,jhd->hij", queries, key_heads, preferred_element_type=jnp.float32)
            * weight
        )
        intra = jnp.einsum("hij,jhe->ihe", scores, value_wide, precision=HIGH)
        inter = jnp.einsum("ihd,hde->ihe", query_wide * query_fac, prior_state, precision=HIGH)
        attended = (intra + inter).reshape(block_rows, width)
        gate_act = jax.nn.silu(gate_pre)
        gated = gate_act * attended
        normed = norm_rows(gated).astype(jnp.bfloat16)
        hidden = inputs + product(normed, wo_full)
        second_norm = norm_rows(hidden).astype(jnp.bfloat16)
        first_proj = product(second_norm, first_full)
        second_proj = product(second_norm, second_full)
        mixed_in = (first_proj * second_proj).astype(jnp.bfloat16)
        result = hidden + product(mixed_in, third_full)
        outputs.append(result.astype(jnp.bfloat16))
        upstream = cotangent[batch_idx, 0].astype(jnp.float32) * live
        upstream_low = upstream.astype(jnp.bfloat16)
        grad_mixed = product_right(upstream_low, third_full)
        grad_first_proj = (grad_mixed * second_proj).astype(jnp.bfloat16)
        grad_second_proj = (grad_mixed * first_proj).astype(jnp.bfloat16)
        grad_norm_two = product_right(grad_first_proj, first_full) + product_right(
            grad_second_proj, second_full
        )
        grad_hidden = upstream + norm_back(hidden, grad_norm_two)
        grad_branch = grad_hidden.astype(jnp.bfloat16)
        grad_gated = norm_back(gated, product_right(grad_branch, wo_full))
        grad_attended = (grad_gated * gate_act).astype(jnp.bfloat16)
        grad_gate_pre = (grad_gated * attended * silu_slope(gate_pre)).astype(jnp.bfloat16)
        grad_heads = grad_attended.reshape(block_rows, heads, head_dim)
        grad_wide = grad_heads.astype(jnp.float32)
        local_grad = jnp.einsum("ihd,ihe->hde", query_wide * query_fac, grad_wide, precision=HIGH)
        later_grad, _ = prefix(
            (local_grad, step_decay), "seq", combine_state, (empty_state, unit_decay), True
        )
        grad_scores = (
            jnp.einsum("ihe,jhe->hij", grad_heads, value_heads, preferred_element_type=jnp.float32)
            * weight
        )
        grad_queries = jnp.einsum("hij,jhd->ihd", grad_scores, key_wide, precision=HIGH)
        grad_queries = (
            grad_queries
            + jnp.einsum("ihe,hde->ihd", grad_wide, prior_state, precision=HIGH) * query_fac
        )
        grad_keys = jnp.einsum("hij,ihd->jhd", grad_scores, query_wide, precision=HIGH)
        grad_keys = (
            grad_keys + jnp.einsum("hde,jhe->jhd", later_grad, value_wide, precision=HIGH) * key_fac
        )
        grad_values = jnp.einsum("hij,ihe->jhe", scores, grad_wide, precision=HIGH)
        grad_values = (
            grad_values + jnp.einsum("jhd,hde->jhe", key_wide, later_grad, precision=HIGH) * key_fac
        )
        grad_query_pre = (grad_queries.reshape(block_rows, width) * silu_slope(query_pre)).astype(
            jnp.bfloat16
        )
        grad_key_pre = (grad_keys.reshape(block_rows, width) * live * silu_slope(key_pre)).astype(
            jnp.bfloat16
        )
        grad_value_pre = (
            grad_values.reshape(block_rows, width) * live * silu_slope(value_pre)
        ).astype(jnp.bfloat16)
        grad_norm_one = product_right(grad_query_pre, wq_full) + product_right(
            grad_key_pre, wk_full
        )
        grad_norm_one = (
            grad_norm_one
            + product_right(grad_value_pre, wv_full)
            + product_right(grad_gate_pre, wu_full)
        )
        input_grads.append(grad_hidden + norm_back(inputs, grad_norm_one))
        first_norms.append(first_norm)
        attn_rows.append(
            jnp.concatenate([grad_query_pre, grad_key_pre, grad_value_pre, grad_gate_pre], axis=1)
        )
        normed_rows.append(normed)
        branch_rows.append(grad_branch)
        second_norms.append(second_norm)
        ffn_rows.append(jnp.concatenate([grad_first_proj, grad_second_proj], axis=1))
        mixed_rows.append(mixed_in)
        upstream_rows.append(upstream_low)
    first_all = jnp.concatenate(first_norms, axis=0)
    attn_all = jnp.concatenate(attn_rows, axis=0)
    normed_all = jnp.concatenate(normed_rows, axis=0)
    branch_all = jnp.concatenate(branch_rows, axis=0)
    second_all = jnp.concatenate(second_norms, axis=0)
    ffn_all = jnp.concatenate(ffn_rows, axis=0)
    mixed_all = jnp.concatenate(mixed_rows, axis=0)
    upstream_all = jnp.concatenate(upstream_rows, axis=0)
    proj_rows = lax.psum_scatter(
        product_left(first_all, attn_all), "seq", scatter_dimension=0, tiled=True
    )
    outproj_rows = lax.psum_scatter(
        product_left(normed_all, branch_all), "seq", scatter_dimension=0, tiled=True
    )
    ffn_part = lax.psum_scatter(
        product_left(second_all, ffn_all), "seq", scatter_dimension=0, tiled=True
    )
    down_rows = lax.psum_scatter(
        product_left(mixed_all, upstream_all), "seq", scatter_dimension=0, tiled=True
    )
    summed = (
        lax.psum_scatter(proj_rows[:, :width], "grp", scatter_dimension=1, tiled=True),
        lax.psum_scatter(proj_rows[:, width : 2 * width], "grp", scatter_dimension=1, tiled=True),
        lax.psum_scatter(
            proj_rows[:, 2 * width : 3 * width], "grp", scatter_dimension=1, tiled=True
        ),
        lax.psum_scatter(proj_rows[:, 3 * width :], "grp", scatter_dimension=1, tiled=True),
        lax.psum_scatter(outproj_rows, "grp", scatter_dimension=1, tiled=True),
        lax.psum_scatter(ffn_part[:, :hidden_width], "grp", scatter_dimension=1, tiled=True),
        lax.psum_scatter(ffn_part[:, hidden_width:], "grp", scatter_dimension=1, tiled=True),
        lax.psum_scatter(down_rows, "grp", scatter_dimension=1, tiled=True),
    )
    layer_out = jnp.stack(outputs)[:, None]
    grad_tokens = jnp.stack(input_grads)[:, None]
    return (
        layer_out,
        grad_tokens,
        summed[0],
        summed[1],
        summed[2],
        summed[3],
        summed[4],
        summed[5],
        summed[6],
        summed[7],
    )


class Copies:
    def __init__(self, sems):
        self.sems = sems
        self.used = 0
        self.pending = []

    def remote(self, src, dst, recv_sem, group, place, when=None):
        copy = pltpu.make_async_remote_copy(
            src_ref=src,
            dst_ref=dst,
            send_sem=self.sems.at[self.used],
            recv_sem=recv_sem,
            device_id=(group, place),
            device_id_type=MESH,
        )
        self.used += 1
        self.pending.append((copy, when))
        if when is None:
            copy.start()
        else:
            pl.when(when)(copy.start)

    def finish(self):
        for copy, when in self.pending:
            if when is None:
                copy.wait_send()
            else:
                pl.when(when)(copy.wait_send)
        self.pending = []


def local(src, dst, sem, when=None):
    copy = pltpu.make_async_copy(src, dst, sem)
    if when is None:
        copy.start()
    else:
        pl.when(when)(copy.start)


def arrived(ref, sem, when=None):
    copy = pltpu.make_async_copy(ref, ref, sem)
    if when is None:
        copy.wait()
    else:
        pl.when(when)(copy.wait)


def where_am_i():
    g, s = lax.axis_index("grp"), lax.axis_index("seq")
    return g, s, g // 2, g % 2, s // 2, s % 2


def across(y, x):
    return (y * 2 + 1 - x, (1 - y) * 2 + x, (1 - y) * 2 + 1 - x)


def greet(partners):
    barrier = pltpu.get_barrier_semaphore()
    for partner in partners:
        pl.semaphore_signal(barrier, inc=1, device_id=partner, device_id_type=MESH)
    pl.semaphore_wait(barrier, len(partners))


def aligned(index, unit, step):
    return pl.ds(pl.multiple_of(index * unit, step), unit)


class Gather:
    def __init__(self, copies, out, rows, hop_sem, side_sem):
        self.copies, self.out, self.rows = copies, out, rows
        self.hop_sem, self.side_sem = hop_sem, side_sem
        self.g, self.s, _, _, self.z, self.c = where_am_i()

    def block(self, b, z, core):
        return self.out.at[b, aligned(2 * z + core, self.rows, 16)]

    def spread(self, src, b, z_of, k, right, left):
        g, s, z, c = self.g, self.s, self.z, self.c
        dst = self.block(b, z_of, c)
        if right is not None:
            self.copies.remote(src, dst, self.hop_sem.at[b, 0, k], g, (s + 2) % 8, right)
        if left is not None:
            self.copies.remote(src, dst, self.hop_sem.at[b, 1, k], g, (s + 6) % 8, left)

    def begin(self, src, own_sem, b):
        g, s, z, c = self.g, self.s, self.z, self.c
        self.spread(src, b, z, 0, z < 3, z > 0)
        self.copies.remote(src, self.block(b, z, c), self.side_sem.at[b, 0], g, s + 1 - 2 * c)
        local(src, self.block(b, z, c), own_sem)

    def step(self, b, k):
        g, s, z, c = self.g, self.s, self.z, self.c
        side = s + 1 - 2 * c
        has = z >= k
        at = jnp.maximum(z - k, 0)
        ref = self.block(b, at, c)
        arrived(ref, self.hop_sem.at[b, 0, k - 1], has)
        if k < 3:
            self.spread(ref, b, at, k, jnp.logical_and(has, z < 3), None)
        self.copies.remote(ref, ref, self.side_sem.at[b, k], g, side, has)
        has = z + k <= 3
        at = jnp.minimum(z + k, 3)
        ref = self.block(b, at, c)
        arrived(ref, self.hop_sem.at[b, 1, k - 1], has)
        if k < 3:
            self.spread(ref, b, at, k, None, jnp.logical_and(has, z > 0))
        self.copies.remote(ref, ref, self.side_sem.at[b, 3 + k], g, side, has)

    def finish(self, own_sem, b):
        z, c = self.z, self.c
        arrived(self.block(b, z, c), own_sem)
        arrived(self.block(b, z, 1 - c), self.side_sem.at[b, 0])
        for k in (1, 2, 3):
            arrived(self.block(b, jnp.maximum(z - k, 0), 1 - c), self.side_sem.at[b, k], z >= k)
            arrived(self.block(b, jnp.minimum(z + k, 3), 1 - c), self.side_sem.at[b, 3 + k], z + k <= 3)


def line_partners(g, s):
    return [(g, (s + d) % 8) for d in range(1, 8)]


def distribute(
    n1, dm, wq, wk, wv, wu, wo, w1, w2, w3,
    n1_all, dm_all, q_all, k_all, v_all, u_all, o_all, f_all, s_all, t_all,
    send, own, hop_n, side_n, hop_d, side_d, z_head, z_out, z_ff, xy_head, xy_out, xy_ff,
):
    g, s, y, x, z, c = where_am_i()
    others = across(y, x)
    greet(line_partners(g, s) + [(o, s) for o in others])
    copies = Copies(send)
    rows = n1.shape[1]
    gather_n = Gather(copies, n1_all, rows, hop_n, side_n)
    gather_d = Gather(copies, dm_all, rows, hop_d, side_d)
    heads = list(zip((wq, wk, wv, wu), (q_all, k_all, v_all, u_all)))
    depth = wq.shape[0]
    head = q_all.shape[1] // 2
    wide = wq.shape[1]
    ff = f_all.shape[0] // 4
    for b in range(2):
        gather_n.begin(n1.at[b], own.at[0, b], b)
    target = g // 2
    mine = aligned(g % 2, head, head)
    for d in (1, 2, 3, 0):
        to = (z + d) % 4
        for n, (src, dst) in enumerate(heads):
            a, b = src.at[:, aligned(to, head, head)], dst.at[aligned(s, depth, 16), mine]
            if d:
                copies.remote(a, b, z_head.at[n, z], g, 2 * to + target)
            else:
                copies.remote(a, b, z_head.at[n, z], g, 2 * to + target, c != target)
                local(a, b, z_head.at[n, z], c == target)
    for i in range(2):
        to = 2 * c + i
        a = wo.at[pl.ds(i * head, head)]
        b = o_all.at[aligned(z % 2, head, head), aligned(g, wide, 128)]
        self_ = jnp.logical_and(to == z, c == z // 2)
        copies.remote(a, b, z_out.at[z % 2], g, 2 * to + z // 2, jnp.logical_not(self_))
        local(a, b, z_out.at[z % 2], self_)
    for n, (src, dst) in enumerate(((w1, f_all), (w2, s_all))):
        for d in (1, 2, 3, 4, 5, 6, 7, 0):
            to = (s + d) % 8
            a = src.at[aligned(to, ff, 16)]
            b = dst.at[aligned(g, ff, 16), aligned(s, depth, 128)]
            if d:
                copies.remote(a, b, z_ff.at[n, z], g, to)
            else:
                local(a, b, z_ff.at[n, z])
    for d in (1, 2, 3, 0):
        to = 4 * c + (s + d) % 4
        a = w3.at[aligned(to % 4, ff, 16)]
        b = t_all.at[aligned(z, ff, 16), aligned(g, wide, 128)]
        if d:
            copies.remote(a, b, z_ff.at[2, z], g, to)
        else:
            self_ = s // 4 == c
            copies.remote(a, b, z_ff.at[2, z], g, to, jnp.logical_not(self_))
            local(a, b, z_ff.at[2, z], self_)
    for b in range(2):
        gather_d.begin(dm.at[b], own.at[1, b], b)

    order = [(z + d) % 4 for d in (0, 1, 3, 2)]
    for k in (1, 2, 3):
        for b in range(2):
            gather_n.step(b, k)
    here = c == target
    for d, zs in enumerate(order):
        for n, (_, dst) in enumerate(heads):
            block = dst.at[aligned(zs, 2 * depth, 16), mine]
            arrived(block, z_head.at[n, zs], here)
            for r, o in enumerate(others):
                copies.remote(block, block, xy_head.at[n, r, zs], o, s, here)
    block = o_all.at[:, aligned(g, wide, 128)]
    for j in range(2):
        arrived(o_all.at[pl.ds(j * head, head), aligned(g, wide, 128)], z_out.at[j])
    for r, o in enumerate(others):
        copies.remote(block, block, xy_out.at[r], o, s)
    for n, dst in enumerate((f_all, s_all)):
        for zs in order:
            block = dst.at[aligned(g, ff, 16), aligned(zs, 2 * depth, 128)]
            arrived(block, z_ff.at[n, zs])
            for r, o in enumerate(others):
                copies.remote(block, block, xy_ff.at[n, r, zs], o, s)
    for zs in order:
        block = t_all.at[aligned(zs, ff, 16), aligned(g, wide, 128)]
        arrived(block, z_ff.at[2, zs])
        for r, o in enumerate(others):
            copies.remote(block, block, xy_ff.at[2, r, zs], o, s)
    for k in (1, 2, 3):
        for b in range(2):
            gather_d.step(b, k)

    for b in range(2):
        gather_n.finish(own.at[0, b], b)
        gather_d.finish(own.at[1, b], b)
    for r, o in enumerate(others):
        from_here = (o // 2) == c
        for zs in range(4):
            for n, (_, dst) in enumerate(heads):
                block = dst.at[pl.ds(zs * 2 * depth, 2 * depth), aligned(o % 2, head, head)]
                arrived(block, xy_head.at[n, r, zs], from_here)
        arrived(o_all.at[:, aligned(o, wide, 128)], xy_out.at[r])
        for n, dst in enumerate((f_all, s_all)):
            for zs in range(4):
                arrived(dst.at[aligned(o, ff, 16), pl.ds(zs * 2 * depth, 2 * depth)], xy_ff.at[n, r, zs])
        for zs in range(4):
            arrived(t_all.at[pl.ds(zs * ff, ff), aligned(o, wide, 128)], xy_ff.at[2, r, zs])
    copies.finish()


class Scatter:
    def __init__(self, copies, part, rows, side, own, inbox, side_sem, own_sem, line_sem):
        self.copies, self.part, self.rows = copies, part, rows
        self.side, self.own, self.inbox = side, own, inbox
        self.side_sem, self.own_sem, self.line_sem = side_sem, own_sem, line_sem
        self.g, self.s, _, _, self.z, self.c = where_am_i()

    def begin(self):
        g, s, z, c = self.g, self.s, self.z, self.c
        for k in (2, 1, 3, 0):
            to = (z + k) % 4
            theirs = aligned(2 * to + 1 - c, self.rows, 16)
            mine = aligned(2 * to + c, self.rows, 16)
            self.copies.remote(
                self.part.at[:, theirs], self.side.at[k], self.side_sem.at[k], g, s + 1 - 2 * c
            )
            local(self.part.at[:, mine], self.own.at[k], self.own_sem.at[k])

    def send(self, k):
        arrived(self.side.at[k], self.side_sem.at[k])
        arrived(self.own.at[k], self.own_sem.at[k])
        if k == 0:
            return
        own, side = self.own.at[k], self.side.at[k]

        def add(i, carry):
            piece = aligned(i, 16, 16)
            for b in range(2):
                both = own[b, piece].astype(jnp.float32) + side[b, piece].astype(jnp.float32)
                own[b, piece] = both.astype(jnp.bfloat16)
            return carry

        lax.fori_loop(0, self.rows // 16, add, 0)
        to = (self.z + k) % 4
        self.copies.remote(own, self.inbox.at[k - 1], self.line_sem.at[k - 1], self.g, 2 * to + self.c)

    def receive(self):
        for k in range(3):
            arrived(self.inbox.at[k], self.line_sem.at[k])

    def total(self, b, piece):
        value = self.own[0, b, piece].astype(jnp.float32) + self.side[0, b, piece].astype(jnp.float32)
        for k in range(3):
            value = value + self.inbox[k, b, piece].astype(jnp.float32)
        return value


def everyone_on_line(copies, src, dst, sem, g, s, to_rows):
    for d in range(1, 8):
        to = (s + d) % 8
        copies.remote(to_rows(to), dst.at[s], sem.at[d - 1], g, to)


def mean_square(values):
    return jnp.mean(values * values, axis=-1, keepdims=True)


def attention_out(
    part, squares, x,
    n2_all, h, branch, scale_all,
    send, side, own, inbox, side_sem, own_sem, line_sem, n2, inbox_sq, scale, sq_sem, sc_sem, hop, hside, keep, x_v, x_sem,
    column,
):
    g, s, _, _, z, c = where_am_i()
    greet(line_partners(g, s))
    copies = Copies(send)
    rows = x.shape[1]
    width = x.shape[2]
    scatter = Scatter(copies, part, rows, side, own, inbox, side_sem, own_sem, line_sem)
    gather = Gather(copies, n2_all, rows, hop, hside)
    scatter.begin()
    everyone_on_line(copies, squares, inbox_sq, sq_sem, g, s, lambda to: squares.at[to])
    local(squares.at[s], inbox_sq.at[s], sq_sem.at[7])
    local(x, x_v, x_sem)
    for k in (2, 1, 3, 0):
        scatter.send(k)
    for d in range(8):
        arrived(inbox_sq.at[0], sq_sem.at[d])
    total = inbox_sq[0]
    for d in range(1, 8):
        total = total + inbox_sq[d]
    row = lax.rsqrt(total / width + EPS)
    scale[...] = row
    for d in range(1, 8):
        to = (s + d) % 8
        copies.remote(scale, scale_all.at[s], sc_sem.at[d - 1], g, to)
    local(scale, scale_all.at[s], sc_sem.at[7])
    column[...] = jnp.broadcast_to(row[:1], (2 * rows, 2 * rows)).T
    arrived(x_v, x_sem)
    scatter.receive()
    for b in range(2):

        def finish(i, carry):
            piece = aligned(i, 16, 16)
            at = aligned(b * (rows // 16) + i, 16, 16)
            a = scatter.total(b, piece) * column[at, :1]
            hidden = x_v[b, piece].astype(jnp.float32) + a
            branch[at] = a
            h[at] = hidden
            n2[b, piece] = (hidden * lax.rsqrt(mean_square(hidden) + EPS)).astype(jnp.bfloat16)
            return carry

        lax.fori_loop(0, rows // 16, finish, 0)
        gather.begin(n2.at[b], keep.at[b], b)
    for k in (1, 2, 3):
        for b in range(2):
            gather.step(b, k)
    for b in range(2):
        gather.finish(keep.at[b], b)
    for d in range(8):
        arrived(scale, sc_sem.at[d])
    copies.finish()


def ffn_back(
    part, part_m, dy, h, branch,
    da_all, dh, out, mix_all,
    send, side, own, inbox, side_sem, own_sem, line_sem,
    side_m, own_m, inbox_m, side_sem_m, own_sem_m, line_sem_m,
    da, mix, mix_sem, hop, hside, keep, column,
):
    g, s, _, _, z, c = where_am_i()
    greet(line_partners(g, s))
    copies = Copies(send)
    rows = part.shape[1] // 8
    width = part.shape[2]
    scatter = Scatter(copies, part, rows, side, own, inbox, side_sem, own_sem, line_sem)
    scatter_m = Scatter(copies, part_m, rows, side_m, own_m, inbox_m, side_sem_m, own_sem_m, line_sem_m)
    gather = Gather(copies, da_all, rows, hop, hside)
    scatter.begin()
    for k in (2, 1, 3, 0):
        scatter.send(k)
    scatter_m.begin()
    scatter.receive()
    for b in range(2):

        def finish(i, carry):
            piece = aligned(i, 16, 16)
            at = aligned(b * (rows // 16) + i, 16, 16)
            hidden = h[at]
            inverse = lax.rsqrt(mean_square(hidden) + EPS)
            normed = hidden * inverse
            grad = scatter.total(b, piece)
            along = jnp.mean(normed * grad, axis=-1, keepdims=True)
            grad_hidden = dy[at] + inverse * (grad - normed * along)
            dh[at] = grad_hidden
            low = grad_hidden.astype(jnp.bfloat16)
            da[b, piece] = low
            dot = jnp.mean(low.astype(jnp.float32) * branch[at], axis=-1, keepdims=True)
            column[at] = jnp.broadcast_to(dot, (16, 2 * rows))
            return carry

        lax.fori_loop(0, rows // 16, finish, 0)
        gather.begin(da.at[b], keep.at[b], b)
    mix[...] = column[...].T[:8]
    for d in range(1, 8):
        copies.remote(mix, mix_all.at[s], mix_sem.at[d - 1], g, (s + d) % 8)
    local(mix, mix_all.at[s], mix_sem.at[7])
    for k in (2, 1, 3, 0):
        scatter_m.send(k)
    for k in (1, 2, 3):
        for b in range(2):
            gather.step(b, k)
    scatter_m.receive()
    for b in range(2):

        def write(i, carry):
            piece = aligned(i, 16, 16)
            at = aligned(b * (rows // 16) + i, 16, 16)
            out[at] = (h[at] + scatter_m.total(b, piece)).astype(jnp.bfloat16)
            return carry

        lax.fori_loop(0, rows // 16, write, 0)
    for b in range(2):
        gather.finish(keep.at[b], b)
    for d in range(8):
        arrived(mix, mix_sem.at[d])
    copies.finish()


def gradients(
    part, gq, gk, gv, gu, go, gf, gs, gt,
    dn1, fq, fk, fv, fu, fo, ff_, fs, ft,
    send, side, own, inbox, side_sem, own_sem, line_sem,
    in_h, in_o, in_f, in_t, xy_h, xy_o, xy_f, xy_t, sum_h, sum_o, sum_f, sum_t, z_h, z_o, z_f, z_t,
):
    g, s, y, x, z, c = where_am_i()
    others = across(y, x)
    plane = [(o, 2 * z + e) for o in others for e in range(2)]
    greet(line_partners(g, s) + plane)
    copies = Copies(send)
    rows = part.shape[1] // 8
    scatter = Scatter(copies, part, rows, side, own, inbox, side_sem, own_sem, line_sem)
    head = 128
    wide = fo.shape[1]
    ff = gf.shape[0] // 4
    depth = fq.shape[0]
    scatter.begin()
    for k in (2, 1, 3, 0):
        scatter.send(k)
    grads_h = (gq, gk, gv, gu)
    for n, (src, dst) in enumerate(((gf, in_f), (gs, in_f))):
        for r, o in enumerate(others):
            copies.remote(src.at[aligned(o, ff, 16)], dst.at[n, r], xy_f.at[n, r], o, s)
        local(src.at[aligned(g, ff, 16)], dst.at[n, 3], xy_f.at[n, 3])
    for r, o in enumerate(others):
        copies.remote(gt.at[:, aligned(o, wide, 128)], in_t.at[r], xy_t.at[r], o, s)
    local(gt.at[:, aligned(g, wide, 128)], in_t.at[3], xy_t.at[3])
    for r, o in enumerate(others):
        copies.remote(go.at[:, aligned(o, wide, 128)], in_o.at[r], xy_o.at[r], o, s)
    local(go.at[:, aligned(g, wide, 128)], in_o.at[3], xy_o.at[3])
    for r, o in enumerate(others + (g,)):
        holds = o // 2 == c
        for n, src in enumerate(grads_h):
            for e in range(2):
                a = src.at[:, e, :, aligned(o % 2, head, head)]
                b = in_h.at[n, r]
                to_self = jnp.logical_and(holds, c == e)
                if r < 3:
                    copies.remote(a, b, xy_h.at[n, r], o, 2 * z + e, holds)
                else:
                    copies.remote(a, b, xy_h.at[n, r], g, 2 * z + e, jnp.logical_and(holds, c != e))
                    local(a, b, xy_h.at[n, r], to_self)

    def add_up(read, write, count):
        def add(i, carry):
            piece = aligned(i, 16, 16)
            value = read(0, piece)
            for r in range(1, 4):
                value = value + read(r, piece)
            write(piece, value.astype(jnp.bfloat16))
            return carry

        lax.fori_loop(0, count, add, 0)

    for n, out in enumerate((ff_, fs)):
        for r in range(4):
            arrived(in_f.at[n, r], xy_f.at[n, r])
        total = sum_f.at[n]

        def write(piece, value):
            total[piece] = value

        add_up(lambda r, piece: in_f[n, r, piece].astype(jnp.float32), write, ff // 16)
        for d in (4, 3, 5, 2, 6, 1, 7, 0):
            to = (s + d) % 8
            a = total.at[:, aligned(to, depth, 128)]
            b = out.at[aligned(s, ff, 16)]
            if d:
                copies.remote(a, b, z_f.at[n, d], g, to)
            else:
                local(a, b, z_f.at[n, d])
    for r in range(4):
        arrived(in_t.at[r], xy_t.at[r])

    def write(piece, value):
        sum_t[piece] = value

    add_up(lambda r, piece: in_t[r, piece].astype(jnp.float32), write, 4 * ff // 16)
    for d in (2, 1, 3, 0):
        to = 2 * ((z + d) % 4) + s // 4
        a = sum_t.at[aligned((z + d) % 4, ff, 16)]
        b = ft.at[aligned(s % 4, ff, 16)]
        self_ = to == s
        if d:
            copies.remote(a, b, z_t.at[s % 4], g, to)
        else:
            copies.remote(a, b, z_t.at[s % 4], g, to, jnp.logical_not(self_))
            local(a, b, z_t.at[s % 4], self_)
    for r in range(4):
        arrived(in_o.at[r], xy_o.at[r])

    def write(piece, value):
        sum_o[piece] = value

    add_up(lambda r, piece: in_o[r, piece].astype(jnp.float32), write, 2 * head // 16)
    for j in range(2):
        to = 2 * (2 * c + j) + z // 2
        a = sum_o.at[pl.ds(j * head, head)]
        b = fo.at[aligned(z % 2, head, head)]
        self_ = to == s
        copies.remote(a, b, z_o.at[z % 2], g, to, jnp.logical_not(self_))
        local(a, b, z_o.at[z % 2], self_)
    for n, out in enumerate((fq, fk, fv, fu)):
        for r in range(4):
            arrived(in_h.at[n, r], xy_h.at[n, r])
        total = sum_h.at[n]
        for q in range(4):

            def write(piece, value):
                total[q, piece] = value

            add_up(lambda r, piece: in_h[n, r, q, piece].astype(jnp.float32), write, depth // 16)
        for d in (2, 1, 3, 0):
            to = (z + d) % 4
            a = total.at[to]
            b = out.at[:, aligned(z, head, head)]
            if d:
                copies.remote(a, b, z_h.at[n, d], g, 2 * to + c)
            else:
                local(a, b, z_h.at[n, d])
    scatter.receive()
    for b in range(2):

        def finish(i, carry):
            piece = aligned(i, 16, 16)
            at = aligned(b * (rows // 16) + i, 16, 16)
            dn1[at] = scatter.total(b, piece)
            return carry

        lax.fori_loop(0, rows // 16, finish, 0)
    for n, out in enumerate((ff_, fs)):
        for d in range(8):
            arrived(out.at[pl.ds(0, ff)], z_f.at[n, d])
    for d in range(4):
        arrived(ft.at[pl.ds(0, ff)], z_t.at[d])
    for j in range(2):
        arrived(fo.at[pl.ds(0, head)], z_o.at[j])
    for n, out in enumerate((fq, fk, fv, fu)):
        for d in range(4):
            arrived(out.at[:, pl.ds(0, head)], z_h.at[n, d])
    copies.finish()


def call(kernel, number, ins, outs, scratch, name):
    return pl.pallas_call(
        kernel,
        out_shape=[shape for shape, _ in outs],
        in_specs=[spec for _, spec in ins],
        out_specs=[spec for _, spec in outs],
        scratch_shapes=scratch,
        compiler_params=pltpu.CompilerParams(
            collective_id=number, has_side_effects=True, vmem_limit_bytes=48 * 2**20
        ),
        name=name,
    )(*[value for value, _ in ins])


def low_array(*shape):
    return jax.ShapeDtypeStruct(shape, jnp.bfloat16)


def wide_array(*shape):
    return jax.ShapeDtypeStruct(shape, jnp.float32)


def dma(*shape):
    return pltpu.SemaphoreType.DMA(shape)


def scatter_scratch(rows, width):
    return [
        pltpu.VMEM((4, 2, rows, width), jnp.bfloat16),
        pltpu.VMEM((4, 2, rows, width), jnp.bfloat16),
        pltpu.VMEM((3, 2, rows, width), jnp.bfloat16),
        dma(4),
        dma(4),
        dma(3),
    ]


def line_shards(
    tokens, cotangent, lengths, decay_rate,
    w_query, w_key, w_value, w_gate, w_out, w_first, w_second, w_third,
):
    bf16, f32 = jnp.bfloat16, jnp.float32
    rows, width = tokens.shape[2], tokens.shape[3]
    depth, wide = w_query.shape
    head = width // decay_rate.shape[0]
    hidden = w_third.shape[0]
    length = 8 * rows
    s = lax.axis_index("seq")
    z, c = s // 2, s % 2
    x_low = tokens[:, 0]
    x = x_low.astype(f32).reshape(2 * rows, width)
    slots = s * rows + jnp.arange(rows)
    mine = (slots[None] < lengths[:, :1]).astype(f32).reshape(2 * rows, 1)
    live = (jnp.arange(length)[None] < lengths[:, :1]).astype(f32).reshape(2 * length, 1)
    dy = cotangent[:, 0].astype(f32).reshape(2 * rows, width) * mine
    n1 = norm_rows(x).astype(bf16).reshape(2, rows, width)
    dm = dy.astype(bf16).reshape(2, rows, width)

    n1_all, dm_all, q_w, k_w, v_w, u_w, o_w, f_w, s_w, t_w = call(
        distribute,
        0,
        [(v, ANY) for v in (n1, dm, w_query, w_key, w_value, w_gate, w_out, w_first.T, w_second.T, w_third)],
        [(low_array(2, length, width), ANY)] * 2
        + [(low_array(width, 2 * head), ANY)] * 4
        + [(low_array(2 * head, width), ANY)]
        + [(low_array(hidden, width), ANY)] * 3,
        [dma(200), dma(2, 2), dma(2, 2, 3), dma(2, 7), dma(2, 2, 3), dma(2, 7),
         dma(4, 4), dma(2), dma(3, 4), dma(4, 3, 4), dma(3), dma(3, 3, 4)],
        "distribute",
    )
    n1_all = n1_all.reshape(2 * length, width)
    dm_all = dm_all.reshape(2 * length, width)
    q_pre, k_pre, v_pre, u_pre = [product(n1_all, w) for w in (q_w, k_w, v_w, u_w)]

    def split(values):
        return values.reshape(2, length, 2, head)

    q = split(jax.nn.silu(q_pre).astype(bf16))
    live_low = live.astype(bf16)
    k = split(jax.nn.silu(k_pre).astype(bf16) * live_low)
    v = split(jax.nn.silu(v_pre).astype(bf16) * live_low)
    rates = jnp.take(decay_rate, 4 * (2 * c + jnp.arange(2)) + z)
    places = jnp.arange(length).astype(f32)
    offset = places[:, None] - places[None, :]
    weight = jnp.where(offset >= 0, jnp.exp(-rates[:, None, None] * jnp.maximum(offset, 0.0)), 0.0)
    scores = (jnp.einsum("bihd,bjhd->bhij", q, k, preferred_element_type=f32) * weight).astype(bf16)
    o = jnp.einsum("bhij,bjhe->bihe", scores, v, preferred_element_type=f32).reshape(2 * length, 2 * head)
    u = jax.nn.silu(u_pre)
    g = u * o
    squares = jnp.sum(g * g, axis=-1).reshape(2, 8, rows).transpose(1, 0, 2).reshape(8, 1, 2 * rows)
    squares = jnp.broadcast_to(squares, (8, 8, 2 * rows))
    part = product(g.astype(bf16), o_w).astype(bf16).reshape(2, length, width)

    n2_all, h, branch, scale_all = call(
        attention_out,
        1,
        [(part, ANY), (squares, ANY), (x_low, ANY)],
        [(low_array(2, length, width), ANY), (wide_array(2 * rows, width), VMEM), (wide_array(2 * rows, width), VMEM),
         (wide_array(8, 8, 2 * rows), ANY)],
        [dma(80)] + scatter_scratch(rows, width)
        + [pltpu.VMEM((2, rows, width), bf16), pltpu.VMEM((8, 8, 2 * rows), f32), pltpu.VMEM((8, 2 * rows), f32), dma(8), dma(8),
           dma(2, 2, 3), dma(2, 7), dma(2), pltpu.VMEM((2, rows, width), bf16), dma(),
           pltpu.VMEM((2 * rows, 2 * rows), f32)],
        "attention_out",
    )

    def per_token(values):
        return values[:, 0].reshape(8, 2, rows).transpose(1, 0, 2).reshape(2 * length, 1)

    n2_all = n2_all.reshape(2 * length, width)
    h1 = product_right(n2_all, f_w)
    h2 = product_right(n2_all, s_w)
    p = (h1 * h2).astype(bf16)
    part_m = product(p, t_w).astype(bf16).reshape(2, length, width)
    dp = product_right(dm_all, t_w)
    dh1 = (dp * h2).astype(bf16)
    dh2 = (dp * h1).astype(bf16)
    part = (product(dh1, f_w) + product(dh2, s_w)).astype(bf16).reshape(2, length, width)
    gf = product_left(dh1, n2_all).astype(bf16)
    gs = product_left(dh2, n2_all).astype(bf16)
    gt = product_left(p, dm_all).astype(bf16)

    da_all, dh, out, mix_all = call(
        ffn_back,
        2,
        [(part, ANY), (part_m, ANY), (dy, VMEM), (h, VMEM), (branch, VMEM)],
        [(low_array(2, length, width), ANY), (wide_array(2 * rows, width), VMEM), (low_array(2 * rows, width), VMEM),
         (wide_array(8, 8, 2 * rows), ANY)],
        [dma(80)] + scatter_scratch(rows, width) + scatter_scratch(rows, width)
        + [pltpu.VMEM((2, rows, width), bf16), pltpu.VMEM((8, 2 * rows), f32), dma(8),
           dma(2, 2, 3), dma(2, 7), dma(2), pltpu.VMEM((2 * rows, 2 * rows), f32)],
        "ffn_back",
    )
    da_all = da_all.reshape(2 * length, width)
    inverse = per_token(scale_all)
    mix = per_token(mix_all)
    nat = g * inverse
    go = product_left(nat.astype(bf16), da_all).astype(bf16)
    dg = inverse * (product_right(da_all, o_w) - nat * mix)
    do = split((dg * u).astype(bf16))
    du_pre = (dg * o * silu_slope(u_pre)).astype(bf16)
    d_scores = (jnp.einsum("bihe,bjhe->bhij", do, v, preferred_element_type=f32) * weight).astype(bf16)
    dq = jnp.einsum("bhij,bjhd->bihd", d_scores, k, preferred_element_type=f32).reshape(2 * length, 2 * head)
    dk = jnp.einsum("bhij,bihd->bjhd", d_scores, q, preferred_element_type=f32).reshape(2 * length, 2 * head)
    dv = jnp.einsum("bhij,bihe->bjhe", scores, do, preferred_element_type=f32).reshape(2 * length, 2 * head)
    dq_pre = (dq * silu_slope(q_pre)).astype(bf16)
    dk_pre = (dk * live * silu_slope(k_pre)).astype(bf16)
    dv_pre = (dv * live * silu_slope(v_pre)).astype(bf16)
    part = product_right(dq_pre, q_w) + product_right(dk_pre, k_w)
    part = (part + product_right(dv_pre, v_w) + product_right(du_pre, u_w)).astype(bf16).reshape(2, length, width)
    heads = [product_left(n1_all, d).astype(bf16).reshape(4, 2, depth, 2 * head) for d in (dq_pre, dk_pre, dv_pre, du_pre)]

    dn1, fq, fk, fv, fu, fo, ff, fs, ft = call(
        gradients,
        3,
        [(v, ANY) for v in [part] + heads + [go, gf, gs, gt]],
        [(wide_array(2 * rows, width), VMEM)] + [(low_array(depth, wide), ANY)] * 4 + [(low_array(depth, wide), ANY)]
        + [(low_array(2 * hidden, depth), ANY)] * 2 + [(low_array(hidden, wide), ANY)],
        [dma(140)] + scatter_scratch(rows, width)
        + [pltpu.VMEM((4, 4, 4, depth, head), bf16), pltpu.VMEM((4, 2 * head, wide), bf16),
           pltpu.VMEM((2, 4, hidden // 4, width), bf16), pltpu.VMEM((4, hidden, wide), bf16),
           dma(4, 4), dma(4), dma(2, 4), dma(4),
           pltpu.VMEM((4, 4, depth, head), bf16), pltpu.VMEM((2 * head, wide), bf16),
           pltpu.VMEM((2, hidden // 4, width), bf16), pltpu.VMEM((hidden, wide), bf16),
           dma(4, 4), dma(2), dma(2, 8), dma(4)],
        "gradients",
    )
    grad_x = dh + norm_back(x, dn1)
    return (
        out.reshape(2, 1, rows, width),
        grad_x.reshape(2, 1, rows, width),
        fq.astype(f32), fk.astype(f32), fv.astype(f32), fu.astype(f32), fo.astype(f32),
        ff.T.astype(f32), fs.T.astype(f32), ft.astype(f32),
    )


def solution(mesh):
    in_specs = (
        P(None, "grp", "seq", None),
        P(None, "grp", "seq", None),
        P(None, "grp"),
        P(),
        P("seq", "grp"),
        P("seq", "grp"),
        P("seq", "grp"),
        P("seq", "grp"),
        P("seq", "grp"),
        P("seq", "grp"),
        P("seq", "grp"),
        P("seq", "grp"),
    )
    out_specs = (
        P(None, "grp", "seq", None),
        P(None, "grp", "seq", None),
        P("seq", "grp"),
        P("seq", "grp"),
        P("seq", "grp"),
        P("seq", "grp"),
        P("seq", "grp"),
        P("seq", "grp"),
        P("seq", "grp"),
        P("seq", "grp"),
    )
    fast = mesh.shape["grp"] == 4 and mesh.shape["seq"] == 8
    return jax.shard_map(line_shards if fast else shards, mesh=mesh, in_specs=in_specs, out_specs=out_specs, check_vma=False)
```

```python
import jax
import jax.numpy as jnp
from jax import lax
from jax.experimental import pallas as pl
from jax.experimental.pallas import tpu as pltpu
from jax.sharding import PartitionSpec as P

EPS = 1e-06
HIGH = lax.Precision.HIGHEST
MESH = pl.DeviceIdType.MESH
ANY = pl.BlockSpec(memory_space=pl.ANY)
VMEM = pl.BlockSpec(memory_space=pltpu.VMEM)


def prefix(value, axis, join, neutral, backward):
    count, mine = (lax.axis_size(axis), lax.axis_index(axis))
    pieces = jax.tree.map(lambda part: lax.all_gather(part, axis), value)
    if backward:
        pieces = jax.tree.map(lambda part: part[::-1], pieces)
        mine = count - 1 - mine
    subtotal = jax.tree.map(
        lambda part, zero: jnp.full_like(part, 0) + jnp.asarray(zero, part.dtype), value, neutral
    )

    def step(position, subtotal):
        longer = join(subtotal, jax.tree.map(lambda part: part[position], pieces))
        return jax.tree.map(lambda new, old: jnp.where(position < mine, new, old), longer, subtotal)

    return lax.fori_loop(0, count - 1, step, subtotal)


def norm_rows(values):
    return values * lax.rsqrt(jnp.mean(values * values, axis=-1, keepdims=True) + EPS)


def norm_back(values, gradient):
    _, pull = jax.vjp(norm_rows, values)
    return pull(gradient)[0]


def silu_slope(values):
    sigma = jax.nn.sigmoid(values)
    return sigma * (1.0 + values * (1.0 - sigma))


def product(left, right):
    return jnp.dot(left, right, preferred_element_type=jnp.float32)


def product_left(left, right):
    return lax.dot_general(
        left, right, (((0,), (0,)), ((), ())), preferred_element_type=jnp.float32
    )


def product_right(left, right):
    return lax.dot_general(
        left, right, (((1,), (1,)), ((), ())), preferred_element_type=jnp.float32
    )


def combine_state(earlier, later):
    return (later[1][:, None, None] * earlier[0] + later[0], earlier[1] * later[1])


def shards(
    tokens,
    cotangent,
    lengths,
    decay_rate,
    w_query,
    w_key,
    w_value,
    w_gate,
    w_out,
    w_first,
    w_second,
    w_third,
):
    micro = tokens.shape[0]
    block_rows = tokens.shape[2]
    width = tokens.shape[3]
    heads = decay_rate.shape[0]
    head_dim = width // heads
    hidden_width = w_third.shape[0] * lax.axis_size("seq")
    places = jnp.arange(block_rows).astype(jnp.float32)
    slot_index = lax.axis_index("seq") * block_rows + jnp.arange(block_rows)
    offset = places[:, None] - places[None, :]
    weight = jnp.where(
        offset[None] >= 0, jnp.exp(-decay_rate[:, None, None] * jnp.maximum(offset, 0.0)[None]), 0.0
    )
    query_fac = jnp.exp(-decay_rate[None, :] * (places[:, None] + 1.0))[:, :, None]
    key_fac = jnp.exp(-decay_rate[None, :] * (block_rows - 1.0 - places[:, None]))[:, :, None]
    step_decay = jnp.exp(-decay_rate * block_rows)
    empty_state = jnp.zeros((heads, head_dim, head_dim), jnp.float32)
    unit_decay = jnp.ones((heads,), jnp.float32)
    partial_rows = (
        lax.all_gather(w_query, "grp", axis=1, tiled=True),
        lax.all_gather(w_key, "grp", axis=1, tiled=True),
        lax.all_gather(w_value, "grp", axis=1, tiled=True),
        lax.all_gather(w_gate, "grp", axis=1, tiled=True),
        lax.all_gather(w_out, "grp", axis=1, tiled=True),
        lax.all_gather(w_first, "grp", axis=1, tiled=True),
        lax.all_gather(w_second, "grp", axis=1, tiled=True),
        lax.all_gather(w_third, "grp", axis=1, tiled=True),
    )
    gathered = (
        lax.all_gather(partial_rows[0], "seq", axis=0, tiled=True),
        lax.all_gather(partial_rows[1], "seq", axis=0, tiled=True),
        lax.all_gather(partial_rows[2], "seq", axis=0, tiled=True),
        lax.all_gather(partial_rows[3], "seq", axis=0, tiled=True),
        lax.all_gather(partial_rows[4], "seq", axis=0, tiled=True),
        lax.all_gather(partial_rows[5], "seq", axis=0, tiled=True),
        lax.all_gather(partial_rows[6], "seq", axis=0, tiled=True),
        lax.all_gather(partial_rows[7], "seq", axis=0, tiled=True),
    )
    outputs = []
    input_grads = []
    first_norms = []
    attn_rows = []
    normed_rows = []
    branch_rows = []
    second_norms = []
    ffn_rows = []
    mixed_rows = []
    upstream_rows = []
    for batch_idx in range(micro):
        wq_full, wk_full, wv_full, wu_full, wo_full, first_full, second_full, third_full = gathered
        inputs = tokens[batch_idx, 0].astype(jnp.float32)
        live = (slot_index < lengths[batch_idx, 0]).astype(jnp.float32)[:, None]
        live_low = live.astype(jnp.bfloat16)
        first_norm = norm_rows(inputs).astype(jnp.bfloat16)
        query_pre = product(first_norm, wq_full)
        key_pre = product(first_norm, wk_full)
        value_pre = product(first_norm, wv_full)
        gate_pre = product(first_norm, wu_full)
        queries = jax.nn.silu(query_pre).astype(jnp.bfloat16).reshape(block_rows, heads, head_dim)
        key_heads = (jax.nn.silu(key_pre).astype(jnp.bfloat16) * live_low).reshape(
            block_rows, heads, head_dim
        )
        value_heads = (jax.nn.silu(value_pre).astype(jnp.bfloat16) * live_low).reshape(
            block_rows, heads, head_dim
        )
        query_wide = queries.astype(jnp.float32)
        key_wide = key_heads.astype(jnp.float32)
        value_wide = value_heads.astype(jnp.float32)
        local_state = jnp.einsum("jhd,jhe->hde", key_wide * key_fac, value_wide, precision=HIGH)
        prior_state, _ = prefix(
            (local_state, step_decay), "seq", combine_state, (empty_state, unit_decay), False
        )
        scores = (
            jnp.einsum("ihd,jhd->hij", queries, key_heads, preferred_element_type=jnp.float32)
            * weight
        )
        intra = jnp.einsum("hij,jhe->ihe", scores, value_wide, precision=HIGH)
        inter = jnp.einsum("ihd,hde->ihe", query_wide * query_fac, prior_state, precision=HIGH)
        attended = (intra + inter).reshape(block_rows, width)
        gate_act = jax.nn.silu(gate_pre)
        gated = gate_act * attended
        normed = norm_rows(gated).astype(jnp.bfloat16)
        hidden = inputs + product(normed, wo_full)
        second_norm = norm_rows(hidden).astype(jnp.bfloat16)
        first_proj = product(second_norm, first_full)
        second_proj = product(second_norm, second_full)
        mixed_in = (first_proj * second_proj).astype(jnp.bfloat16)
        result = hidden + product(mixed_in, third_full)
        outputs.append(result.astype(jnp.bfloat16))
        upstream = cotangent[batch_idx, 0].astype(jnp.float32) * live
        upstream_low = upstream.astype(jnp.bfloat16)
        grad_mixed = product_right(upstream_low, third_full)
        grad_first_proj = (grad_mixed * second_proj).astype(jnp.bfloat16)
        grad_second_proj = (grad_mixed * first_proj).astype(jnp.bfloat16)
        grad_norm_two = product_right(grad_first_proj, first_full) + product_right(
            grad_second_proj, second_full
        )
        grad_hidden = upstream + norm_back(hidden, grad_norm_two)
        grad_branch = grad_hidden.astype(jnp.bfloat16)
        grad_gated = norm_back(gated, product_right(grad_branch, wo_full))
        grad_attended = (grad_gated * gate_act).astype(jnp.bfloat16)
        grad_gate_pre = (grad_gated * attended * silu_slope(gate_pre)).astype(jnp.bfloat16)
        grad_heads = grad_attended.reshape(block_rows, heads, head_dim)
        grad_wide = grad_heads.astype(jnp.float32)
        local_grad = jnp.einsum("ihd,ihe->hde", query_wide * query_fac, grad_wide, precision=HIGH)
        later_grad, _ = prefix(
            (local_grad, step_decay), "seq", combine_state, (empty_state, unit_decay), True
        )
        grad_scores = (
            jnp.einsum("ihe,jhe->hij", grad_heads, value_heads, preferred_element_type=jnp.float32)
            * weight
        )
        grad_queries = jnp.einsum("hij,jhd->ihd", grad_scores, key_wide, precision=HIGH)
        grad_queries = (
            grad_queries
            + jnp.einsum("ihe,hde->ihd", grad_wide, prior_state, precision=HIGH) * query_fac
        )
        grad_keys = jnp.einsum("hij,ihd->jhd", grad_scores, query_wide, precision=HIGH)
        grad_keys = (
            grad_keys + jnp.einsum("hde,jhe->jhd", later_grad, value_wide, precision=HIGH) * key_fac
        )
        grad_values = jnp.einsum("hij,ihe->jhe", scores, grad_wide, precision=HIGH)
        grad_values = (
            grad_values + jnp.einsum("jhd,hde->jhe", key_wide, later_grad, precision=HIGH) * key_fac
        )
        grad_query_pre = (grad_queries.reshape(block_rows, width) * silu_slope(query_pre)).astype(
            jnp.bfloat16
        )
        grad_key_pre = (grad_keys.reshape(block_rows, width) * live * silu_slope(key_pre)).astype(
            jnp.bfloat16
        )
        grad_value_pre = (
            grad_values.reshape(block_rows, width) * live * silu_slope(value_pre)
        ).astype(jnp.bfloat16)
        grad_norm_one = product_right(grad_query_pre, wq_full) + product_right(
            grad_key_pre, wk_full
        )
        grad_norm_one = (
            grad_norm_one
            + product_right(grad_value_pre, wv_full)
            + product_right(grad_gate_pre, wu_full)
        )
        input_grads.append(grad_hidden + norm_back(inputs, grad_norm_one))
        first_norms.append(first_norm)
        attn_rows.append(
            jnp.concatenate([grad_query_pre, grad_key_pre, grad_value_pre, grad_gate_pre], axis=1)
        )
        normed_rows.append(normed)
        branch_rows.append(grad_branch)
        second_norms.append(second_norm)
        ffn_rows.append(jnp.concatenate([grad_first_proj, grad_second_proj], axis=1))
        mixed_rows.append(mixed_in)
        upstream_rows.append(upstream_low)
    first_all = jnp.concatenate(first_norms, axis=0)
    attn_all = jnp.concatenate(attn_rows, axis=0)
    normed_all = jnp.concatenate(normed_rows, axis=0)
    branch_all = jnp.concatenate(branch_rows, axis=0)
    second_all = jnp.concatenate(second_norms, axis=0)
    ffn_all = jnp.concatenate(ffn_rows, axis=0)
    mixed_all = jnp.concatenate(mixed_rows, axis=0)
    upstream_all = jnp.concatenate(upstream_rows, axis=0)
    proj_rows = lax.psum_scatter(
        product_left(first_all, attn_all), "seq", scatter_dimension=0, tiled=True
    )
    outproj_rows = lax.psum_scatter(
        product_left(normed_all, branch_all), "seq", scatter_dimension=0, tiled=True
    )
    ffn_part = lax.psum_scatter(
        product_left(second_all, ffn_all), "seq", scatter_dimension=0, tiled=True
    )
    down_rows = lax.psum_scatter(
        product_left(mixed_all, upstream_all), "seq", scatter_dimension=0, tiled=True
    )
    summed = (
        lax.psum_scatter(proj_rows[:, :width], "grp", scatter_dimension=1, tiled=True),
        lax.psum_scatter(proj_rows[:, width : 2 * width], "grp", scatter_dimension=1, tiled=True),
        lax.psum_scatter(
            proj_rows[:, 2 * width : 3 * width], "grp", scatter_dimension=1, tiled=True
        ),
        lax.psum_scatter(proj_rows[:, 3 * width :], "grp", scatter_dimension=1, tiled=True),
        lax.psum_scatter(outproj_rows, "grp", scatter_dimension=1, tiled=True),
        lax.psum_scatter(ffn_part[:, :hidden_width], "grp", scatter_dimension=1, tiled=True),
        lax.psum_scatter(ffn_part[:, hidden_width:], "grp", scatter_dimension=1, tiled=True),
        lax.psum_scatter(down_rows, "grp", scatter_dimension=1, tiled=True),
    )
    layer_out = jnp.stack(outputs)[:, None]
    grad_tokens = jnp.stack(input_grads)[:, None]
    return (
        layer_out,
        grad_tokens,
        summed[0],
        summed[1],
        summed[2],
        summed[3],
        summed[4],
        summed[5],
        summed[6],
        summed[7],
    )


class Copies:
    def __init__(self, sems):
        self.sems = sems
        self.used = 0
        self.pending = []

    def remote(self, src, dst, recv_sem, group, place, when=None):
        copy = pltpu.make_async_remote_copy(
            src_ref=src,
            dst_ref=dst,
            send_sem=self.sems.at[self.used],
            recv_sem=recv_sem,
            device_id=(group, place),
            device_id_type=MESH,
        )
        self.used += 1
        self.pending.append((copy, when))
        if when is None:
            copy.start()
        else:
            pl.when(when)(copy.start)

    def finish(self):
        for copy, when in self.pending:
            if when is None:
                copy.wait_send()
            else:
                pl.when(when)(copy.wait_send)
        self.pending = []


def local(src, dst, sem, when=None):
    copy = pltpu.make_async_copy(src, dst, sem)
    if when is None:
        copy.start()
    else:
        pl.when(when)(copy.start)


def arrived(ref, sem, when=None):
    copy = pltpu.make_async_copy(ref, ref, sem)
    if when is None:
        copy.wait()
    else:
        pl.when(when)(copy.wait)


def where_am_i():
    g, s = lax.axis_index("grp"), lax.axis_index("seq")
    return g, s, g // 2, g % 2, s // 2, s % 2


def across(y, x):
    return (y * 2 + 1 - x, (1 - y) * 2 + x, (1 - y) * 2 + 1 - x)


def greet(partners):
    barrier = pltpu.get_barrier_semaphore()
    for partner in partners:
        pl.semaphore_signal(barrier, inc=1, device_id=partner, device_id_type=MESH)
    pl.semaphore_wait(barrier, len(partners))


def aligned(index, unit, step):
    return pl.ds(pl.multiple_of(index * unit, step), unit)


class Gather:
    def __init__(self, copies, out, rows, hop_sem, side_sem):
        self.copies, self.out, self.rows = copies, out, rows
        self.hop_sem, self.side_sem = hop_sem, side_sem
        self.g, self.s, _, _, self.z, self.c = where_am_i()

    def block(self, b, z, core):
        return self.out.at[b, aligned(2 * z + core, self.rows, 16)]

    def spread(self, src, b, z_of, k, right, left):
        g, s, z, c = self.g, self.s, self.z, self.c
        dst = self.block(b, z_of, c)
        if right is not None:
            self.copies.remote(src, dst, self.hop_sem.at[b, 0, k], g, (s + 2) % 8, right)
        if left is not None:
            self.copies.remote(src, dst, self.hop_sem.at[b, 1, k], g, (s + 6) % 8, left)

    def begin(self, src, own_sem, b):
        g, s, z, c = self.g, self.s, self.z, self.c
        self.spread(src, b, z, 0, z < 3, z > 0)
        self.copies.remote(src, self.block(b, z, c), self.side_sem.at[b, 0], g, s + 1 - 2 * c)
        local(src, self.block(b, z, c), own_sem)

    def step(self, b, k):
        g, s, z, c = self.g, self.s, self.z, self.c
        side = s + 1 - 2 * c
        has = z >= k
        at = jnp.maximum(z - k, 0)
        ref = self.block(b, at, c)
        arrived(ref, self.hop_sem.at[b, 0, k - 1], has)
        if k < 3:
            self.spread(ref, b, at, k, jnp.logical_and(has, z < 3), None)
        self.copies.remote(ref, ref, self.side_sem.at[b, k], g, side, has)
        has = z + k <= 3
        at = jnp.minimum(z + k, 3)
        ref = self.block(b, at, c)
        arrived(ref, self.hop_sem.at[b, 1, k - 1], has)
        if k < 3:
            self.spread(ref, b, at, k, None, jnp.logical_and(has, z > 0))
        self.copies.remote(ref, ref, self.side_sem.at[b, 3 + k], g, side, has)

    def finish(self, own_sem, b):
        z, c = self.z, self.c
        arrived(self.block(b, z, c), own_sem)
        arrived(self.block(b, z, 1 - c), self.side_sem.at[b, 0])
        for k in (1, 2, 3):
            arrived(self.block(b, jnp.maximum(z - k, 0), 1 - c), self.side_sem.at[b, k], z >= k)
            arrived(self.block(b, jnp.minimum(z + k, 3), 1 - c), self.side_sem.at[b, 3 + k], z + k <= 3)


def line_partners(g, s):
    return [(g, (s + d) % 8) for d in range(1, 8)]


class Scatter:
    def __init__(self, copies, part, rows, side, own, inbox, side_sem, own_sem, line_sem):
        self.copies, self.part, self.rows = copies, part, rows
        self.side, self.own, self.inbox = side, own, inbox
        self.side_sem, self.own_sem, self.line_sem = side_sem, own_sem, line_sem
        self.g, self.s, _, _, self.z, self.c = where_am_i()

    def begin(self):
        g, s, z, c = self.g, self.s, self.z, self.c
        for k in (2, 1, 3, 0):
            to = (z + k) % 4
            theirs = aligned(2 * to + 1 - c, self.rows, 16)
            mine = aligned(2 * to + c, self.rows, 16)
            self.copies.remote(
                self.part.at[:, theirs], self.side.at[k], self.side_sem.at[k], g, s + 1 - 2 * c
            )
            local(self.part.at[:, mine], self.own.at[k], self.own_sem.at[k])

    def send(self, k):
        arrived(self.side.at[k], self.side_sem.at[k])
        arrived(self.own.at[k], self.own_sem.at[k])
        if k == 0:
            return
        own, side = self.own.at[k], self.side.at[k]

        def add(i, carry):
            piece = aligned(i, 16, 16)
            for b in range(2):
                both = own[b, piece].astype(jnp.float32) + side[b, piece].astype(jnp.float32)
                own[b, piece] = both.astype(jnp.bfloat16)
            return carry

        lax.fori_loop(0, self.rows // 16, add, 0)
        to = (self.z + k) % 4
        self.copies.remote(own, self.inbox.at[k - 1], self.line_sem.at[k - 1], self.g, 2 * to + self.c)

    def receive(self):
        for k in range(3):
            arrived(self.inbox.at[k], self.line_sem.at[k])

    def total(self, b, piece):
        value = self.own[0, b, piece].astype(jnp.float32) + self.side[0, b, piece].astype(jnp.float32)
        for k in range(3):
            value = value + self.inbox[k, b, piece].astype(jnp.float32)
        return value


def everyone_on_line(copies, src, dst, sem, g, s, to_rows):
    for d in range(1, 8):
        to = (s + d) % 8
        copies.remote(to_rows(to), dst.at[s], sem.at[d - 1], g, to)


def mean_square(values):
    return jnp.mean(values * values, axis=-1, keepdims=True)


def pour(read, write, count):
    def piece(i, carry):
        at = aligned(i, 16, 16)
        write(at, read(at))
        return carry

    lax.fori_loop(0, count, piece, 0)


class HalfScatter:
    def __init__(self, copies, part, rows, side, inbox, side_sem, line_sem):
        self.copies, self.part, self.rows = copies, part, rows
        self.side, self.inbox, self.side_sem, self.line_sem = side, inbox, side_sem, line_sem
        self.g, self.s, _, _, self.z, self.c = where_am_i()

    def mine(self, k):
        return self.part.at[aligned(2 * ((self.z + k) % 4) + self.c, self.rows, 16)]

    def begin(self):
        for k in (2, 1, 3, 0):
            theirs = aligned(2 * ((self.z + k) % 4) + 1 - self.c, self.rows, 16)
            self.copies.remote(
                self.part.at[theirs], self.side.at[k], self.side_sem.at[k], self.g, self.s + 1 - 2 * self.c
            )

    def send(self):
        for k in (2, 1, 3, 0):
            arrived(self.side.at[k], self.side_sem.at[k])
            if k == 0:
                continue
            own, side = self.mine(k), self.side.at[k]

            def write(at, value):
                own[at] = value.astype(jnp.bfloat16)

            pour(lambda at: own[at].astype(jnp.float32) + side[at].astype(jnp.float32), write, self.rows // 16)
            to = (self.z + k) % 4
            self.copies.remote(own, self.inbox.at[k - 1], self.line_sem.at[k - 1], self.g, 2 * to + self.c)

    def receive(self):
        for k in range(3):
            arrived(self.inbox.at[k], self.line_sem.at[k])

    def total(self, at):
        value = self.mine(0)[at].astype(jnp.float32) + self.side[0, at].astype(jnp.float32)
        for k in range(3):
            value = value + self.inbox[k, at].astype(jnp.float32)
        return value


def silu(values):
    return values / (1.0 + jnp.exp(-values))


def decay_table(rate, length):
    offset = lax.broadcasted_iota(jnp.int32, (length, length), 0) - lax.broadcasted_iota(jnp.int32, (length, length), 1)
    steps = jnp.maximum(offset, 0).astype(jnp.float32)
    return jnp.where(offset >= 0, jnp.exp(-rate * steps), 0.0)


def live_rows(first, count, length):
    return ((first + lax.broadcasted_iota(jnp.int32, (count, 1), 0)) < length).astype(jnp.float32)


def forward_part(
    lengths, decay, x, cot, wq, wk, wv, wu, wo, w1, w2, w3,
    n1_all, dm_all, n2_all, q_all, k_all, v_all, u_all, o_all, f_all, s_all, t_all, pre_all, h, branch, scale_all,
    send, own, hop_n, side_n, hop_d, side_d, hop_m, side_m, z_head, z_out, z_ff, xy_head, xy_out, xy_ff,
    n1, dm, n2, n1_v, w_v, wo_v, load, pre_v, pre_sem, part, side, inbox, side_sem, line_sem,
    table, squares, inbox_sq, scale, sq_sem, sc_sem, column,
):
    g, s, y, x_, z, c = where_am_i()
    others = across(y, x_)
    greet(line_partners(g, s) + [(o, s) for o in others])
    copies = Copies(send)
    rows, width = x.shape[1], x.shape[2]
    length = 8 * rows
    gather_n = Gather(copies, n1_all, rows, hop_n, side_n)
    gather_d = Gather(copies, dm_all, rows, hop_d, side_d)
    gather_m = Gather(copies, n2_all, rows, hop_m, side_m)
    heads = list(zip((wq, wk, wv, wu), (q_all, k_all, v_all, u_all)))
    depth, wide = wq.shape
    head = q_all.shape[1] // 2
    ff = f_all.shape[0] // 4
    target = g // 2
    mine = aligned(g % 2, head, head)
    here = c == target
    order = [(z + d) % 4 for d in (0, 1, 3, 2)]

    def send_heads(n):
        src, dst = heads[n]
        for d in (2, 1, 3, 0):
            to = (z + d) % 4
            a, b = src.at[:, aligned(to, head, head)], dst.at[aligned(s, depth, 16), mine]
            if d:
                copies.remote(a, b, z_head.at[n, z], g, 2 * to + target)
            else:
                copies.remote(a, b, z_head.at[n, z], g, 2 * to + target, c != target)
                local(a, b, z_head.at[n, z], here)

    def pass_heads(n):
        dst = heads[n][1]
        for zs in order:
            block = dst.at[aligned(zs, 2 * depth, 16), mine]
            arrived(block, z_head.at[n, zs], here)
            for r, o in enumerate(others):
                copies.remote(block, block, xy_head.at[n, r, zs], o, s, here)

    def send_out():
        for i in range(2):
            to = 2 * c + i
            a = wo.at[pl.ds(i * head, head)]
            b = o_all.at[aligned(z % 2, head, head), aligned(g, wide, 128)]
            self_ = jnp.logical_and(to == z, c == z // 2)
            copies.remote(a, b, z_out.at[z % 2], g, 2 * to + z // 2, jnp.logical_not(self_))
            local(a, b, z_out.at[z % 2], self_)

    def pass_out():
        for j in range(2):
            arrived(o_all.at[pl.ds(j * head, head), aligned(g, wide, 128)], z_out.at[j])
        block = o_all.at[:, aligned(g, wide, 128)]
        for r, o in enumerate(others):
            copies.remote(block, block, xy_out.at[r], o, s)

    def send_ff(n):
        src, dst = ((w1, f_all), (w2, s_all))[n]
        for d in (4, 3, 5, 2, 6, 1, 7, 0):
            to = (s + d) % 8
            a = src.at[aligned(to, ff, 16)]
            b = dst.at[aligned(g, ff, 16), aligned(s, depth, 128)]
            if d:
                copies.remote(a, b, z_ff.at[n, z], g, to)
            else:
                local(a, b, z_ff.at[n, z])

    def pass_ff(n):
        dst = (f_all, s_all)[n]
        for zs in order:
            block = dst.at[aligned(g, ff, 16), aligned(zs, 2 * depth, 128)]
            arrived(block, z_ff.at[n, zs])
            for r, o in enumerate(others):
                copies.remote(block, block, xy_ff.at[n, r, zs], o, s)

    def send_third():
        for d in (2, 1, 3, 0):
            to = 4 * c + (s + d) % 4
            a = w3.at[aligned(to % 4, ff, 16)]
            b = t_all.at[aligned(z, ff, 16), aligned(g, wide, 128)]
            if d:
                copies.remote(a, b, z_ff.at[2, z], g, to)
            else:
                self_ = s // 4 == c
                copies.remote(a, b, z_ff.at[2, z], g, to, jnp.logical_not(self_))
                local(a, b, z_ff.at[2, z], self_)

    def pass_third():
        for zs in order:
            block = t_all.at[aligned(zs, ff, 16), aligned(g, wide, 128)]
            arrived(block, z_ff.at[2, zs])
            for r, o in enumerate(others):
                copies.remote(block, block, xy_ff.at[2, r, zs], o, s)

    send_heads(0)
    send_heads(1)
    for b in range(2):

        def norm(at):
            v = x[b, at].astype(jnp.float32)
            return v * lax.rsqrt(mean_square(v) + EPS)

        def keep(at, value):
            n1[b, at] = value.astype(jnp.bfloat16)

        pour(norm, keep, rows // 16)
        first = s * rows

        def masked(i, carry):
            at = aligned(i, 16, 16)
            live = live_rows(first + i * 16, 16, lengths[b, 0])
            dm[b, at] = (cot[b, at].astype(jnp.float32) * live).astype(jnp.bfloat16)
            return carry

        lax.fori_loop(0, rows // 16, masked, 0)
    pass_heads(0)
    send_heads(2)
    pass_heads(1)
    send_heads(3)
    for b in range(2):
        gather_n.begin(n1.at[b], own.at[0, b], b)
    send_out()
    pass_heads(2)
    pass_heads(3)
    gather_n.step(0, 1)
    gather_n.step(1, 1)
    pass_out()
    gather_n.step(0, 2)
    gather_n.step(1, 2)
    send_ff(0)
    gather_n.step(0, 3)
    gather_n.step(1, 3)
    for r, o in enumerate(others):
        from_here = (o // 2) == c
        for n, (_, dst) in enumerate(heads):
            for zs in range(4):
                block = dst.at[pl.ds(zs * 2 * depth, 2 * depth), aligned(o % 2, head, head)]
                arrived(block, xy_head.at[n, r, zs], from_here)
        arrived(o_all.at[:, aligned(o, wide, 128)], xy_out.at[r])
    for n, (_, dst) in enumerate(heads):
        local(dst, w_v.at[n], load.at[n])
    local(o_all, wo_v, load.at[4])
    for b in range(2):
        gather_n.finish(own.at[0, b], b)
        local(n1_all.at[b], n1_v.at[b], load.at[5 + b])
    for j in range(2):
        table[j] = decay_table(decay[4 * (2 * c + j) + z], length)
    for n in range(4):
        arrived(w_v.at[n], load.at[n])
    arrived(wo_v, load.at[4])
    scatters = []
    for b in range(2):
        arrived(n1_v.at[b], load.at[5 + b])
        half = length // 2

        def project(i, carry):
            at = aligned(i, half, 16)
            for n in range(4):
                pre_v[n, b, at] = product(n1_v[b, at], w_v[n])
            return carry

        lax.fori_loop(0, 2, project, 0)
        live = live_rows(0, length, lengths[b, 0])
        for j in range(2):
            lanes = pl.ds(j * head, head)
            q = silu(pre_v[0, b, :, lanes]).astype(jnp.bfloat16)
            k = (silu(pre_v[1, b, :, lanes]) * live).astype(jnp.bfloat16)
            v = (silu(pre_v[2, b, :, lanes]) * live).astype(jnp.bfloat16)
            scores = (product_right(q, k) * table[j]).astype(jnp.bfloat16)
            pre_v[4, b, :, lanes] = product(scores, v)
        gated = silu(pre_v[3, b]) * pre_v[4, b]
        square = jnp.sum(gated * gated, axis=-1, keepdims=True)
        row = jnp.broadcast_to(square, (length, 128)).T[:8]
        for to in range(8):
            squares[b, to, :, :rows] = row[:, to * rows : (to + 1) * rows]
        low = gated.astype(jnp.bfloat16)

        def out_part(i, carry):
            at = aligned(i, 256, 256)
            part[b, :, at] = product(low, wo_v[:, at]).astype(jnp.bfloat16)
            return carry

        lax.fori_loop(0, width // 256, out_part, 0)
        scatter = HalfScatter(copies, part.at[b], rows, side.at[b], inbox.at[b], side_sem.at[b], line_sem.at[b])
        scatter.begin()
        everyone_on_line(copies, squares, inbox_sq.at[b], sq_sem.at[b], g, s, lambda to: squares.at[b, to])
        local(squares.at[b, s], inbox_sq.at[b, s], sq_sem.at[b, 7])
        scatter.send()
        scatters.append(scatter)
    local(pre_v, pre_all, pre_sem)
    pass_ff(0)
    for b in range(2):
        for d in range(8):
            arrived(inbox_sq.at[b, 0], sq_sem.at[b, d])
        total = inbox_sq[b, 0]
        for d in range(1, 8):
            total = total + inbox_sq[b, d]
        row = lax.rsqrt(total / width + EPS)
        scale[b] = row
        for d in range(1, 8):
            copies.remote(scale.at[b], scale_all.at[b, s], sc_sem.at[b, d - 1], g, (s + d) % 8)
        local(scale.at[b], scale_all.at[b, s], sc_sem.at[b, 7])
        column[b] = jnp.broadcast_to(row[:1], (128, 128)).T
    for b in range(2):
        scatter = scatters[b]
        scatter.receive()
        if b == 0:
            send_ff(1)
        else:
            send_third()

        def finish(i, carry):
            piece = aligned(i, 16, 16)
            at = aligned(b * (rows // 16) + i, 16, 16)
            a = scatter.total(piece) * column[b, piece, :1]
            hidden = x[b, piece].astype(jnp.float32) + a
            branch[at] = a
            h[at] = hidden
            n2[b, piece] = (hidden * lax.rsqrt(mean_square(hidden) + EPS)).astype(jnp.bfloat16)
            return carry

        lax.fori_loop(0, rows // 16, finish, 0)
        gather_m.begin(n2.at[b], own.at[2, b], b)
    for b in range(2):
        gather_d.begin(dm.at[b], own.at[1, b], b)
    gather_m.step(0, 1)
    gather_m.step(1, 1)
    pass_ff(1)
    gather_m.step(0, 2)
    gather_m.step(1, 2)
    gather_d.step(0, 1)
    gather_d.step(1, 1)
    pass_third()
    gather_m.step(0, 3)
    gather_m.step(1, 3)
    for k in (2, 3):
        for b in range(2):
            gather_d.step(b, k)

    for b in range(2):
        gather_d.finish(own.at[1, b], b)
        gather_m.finish(own.at[2, b], b)
    for r, o in enumerate(others):
        for n, dst in enumerate((f_all, s_all)):
            for zs in range(4):
                arrived(dst.at[aligned(o, ff, 16), pl.ds(zs * 2 * depth, 2 * depth)], xy_ff.at[n, r, zs])
        for zs in range(4):
            arrived(t_all.at[pl.ds(zs * ff, ff), aligned(o, wide, 128)], xy_ff.at[2, r, zs])
    for b in range(2):
        for d in range(8):
            arrived(scale.at[b], sc_sem.at[b, d])
    arrived(pre_v, pre_sem)
    copies.finish()


def ffn_back(
    part, part_m, dy, h, branch,
    da_all, dh, out, mix_all,
    send, side, own, inbox, side_sem, own_sem, line_sem,
    side_m, own_m, inbox_m, side_sem_m, own_sem_m, line_sem_m,
    da, mix, mix_sem, hop, hside, keep, column,
):
    g, s, _, _, z, c = where_am_i()
    greet(line_partners(g, s))
    copies = Copies(send)
    rows = part.shape[1] // 8
    width = part.shape[2]
    scatter = Scatter(copies, part, rows, side, own, inbox, side_sem, own_sem, line_sem)
    scatter_m = Scatter(copies, part_m, rows, side_m, own_m, inbox_m, side_sem_m, own_sem_m, line_sem_m)
    gather = Gather(copies, da_all, rows, hop, hside)
    scatter.begin()
    for k in (2, 1, 3, 0):
        scatter.send(k)
    scatter_m.begin()
    scatter.receive()
    for b in range(2):

        def finish(i, carry):
            piece = aligned(i, 16, 16)
            at = aligned(b * (rows // 16) + i, 16, 16)
            hidden = h[at]
            inverse = lax.rsqrt(mean_square(hidden) + EPS)
            normed = hidden * inverse
            grad = scatter.total(b, piece)
            along = jnp.mean(normed * grad, axis=-1, keepdims=True)
            grad_hidden = dy[at] + inverse * (grad - normed * along)
            dh[at] = grad_hidden
            low = grad_hidden.astype(jnp.bfloat16)
            da[b, piece] = low
            dot = jnp.mean(low.astype(jnp.float32) * branch[at], axis=-1, keepdims=True)
            column[at] = jnp.broadcast_to(dot, (16, 2 * rows))
            return carry

        lax.fori_loop(0, rows // 16, finish, 0)
        gather.begin(da.at[b], keep.at[b], b)
    mix[...] = column[...].T[:8]
    for d in range(1, 8):
        copies.remote(mix, mix_all.at[s], mix_sem.at[d - 1], g, (s + d) % 8)
    local(mix, mix_all.at[s], mix_sem.at[7])
    for k in (2, 1, 3, 0):
        scatter_m.send(k)
    for k in (1, 2, 3):
        for b in range(2):
            gather.step(b, k)
    scatter_m.receive()
    for b in range(2):

        def write(i, carry):
            piece = aligned(i, 16, 16)
            at = aligned(b * (rows // 16) + i, 16, 16)
            out[at] = (h[at] + scatter_m.total(b, piece)).astype(jnp.bfloat16)
            return carry

        lax.fori_loop(0, rows // 16, write, 0)
    for b in range(2):
        gather.finish(keep.at[b], b)
    for d in range(8):
        arrived(mix, mix_sem.at[d])
    copies.finish()


def gradients(
    part, gq, gk, gv, gu, go, gf, gs, gt,
    dn1, fq, fk, fv, fu, fo, ff_, fs, ft,
    send, side, own, inbox, side_sem, own_sem, line_sem,
    in_h, in_o, in_f, in_t, xy_h, xy_o, xy_f, xy_t, sum_h, sum_o, sum_f, sum_t, z_h, z_o, z_f, z_t,
):
    g, s, y, x, z, c = where_am_i()
    others = across(y, x)
    plane = [(o, 2 * z + e) for o in others for e in range(2)]
    greet(line_partners(g, s) + plane)
    copies = Copies(send)
    rows = part.shape[1] // 8
    scatter = Scatter(copies, part, rows, side, own, inbox, side_sem, own_sem, line_sem)
    head = 128
    wide = fo.shape[1]
    ff = gf.shape[0] // 4
    depth = fq.shape[0]
    scatter.begin()
    for k in (2, 1, 3, 0):
        scatter.send(k)
    grads_h = (gq, gk, gv, gu)
    for n, (src, dst) in enumerate(((gf, in_f), (gs, in_f))):
        for r, o in enumerate(others):
            copies.remote(src.at[aligned(o, ff, 16)], dst.at[n, r], xy_f.at[n, r], o, s)
        local(src.at[aligned(g, ff, 16)], dst.at[n, 3], xy_f.at[n, 3])
    for r, o in enumerate(others):
        copies.remote(gt.at[:, aligned(o, wide, 128)], in_t.at[r], xy_t.at[r], o, s)
    local(gt.at[:, aligned(g, wide, 128)], in_t.at[3], xy_t.at[3])
    for r, o in enumerate(others):
        copies.remote(go.at[:, aligned(o, wide, 128)], in_o.at[r], xy_o.at[r], o, s)
    local(go.at[:, aligned(g, wide, 128)], in_o.at[3], xy_o.at[3])
    for r, o in enumerate(others + (g,)):
        holds = o // 2 == c
        for n, src in enumerate(grads_h):
            for e in range(2):
                a = src.at[:, e, :, aligned(o % 2, head, head)]
                b = in_h.at[n, r]
                to_self = jnp.logical_and(holds, c == e)
                if r < 3:
                    copies.remote(a, b, xy_h.at[n, r], o, 2 * z + e, holds)
                else:
                    copies.remote(a, b, xy_h.at[n, r], g, 2 * z + e, jnp.logical_and(holds, c != e))
                    local(a, b, xy_h.at[n, r], to_self)

    def add_up(read, write, count):
        def add(i, carry):
            piece = aligned(i, 16, 16)
            value = read(0, piece)
            for r in range(1, 4):
                value = value + read(r, piece)
            write(piece, value.astype(jnp.bfloat16))
            return carry

        lax.fori_loop(0, count, add, 0)

    for n, out in enumerate((ff_, fs)):
        for r in range(4):
            arrived(in_f.at[n, r], xy_f.at[n, r])
        total = sum_f.at[n]

        def write(piece, value):
            total[piece] = value

        add_up(lambda r, piece: in_f[n, r, piece].astype(jnp.float32), write, ff // 16)
        for d in (4, 3, 5, 2, 6, 1, 7, 0):
            to = (s + d) % 8
            a = total.at[:, aligned(to, depth, 128)]
            b = out.at[aligned(s, ff, 16)]
            if d:
                copies.remote(a, b, z_f.at[n, d], g, to)
            else:
                local(a, b, z_f.at[n, d])
    for r in range(4):
        arrived(in_t.at[r], xy_t.at[r])

    def write(piece, value):
        sum_t[piece] = value

    add_up(lambda r, piece: in_t[r, piece].astype(jnp.float32), write, 4 * ff // 16)
    for d in (2, 1, 3, 0):
        to = 2 * ((z + d) % 4) + s // 4
        a = sum_t.at[aligned((z + d) % 4, ff, 16)]
        b = ft.at[aligned(s % 4, ff, 16)]
        self_ = to == s
        if d:
            copies.remote(a, b, z_t.at[s % 4], g, to)
        else:
            copies.remote(a, b, z_t.at[s % 4], g, to, jnp.logical_not(self_))
            local(a, b, z_t.at[s % 4], self_)
    for r in range(4):
        arrived(in_o.at[r], xy_o.at[r])

    def write(piece, value):
        sum_o[piece] = value

    add_up(lambda r, piece: in_o[r, piece].astype(jnp.float32), write, 2 * head // 16)
    for j in range(2):
        to = 2 * (2 * c + j) + z // 2
        a = sum_o.at[pl.ds(j * head, head)]
        b = fo.at[aligned(z % 2, head, head)]
        self_ = to == s
        copies.remote(a, b, z_o.at[z % 2], g, to, jnp.logical_not(self_))
        local(a, b, z_o.at[z % 2], self_)
    for n, out in enumerate((fq, fk, fv, fu)):
        for r in range(4):
            arrived(in_h.at[n, r], xy_h.at[n, r])
        total = sum_h.at[n]
        for q in range(4):

            def write(piece, value):
                total[q, piece] = value

            add_up(lambda r, piece: in_h[n, r, q, piece].astype(jnp.float32), write, depth // 16)
        for d in (2, 1, 3, 0):
            to = (z + d) % 4
            a = total.at[to]
            b = out.at[:, aligned(z, head, head)]
            if d:
                copies.remote(a, b, z_h.at[n, d], g, 2 * to + c)
            else:
                local(a, b, z_h.at[n, d])
    scatter.receive()
    for b in range(2):

        def finish(i, carry):
            piece = aligned(i, 16, 16)
            at = aligned(b * (rows // 16) + i, 16, 16)
            dn1[at] = scatter.total(b, piece)
            return carry

        lax.fori_loop(0, rows // 16, finish, 0)
    for n, out in enumerate((ff_, fs)):
        for d in range(8):
            arrived(out.at[pl.ds(0, ff)], z_f.at[n, d])
    for d in range(4):
        arrived(ft.at[pl.ds(0, ff)], z_t.at[d])
    for j in range(2):
        arrived(fo.at[pl.ds(0, head)], z_o.at[j])
    for n, out in enumerate((fq, fk, fv, fu)):
        for d in range(4):
            arrived(out.at[:, pl.ds(0, head)], z_h.at[n, d])
    copies.finish()


def call(kernel, number, ins, outs, scratch, name):
    return pl.pallas_call(
        kernel,
        out_shape=[shape for shape, _ in outs],
        in_specs=[spec for _, spec in ins],
        out_specs=[spec for _, spec in outs],
        scratch_shapes=scratch,
        compiler_params=pltpu.CompilerParams(
            collective_id=number, has_side_effects=True, vmem_limit_bytes=48 * 2**20
        ),
        name=name,
    )(*[value for value, _ in ins])


def low_array(*shape):
    return jax.ShapeDtypeStruct(shape, jnp.bfloat16)


def wide_array(*shape):
    return jax.ShapeDtypeStruct(shape, jnp.float32)


def dma(*shape):
    return pltpu.SemaphoreType.DMA(shape)


def scatter_scratch(rows, width):
    return [
        pltpu.VMEM((4, 2, rows, width), jnp.bfloat16),
        pltpu.VMEM((4, 2, rows, width), jnp.bfloat16),
        pltpu.VMEM((3, 2, rows, width), jnp.bfloat16),
        dma(4),
        dma(4),
        dma(3),
    ]


def line_shards(
    tokens, cotangent, lengths, decay_rate,
    w_query, w_key, w_value, w_gate, w_out, w_first, w_second, w_third,
):
    bf16, f32 = jnp.bfloat16, jnp.float32
    rows, width = tokens.shape[2], tokens.shape[3]
    depth, wide = w_query.shape
    head = width // decay_rate.shape[0]
    hidden = w_third.shape[0]
    length = 8 * rows
    s = lax.axis_index("seq")
    z, c = s // 2, s % 2
    x_low = tokens[:, 0]
    x = x_low.astype(f32).reshape(2 * rows, width)
    slots = s * rows + jnp.arange(rows)
    mine = (slots[None] < lengths[:, :1]).astype(f32).reshape(2 * rows, 1)
    live = (jnp.arange(length)[None] < lengths[:, :1]).astype(f32).reshape(2 * length, 1)
    dy = cotangent[:, 0].astype(f32).reshape(2 * rows, width) * mine
    in_smem = pl.BlockSpec(memory_space=pltpu.SMEM)

    (n1_all, dm_all, n2_all, q_w, k_w, v_w, u_w, o_w, f_w, s_w, t_w, pre_all, h, branch, scale_all) = call(
        forward_part,
        0,
        [(lengths, in_smem), (decay_rate, in_smem), (x_low, VMEM), (cotangent[:, 0], VMEM)]
        + [(v, ANY) for v in (w_query, w_key, w_value, w_gate, w_out, w_first.T, w_second.T, w_third)],
        [(low_array(2, length, width), ANY)] * 3
        + [(low_array(width, 2 * head), ANY)] * 4
        + [(low_array(2 * head, width), ANY)]
        + [(low_array(hidden, width), ANY)] * 3
        + [(wide_array(5, 2, length, 2 * head), ANY), (wide_array(2 * rows, width), VMEM), (wide_array(2 * rows, width), VMEM),
           (wide_array(2, 8, 8, 128), ANY)],
        [dma(260), dma(3, 2), dma(2, 2, 3), dma(2, 7), dma(2, 2, 3), dma(2, 7), dma(2, 2, 3), dma(2, 7),
         dma(4, 4), dma(2), dma(3, 4), dma(4, 3, 4), dma(3), dma(3, 3, 4),
         pltpu.VMEM((2, rows, width), bf16), pltpu.VMEM((2, rows, width), bf16), pltpu.VMEM((2, rows, width), bf16),
         pltpu.VMEM((2, length, width), bf16), pltpu.VMEM((4, width, 2 * head), bf16), pltpu.VMEM((2 * head, width), bf16), dma(7),
         pltpu.VMEM((5, 2, length, 2 * head), f32), dma(),
         pltpu.VMEM((2, length, width), bf16), pltpu.VMEM((2, 4, rows, width), bf16), pltpu.VMEM((2, 3, rows, width), bf16),
         dma(2, 4), dma(2, 3),
         pltpu.VMEM((2, length, length), f32), pltpu.VMEM((2, 8, 8, 128), f32), pltpu.VMEM((2, 8, 8, 128), f32),
         pltpu.VMEM((2, 8, 128), f32), dma(2, 8), dma(2, 8), pltpu.VMEM((2, 128, 128), f32)],
        "forward_part",
    )
    n1_all = n1_all.reshape(2 * length, width)
    dm_all = dm_all.reshape(2 * length, width)
    q_pre, k_pre, v_pre, u_pre, o = [pre_all[n].reshape(2 * length, 2 * head) for n in range(5)]

    def split(values):
        return values.reshape(2, length, 2, head)

    q = split(jax.nn.silu(q_pre).astype(bf16))
    live_low = live.astype(bf16)
    k = split(jax.nn.silu(k_pre).astype(bf16) * live_low)
    v = split(jax.nn.silu(v_pre).astype(bf16) * live_low)
    rates = jnp.take(decay_rate, 4 * (2 * c + jnp.arange(2)) + z)
    places = jnp.arange(length).astype(f32)
    offset = places[:, None] - places[None, :]
    weight = jnp.where(offset >= 0, jnp.exp(-rates[:, None, None] * jnp.maximum(offset, 0.0)), 0.0)
    scores = (jnp.einsum("bihd,bjhd->bhij", q, k, preferred_element_type=f32) * weight).astype(bf16)
    u = jax.nn.silu(u_pre)
    g = u * o

    def per_token(values):
        return values[:, 0].reshape(8, 2, rows).transpose(1, 0, 2).reshape(2 * length, 1)

    n2_all = n2_all.reshape(2 * length, width)
    h1 = product_right(n2_all, f_w)
    h2 = product_right(n2_all, s_w)
    p = (h1 * h2).astype(bf16)
    part_m = product(p, t_w).astype(bf16).reshape(2, length, width)
    dp = product_right(dm_all, t_w)
    dh1 = (dp * h2).astype(bf16)
    dh2 = (dp * h1).astype(bf16)
    part = (product(dh1, f_w) + product(dh2, s_w)).astype(bf16).reshape(2, length, width)
    gf = product_left(dh1, n2_all).astype(bf16)
    gs = product_left(dh2, n2_all).astype(bf16)
    gt = product_left(p, dm_all).astype(bf16)

    da_all, dh, out, mix_all = call(
        ffn_back,
        2,
        [(part, ANY), (part_m, ANY), (dy, VMEM), (h, VMEM), (branch, VMEM)],
        [(low_array(2, length, width), ANY), (wide_array(2 * rows, width), VMEM), (low_array(2 * rows, width), VMEM),
         (wide_array(8, 8, 2 * rows), ANY)],
        [dma(80)] + scatter_scratch(rows, width) + scatter_scratch(rows, width)
        + [pltpu.VMEM((2, rows, width), bf16), pltpu.VMEM((8, 2 * rows), f32), dma(8),
           dma(2, 2, 3), dma(2, 7), dma(2), pltpu.VMEM((2 * rows, 2 * rows), f32)],
        "ffn_back",
    )
    da_all = da_all.reshape(2 * length, width)
    inverse = scale_all[:, :, 0, :rows].reshape(2 * length, 1)
    mix = per_token(mix_all)
    nat = g * inverse
    go = product_left(nat.astype(bf16), da_all).astype(bf16)
    dg = inverse * (product_right(da_all, o_w) - nat * mix)
    do = split((dg * u).astype(bf16))
    du_pre = (dg * o * silu_slope(u_pre)).astype(bf16)
    d_scores = (jnp.einsum("bihe,bjhe->bhij", do, v, preferred_element_type=f32) * weight).astype(bf16)
    dq = jnp.einsum("bhij,bjhd->bihd", d_scores, k, preferred_element_type=f32).reshape(2 * length, 2 * head)
    dk = jnp.einsum("bhij,bihd->bjhd", d_scores, q, preferred_element_type=f32).reshape(2 * length, 2 * head)
    dv = jnp.einsum("bhij,bihe->bjhe", scores, do, preferred_element_type=f32).reshape(2 * length, 2 * head)
    dq_pre = (dq * silu_slope(q_pre)).astype(bf16)
    dk_pre = (dk * live * silu_slope(k_pre)).astype(bf16)
    dv_pre = (dv * live * silu_slope(v_pre)).astype(bf16)
    part = product_right(dq_pre, q_w) + product_right(dk_pre, k_w)
    part = (part + product_right(dv_pre, v_w) + product_right(du_pre, u_w)).astype(bf16).reshape(2, length, width)
    heads = [product_left(n1_all, d).astype(bf16).reshape(4, 2, depth, 2 * head) for d in (dq_pre, dk_pre, dv_pre, du_pre)]

    dn1, fq, fk, fv, fu, fo, ff, fs, ft = call(
        gradients,
        3,
        [(v, ANY) for v in [part] + heads + [go, gf, gs, gt]],
        [(wide_array(2 * rows, width), VMEM)] + [(low_array(depth, wide), ANY)] * 4 + [(low_array(depth, wide), ANY)]
        + [(low_array(2 * hidden, depth), ANY)] * 2 + [(low_array(hidden, wide), ANY)],
        [dma(140)] + scatter_scratch(rows, width)
        + [pltpu.VMEM((4, 4, 4, depth, head), bf16), pltpu.VMEM((4, 2 * head, wide), bf16),
           pltpu.VMEM((2, 4, hidden // 4, width), bf16), pltpu.VMEM((4, hidden, wide), bf16),
           dma(4, 4), dma(4), dma(2, 4), dma(4),
           pltpu.VMEM((4, 4, depth, head), bf16), pltpu.VMEM((2 * head, wide), bf16),
           pltpu.VMEM((2, hidden // 4, width), bf16), pltpu.VMEM((hidden, wide), bf16),
           dma(4, 4), dma(2), dma(2, 8), dma(4)],
        "gradients",
    )
    grad_x = dh + norm_back(x, dn1)
    return (
        out.reshape(2, 1, rows, width),
        grad_x.reshape(2, 1, rows, width),
        fq.astype(f32), fk.astype(f32), fv.astype(f32), fu.astype(f32), fo.astype(f32),
        ff.T.astype(f32), fs.T.astype(f32), ft.astype(f32),
    )


def solution(mesh):
    in_specs = (
        P(None, "grp", "seq", None),
        P(None, "grp", "seq", None),
        P(None, "grp"),
        P(),
        P("seq", "grp"),
        P("seq", "grp"),
        P("seq", "grp"),
        P("seq", "grp"),
        P("seq", "grp"),
        P("seq", "grp"),
        P("seq", "grp"),
        P("seq", "grp"),
    )
    out_specs = (
        P(None, "grp", "seq", None),
        P(None, "grp", "seq", None),
        P("seq", "grp"),
        P("seq", "grp"),
        P("seq", "grp"),
        P("seq", "grp"),
        P("seq", "grp"),
        P("seq", "grp"),
        P("seq", "grp"),
        P("seq", "grp"),
    )
    fast = mesh.shape["grp"] == 4 and mesh.shape["seq"] == 8
    return jax.shard_map(line_shards if fast else shards, mesh=mesh, in_specs=in_specs, out_specs=out_specs, check_vma=False)
```

```python
import jax
import jax.numpy as jnp
from jax import lax
from jax.experimental import pallas as pl
from jax.experimental.pallas import tpu as pltpu
from jax.sharding import PartitionSpec as P

EPS = 1e-06
HIGH = lax.Precision.HIGHEST
MESH = pl.DeviceIdType.MESH
ANY = pl.BlockSpec(memory_space=pl.ANY)
VMEM = pl.BlockSpec(memory_space=pltpu.VMEM)


def prefix(value, axis, join, neutral, backward):
    count, mine = (lax.axis_size(axis), lax.axis_index(axis))
    pieces = jax.tree.map(lambda part: lax.all_gather(part, axis), value)
    if backward:
        pieces = jax.tree.map(lambda part: part[::-1], pieces)
        mine = count - 1 - mine
    subtotal = jax.tree.map(
        lambda part, zero: jnp.full_like(part, 0) + jnp.asarray(zero, part.dtype), value, neutral
    )

    def step(position, subtotal):
        longer = join(subtotal, jax.tree.map(lambda part: part[position], pieces))
        return jax.tree.map(lambda new, old: jnp.where(position < mine, new, old), longer, subtotal)

    return lax.fori_loop(0, count - 1, step, subtotal)


def norm_rows(values):
    return values * lax.rsqrt(jnp.mean(values * values, axis=-1, keepdims=True) + EPS)


def norm_back(values, gradient):
    _, pull = jax.vjp(norm_rows, values)
    return pull(gradient)[0]


def silu_slope(values):
    sigma = jax.nn.sigmoid(values)
    return sigma * (1.0 + values * (1.0 - sigma))


def product(left, right):
    return jnp.dot(left, right, preferred_element_type=jnp.float32)


def product_left(left, right):
    return lax.dot_general(
        left, right, (((0,), (0,)), ((), ())), preferred_element_type=jnp.float32
    )


def product_right(left, right):
    return lax.dot_general(
        left, right, (((1,), (1,)), ((), ())), preferred_element_type=jnp.float32
    )


def combine_state(earlier, later):
    return (later[1][:, None, None] * earlier[0] + later[0], earlier[1] * later[1])


def shards(
    tokens,
    cotangent,
    lengths,
    decay_rate,
    w_query,
    w_key,
    w_value,
    w_gate,
    w_out,
    w_first,
    w_second,
    w_third,
):
    micro = tokens.shape[0]
    block_rows = tokens.shape[2]
    width = tokens.shape[3]
    heads = decay_rate.shape[0]
    head_dim = width // heads
    hidden_width = w_third.shape[0] * lax.axis_size("seq")
    places = jnp.arange(block_rows).astype(jnp.float32)
    slot_index = lax.axis_index("seq") * block_rows + jnp.arange(block_rows)
    offset = places[:, None] - places[None, :]
    weight = jnp.where(
        offset[None] >= 0, jnp.exp(-decay_rate[:, None, None] * jnp.maximum(offset, 0.0)[None]), 0.0
    )
    query_fac = jnp.exp(-decay_rate[None, :] * (places[:, None] + 1.0))[:, :, None]
    key_fac = jnp.exp(-decay_rate[None, :] * (block_rows - 1.0 - places[:, None]))[:, :, None]
    step_decay = jnp.exp(-decay_rate * block_rows)
    empty_state = jnp.zeros((heads, head_dim, head_dim), jnp.float32)
    unit_decay = jnp.ones((heads,), jnp.float32)
    partial_rows = (
        lax.all_gather(w_query, "grp", axis=1, tiled=True),
        lax.all_gather(w_key, "grp", axis=1, tiled=True),
        lax.all_gather(w_value, "grp", axis=1, tiled=True),
        lax.all_gather(w_gate, "grp", axis=1, tiled=True),
        lax.all_gather(w_out, "grp", axis=1, tiled=True),
        lax.all_gather(w_first, "grp", axis=1, tiled=True),
        lax.all_gather(w_second, "grp", axis=1, tiled=True),
        lax.all_gather(w_third, "grp", axis=1, tiled=True),
    )
    gathered = (
        lax.all_gather(partial_rows[0], "seq", axis=0, tiled=True),
        lax.all_gather(partial_rows[1], "seq", axis=0, tiled=True),
        lax.all_gather(partial_rows[2], "seq", axis=0, tiled=True),
        lax.all_gather(partial_rows[3], "seq", axis=0, tiled=True),
        lax.all_gather(partial_rows[4], "seq", axis=0, tiled=True),
        lax.all_gather(partial_rows[5], "seq", axis=0, tiled=True),
        lax.all_gather(partial_rows[6], "seq", axis=0, tiled=True),
        lax.all_gather(partial_rows[7], "seq", axis=0, tiled=True),
    )
    outputs = []
    input_grads = []
    first_norms = []
    attn_rows = []
    normed_rows = []
    branch_rows = []
    second_norms = []
    ffn_rows = []
    mixed_rows = []
    upstream_rows = []
    for batch_idx in range(micro):
        wq_full, wk_full, wv_full, wu_full, wo_full, first_full, second_full, third_full = gathered
        inputs = tokens[batch_idx, 0].astype(jnp.float32)
        live = (slot_index < lengths[batch_idx, 0]).astype(jnp.float32)[:, None]
        live_low = live.astype(jnp.bfloat16)
        first_norm = norm_rows(inputs).astype(jnp.bfloat16)
        query_pre = product(first_norm, wq_full)
        key_pre = product(first_norm, wk_full)
        value_pre = product(first_norm, wv_full)
        gate_pre = product(first_norm, wu_full)
        queries = jax.nn.silu(query_pre).astype(jnp.bfloat16).reshape(block_rows, heads, head_dim)
        key_heads = (jax.nn.silu(key_pre).astype(jnp.bfloat16) * live_low).reshape(
            block_rows, heads, head_dim
        )
        value_heads = (jax.nn.silu(value_pre).astype(jnp.bfloat16) * live_low).reshape(
            block_rows, heads, head_dim
        )
        query_wide = queries.astype(jnp.float32)
        key_wide = key_heads.astype(jnp.float32)
        value_wide = value_heads.astype(jnp.float32)
        local_state = jnp.einsum("jhd,jhe->hde", key_wide * key_fac, value_wide, precision=HIGH)
        prior_state, _ = prefix(
            (local_state, step_decay), "seq", combine_state, (empty_state, unit_decay), False
        )
        scores = (
            jnp.einsum("ihd,jhd->hij", queries, key_heads, preferred_element_type=jnp.float32)
            * weight
        )
        intra = jnp.einsum("hij,jhe->ihe", scores, value_wide, precision=HIGH)
        inter = jnp.einsum("ihd,hde->ihe", query_wide * query_fac, prior_state, precision=HIGH)
        attended = (intra + inter).reshape(block_rows, width)
        gate_act = jax.nn.silu(gate_pre)
        gated = gate_act * attended
        normed = norm_rows(gated).astype(jnp.bfloat16)
        hidden = inputs + product(normed, wo_full)
        second_norm = norm_rows(hidden).astype(jnp.bfloat16)
        first_proj = product(second_norm, first_full)
        second_proj = product(second_norm, second_full)
        mixed_in = (first_proj * second_proj).astype(jnp.bfloat16)
        result = hidden + product(mixed_in, third_full)
        outputs.append(result.astype(jnp.bfloat16))
        upstream = cotangent[batch_idx, 0].astype(jnp.float32) * live
        upstream_low = upstream.astype(jnp.bfloat16)
        grad_mixed = product_right(upstream_low, third_full)
        grad_first_proj = (grad_mixed * second_proj).astype(jnp.bfloat16)
        grad_second_proj = (grad_mixed * first_proj).astype(jnp.bfloat16)
        grad_norm_two = product_right(grad_first_proj, first_full) + product_right(
            grad_second_proj, second_full
        )
        grad_hidden = upstream + norm_back(hidden, grad_norm_two)
        grad_branch = grad_hidden.astype(jnp.bfloat16)
        grad_gated = norm_back(gated, product_right(grad_branch, wo_full))
        grad_attended = (grad_gated * gate_act).astype(jnp.bfloat16)
        grad_gate_pre = (grad_gated * attended * silu_slope(gate_pre)).astype(jnp.bfloat16)
        grad_heads = grad_attended.reshape(block_rows, heads, head_dim)
        grad_wide = grad_heads.astype(jnp.float32)
        local_grad = jnp.einsum("ihd,ihe->hde", query_wide * query_fac, grad_wide, precision=HIGH)
        later_grad, _ = prefix(
            (local_grad, step_decay), "seq", combine_state, (empty_state, unit_decay), True
        )
        grad_scores = (
            jnp.einsum("ihe,jhe->hij", grad_heads, value_heads, preferred_element_type=jnp.float32)
            * weight
        )
        grad_queries = jnp.einsum("hij,jhd->ihd", grad_scores, key_wide, precision=HIGH)
        grad_queries = (
            grad_queries
            + jnp.einsum("ihe,hde->ihd", grad_wide, prior_state, precision=HIGH) * query_fac
        )
        grad_keys = jnp.einsum("hij,ihd->jhd", grad_scores, query_wide, precision=HIGH)
        grad_keys = (
            grad_keys + jnp.einsum("hde,jhe->jhd", later_grad, value_wide, precision=HIGH) * key_fac
        )
        grad_values = jnp.einsum("hij,ihe->jhe", scores, grad_wide, precision=HIGH)
        grad_values = (
            grad_values + jnp.einsum("jhd,hde->jhe", key_wide, later_grad, precision=HIGH) * key_fac
        )
        grad_query_pre = (grad_queries.reshape(block_rows, width) * silu_slope(query_pre)).astype(
            jnp.bfloat16
        )
        grad_key_pre = (grad_keys.reshape(block_rows, width) * live * silu_slope(key_pre)).astype(
            jnp.bfloat16
        )
        grad_value_pre = (
            grad_values.reshape(block_rows, width) * live * silu_slope(value_pre)
        ).astype(jnp.bfloat16)
        grad_norm_one = product_right(grad_query_pre, wq_full) + product_right(
            grad_key_pre, wk_full
        )
        grad_norm_one = (
            grad_norm_one
            + product_right(grad_value_pre, wv_full)
            + product_right(grad_gate_pre, wu_full)
        )
        input_grads.append(grad_hidden + norm_back(inputs, grad_norm_one))
        first_norms.append(first_norm)
        attn_rows.append(
            jnp.concatenate([grad_query_pre, grad_key_pre, grad_value_pre, grad_gate_pre], axis=1)
        )
        normed_rows.append(normed)
        branch_rows.append(grad_branch)
        second_norms.append(second_norm)
        ffn_rows.append(jnp.concatenate([grad_first_proj, grad_second_proj], axis=1))
        mixed_rows.append(mixed_in)
        upstream_rows.append(upstream_low)
    first_all = jnp.concatenate(first_norms, axis=0)
    attn_all = jnp.concatenate(attn_rows, axis=0)
    normed_all = jnp.concatenate(normed_rows, axis=0)
    branch_all = jnp.concatenate(branch_rows, axis=0)
    second_all = jnp.concatenate(second_norms, axis=0)
    ffn_all = jnp.concatenate(ffn_rows, axis=0)
    mixed_all = jnp.concatenate(mixed_rows, axis=0)
    upstream_all = jnp.concatenate(upstream_rows, axis=0)
    proj_rows = lax.psum_scatter(
        product_left(first_all, attn_all), "seq", scatter_dimension=0, tiled=True
    )
    outproj_rows = lax.psum_scatter(
        product_left(normed_all, branch_all), "seq", scatter_dimension=0, tiled=True
    )
    ffn_part = lax.psum_scatter(
        product_left(second_all, ffn_all), "seq", scatter_dimension=0, tiled=True
    )
    down_rows = lax.psum_scatter(
        product_left(mixed_all, upstream_all), "seq", scatter_dimension=0, tiled=True
    )
    summed = (
        lax.psum_scatter(proj_rows[:, :width], "grp", scatter_dimension=1, tiled=True),
        lax.psum_scatter(proj_rows[:, width : 2 * width], "grp", scatter_dimension=1, tiled=True),
        lax.psum_scatter(
            proj_rows[:, 2 * width : 3 * width], "grp", scatter_dimension=1, tiled=True
        ),
        lax.psum_scatter(proj_rows[:, 3 * width :], "grp", scatter_dimension=1, tiled=True),
        lax.psum_scatter(outproj_rows, "grp", scatter_dimension=1, tiled=True),
        lax.psum_scatter(ffn_part[:, :hidden_width], "grp", scatter_dimension=1, tiled=True),
        lax.psum_scatter(ffn_part[:, hidden_width:], "grp", scatter_dimension=1, tiled=True),
        lax.psum_scatter(down_rows, "grp", scatter_dimension=1, tiled=True),
    )
    layer_out = jnp.stack(outputs)[:, None]
    grad_tokens = jnp.stack(input_grads)[:, None]
    return (
        layer_out,
        grad_tokens,
        summed[0],
        summed[1],
        summed[2],
        summed[3],
        summed[4],
        summed[5],
        summed[6],
        summed[7],
    )


class Copies:
    def __init__(self, sems):
        self.sems = sems
        self.used = 0
        self.pending = []

    def remote(self, src, dst, recv_sem, group, place, when=None):
        assert self.used < self.sems.shape[0]
        copy = pltpu.make_async_remote_copy(
            src_ref=src,
            dst_ref=dst,
            send_sem=self.sems.at[self.used],
            recv_sem=recv_sem,
            device_id=(group, place),
            device_id_type=MESH,
        )
        self.used += 1
        self.pending.append((copy, when))
        if when is None:
            copy.start()
        else:
            pl.when(when)(copy.start)

    def finish(self):
        for copy, when in self.pending:
            if when is None:
                copy.wait_send()
            else:
                pl.when(when)(copy.wait_send)
        self.pending = []


def local(src, dst, sem, when=None):
    copy = pltpu.make_async_copy(src, dst, sem)
    if when is None:
        copy.start()
    else:
        pl.when(when)(copy.start)


def arrived(ref, sem, when=None):
    copy = pltpu.make_async_copy(ref, ref, sem)
    if when is None:
        copy.wait()
    else:
        pl.when(when)(copy.wait)


def where_am_i():
    g, s = lax.axis_index("grp"), lax.axis_index("seq")
    return g, s, g // 2, g % 2, s // 2, s % 2


def across(y, x):
    return (y * 2 + 1 - x, (1 - y) * 2 + x, (1 - y) * 2 + 1 - x)


def greet(partners):
    barrier = pltpu.get_barrier_semaphore()
    for partner in partners:
        pl.semaphore_signal(barrier, inc=1, device_id=partner, device_id_type=MESH)
    pl.semaphore_wait(barrier, len(partners))


def aligned(index, unit, step):
    return pl.ds(pl.multiple_of(index * unit, step), unit)


class Gather:
    def __init__(self, copies, out, rows, hop_sem, side_sem):
        self.copies, self.out, self.rows = copies, out, rows
        self.hop_sem, self.side_sem = hop_sem, side_sem
        self.g, self.s, _, _, self.z, self.c = where_am_i()

    def block(self, b, z, core):
        return self.out.at[b, aligned(2 * z + core, self.rows, 16)]

    def spread(self, src, b, z_of, k, right, left):
        g, s, z, c = self.g, self.s, self.z, self.c
        dst = self.block(b, z_of, c)
        if right is not None:
            self.copies.remote(src, dst, self.hop_sem.at[b, 0, k], g, (s + 2) % 8, right)
        if left is not None:
            self.copies.remote(src, dst, self.hop_sem.at[b, 1, k], g, (s + 6) % 8, left)

    def begin(self, src, own_sem, b):
        g, s, z, c = self.g, self.s, self.z, self.c
        self.spread(src, b, z, 0, z < 3, z > 0)
        self.copies.remote(src, self.block(b, z, c), self.side_sem.at[b, 0], g, s + 1 - 2 * c)
        local(src, self.block(b, z, c), own_sem)

    def step(self, b, k):
        g, s, z, c = self.g, self.s, self.z, self.c
        side = s + 1 - 2 * c
        has = z >= k
        at = jnp.maximum(z - k, 0)
        ref = self.block(b, at, c)
        arrived(ref, self.hop_sem.at[b, 0, k - 1], has)
        if k < 3:
            self.spread(ref, b, at, k, jnp.logical_and(has, z < 3), None)
        self.copies.remote(ref, ref, self.side_sem.at[b, k], g, side, has)
        has = z + k <= 3
        at = jnp.minimum(z + k, 3)
        ref = self.block(b, at, c)
        arrived(ref, self.hop_sem.at[b, 1, k - 1], has)
        if k < 3:
            self.spread(ref, b, at, k, None, jnp.logical_and(has, z > 0))
        self.copies.remote(ref, ref, self.side_sem.at[b, 3 + k], g, side, has)

    def finish(self, own_sem, b):
        z, c = self.z, self.c
        arrived(self.block(b, z, c), own_sem)
        arrived(self.block(b, z, 1 - c), self.side_sem.at[b, 0])
        for k in (1, 2, 3):
            arrived(self.block(b, jnp.maximum(z - k, 0), 1 - c), self.side_sem.at[b, k], z >= k)
            arrived(self.block(b, jnp.minimum(z + k, 3), 1 - c), self.side_sem.at[b, 3 + k], z + k <= 3)


def line_partners(g, s):
    return [(g, (s + d) % 8) for d in range(1, 8)]


def everyone_on_line(copies, src, dst, sem, g, s, to_rows):
    for d in range(1, 8):
        to = (s + d) % 8
        copies.remote(to_rows(to), dst.at[s], sem.at[d - 1], g, to)


def mean_square(values):
    return jnp.mean(values * values, axis=-1, keepdims=True)


def pour(read, write, count):
    def piece(i, carry):
        at = aligned(i, 16, 16)
        write(at, read(at))
        return carry

    lax.fori_loop(0, count, piece, 0)


class LineScatter:
    def __init__(self, copies, part, rows, side, inbox, side_sem, line_sem):
        self.copies, self.part, self.rows = copies, part, rows
        self.side, self.inbox, self.side_sem, self.line_sem = side, inbox, side_sem, line_sem
        self.g, self.s, _, _, self.z, self.c = where_am_i()

    def mine(self, chip):
        return self.part.at[aligned(2 * chip + self.c, self.rows, 16)]

    def begin(self):
        for chip in (3, 0, 2, 1):
            theirs = aligned(2 * chip + 1 - self.c, self.rows, 16)
            self.copies.remote(
                self.part.at[theirs], self.side.at[chip], self.side_sem.at[chip], self.g, self.s + 1 - 2 * self.c
            )

    def pass_on(self, chip, way, edge):
        z = self.z
        slot = chip - 1 if way == 0 else chip
        own, side, come = self.mine(chip), self.side.at[chip], self.inbox.at[way, slot]
        before = (z < chip) if way == 0 else (z > chip)
        first = (z == 0) if way == 0 else (z == 3)
        go = jnp.logical_and(before, first if edge else jnp.logical_not(first))

        def write(at, value):
            own[at] = value.astype(jnp.bfloat16)

        def two(at):
            return own[at].astype(jnp.float32) + side[at].astype(jnp.float32)

        @pl.when(go)
        def _():
            arrived(side, self.side_sem.at[chip])
            if edge:
                pour(two, write, self.rows // 16)
            else:
                arrived(come, self.line_sem.at[way, slot])
                pour(lambda at: two(at) + come[at].astype(jnp.float32), write, self.rows // 16)

        to = (self.s + 2) % 8 if way == 0 else (self.s + 6) % 8
        self.copies.remote(own, come, self.line_sem.at[way, slot], self.g, to, go)

    def ends(self):
        for i in range(3):
            self.pass_on(3 - i, 0, True)
            self.pass_on(i, 1, True)

    def hop(self, i):
        self.pass_on(3 - i, 0, False)
        self.pass_on(i, 1, False)

    def receive(self):
        z = self.z
        arrived(self.side.at[z], self.side_sem.at[z])
        left, right = jnp.maximum(z - 1, 0), jnp.minimum(z, 2)
        arrived(self.inbox.at[0, left], self.line_sem.at[0, left], z > 0)
        arrived(self.inbox.at[1, right], self.line_sem.at[1, right], z < 3)

    def total(self, at):
        z = self.z
        value = self.mine(z)[at].astype(jnp.float32) + self.side[z, at].astype(jnp.float32)
        from_left = self.inbox[0, jnp.maximum(z - 1, 0), at].astype(jnp.float32)
        from_right = self.inbox[1, jnp.minimum(z, 2), at].astype(jnp.float32)
        return value + jnp.where(z > 0, from_left, 0.0) + jnp.where(z < 3, from_right, 0.0)


def silu(values):
    return values / (1.0 + jnp.exp(-values))


def decay_table(rate, length):
    offset = lax.broadcasted_iota(jnp.int32, (length, length), 0) - lax.broadcasted_iota(jnp.int32, (length, length), 1)
    steps = jnp.maximum(offset, 0).astype(jnp.float32)
    return jnp.where(offset >= 0, jnp.exp(-rate * steps), 0.0)


def live_rows(first, count, length):
    return ((first + lax.broadcasted_iota(jnp.int32, (count, 1), 0)) < length).astype(jnp.float32)


def forward_part(
    lengths, decay, x, cot, wq, wk, wv, wu, wo, w1, w2, w3,
    n1_all, dm_all, n2_all, q_all, k_all, v_all, u_all, o_all, f_all, s_all, t_all, pre_all, h, scale_all,
    send, own, hop_n, side_n, hop_d, side_d, hop_m, side_m, z_head, z_out, z_ff, xy_head, xy_out, xy_ff,
    n1, dm, n2, n1_v, w_v, wo_v, load, pre_v, pre_sem, part, side, inbox, side_sem, line_sem,
    table, squares, inbox_sq, scale, sq_sem, sc_sem, column,
):
    g, s, y, x_, z, c = where_am_i()
    others = across(y, x_)
    greet(line_partners(g, s) + [(o, s) for o in others])
    copies = Copies(send)
    rows, width = x.shape[1], x.shape[2]
    length = 8 * rows
    gather_n = Gather(copies, n1_all, rows, hop_n, side_n)
    gather_d = Gather(copies, dm_all, rows, hop_d, side_d)
    gather_m = Gather(copies, n2_all, rows, hop_m, side_m)
    heads = list(zip((wq, wk, wv, wu), (q_all, k_all, v_all, u_all)))
    depth, wide = wq.shape
    head = q_all.shape[1] // 2
    ff = f_all.shape[0] // 4
    target = g // 2
    mine = aligned(g % 2, head, head)
    here = c == target
    order = [(z + d) % 4 for d in (0, 1, 3, 2)]

    def send_heads(n):
        src, dst = heads[n]
        for d in (2, 1, 3, 0):
            to = (z + d) % 4
            a, b = src.at[:, aligned(to, head, head)], dst.at[aligned(s, depth, 16), mine]
            if d:
                copies.remote(a, b, z_head.at[n, z], g, 2 * to + target)
            else:
                copies.remote(a, b, z_head.at[n, z], g, 2 * to + target, c != target)
                local(a, b, z_head.at[n, z], here)

    def pass_heads(n):
        dst = heads[n][1]
        for zs in order:
            block = dst.at[aligned(zs, 2 * depth, 16), mine]
            arrived(block, z_head.at[n, zs], here)
            for r, o in enumerate(others):
                copies.remote(block, block, xy_head.at[n, r, zs], o, s, here)

    def send_out():
        for i in range(2):
            to = 2 * c + i
            a = wo.at[pl.ds(i * head, head)]
            b = o_all.at[aligned(z % 2, head, head), aligned(g, wide, 128)]
            self_ = jnp.logical_and(to == z, c == z // 2)
            copies.remote(a, b, z_out.at[z % 2], g, 2 * to + z // 2, jnp.logical_not(self_))
            local(a, b, z_out.at[z % 2], self_)

    def pass_out():
        for j in range(2):
            arrived(o_all.at[pl.ds(j * head, head), aligned(g, wide, 128)], z_out.at[j])
        block = o_all.at[:, aligned(g, wide, 128)]
        for r, o in enumerate(others):
            copies.remote(block, block, xy_out.at[r], o, s)

    def send_ff(n):
        src, dst = ((w1, f_all), (w2, s_all))[n]
        for d in (4, 3, 5, 2, 6, 1, 7, 0):
            to = (s + d) % 8
            a = src.at[aligned(to, ff, 16)]
            b = dst.at[aligned(g, ff, 16), aligned(s, depth, 128)]
            if d:
                copies.remote(a, b, z_ff.at[n, z], g, to)
            else:
                local(a, b, z_ff.at[n, z])

    def pass_ff(n):
        dst = (f_all, s_all)[n]
        for zs in order:
            block = dst.at[aligned(g, ff, 16), aligned(zs, 2 * depth, 128)]
            arrived(block, z_ff.at[n, zs])
            for r, o in enumerate(others):
                copies.remote(block, block, xy_ff.at[n, r, zs], o, s)

    def send_third():
        for d in (2, 1, 3, 0):
            to = 4 * c + (s + d) % 4
            a = w3.at[aligned(to % 4, ff, 16)]
            b = t_all.at[aligned(z, ff, 16), aligned(g, wide, 128)]
            if d:
                copies.remote(a, b, z_ff.at[2, z], g, to)
            else:
                self_ = s // 4 == c
                copies.remote(a, b, z_ff.at[2, z], g, to, jnp.logical_not(self_))
                local(a, b, z_ff.at[2, z], self_)

    def pass_third():
        for zs in order:
            block = t_all.at[aligned(zs, ff, 16), aligned(g, wide, 128)]
            arrived(block, z_ff.at[2, zs])
            for r, o in enumerate(others):
                copies.remote(block, block, xy_ff.at[2, r, zs], o, s)

    send_heads(0)
    send_heads(1)
    for b in range(2):

        def norm(at):
            v = x[b, at].astype(jnp.float32)
            return v * lax.rsqrt(mean_square(v) + EPS)

        def keep(at, value):
            n1[b, at] = value.astype(jnp.bfloat16)

        pour(norm, keep, rows // 16)
        first = s * rows

        def masked(i, carry):
            at = aligned(i, 16, 16)
            live = live_rows(first + i * 16, 16, lengths[b, 0])
            dm[b, at] = (cot[b, at].astype(jnp.float32) * live).astype(jnp.bfloat16)
            return carry

        lax.fori_loop(0, rows // 16, masked, 0)
    pass_heads(0)
    send_heads(2)
    pass_heads(1)
    send_heads(3)
    for b in range(2):
        gather_n.begin(n1.at[b], own.at[0, b], b)
    send_out()
    pass_heads(2)
    pass_heads(3)
    gather_n.step(0, 1)
    gather_n.step(1, 1)
    pass_out()
    gather_n.step(0, 2)
    gather_n.step(1, 2)
    send_ff(0)
    gather_n.step(0, 3)
    gather_n.step(1, 3)
    for r, o in enumerate(others):
        from_here = (o // 2) == c
        for n, (_, dst) in enumerate(heads):
            for zs in range(4):
                block = dst.at[pl.ds(zs * 2 * depth, 2 * depth), aligned(o % 2, head, head)]
                arrived(block, xy_head.at[n, r, zs], from_here)
        arrived(o_all.at[:, aligned(o, wide, 128)], xy_out.at[r])
    for n, (_, dst) in enumerate(heads):
        local(dst, w_v.at[n], load.at[n])
    local(o_all, wo_v, load.at[4])
    for b in range(2):
        gather_n.finish(own.at[0, b], b)
        local(n1_all.at[b], n1_v.at[b], load.at[5 + b])
    for j in range(2):
        table[j] = decay_table(decay[4 * (2 * c + j) + z], length)
    for n in range(4):
        arrived(w_v.at[n], load.at[n])
    arrived(wo_v, load.at[4])
    scatters = []
    for b in range(2):
        arrived(n1_v.at[b], load.at[5 + b])
        half = length // 2

        def project(i, carry):
            at = aligned(i, half, 16)
            for n in range(4):
                pre_v[n, b, at] = product(n1_v[b, at], w_v[n])
            return carry

        lax.fori_loop(0, 2, project, 0)
        live = live_rows(0, length, lengths[b, 0])
        for j in range(2):
            lanes = pl.ds(j * head, head)
            q = silu(pre_v[0, b, :, lanes]).astype(jnp.bfloat16)
            k = (silu(pre_v[1, b, :, lanes]) * live).astype(jnp.bfloat16)
            v = (silu(pre_v[2, b, :, lanes]) * live).astype(jnp.bfloat16)
            scores = (product_right(q, k) * table[j]).astype(jnp.bfloat16)
            pre_v[4, b, :, lanes] = product(scores, v)
        gated = silu(pre_v[3, b]) * pre_v[4, b]
        square = jnp.sum(gated * gated, axis=-1, keepdims=True)
        row = jnp.broadcast_to(square, (length, 128)).T[:8]
        for to in range(8):
            squares[b, to, :, :rows] = row[:, to * rows : (to + 1) * rows]
        low = gated.astype(jnp.bfloat16)

        def out_part(i, carry):
            at = aligned(i, 256, 256)
            part[b, :, at] = product(low, wo_v[:, at]).astype(jnp.bfloat16)
            return carry

        lax.fori_loop(0, width // 256, out_part, 0)
        scatter = LineScatter(copies, part.at[b], rows, side.at[b], inbox.at[b], side_sem.at[b], line_sem.at[b])
        scatter.begin()
        scatter.ends()
        everyone_on_line(copies, squares, inbox_sq.at[b], sq_sem.at[b], g, s, lambda to: squares.at[b, to])
        local(squares.at[b, s], inbox_sq.at[b, s], sq_sem.at[b, 7])
        scatters.append(scatter)
    local(pre_v, pre_all, pre_sem)
    scatters[0].hop(0)
    scatters[0].hop(1)
    scatters[1].hop(0)
    scatters[0].hop(2)
    scatters[1].hop(1)
    scatters[1].hop(2)
    pass_ff(0)
    for b in range(2):
        for d in range(8):
            arrived(inbox_sq.at[b, 0], sq_sem.at[b, d])
        total = inbox_sq[b, 0]
        for d in range(1, 8):
            total = total + inbox_sq[b, d]
        row = lax.rsqrt(total / width + EPS)
        scale[b] = row
        for d in range(1, 8):
            copies.remote(scale.at[b], scale_all.at[b, s], sc_sem.at[b, d - 1], g, (s + d) % 8)
        local(scale.at[b], scale_all.at[b, s], sc_sem.at[b, 7])
        column[b] = jnp.broadcast_to(row[:1], (128, 128)).T
    for b in range(2):
        scatter = scatters[b]
        scatter.receive()
        if b == 0:
            send_ff(1)
        else:
            send_third()

        def finish(i, carry):
            piece = aligned(i, 16, 16)
            at = aligned(b * (rows // 16) + i, 16, 16)
            a = scatter.total(piece) * column[b, piece, :1]
            hidden = x[b, piece].astype(jnp.float32) + a
            h[at] = hidden
            n2[b, piece] = (hidden * lax.rsqrt(mean_square(hidden) + EPS)).astype(jnp.bfloat16)
            return carry

        lax.fori_loop(0, rows // 16, finish, 0)
        gather_m.begin(n2.at[b], own.at[2, b], b)
    for b in range(2):
        gather_d.begin(dm.at[b], own.at[1, b], b)
    gather_m.step(0, 1)
    gather_m.step(1, 1)
    pass_ff(1)
    gather_m.step(0, 2)
    gather_m.step(1, 2)
    gather_d.step(0, 1)
    gather_d.step(1, 1)
    pass_third()
    gather_m.step(0, 3)
    gather_m.step(1, 3)
    for k in (2, 3):
        for b in range(2):
            gather_d.step(b, k)

    for b in range(2):
        gather_d.finish(own.at[1, b], b)
        gather_m.finish(own.at[2, b], b)
    for r, o in enumerate(others):
        for n, dst in enumerate((f_all, s_all)):
            for zs in range(4):
                arrived(dst.at[aligned(o, ff, 16), pl.ds(zs * 2 * depth, 2 * depth)], xy_ff.at[n, r, zs])
        for zs in range(4):
            arrived(t_all.at[pl.ds(zs * ff, ff), aligned(o, wide, 128)], xy_ff.at[2, r, zs])
    for b in range(2):
        for d in range(8):
            arrived(scale.at[b], sc_sem.at[b, d])
    arrived(pre_v, pre_sem)
    copies.finish()


def slope(values):
    sigma = 1.0 / (1.0 + jnp.exp(-values))
    return sigma * (1.0 + values * (1.0 - sigma))


def turned_table(rate, length):
    offset = lax.broadcasted_iota(jnp.int32, (length, length), 1) - lax.broadcasted_iota(jnp.int32, (length, length), 0)
    steps = jnp.maximum(offset, 0).astype(jnp.float32)
    return jnp.where(offset >= 0, jnp.exp(-rate * steps), 0.0)


def columns_of(out, tiles, b, rows):
    for owner in range(8):
        out[pl.ds(owner * rows, rows)] = jnp.broadcast_to(tiles[b, owner, :1], (128, 128)).T[:rows]


def turn(dst, read, count, columns):
    def block(i, carry):
        dst[pl.ds(0, columns), aligned(i, 128, 128)] = read(aligned(i, 128, 128)).T
        return carry

    lax.fori_loop(0, count, block, 0)


def tiles_of(width, body):
    def tile(i, carry):
        body(aligned(i, 256, 256), i)
        return carry

    lax.fori_loop(0, width // 256, tile, 0)


def backward_part(
    lengths, decay, x, cot, h, n1_all, dm_all, n2_all, q_all, k_all, v_all, u_all, o_all, f_all, s_all, t_all, pre_all, scale_all,
    da_all, mix_all, out, grad_x, fq, fk, fv, fu, fo, ff_, fs, ft, in_f, in_t, in_o, in_h,
    send_a, send_b, send_c, send_d, load, own, hop, hside,
    a_v, b_v, w_v, wa_v, wo_v, p_v, turned, part, side, inbox, side_sem, line_sem, side_m, inbox_m, side_sem_m, line_sem_m,
    scale, mix, mix_in, mix_sem, column, inverse, mixed, da, table, pre, dz, nat_v, go_v, grads_h,
    xy_f, xy_t, xy_o, xy_h, z_f, z_t, z_o, z_h,
):
    g, s, y, x_, z, c = where_am_i()
    others = across(y, x_)
    plane = [(o, 2 * z + e) for o in others for e in range(2)]
    rows, width = x.shape[1], x.shape[2]
    length = 8 * rows
    tokens = 2 * length
    ff = in_f.shape[2]
    hidden = 4 * ff
    head = dz.shape[2] // 2
    wide, depth = fo.shape[1], fo.shape[0]

    def at_b(b):
        return pl.ds(b * length, length)

    for b in range(2):
        local(n2_all.at[b], a_v.at[at_b(b)], load.at[b])
        local(dm_all.at[b], b_v.at[at_b(b)], load.at[2 + b])
    for n, src in enumerate((f_all, s_all, t_all)):
        local(src, w_v.at[pl.ds(n * hidden, hidden)], load.at[4 + n])
    for n, src in enumerate((q_all, k_all, v_all, u_all)):
        local(src, wa_v.at[n], load.at[7 + n])
    local(o_all, wo_v, load.at[11])
    local(scale_all, scale, load.at[12])
    greet(line_partners(g, s) + plane)
    sums = Copies(send_a)
    bulk = Copies(send_b)
    last = Copies(send_c)
    early = Copies(send_d)
    gather = Gather(last, da_all, rows, hop, hside)
    w1 = w_v.at[pl.ds(0, hidden)]
    w2 = w_v.at[pl.ds(hidden, hidden)]
    w3 = w_v.at[pl.ds(2 * hidden, hidden)]

    def feed_forward(b):
        def tile(i, carry):
            at = aligned(b * 2 + i, length // 2, 16)
            first = product_right(a_v[at], w1[...])
            second = product_right(a_v[at], w2[...])
            back = product_right(b_v[at], w3[...])
            p_v[0, at] = (back * second).astype(jnp.bfloat16)
            p_v[1, at] = (back * first).astype(jnp.bfloat16)
            p_v[2, at] = (first * second).astype(jnp.bfloat16)
            return carry

        lax.fori_loop(0, 2, tile, 0)

    def norm_part(b):
        def body(at, i):
            value = product(p_v[0, at_b(b)], w1[:, at]) + product(p_v[1, at_b(b)], w2[:, at])
            part[b, :, at] = value.astype(jnp.bfloat16)

        tiles_of(width, body)

    def scatter_of(b, copies):
        return LineScatter(copies, part.at[b], rows, side.at[b], inbox.at[b], side_sem.at[b], line_sem.at[b])

    def scatter_m_of(b, copies):
        return LineScatter(copies, part.at[b], rows, side_m.at[b], inbox_m.at[b], side_sem_m.at[b], line_sem_m.at[b])

    second = [scatter_of(b, early) for b in range(2)]
    for n in (0, 4, 5, 2, 6):
        ref = {0: a_v.at[at_b(0)], 2: b_v.at[at_b(0)], 4: w1, 5: w2, 6: w3}[n]
        arrived(ref, load.at[n])
    feed_forward(0)
    norm_part(0)
    second[0].begin()
    second[0].ends()
    arrived(a_v.at[at_b(1)], load.at[1])
    arrived(b_v.at[at_b(1)], load.at[3])
    feed_forward(1)
    second[0].hop(0)
    norm_part(1)
    second[1].begin()
    second[1].ends()
    second[0].hop(1)
    second[0].hop(2)

    def weight_part(n, operand):
        turn(turned, lambda t: p_v[n, t], tokens // 128, hidden)

        def body(at, i):
            w_v[pl.ds(n * hidden, hidden), at] = product(turned[...], operand[:, at]).astype(jnp.bfloat16)

        tiles_of(width, body)
        for r, o in enumerate(others):
            if n < 2:
                bulk.remote(w_v.at[aligned(4 * n + o, ff, 16)], in_f.at[n, r], xy_f.at[n, r], o, s)
            else:
                bulk.remote(w_v.at[pl.ds(n * hidden, hidden), aligned(o, wide, 128)], in_t.at[r], xy_t.at[r], o, s)

    weight_part(0, a_v)
    second[1].hop(0)
    second[1].hop(1)
    weight_part(1, a_v)
    second[1].hop(2)

    for b in range(2):
        second[b].receive()
        scatter = second[b]

        def finish(i, carry):
            piece = aligned(i, 16, 16)
            at = aligned(b * (rows // 16) + i, 16, 16)
            hidden_state = h[at]
            scale_h = lax.rsqrt(mean_square(hidden_state) + EPS)
            normed = hidden_state * scale_h
            grad = scatter.total(piece)
            along = jnp.mean(normed * grad, axis=-1, keepdims=True)
            live = live_rows(s * rows + i * 16, 16, lengths[b, 0])
            upstream = cot[b, piece].astype(jnp.float32) * live
            grad_hidden = upstream + scale_h * (grad - normed * along)
            grad_x[at] = grad_hidden
            low = grad_hidden.astype(jnp.bfloat16)
            da[b, piece] = low
            dot = jnp.mean(low.astype(jnp.float32) * (hidden_state - x[b, piece].astype(jnp.float32)), axis=-1, keepdims=True)
            column[b, piece] = jnp.broadcast_to(dot, (16, 128))
            return carry

        lax.fori_loop(0, rows // 16, finish, 0)
        gather.begin(da.at[b], own.at[b], b)
        mix[b, :, :rows] = column[b].T[:8, :rows]
        for d in range(1, 8):
            last.remote(mix.at[b], mix_in.at[b, s], mix_sem.at[b, d - 1], g, (s + d) % 8)
        local(mix.at[b], mix_in.at[b, s], mix_sem.at[b, 7])
    early.finish()

    third = [scatter_m_of(b, sums) for b in range(2)]
    for b in range(2):

        def body(at, i):
            part[b, :, at] = product(p_v[2, at_b(b)], w3[:, at]).astype(jnp.bfloat16)

        tiles_of(width, body)
        third[b].begin()
    gather.step(0, 1)
    gather.step(1, 1)
    for b in range(2):
        third[b].ends()
    weight_part(2, b_v)
    gather.step(0, 2)
    gather.step(1, 2)
    third[0].hop(0)
    third[1].hop(0)
    gather.step(0, 3)
    gather.step(1, 3)
    for i in (1, 2):
        third[0].hop(i)
        third[1].hop(i)
    for b in range(2):
        third[b].receive()
        scatter = third[b]

        def result(i, carry):
            piece = aligned(i, 16, 16)
            at = aligned(b * (rows // 16) + i, 16, 16)
            out[at] = (h[at] + scatter.total(piece)).astype(jnp.bfloat16)
            return carry

        lax.fori_loop(0, rows // 16, result, 0)
    for j in range(2):
        table[j] = turned_table(decay[4 * (2 * c + j) + z], length)
    arrived(scale, load.at[12])
    for b in range(2):
        columns_of(inverse.at[at_b(b)], scale, b, rows)
    for n in range(4):
        arrived(wa_v.at[n], load.at[7 + n])
    arrived(wo_v, load.at[11])

    def sum_ff(n, result):
        for r in range(3):
            arrived(in_f.at[n, r], xy_f.at[n, r])
            local(in_f.at[n, r], b_v.at[pl.ds(r * ff, ff)], load.at[13 + r])
        for r in range(3):
            arrived(b_v.at[pl.ds(r * ff, ff)], load.at[13 + r])
        mine = w_v.at[aligned(4 * n + g, ff, 16)]

        def read(at):
            value = mine[at].astype(jnp.float32)
            for r in range(3):
                value = value + b_v.at[pl.ds(r * ff, ff)][at].astype(jnp.float32)
            return value

        def write(at, value):
            mine[at] = value.astype(jnp.bfloat16)

        pour(read, write, ff // 16)
        for d in (4, 3, 5, 2, 6, 1, 7, 0):
            to = (s + d) % 8
            src = mine.at[:, aligned(to, depth, 128)]
            dst = result.at[aligned(s, ff, 16)]
            if d:
                last.remote(src, dst, z_f.at[n, d], g, to)
            else:
                local(src, dst, z_f.at[n, d])

    def sum_third():
        for r in range(3):
            arrived(in_t.at[r], xy_t.at[r])
            local(in_t.at[r], b_v.at[pl.ds(0, hidden), pl.ds(r * wide, wide)], load.at[13 + r])
        for r in range(3):
            arrived(b_v.at[pl.ds(0, hidden), pl.ds(r * wide, wide)], load.at[13 + r])
        mine = w_v.at[pl.ds(2 * hidden, hidden), aligned(g, wide, 128)]

        def read(at):
            value = mine[at].astype(jnp.float32)
            for r in range(3):
                value = value + b_v[at, pl.ds(r * wide, wide)].astype(jnp.float32)
            return value

        def write(at, value):
            mine[at] = value.astype(jnp.bfloat16)

        pour(read, write, hidden // 16)
        for d in (2, 1, 3, 0):
            chip = (z + d) % 4
            to = 2 * chip + s // 4
            src = mine.at[aligned(chip, ff, 16)]
            dst = ft.at[aligned(s % 4, ff, 16)]
            if d:
                last.remote(src, dst, z_t.at[s % 4], g, to)
            else:
                last.remote(src, dst, z_t.at[s % 4], g, to, to != s)
                local(src, dst, z_t.at[s % 4], to == s)

    sum_ff(0, ff_)
    sum_ff(1, fs)

    sums.finish()
    fourth = [scatter_of(b, early) for b in range(2)]

    def load_pre(b, j, slot):
        local(pre_all.at[:, b, :, pl.ds(j * head, head)], pre.at[slot], load.at[16 + slot])

    load_pre(0, 0, 0)
    load_pre(0, 1, 1)
    for b in range(2):
        gather.finish(own.at[b], b)
        local(da_all.at[b], a_v.at[at_b(b)], load.at[b])
        for d in range(8):
            arrived(mix_in.at[b, 0], mix_sem.at[b, d])
        columns_of(mixed, mix_in, b, rows)
        live = live_rows(0, length, lengths[b, 0])
        arrived(a_v.at[at_b(b)], load.at[b])
        for j in range(2):
            arrived(pre.at[j], load.at[16 + j])
            lanes = pl.ds(j * head, head)
            error = product_right(a_v[at_b(b)], wo_v[pl.ds(j * head, head)])
            q_pre, k_pre, v_pre, u_pre, o = [pre[j, n] for n in range(5)]
            sigma = 1.0 / (1.0 + jnp.exp(-u_pre))
            u = u_pre * sigma
            scale_g = inverse[at_b(b), :1]
            nat = u * o * scale_g
            nat_v[at_b(b), lanes] = nat.astype(jnp.bfloat16)
            dg = scale_g * (error - nat * mixed[:, :1])
            dz[3, at_b(b), lanes] = (dg * o * (sigma * (1.0 + u_pre * (1.0 - sigma)))).astype(jnp.bfloat16)
            do = (dg * u).astype(jnp.bfloat16)
            q = silu(q_pre).astype(jnp.bfloat16)
            k = (silu(k_pre) * live).astype(jnp.bfloat16)
            v = (silu(v_pre) * live).astype(jnp.bfloat16)
            scores = (product_right(k, q) * table[j]).astype(jnp.bfloat16)
            dv = product(scores, do)
            d_scores = (product_right(v, do) * table[j]).astype(jnp.bfloat16)
            dk = product(d_scores, q)
            dq = product_left(d_scores, k)
            dz[0, at_b(b), lanes] = (dq * slope(pre[j, 0])).astype(jnp.bfloat16)
            dz[1, at_b(b), lanes] = (dk * live * slope(pre[j, 1])).astype(jnp.bfloat16)
            dz[2, at_b(b), lanes] = (dv * live * slope(pre[j, 2])).astype(jnp.bfloat16)
            if b == 0:
                load_pre(1, j, j)

        def body(at, i):
            value = product_right(dz[0, at_b(b)], wa_v[0, at])
            for n in range(1, 4):
                value = value + product_right(dz[n, at_b(b)], wa_v[n, at])
            part[b, :, at] = value.astype(jnp.bfloat16)

        tiles_of(width, body)
        fourth[b].begin()
        fourth[b].ends()
    sum_third()
    fourth[0].hop(0)
    fourth[0].hop(1)

    for b in range(2):
        local(n1_all.at[b], b_v.at[at_b(b)], load.at[2 + b])
    turn(turned, lambda t: nat_v[t], tokens // 128, 2 * head)

    def body_o(at, i):
        go_v[:, at] = product(turned[pl.ds(0, 2 * head)], a_v[:, at]).astype(jnp.bfloat16)

    tiles_of(width, body_o)
    for r, o in enumerate(others):
        last.remote(go_v.at[:, aligned(o, wide, 128)], in_o.at[r], xy_o.at[r], o, s)
    fourth[0].hop(2)
    fourth[1].hop(0)
    for b in range(2):
        arrived(b_v.at[at_b(b)], load.at[2 + b])
    half = width // 2
    for n in range(4):
        turn(turned, lambda t: dz[n, t], tokens // 128, 2 * head)
        grad = grads_h.at[n]

        def body_h(at, i):
            place = pl.ds(pl.multiple_of((i % 2) * half + (i // 2) * 256, 256), 256)
            grad[:, place] = product(turned[pl.ds(0, 2 * head)], b_v[:, at]).astype(jnp.bfloat16)

        tiles_of(width, body_h)
        for r, o in enumerate(others + (g,)):
            holds = o // 2 == c
            for e in range(2):
                src = grad.at[aligned(o % 2, head, head), pl.ds(e * half, half)]
                dst = in_h.at[n, r]
                if r < 3:
                    last.remote(src, dst, xy_h.at[n, r], o, 2 * z + e, holds)
                else:
                    last.remote(src, dst, xy_h.at[n, r], g, 2 * z + e, jnp.logical_and(holds, c != e))
                    local(src, dst, xy_h.at[n, r], jnp.logical_and(holds, c == e))
        if n < 2:
            fourth[1].hop(n + 1)
    for b in range(2):
        fourth[b].receive()
        scatter = fourth[b]

        def finish_x(i, carry):
            piece = aligned(i, 16, 16)
            at = aligned(b * (rows // 16) + i, 16, 16)
            v = x[b, piece].astype(jnp.float32)
            scale_x = lax.rsqrt(mean_square(v) + EPS)
            normed = v * scale_x
            grad = scatter.total(piece)
            along = jnp.mean(normed * grad, axis=-1, keepdims=True)
            grad_x[at] = grad_x[at] + scale_x * (grad - normed * along)
            return carry

        lax.fori_loop(0, rows // 16, finish_x, 0)

    for r in range(3):
        arrived(in_o.at[r], xy_o.at[r])
        local(in_o.at[r], b_v.at[pl.ds(0, 2 * head), pl.ds(r * wide, wide)], load.at[13 + r])

    def held(n, r):
        return a_v.at[pl.ds((2 * n + r // 2) * head, head), pl.ds((r % 2) * half, half)]

    for n in range(4):
        for r in range(4):
            arrived(in_h.at[n, r], xy_h.at[n, r])
            local(in_h.at[n, r], held(n, r), load.at[18 + 4 * n + r])
    for r in range(3):
        arrived(b_v.at[pl.ds(0, 2 * head), pl.ds(r * wide, wide)], load.at[13 + r])
    mine_o = go_v.at[:, aligned(g, wide, 128)]

    def read_o(at):
        value = mine_o[at].astype(jnp.float32)
        for r in range(3):
            value = value + b_v[at, pl.ds(r * wide, wide)].astype(jnp.float32)
        return value

    def write_o(at, value):
        mine_o[at] = value.astype(jnp.bfloat16)

    pour(read_o, write_o, 2 * head // 16)
    for j in range(2):
        to = 2 * (2 * c + j) + z // 2
        src = mine_o.at[pl.ds(j * head, head)]
        dst = fo.at[aligned(z % 2, head, head)]
        last.remote(src, dst, z_o.at[z % 2], g, to, to != s)
        local(src, dst, z_o.at[z % 2], to == s)
    for n, result in enumerate((fq, fk, fv, fu)):
        for r in range(4):
            arrived(held(n, r), load.at[18 + 4 * n + r])

        def read_h(at):
            value = held(n, 0)[at].astype(jnp.float32)
            for r in range(1, 4):
                value = value + held(n, r)[at].astype(jnp.float32)
            return value

        def write_h(at, value):
            held(n, 0)[at] = value.astype(jnp.bfloat16)

        pour(read_h, write_h, head // 16)
        for d in (2, 1, 3, 0):
            chip = (z + d) % 4
            src = held(n, 0).at[:, aligned(chip, depth, 128)]
            dst = result.at[aligned(z, head, head)]
            if d:
                last.remote(src, dst, z_h.at[n, d], g, 2 * chip + c)
            else:
                local(src, dst, z_h.at[n, d])

    for n, result in enumerate((ff_, fs)):
        for d in range(8):
            arrived(result.at[pl.ds(0, ff)], z_f.at[n, d])
    for d in range(4):
        arrived(ft.at[pl.ds(0, ff)], z_t.at[d])
    for j in range(2):
        arrived(fo.at[pl.ds(0, head)], z_o.at[j])
    for n, result in enumerate((fq, fk, fv, fu)):
        for d in range(4):
            arrived(result.at[pl.ds(0, head)], z_h.at[n, d])
    early.finish()
    bulk.finish()
    last.finish()


def call(kernel, number, ins, outs, scratch, name):
    return pl.pallas_call(
        kernel,
        out_shape=[shape for shape, _ in outs],
        in_specs=[spec for _, spec in ins],
        out_specs=[spec for _, spec in outs],
        scratch_shapes=scratch,
        compiler_params=pltpu.CompilerParams(
            collective_id=number, has_side_effects=True, vmem_limit_bytes=63 * 2**20
        ),
        name=name,
    )(*[value for value, _ in ins])


def low_array(*shape):
    return jax.ShapeDtypeStruct(shape, jnp.bfloat16)


def wide_array(*shape):
    return jax.ShapeDtypeStruct(shape, jnp.float32)


def dma(*shape):
    return pltpu.SemaphoreType.DMA(shape)


def scatter_scratch(rows, width):
    return [
        pltpu.VMEM((2, 4, rows, width), jnp.bfloat16),
        pltpu.VMEM((2, 2, 3, rows, width), jnp.bfloat16),
        dma(2, 4),
        dma(2, 2, 3),
    ]


def line_shards(
    tokens, cotangent, lengths, decay_rate,
    w_query, w_key, w_value, w_gate, w_out, w_first, w_second, w_third,
):
    bf16, f32 = jnp.bfloat16, jnp.float32
    rows, width = tokens.shape[2], tokens.shape[3]
    depth, wide = w_query.shape
    head = width // decay_rate.shape[0]
    hidden = w_third.shape[0]
    length = 8 * rows
    s = lax.axis_index("seq")
    z, c = s // 2, s % 2
    x_low = tokens[:, 0]
    x = x_low.astype(f32).reshape(2 * rows, width)
    in_smem = pl.BlockSpec(memory_space=pltpu.SMEM)

    (n1_all, dm_all, n2_all, q_w, k_w, v_w, u_w, o_w, f_w, s_w, t_w, pre_all, h, scale_all) = call(
        forward_part,
        0,
        [(lengths, in_smem), (decay_rate, in_smem), (x_low, VMEM), (cotangent[:, 0], VMEM)]
        + [(v, ANY) for v in (w_query, w_key, w_value, w_gate, w_out, w_first.T, w_second.T, w_third)],
        [(low_array(2, length, width), ANY)] * 3
        + [(low_array(width, 2 * head), ANY)] * 4
        + [(low_array(2 * head, width), ANY)]
        + [(low_array(hidden, width), ANY)] * 3
        + [(wide_array(5, 2, length, 2 * head), ANY), (wide_array(2 * rows, width), VMEM), (wide_array(2, 8, 8, 128), ANY)],
        [dma(280), dma(3, 2), dma(2, 2, 3), dma(2, 7), dma(2, 2, 3), dma(2, 7), dma(2, 2, 3), dma(2, 7),
         dma(4, 4), dma(2), dma(3, 4), dma(4, 3, 4), dma(3), dma(3, 3, 4),
         pltpu.VMEM((2, rows, width), bf16), pltpu.VMEM((2, rows, width), bf16), pltpu.VMEM((2, rows, width), bf16),
         pltpu.VMEM((2, length, width), bf16), pltpu.VMEM((4, width, 2 * head), bf16), pltpu.VMEM((2 * head, width), bf16), dma(7),
         pltpu.VMEM((5, 2, length, 2 * head), f32), dma(),
         pltpu.VMEM((2, length, width), bf16)] + scatter_scratch(rows, width) + [
         pltpu.VMEM((2, length, length), f32), pltpu.VMEM((2, 8, 8, 128), f32), pltpu.VMEM((2, 8, 8, 128), f32),
         pltpu.VMEM((2, 8, 128), f32), dma(2, 8), dma(2, 8), pltpu.VMEM((2, 128, 128), f32)],
        "forward_part",
    )
    da_all, mix_all, out, grad_x, fq, fk, fv, fu, fo, ff, fs, ft, _, _, _, _ = call(
        backward_part,
        1,
        [(lengths, in_smem), (decay_rate, in_smem), (x_low, VMEM), (cotangent[:, 0], VMEM), (h, VMEM)]
        + [(v, ANY) for v in (n1_all, dm_all, n2_all, q_w, k_w, v_w, u_w, o_w, f_w, s_w, t_w, pre_all, scale_all)],
        [(low_array(2, length, width), ANY), (wide_array(8, 128), VMEM), (low_array(2 * rows, width), VMEM),
         (wide_array(2 * rows, width), VMEM)]
        + [(low_array(wide, depth), ANY)] * 4 + [(low_array(depth, wide), ANY)]
        + [(low_array(2 * hidden, depth), ANY)] * 2 + [(low_array(hidden, wide), ANY)]
        + [(low_array(2, 3, hidden // 4, width), ANY), (low_array(3, hidden, wide), ANY), (low_array(3, 2 * head, wide), ANY),
           (low_array(4, 4, head, width // 2), ANY)],
        [dma(40), dma(12), dma(120), dma(70), dma(40), dma(2), dma(2, 2, 3), dma(2, 7),
         pltpu.VMEM((2 * length, width), bf16), pltpu.VMEM((2 * length, width), bf16), pltpu.VMEM((3 * hidden, width), bf16),
         pltpu.VMEM((4, width, 2 * head), bf16), pltpu.VMEM((2 * head, width), bf16),
         pltpu.VMEM((3, 2 * length, hidden), bf16), pltpu.VMEM((hidden, 2 * length), bf16),
         pltpu.VMEM((2, length, width), bf16)]
        + scatter_scratch(rows, width) + scatter_scratch(rows, width)
        + [pltpu.VMEM((2, 8, 8, 128), f32), pltpu.VMEM((2, 8, 128), f32), pltpu.VMEM((2, 8, 8, 128), f32), dma(2, 8),
           pltpu.VMEM((2, 128, 128), f32), pltpu.VMEM((2 * length, 128), f32), pltpu.VMEM((length, 128), f32),
           pltpu.VMEM((2, rows, width), bf16), pltpu.VMEM((2, length, length), f32), pltpu.VMEM((2, 5, length, head), f32),
           pltpu.VMEM((4, 2 * length, 2 * head), bf16), pltpu.VMEM((2 * length, 2 * head), bf16),
           pltpu.VMEM((2 * head, width), bf16), pltpu.VMEM((4, 2 * head, width), bf16),
           dma(2, 3), dma(3), dma(3), dma(4, 4), dma(2, 8), dma(4), dma(2), dma(4, 4)],
        "backward_part",
    )
    return (
        out.reshape(2, 1, rows, width),
        grad_x.reshape(2, 1, rows, width),
        fq.T.astype(f32), fk.T.astype(f32), fv.T.astype(f32), fu.T.astype(f32), fo.astype(f32),
        ff.T.astype(f32), fs.T.astype(f32), ft.astype(f32),
    )


def solution(mesh):
    in_specs = (
        P(None, "grp", "seq", None),
        P(None, "grp", "seq", None),
        P(None, "grp"),
        P(),
        P("seq", "grp"),
        P("seq", "grp"),
        P("seq", "grp"),
        P("seq", "grp"),
        P("seq", "grp"),
        P("seq", "grp"),
        P("seq", "grp"),
        P("seq", "grp"),
    )
    out_specs = (
        P(None, "grp", "seq", None),
        P(None, "grp", "seq", None),
        P("seq", "grp"),
        P("seq", "grp"),
        P("seq", "grp"),
        P("seq", "grp"),
        P("seq", "grp"),
        P("seq", "grp"),
        P("seq", "grp"),
        P("seq", "grp"),
    )
    fast = mesh.shape["grp"] == 4 and mesh.shape["seq"] == 8
    return jax.shard_map(line_shards if fast else shards, mesh=mesh, in_specs=in_specs, out_specs=out_specs, check_vma=False)
```

```python
import jax
import jax.numpy as jnp
from jax import lax
from jax.experimental import pallas as pl
from jax.experimental.pallas import tpu as pltpu
from jax.sharding import PartitionSpec as P

EPS = 1e-06
HIGH = lax.Precision.HIGHEST
MESH = pl.DeviceIdType.MESH
ANY = pl.BlockSpec(memory_space=pl.ANY)
VMEM = pl.BlockSpec(memory_space=pltpu.VMEM)


def prefix(value, axis, join, neutral, backward):
    count, mine = (lax.axis_size(axis), lax.axis_index(axis))
    pieces = jax.tree.map(lambda part: lax.all_gather(part, axis), value)
    if backward:
        pieces = jax.tree.map(lambda part: part[::-1], pieces)
        mine = count - 1 - mine
    subtotal = jax.tree.map(
        lambda part, zero: jnp.full_like(part, 0) + jnp.asarray(zero, part.dtype), value, neutral
    )

    def step(position, subtotal):
        longer = join(subtotal, jax.tree.map(lambda part: part[position], pieces))
        return jax.tree.map(lambda new, old: jnp.where(position < mine, new, old), longer, subtotal)

    return lax.fori_loop(0, count - 1, step, subtotal)


def norm_rows(values):
    return values * lax.rsqrt(jnp.mean(values * values, axis=-1, keepdims=True) + EPS)


def norm_back(values, gradient):
    _, pull = jax.vjp(norm_rows, values)
    return pull(gradient)[0]


def silu_slope(values):
    sigma = jax.nn.sigmoid(values)
    return sigma * (1.0 + values * (1.0 - sigma))


def product(left, right):
    return jnp.dot(left, right, preferred_element_type=jnp.float32)


def product_left(left, right):
    return lax.dot_general(
        left, right, (((0,), (0,)), ((), ())), preferred_element_type=jnp.float32
    )


def product_right(left, right):
    return lax.dot_general(
        left, right, (((1,), (1,)), ((), ())), preferred_element_type=jnp.float32
    )


def combine_state(earlier, later):
    return (later[1][:, None, None] * earlier[0] + later[0], earlier[1] * later[1])


def shards(
    tokens,
    cotangent,
    lengths,
    decay_rate,
    w_query,
    w_key,
    w_value,
    w_gate,
    w_out,
    w_first,
    w_second,
    w_third,
):
    micro = tokens.shape[0]
    block_rows = tokens.shape[2]
    width = tokens.shape[3]
    heads = decay_rate.shape[0]
    head_dim = width // heads
    hidden_width = w_third.shape[0] * lax.axis_size("seq")
    places = jnp.arange(block_rows).astype(jnp.float32)
    slot_index = lax.axis_index("seq") * block_rows + jnp.arange(block_rows)
    offset = places[:, None] - places[None, :]
    weight = jnp.where(
        offset[None] >= 0, jnp.exp(-decay_rate[:, None, None] * jnp.maximum(offset, 0.0)[None]), 0.0
    )
    query_fac = jnp.exp(-decay_rate[None, :] * (places[:, None] + 1.0))[:, :, None]
    key_fac = jnp.exp(-decay_rate[None, :] * (block_rows - 1.0 - places[:, None]))[:, :, None]
    step_decay = jnp.exp(-decay_rate * block_rows)
    empty_state = jnp.zeros((heads, head_dim, head_dim), jnp.float32)
    unit_decay = jnp.ones((heads,), jnp.float32)
    partial_rows = (
        lax.all_gather(w_query, "grp", axis=1, tiled=True),
        lax.all_gather(w_key, "grp", axis=1, tiled=True),
        lax.all_gather(w_value, "grp", axis=1, tiled=True),
        lax.all_gather(w_gate, "grp", axis=1, tiled=True),
        lax.all_gather(w_out, "grp", axis=1, tiled=True),
        lax.all_gather(w_first, "grp", axis=1, tiled=True),
        lax.all_gather(w_second, "grp", axis=1, tiled=True),
        lax.all_gather(w_third, "grp", axis=1, tiled=True),
    )
    gathered = (
        lax.all_gather(partial_rows[0], "seq", axis=0, tiled=True),
        lax.all_gather(partial_rows[1], "seq", axis=0, tiled=True),
        lax.all_gather(partial_rows[2], "seq", axis=0, tiled=True),
        lax.all_gather(partial_rows[3], "seq", axis=0, tiled=True),
        lax.all_gather(partial_rows[4], "seq", axis=0, tiled=True),
        lax.all_gather(partial_rows[5], "seq", axis=0, tiled=True),
        lax.all_gather(partial_rows[6], "seq", axis=0, tiled=True),
        lax.all_gather(partial_rows[7], "seq", axis=0, tiled=True),
    )
    outputs = []
    input_grads = []
    first_norms = []
    attn_rows = []
    normed_rows = []
    branch_rows = []
    second_norms = []
    ffn_rows = []
    mixed_rows = []
    upstream_rows = []
    for batch_idx in range(micro):
        wq_full, wk_full, wv_full, wu_full, wo_full, first_full, second_full, third_full = gathered
        inputs = tokens[batch_idx, 0].astype(jnp.float32)
        live = (slot_index < lengths[batch_idx, 0]).astype(jnp.float32)[:, None]
        live_low = live.astype(jnp.bfloat16)
        first_norm = norm_rows(inputs).astype(jnp.bfloat16)
        query_pre = product(first_norm, wq_full)
        key_pre = product(first_norm, wk_full)
        value_pre = product(first_norm, wv_full)
        gate_pre = product(first_norm, wu_full)
        queries = jax.nn.silu(query_pre).astype(jnp.bfloat16).reshape(block_rows, heads, head_dim)
        key_heads = (jax.nn.silu(key_pre).astype(jnp.bfloat16) * live_low).reshape(
            block_rows, heads, head_dim
        )
        value_heads = (jax.nn.silu(value_pre).astype(jnp.bfloat16) * live_low).reshape(
            block_rows, heads, head_dim
        )
        query_wide = queries.astype(jnp.float32)
        key_wide = key_heads.astype(jnp.float32)
        value_wide = value_heads.astype(jnp.float32)
        local_state = jnp.einsum("jhd,jhe->hde", key_wide * key_fac, value_wide, precision=HIGH)
        prior_state, _ = prefix(
            (local_state, step_decay), "seq", combine_state, (empty_state, unit_decay), False
        )
        scores = (
            jnp.einsum("ihd,jhd->hij", queries, key_heads, preferred_element_type=jnp.float32)
            * weight
        )
        intra = jnp.einsum("hij,jhe->ihe", scores, value_wide, precision=HIGH)
        inter = jnp.einsum("ihd,hde->ihe", query_wide * query_fac, prior_state, precision=HIGH)
        attended = (intra + inter).reshape(block_rows, width)
        gate_act = jax.nn.silu(gate_pre)
        gated = gate_act * attended
        normed = norm_rows(gated).astype(jnp.bfloat16)
        hidden = inputs + product(normed, wo_full)
        second_norm = norm_rows(hidden).astype(jnp.bfloat16)
        first_proj = product(second_norm, first_full)
        second_proj = product(second_norm, second_full)
        mixed_in = (first_proj * second_proj).astype(jnp.bfloat16)
        result = hidden + product(mixed_in, third_full)
        outputs.append(result.astype(jnp.bfloat16))
        upstream = cotangent[batch_idx, 0].astype(jnp.float32) * live
        upstream_low = upstream.astype(jnp.bfloat16)
        grad_mixed = product_right(upstream_low, third_full)
        grad_first_proj = (grad_mixed * second_proj).astype(jnp.bfloat16)
        grad_second_proj = (grad_mixed * first_proj).astype(jnp.bfloat16)
        grad_norm_two = product_right(grad_first_proj, first_full) + product_right(
            grad_second_proj, second_full
        )
        grad_hidden = upstream + norm_back(hidden, grad_norm_two)
        grad_branch = grad_hidden.astype(jnp.bfloat16)
        grad_gated = norm_back(gated, product_right(grad_branch, wo_full))
        grad_attended = (grad_gated * gate_act).astype(jnp.bfloat16)
        grad_gate_pre = (grad_gated * attended * silu_slope(gate_pre)).astype(jnp.bfloat16)
        grad_heads = grad_attended.reshape(block_rows, heads, head_dim)
        grad_wide = grad_heads.astype(jnp.float32)
        local_grad = jnp.einsum("ihd,ihe->hde", query_wide * query_fac, grad_wide, precision=HIGH)
        later_grad, _ = prefix(
            (local_grad, step_decay), "seq", combine_state, (empty_state, unit_decay), True
        )
        grad_scores = (
            jnp.einsum("ihe,jhe->hij", grad_heads, value_heads, preferred_element_type=jnp.float32)
            * weight
        )
        grad_queries = jnp.einsum("hij,jhd->ihd", grad_scores, key_wide, precision=HIGH)
        grad_queries = (
            grad_queries
            + jnp.einsum("ihe,hde->ihd", grad_wide, prior_state, precision=HIGH) * query_fac
        )
        grad_keys = jnp.einsum("hij,ihd->jhd", grad_scores, query_wide, precision=HIGH)
        grad_keys = (
            grad_keys + jnp.einsum("hde,jhe->jhd", later_grad, value_wide, precision=HIGH) * key_fac
        )
        grad_values = jnp.einsum("hij,ihe->jhe", scores, grad_wide, precision=HIGH)
        grad_values = (
            grad_values + jnp.einsum("jhd,hde->jhe", key_wide, later_grad, precision=HIGH) * key_fac
        )
        grad_query_pre = (grad_queries.reshape(block_rows, width) * silu_slope(query_pre)).astype(
            jnp.bfloat16
        )
        grad_key_pre = (grad_keys.reshape(block_rows, width) * live * silu_slope(key_pre)).astype(
            jnp.bfloat16
        )
        grad_value_pre = (
            grad_values.reshape(block_rows, width) * live * silu_slope(value_pre)
        ).astype(jnp.bfloat16)
        grad_norm_one = product_right(grad_query_pre, wq_full) + product_right(
            grad_key_pre, wk_full
        )
        grad_norm_one = (
            grad_norm_one
            + product_right(grad_value_pre, wv_full)
            + product_right(grad_gate_pre, wu_full)
        )
        input_grads.append(grad_hidden + norm_back(inputs, grad_norm_one))
        first_norms.append(first_norm)
        attn_rows.append(
            jnp.concatenate([grad_query_pre, grad_key_pre, grad_value_pre, grad_gate_pre], axis=1)
        )
        normed_rows.append(normed)
        branch_rows.append(grad_branch)
        second_norms.append(second_norm)
        ffn_rows.append(jnp.concatenate([grad_first_proj, grad_second_proj], axis=1))
        mixed_rows.append(mixed_in)
        upstream_rows.append(upstream_low)
    first_all = jnp.concatenate(first_norms, axis=0)
    attn_all = jnp.concatenate(attn_rows, axis=0)
    normed_all = jnp.concatenate(normed_rows, axis=0)
    branch_all = jnp.concatenate(branch_rows, axis=0)
    second_all = jnp.concatenate(second_norms, axis=0)
    ffn_all = jnp.concatenate(ffn_rows, axis=0)
    mixed_all = jnp.concatenate(mixed_rows, axis=0)
    upstream_all = jnp.concatenate(upstream_rows, axis=0)
    proj_rows = lax.psum_scatter(
        product_left(first_all, attn_all), "seq", scatter_dimension=0, tiled=True
    )
    outproj_rows = lax.psum_scatter(
        product_left(normed_all, branch_all), "seq", scatter_dimension=0, tiled=True
    )
    ffn_part = lax.psum_scatter(
        product_left(second_all, ffn_all), "seq", scatter_dimension=0, tiled=True
    )
    down_rows = lax.psum_scatter(
        product_left(mixed_all, upstream_all), "seq", scatter_dimension=0, tiled=True
    )
    summed = (
        lax.psum_scatter(proj_rows[:, :width], "grp", scatter_dimension=1, tiled=True),
        lax.psum_scatter(proj_rows[:, width : 2 * width], "grp", scatter_dimension=1, tiled=True),
        lax.psum_scatter(
            proj_rows[:, 2 * width : 3 * width], "grp", scatter_dimension=1, tiled=True
        ),
        lax.psum_scatter(proj_rows[:, 3 * width :], "grp", scatter_dimension=1, tiled=True),
        lax.psum_scatter(outproj_rows, "grp", scatter_dimension=1, tiled=True),
        lax.psum_scatter(ffn_part[:, :hidden_width], "grp", scatter_dimension=1, tiled=True),
        lax.psum_scatter(ffn_part[:, hidden_width:], "grp", scatter_dimension=1, tiled=True),
        lax.psum_scatter(down_rows, "grp", scatter_dimension=1, tiled=True),
    )
    layer_out = jnp.stack(outputs)[:, None]
    grad_tokens = jnp.stack(input_grads)[:, None]
    return (
        layer_out,
        grad_tokens,
        summed[0],
        summed[1],
        summed[2],
        summed[3],
        summed[4],
        summed[5],
        summed[6],
        summed[7],
    )


class Copies:
    def __init__(self, sems):
        self.sems = sems
        self.used = 0
        self.pending = []

    def remote(self, src, dst, recv_sem, group, place, when=None):
        assert self.used < self.sems.shape[0]
        copy = pltpu.make_async_remote_copy(
            src_ref=src,
            dst_ref=dst,
            send_sem=self.sems.at[self.used],
            recv_sem=recv_sem,
            device_id=(group, place),
            device_id_type=MESH,
        )
        self.used += 1
        self.pending.append((copy, when))
        if when is None:
            copy.start()
        else:
            pl.when(when)(copy.start)
        return self.pending[-1]

    def settle(self, entry):
        self.pending = [other for other in self.pending if other is not entry]
        copy, when = entry
        if when is None:
            copy.wait_send()
        else:
            pl.when(when)(copy.wait_send)

    def finish(self):
        while self.pending:
            self.settle(self.pending[0])


def local(src, dst, sem, when=None):
    copy = pltpu.make_async_copy(src, dst, sem)
    if when is None:
        copy.start()
    else:
        pl.when(when)(copy.start)


def arrived(ref, sem, when=None):
    copy = pltpu.make_async_copy(ref, ref, sem)
    if when is None:
        copy.wait()
    else:
        pl.when(when)(copy.wait)


def where_am_i():
    g, s = lax.axis_index("grp"), lax.axis_index("seq")
    return g, s, g // 2, g % 2, s // 2, s % 2


def across(y, x):
    return (y * 2 + 1 - x, (1 - y) * 2 + x, (1 - y) * 2 + 1 - x)


def greet(partners):
    barrier = pltpu.get_barrier_semaphore()
    for partner in partners:
        pl.semaphore_signal(barrier, inc=1, device_id=partner, device_id_type=MESH)
    pl.semaphore_wait(barrier, len(partners))


def aligned(index, unit, step):
    return pl.ds(pl.multiple_of(index * unit, step), unit)


class Gather:
    def __init__(self, copies, out, rows, hop_sem, side_sem):
        self.copies, self.out, self.rows = copies, out, rows
        self.hop_sem, self.side_sem = hop_sem, side_sem
        self.g, self.s, _, _, self.z, self.c = where_am_i()

    def block(self, b, z, core):
        return self.out.at[b, aligned(2 * z + core, self.rows, 16)]

    def spread(self, src, b, z_of, k, right, left):
        g, s, z, c = self.g, self.s, self.z, self.c
        dst = self.block(b, z_of, c)
        if right is not None:
            self.copies.remote(src, dst, self.hop_sem.at[b, 0, k], g, (s + 2) % 8, right)
        if left is not None:
            self.copies.remote(src, dst, self.hop_sem.at[b, 1, k], g, (s + 6) % 8, left)

    def begin(self, src, own_sem, b):
        g, s, z, c = self.g, self.s, self.z, self.c
        self.spread(src, b, z, 0, z < 3, z > 0)
        self.copies.remote(src, self.block(b, z, c), self.side_sem.at[b, 0], g, s + 1 - 2 * c)
        local(src, self.block(b, z, c), own_sem)

    def step(self, b, k):
        g, s, z, c = self.g, self.s, self.z, self.c
        side = s + 1 - 2 * c
        has = z >= k
        at = jnp.maximum(z - k, 0)
        ref = self.block(b, at, c)
        arrived(ref, self.hop_sem.at[b, 0, k - 1], has)
        if k < 3:
            self.spread(ref, b, at, k, jnp.logical_and(has, z < 3), None)
        self.copies.remote(ref, ref, self.side_sem.at[b, k], g, side, has)
        has = z + k <= 3
        at = jnp.minimum(z + k, 3)
        ref = self.block(b, at, c)
        arrived(ref, self.hop_sem.at[b, 1, k - 1], has)
        if k < 3:
            self.spread(ref, b, at, k, None, jnp.logical_and(has, z > 0))
        self.copies.remote(ref, ref, self.side_sem.at[b, 3 + k], g, side, has)

    def finish(self, own_sem, b):
        z, c = self.z, self.c
        arrived(self.block(b, z, c), own_sem)
        arrived(self.block(b, z, 1 - c), self.side_sem.at[b, 0])
        for k in (1, 2, 3):
            arrived(self.block(b, jnp.maximum(z - k, 0), 1 - c), self.side_sem.at[b, k], z >= k)
            arrived(self.block(b, jnp.minimum(z + k, 3), 1 - c), self.side_sem.at[b, 3 + k], z + k <= 3)


def line_partners(g, s):
    return [(g, (s + d) % 8) for d in range(1, 8)]


def everyone_on_line(copies, src, dst, sem, g, s, to_rows):
    for d in range(1, 8):
        to = (s + d) % 8
        copies.remote(to_rows(to), dst.at[s], sem.at[d - 1], g, to)


def mean_square(values):
    return jnp.mean(values * values, axis=-1, keepdims=True)


def pour(read, write, count):
    def piece(i, carry):
        at = aligned(i, 16, 16)
        write(at, read(at))
        return carry

    lax.fori_loop(0, count, piece, 0)


class LineScatter:
    def __init__(self, copies, part, rows, side, inbox, side_sem, line_sem, queue):
        self.copies, self.part, self.rows, self.queue = copies, part, rows, queue
        self.side, self.inbox, self.side_sem, self.line_sem = side, inbox, side_sem, line_sem
        self.g, self.s, _, _, self.z, self.c = where_am_i()

    def mine(self, chip):
        return self.part.at[aligned(2 * chip + self.c, self.rows, 16)]

    def begin(self):
        for chip in (3, 0, 2, 1):
            theirs = aligned(2 * chip + 1 - self.c, self.rows, 16)
            self.copies.remote(
                self.part.at[theirs], self.side.at[chip], self.side_sem.at[chip], self.g, self.s + 1 - 2 * self.c
            )

    def add_on(self, chip, way):
        own, side = self.mine(chip), self.side.at[chip]
        slot = chip - 1 if way == 0 else chip
        come = self.inbox.at[way, slot]
        arrived(side, self.side_sem.at[chip])
        arrived(come, self.line_sem.at[way, slot])

        def three(at):
            return own[at].astype(jnp.float32) + side[at].astype(jnp.float32) + come[at].astype(jnp.float32)

        def write(at, value):
            own[at] = value.astype(jnp.bfloat16)

        pour(three, write, self.rows // 16)

    def push(self, chip, way, when):
        slot = chip - 1 if way == 0 else chip
        to = (self.s + 2) % 8 if way == 0 else (self.s + 6) % 8
        return self.copies.remote(
            self.mine(chip), self.inbox.at[way, slot], self.line_sem.at[way, slot], self.g, to, when
        )

    def pass_on(self, chip, way):
        end = self.z == (0 if way == 0 else 3)
        own, side = self.mine(chip), self.side.at[chip]

        def two(at):
            return own[at].astype(jnp.float32) + side[at].astype(jnp.float32)

        def write(at, value):
            own[at] = value.astype(jnp.bfloat16)

        @pl.when(end)
        def _():
            arrived(side, self.side_sem.at[chip])
            pour(two, write, self.rows // 16)

        if way in self.queue:
            self.copies.settle(self.queue.pop(way))
        self.queue[way] = self.push(chip, way, end)

    def start(self, i):
        self.pass_on(3 - i, 0)
        self.pass_on(i, 1)

    def hop(self, i):
        z = self.z
        for inner in (1, 2):

            @pl.when(z == inner)
            def _():
                near = inner == 1
                if i < 2:
                    self.add_on(3 - i if near else i, 0 if near else 1)
                else:
                    self.add_on(0 if near else 3, 1 if near else 0)

        for inner in (1, 2):
            near = inner == 1
            if i < 2:
                self.push(3 - i if near else i, 0 if near else 1, z == inner)
            else:
                self.push(0 if near else 3, 1 if near else 0, z == inner)

    def receive(self):
        z = self.z
        arrived(self.side.at[z], self.side_sem.at[z])
        left, right = jnp.maximum(z - 1, 0), jnp.minimum(z, 2)
        arrived(self.inbox.at[0, left], self.line_sem.at[0, left], z > 0)
        arrived(self.inbox.at[1, right], self.line_sem.at[1, right], z < 3)

    def total(self, at):
        z = self.z
        value = self.mine(z)[at].astype(jnp.float32) + self.side[z, at].astype(jnp.float32)
        from_left = self.inbox[0, jnp.maximum(z - 1, 0), at].astype(jnp.float32)
        from_right = self.inbox[1, jnp.minimum(z, 2), at].astype(jnp.float32)
        return value + jnp.where(z > 0, from_left, 0.0) + jnp.where(z < 3, from_right, 0.0)


def silu(values):
    return values / (1.0 + jnp.exp(-values))


def decay_table(rate, length):
    offset = lax.broadcasted_iota(jnp.int32, (length, length), 0) - lax.broadcasted_iota(jnp.int32, (length, length), 1)
    steps = jnp.maximum(offset, 0).astype(jnp.float32)
    return jnp.where(offset >= 0, jnp.exp(-rate * steps), 0.0)


def live_rows(first, count, length):
    return ((first + lax.broadcasted_iota(jnp.int32, (count, 1), 0)) < length).astype(jnp.float32)


def forward_part(
    lengths, decay, x, cot, wq, wk, wv, wu, wo, w1, w2, w3,
    n1_all, dm_all, n2_all, q_all, k_all, v_all, u_all, o_all, f_all, s_all, t_all, pre_all, h, scale_all,
    w1_t, w2_t, send, own, hop_n, side_n, hop_d, side_d, hop_m, side_m, z_head, z_out, z_ff, xy_head, xy_out, xy_ff,
    n1, dm, n2, n1_v, w_v, wo_v, load, pre_v, pre_sem, part, side, inbox, side_sem, line_sem,
    table, squares, inbox_sq, scale, sq_sem, sc_sem, column,
):
    g, s, y, x_, z, c = where_am_i()
    others = across(y, x_)
    greet(line_partners(g, s) + [(o, s) for o in others])
    copies = Copies(send)
    rows, width = x.shape[1], x.shape[2]
    length = 8 * rows
    gather_n = Gather(copies, n1_all, rows, hop_n, side_n)
    gather_d = Gather(copies, dm_all, rows, hop_d, side_d)
    gather_m = Gather(copies, n2_all, rows, hop_m, side_m)
    heads = list(zip((wq, wk, wv, wu), (q_all, k_all, v_all, u_all)))
    depth, wide = wq.shape
    head = q_all.shape[1] // 2
    ff = f_all.shape[0] // 4
    target = g // 2
    mine = aligned(g % 2, head, head)
    here = c == target
    order = [(z + d) % 4 for d in (0, 1, 3, 2)]

    def send_heads(n):
        src, dst = heads[n]
        for d in (2, 1, 3, 0):
            to = (z + d) % 4
            a, b = src.at[:, aligned(to, head, head)], dst.at[aligned(s, depth, 16), mine]
            if d:
                copies.remote(a, b, z_head.at[n, z], g, 2 * to + target)
            else:
                copies.remote(a, b, z_head.at[n, z], g, 2 * to + target, c != target)
                local(a, b, z_head.at[n, z], here)

    def pass_heads(n):
        dst = heads[n][1]
        for zs in order:
            block = dst.at[aligned(zs, 2 * depth, 16), mine]
            arrived(block, z_head.at[n, zs], here)
            for r, o in enumerate(others):
                copies.remote(block, block, xy_head.at[n, r, zs], o, s, here)

    def send_out():
        for i in range(2):
            to = 2 * c + i
            a = wo.at[pl.ds(i * head, head)]
            b = o_all.at[aligned(z % 2, head, head), aligned(g, wide, 128)]
            self_ = jnp.logical_and(to == z, c == z // 2)
            copies.remote(a, b, z_out.at[z % 2], g, 2 * to + z // 2, jnp.logical_not(self_))
            local(a, b, z_out.at[z % 2], self_)

    def pass_out():
        for j in range(2):
            arrived(o_all.at[pl.ds(j * head, head), aligned(g, wide, 128)], z_out.at[j])
        block = o_all.at[:, aligned(g, wide, 128)]
        for r, o in enumerate(others):
            copies.remote(block, block, xy_out.at[r], o, s)

    def send_ff(n):
        src, dst = ((w1_t, f_all), (w2_t, s_all))[n]
        for d in (4, 3, 5, 2, 6, 1, 7, 0):
            to = (s + d) % 8
            a = src.at[aligned(to, ff, 16)]
            b = dst.at[aligned(g, ff, 16), aligned(s, depth, 128)]
            if d:
                copies.remote(a, b, z_ff.at[n, z], g, to)
            else:
                local(a, b, z_ff.at[n, z])

    def pass_ff(n):
        dst = (f_all, s_all)[n]
        for zs in order:
            block = dst.at[aligned(g, ff, 16), aligned(zs, 2 * depth, 128)]
            arrived(block, z_ff.at[n, zs])
            for r, o in enumerate(others):
                copies.remote(block, block, xy_ff.at[n, r, zs], o, s)

    def send_third():
        for d in (2, 1, 3, 0):
            to = 4 * c + (s + d) % 4
            a = w3.at[aligned(to % 4, ff, 16)]
            b = t_all.at[aligned(z, ff, 16), aligned(g, wide, 128)]
            if d:
                copies.remote(a, b, z_ff.at[2, z], g, to)
            else:
                self_ = s // 4 == c
                copies.remote(a, b, z_ff.at[2, z], g, to, jnp.logical_not(self_))
                local(a, b, z_ff.at[2, z], self_)

    def pass_third():
        for zs in order:
            block = t_all.at[aligned(zs, ff, 16), aligned(g, wide, 128)]
            arrived(block, z_ff.at[2, zs])
            for r, o in enumerate(others):
                copies.remote(block, block, xy_ff.at[2, r, zs], o, s)

    send_heads(0)
    send_heads(1)
    for b in range(2):

        def norm(at):
            v = x[b, at].astype(jnp.float32)
            return v * lax.rsqrt(mean_square(v) + EPS)

        def keep(at, value):
            n1[b, at] = value.astype(jnp.bfloat16)

        pour(norm, keep, rows // 16)
        first = s * rows

        def masked(i, carry):
            at = aligned(i, 16, 16)
            live = live_rows(first + i * 16, 16, lengths[0, b])
            dm[b, at] = (cot[b, at].astype(jnp.float32) * live).astype(jnp.bfloat16)
            return carry

        lax.fori_loop(0, rows // 16, masked, 0)
    for src, dst in ((w1, w1_t), (w2, w2_t)):
        dst[...] = src[...].T
    pass_heads(0)
    send_heads(2)
    pass_heads(1)
    send_heads(3)
    send_ff(0)
    pass_heads(2)
    pass_heads(3)
    send_out()
    send_ff(1)
    pass_ff(0)
    for b in range(2):
        gather_n.begin(n1.at[b], own.at[0, b], b)
    pass_out()
    pass_ff(1)
    for k in (1, 2, 3):
        gather_n.step(0, k)
        gather_n.step(1, k)
    send_third()
    for r, o in enumerate(others):
        from_here = (o // 2) == c
        for n, (_, dst) in enumerate(heads):
            for zs in range(4):
                block = dst.at[pl.ds(zs * 2 * depth, 2 * depth), aligned(o % 2, head, head)]
                arrived(block, xy_head.at[n, r, zs], from_here)
        arrived(o_all.at[:, aligned(o, wide, 128)], xy_out.at[r])
    for n, (_, dst) in enumerate(heads):
        local(dst, w_v.at[n], load.at[n])
    local(o_all, wo_v, load.at[4])
    for b in range(2):
        gather_n.finish(own.at[0, b], b)
        local(n1_all.at[b], n1_v.at[b], load.at[5 + b])
    for j in range(2):
        table[j] = decay_table(decay[4 * (2 * c + j) + z], length)
    for n in range(4):
        arrived(w_v.at[n], load.at[n])
    arrived(wo_v, load.at[4])
    queue = {}
    scatters = [
        LineScatter(copies, part.at[b], rows, side.at[b], inbox.at[b], side_sem.at[b], line_sem.at[b], queue) for b in range(2)
    ]
    half = length // 2
    for b in range(2):
        arrived(n1_v.at[b], load.at[5 + b])

        def project(i, carry):
            at = aligned(i, half, 16)
            for n in range(4):
                pre_v[n, b, at] = product(n1_v[b, at], w_v[n])
            return carry

        lax.fori_loop(0, 2, project, 0)
        if b == 1:
            scatters[0].start(1)
        live = live_rows(0, length, lengths[0, b])
        for j in range(2):
            lanes = pl.ds(j * head, head)
            q = silu(pre_v[0, b, :, lanes]).astype(jnp.bfloat16)
            k = (silu(pre_v[1, b, :, lanes]) * live).astype(jnp.bfloat16)
            v = (silu(pre_v[2, b, :, lanes]) * live).astype(jnp.bfloat16)
            scores = (product_right(q, k) * table[j]).astype(jnp.bfloat16)
            pre_v[4, b, :, lanes] = product(scores, v)
        gated = silu(pre_v[3, b]) * pre_v[4, b]
        square = jnp.sum(gated * gated, axis=-1, keepdims=True)
        row = jnp.broadcast_to(square, (length, 128)).T[:8]
        for to in range(8):
            squares[b, to, :, :rows] = row[:, to * rows : (to + 1) * rows]
        everyone_on_line(copies, squares, inbox_sq.at[b], sq_sem.at[b], g, s, lambda to: squares.at[b, to])
        local(squares.at[b, s], inbox_sq.at[b, s], sq_sem.at[b, 7])
        low = gated.astype(jnp.bfloat16)

        def out_part(i, carry):
            at = aligned(i, 256, 256)
            part[b, :, at] = product(low, wo_v[:, at]).astype(jnp.bfloat16)
            return carry

        lax.fori_loop(0, width // 256, out_part, 0)
        scatters[b].begin()
        if b == 0:
            scatters[0].start(0)
    local(pre_v, pre_all, pre_sem)
    for b in range(2):
        gather_d.begin(dm.at[b], own.at[1, b], b)
    scatters[0].hop(0)
    scatters[0].start(2)
    scatters[0].hop(1)
    scatters[1].start(0)
    scatters[0].hop(2)
    gather_d.step(0, 1)
    gather_d.step(1, 1)
    scatters[1].start(1)
    scatters[1].hop(0)
    pass_third()
    scatters[1].start(2)
    scatters[1].hop(1)
    gather_d.step(0, 2)
    scatters[1].hop(2)
    gather_d.step(1, 2)
    for b in range(2):
        for d in range(8):
            arrived(inbox_sq.at[b, 0], sq_sem.at[b, d])
        total = inbox_sq[b, 0]
        for d in range(1, 8):
            total = total + inbox_sq[b, d]
        row = lax.rsqrt(total / width + EPS)
        scale[b] = row
        column[b] = jnp.broadcast_to(row[:1], (128, 128)).T
    for b in range(2):
        scatter = scatters[b]
        scatter.receive()

        def finish(i, carry):
            piece = aligned(i, 16, 16)
            at = aligned(b * (rows // 16) + i, 16, 16)
            a = scatter.total(piece) * column[b, piece, :1]
            hidden = x[b, piece].astype(jnp.float32) + a
            h[at] = hidden
            n2[b, piece] = (hidden * lax.rsqrt(mean_square(hidden) + EPS)).astype(jnp.bfloat16)
            return carry

        lax.fori_loop(0, rows // 16, finish, 0)
        gather_m.begin(n2.at[b], own.at[2, b], b)
    for b in range(2):
        for d in range(1, 8):
            copies.remote(scale.at[b], scale_all.at[b, s], sc_sem.at[b, d - 1], g, (s + d) % 8)
        local(scale.at[b], scale_all.at[b, s], sc_sem.at[b, 7])
    gather_d.step(0, 3)
    gather_d.step(1, 3)
    for k in (1, 2, 3):
        gather_m.step(0, k)
        gather_m.step(1, k)

    for b in range(2):
        gather_d.finish(own.at[1, b], b)
        gather_m.finish(own.at[2, b], b)
    for r, o in enumerate(others):
        for n, dst in enumerate((f_all, s_all)):
            for zs in range(4):
                arrived(dst.at[aligned(o, ff, 16), pl.ds(zs * 2 * depth, 2 * depth)], xy_ff.at[n, r, zs])
        for zs in range(4):
            arrived(t_all.at[pl.ds(zs * ff, ff), aligned(o, wide, 128)], xy_ff.at[2, r, zs])
    for b in range(2):
        for d in range(8):
            arrived(scale.at[b], sc_sem.at[b, d])
    arrived(pre_v, pre_sem)
    copies.finish()


def slope(values):
    sigma = 1.0 / (1.0 + jnp.exp(-values))
    return sigma * (1.0 + values * (1.0 - sigma))


def turned_table(rate, length):
    offset = lax.broadcasted_iota(jnp.int32, (length, length), 1) - lax.broadcasted_iota(jnp.int32, (length, length), 0)
    steps = jnp.maximum(offset, 0).astype(jnp.float32)
    return jnp.where(offset >= 0, jnp.exp(-rate * steps), 0.0)


def columns_of(out, tiles, b, rows):
    for owner in range(8):
        out[pl.ds(owner * rows, rows)] = jnp.broadcast_to(tiles[b, owner, :1], (128, 128)).T[:rows]


def turn(dst, read, count, columns):
    def block(i, carry):
        dst[pl.ds(0, columns), aligned(i, 128, 128)] = read(aligned(i, 128, 128)).T
        return carry

    lax.fori_loop(0, count, block, 0)


def tiles_of(width, body):
    def tile(i, carry):
        body(aligned(i, 256, 256), i)
        return carry

    lax.fori_loop(0, width // 256, tile, 0)


def backward_part(
    lengths, decay, x, cot, h, n1_all, dm_all, n2_all, q_all, k_all, v_all, u_all, o_all, f_all, s_all, t_all, pre_all, scale_all,
    da_all, mix_all, out, grad_x, fq, fk, fv, fu, fo, ff_, fs, ft, in_f, in_t, in_o, in_h,
    send_a, send_b, send_c, send_d, load, own, hop, hside,
    a_v, b_v, w_v, wa_v, wo_v, p_v, turned, part, side, inbox, side_sem, line_sem, side_m, inbox_m, side_sem_m, line_sem_m,
    scale, mix, mix_in, mix_sem, column, inverse, mixed, da, table, pre, dz, nat_v, go_v, grads_h,
    xy_f, xy_t, xy_o, xy_h, z_f, z_t, z_o, z_h,
):
    g, s, y, x_, z, c = where_am_i()
    others = across(y, x_)
    plane = [(o, 2 * z + e) for o in others for e in range(2)]
    rows, width = x.shape[1], x.shape[2]
    length = 8 * rows
    tokens = 2 * length
    ff = in_f.shape[2]
    hidden = 4 * ff
    head = dz.shape[2] // 2
    wide, depth = fo.shape[1], fo.shape[0]

    def at_b(b):
        return pl.ds(b * length, length)

    for b in range(2):
        local(n2_all.at[b], a_v.at[at_b(b)], load.at[b])
        local(dm_all.at[b], b_v.at[at_b(b)], load.at[2 + b])
    for n, src in enumerate((f_all, s_all, t_all)):
        local(src, w_v.at[pl.ds(n * hidden, hidden)], load.at[4 + n])
    for n, src in enumerate((q_all, k_all, v_all, u_all)):
        local(src, wa_v.at[n], load.at[7 + n])
    local(o_all, wo_v, load.at[11])
    local(scale_all, scale, load.at[12])
    greet(line_partners(g, s) + plane)
    sums = Copies(send_a)
    bulk = Copies(send_b)
    last = Copies(send_c)
    early = Copies(send_d)
    gather = Gather(last, da_all, rows, hop, hside)
    w1 = w_v.at[pl.ds(0, hidden)]
    w2 = w_v.at[pl.ds(hidden, hidden)]
    w3 = w_v.at[pl.ds(2 * hidden, hidden)]

    def feed_forward(b):
        def tile(i, carry):
            at = aligned(b * 2 + i, length // 2, 16)
            first = product_right(a_v[at], w1[...])
            second = product_right(a_v[at], w2[...])
            back = product_right(b_v[at], w3[...])
            p_v[0, at] = (back * second).astype(jnp.bfloat16)
            p_v[1, at] = (back * first).astype(jnp.bfloat16)
            p_v[2, at] = (first * second).astype(jnp.bfloat16)
            return carry

        lax.fori_loop(0, 2, tile, 0)

    def norm_part(b):
        def body(at, i):
            value = product(p_v[0, at_b(b)], w1[:, at]) + product(p_v[1, at_b(b)], w2[:, at])
            part[b, :, at] = value.astype(jnp.bfloat16)

        tiles_of(width, body)

    def scatter_of(b, copies):
        return LineScatter(copies, part.at[b], rows, side.at[b], inbox.at[b], side_sem.at[b], line_sem.at[b], queue)

    def scatter_m_of(b, copies):
        return LineScatter(
            copies, part.at[b], rows, side_m.at[b], inbox_m.at[b], side_sem_m.at[b], line_sem_m.at[b], queue_m
        )

    queue, queue_m = {}, {}
    second = [scatter_of(b, early) for b in range(2)]
    for n in (0, 4, 5, 2, 6):
        ref = {0: a_v.at[at_b(0)], 2: b_v.at[at_b(0)], 4: w1, 5: w2, 6: w3}[n]
        arrived(ref, load.at[n])
    feed_forward(0)
    norm_part(0)
    second[0].begin()
    second[0].start(0)
    arrived(a_v.at[at_b(1)], load.at[1])
    arrived(b_v.at[at_b(1)], load.at[3])
    feed_forward(1)
    second[0].start(1)
    second[0].hop(0)
    norm_part(1)
    second[1].begin()
    second[0].start(2)
    second[0].hop(1)
    second[0].hop(2)
    second[1].start(0)

    def weight_part(n, operand):
        turn(turned, lambda t: p_v[n, t], tokens // 128, hidden)

        def body(at, i):
            w_v[pl.ds(n * hidden, hidden), at] = product(turned[...], operand[:, at]).astype(jnp.bfloat16)

        tiles_of(width, body)
        for r, o in enumerate(others):
            if n < 2:
                bulk.remote(w_v.at[aligned(4 * n + o, ff, 16)], in_f.at[n, r], xy_f.at[n, r], o, s)
            else:
                bulk.remote(w_v.at[pl.ds(n * hidden, hidden), aligned(o, wide, 128)], in_t.at[r], xy_t.at[r], o, s)

    weight_part(0, a_v)
    second[1].start(1)
    second[1].hop(0)
    weight_part(1, a_v)
    second[1].start(2)
    second[1].hop(1)
    second[1].hop(2)

    for b in range(2):
        second[b].receive()
        scatter = second[b]
        if b == 1:
            queue.clear()

        def finish(i, carry):
            piece = aligned(i, 16, 16)
            at = aligned(b * (rows // 16) + i, 16, 16)
            hidden_state = h[at]
            scale_h = lax.rsqrt(mean_square(hidden_state) + EPS)
            normed = hidden_state * scale_h
            grad = scatter.total(piece)
            along = jnp.mean(normed * grad, axis=-1, keepdims=True)
            live = live_rows(s * rows + i * 16, 16, lengths[0, b])
            upstream = cot[b, piece].astype(jnp.float32) * live
            grad_hidden = upstream + scale_h * (grad - normed * along)
            grad_x[at] = grad_hidden
            low = grad_hidden.astype(jnp.bfloat16)
            da[b, piece] = low
            dot = jnp.mean(low.astype(jnp.float32) * (hidden_state - x[b, piece].astype(jnp.float32)), axis=-1, keepdims=True)
            column[b, piece] = jnp.broadcast_to(dot, (16, 128))
            return carry

        lax.fori_loop(0, rows // 16, finish, 0)
        gather.begin(da.at[b], own.at[b], b)
        mix[b, :, :rows] = column[b].T[:8, :rows]
        for d in range(1, 8):
            last.remote(mix.at[b], mix_in.at[b, s], mix_sem.at[b, d - 1], g, (s + d) % 8)
        local(mix.at[b], mix_in.at[b, s], mix_sem.at[b, 7])
    early.finish()

    third = [scatter_m_of(b, sums) for b in range(2)]
    for b in range(2):

        def body(at, i):
            part[b, :, at] = product(p_v[2, at_b(b)], w3[:, at]).astype(jnp.bfloat16)

        tiles_of(width, body)
        third[b].begin()
    third[0].start(0)
    gather.step(0, 1)
    gather.step(1, 1)
    third[0].start(1)
    third[0].hop(0)
    weight_part(2, b_v)
    gather.step(0, 2)
    third[0].start(2)
    third[0].hop(1)
    third[0].hop(2)
    third[1].start(0)
    gather.step(1, 2)
    third[1].start(1)
    third[1].hop(0)
    gather.step(0, 3)
    third[1].start(2)
    third[1].hop(1)
    third[1].hop(2)
    gather.step(1, 3)
    for b in range(2):
        third[b].receive()
        scatter = third[b]

        def result(i, carry):
            piece = aligned(i, 16, 16)
            at = aligned(b * (rows // 16) + i, 16, 16)
            out[at] = (h[at] + scatter.total(piece)).astype(jnp.bfloat16)
            return carry

        lax.fori_loop(0, rows // 16, result, 0)
    for j in range(2):
        table[j] = turned_table(decay[4 * (2 * c + j) + z], length)
    arrived(scale, load.at[12])
    for b in range(2):
        columns_of(inverse.at[at_b(b)], scale, b, rows)
    for n in range(4):
        arrived(wa_v.at[n], load.at[7 + n])
    arrived(wo_v, load.at[11])

    def sum_ff(n, result):
        for r in range(3):
            arrived(in_f.at[n, r], xy_f.at[n, r])
            local(in_f.at[n, r], b_v.at[pl.ds(r * ff, ff)], load.at[13 + r])
        for r in range(3):
            arrived(b_v.at[pl.ds(r * ff, ff)], load.at[13 + r])
        mine = w_v.at[aligned(4 * n + g, ff, 16)]

        def read(at):
            value = mine[at].astype(jnp.float32)
            for r in range(3):
                value = value + b_v.at[pl.ds(r * ff, ff)][at].astype(jnp.float32)
            return value

        def write(at, value):
            mine[at] = value.astype(jnp.bfloat16)

        pour(read, write, ff // 16)
        for d in (4, 3, 5, 2, 6, 1, 7, 0):
            to = (s + d) % 8
            src = mine.at[:, aligned(to, depth, 128)]
            dst = result.at[aligned(s, ff, 16)]
            if d:
                last.remote(src, dst, z_f.at[n, d], g, to)
            else:
                local(src, dst, z_f.at[n, d])

    def sum_third():
        for r in range(3):
            arrived(in_t.at[r], xy_t.at[r])
            local(in_t.at[r], b_v.at[pl.ds(0, hidden), pl.ds(r * wide, wide)], load.at[13 + r])
        for r in range(3):
            arrived(b_v.at[pl.ds(0, hidden), pl.ds(r * wide, wide)], load.at[13 + r])
        mine = w_v.at[pl.ds(2 * hidden, hidden), aligned(g, wide, 128)]

        def read(at):
            value = mine[at].astype(jnp.float32)
            for r in range(3):
                value = value + b_v[at, pl.ds(r * wide, wide)].astype(jnp.float32)
            return value

        def write(at, value):
            mine[at] = value.astype(jnp.bfloat16)

        pour(read, write, hidden // 16)
        for d in (2, 1, 3, 0):
            chip = (z + d) % 4
            to = 2 * chip + s // 4
            src = mine.at[aligned(chip, ff, 16)]
            dst = ft.at[aligned(s % 4, ff, 16)]
            if d:
                last.remote(src, dst, z_t.at[s % 4], g, to)
            else:
                last.remote(src, dst, z_t.at[s % 4], g, to, to != s)
                local(src, dst, z_t.at[s % 4], to == s)

    sum_ff(0, ff_)
    sum_ff(1, fs)

    sums.finish()
    queue = {}
    fourth = [scatter_of(b, early) for b in range(2)]

    def load_pre(b, j, slot):
        local(pre_all.at[:, b, :, pl.ds(j * head, head)], pre.at[slot], load.at[16 + slot])

    load_pre(0, 0, 0)
    load_pre(0, 1, 1)
    for b in range(2):
        gather.finish(own.at[b], b)
        local(da_all.at[b], a_v.at[at_b(b)], load.at[b])
        for d in range(8):
            arrived(mix_in.at[b, 0], mix_sem.at[b, d])
        columns_of(mixed, mix_in, b, rows)
        live = live_rows(0, length, lengths[0, b])
        arrived(a_v.at[at_b(b)], load.at[b])
        for j in range(2):
            arrived(pre.at[j], load.at[16 + j])
            lanes = pl.ds(j * head, head)
            error = product_right(a_v[at_b(b)], wo_v[pl.ds(j * head, head)])
            q_pre, k_pre, v_pre, u_pre, o = [pre[j, n] for n in range(5)]
            sigma = 1.0 / (1.0 + jnp.exp(-u_pre))
            u = u_pre * sigma
            scale_g = inverse[at_b(b), :1]
            nat = u * o * scale_g
            nat_v[at_b(b), lanes] = nat.astype(jnp.bfloat16)
            dg = scale_g * (error - nat * mixed[:, :1])
            dz[3, at_b(b), lanes] = (dg * o * (sigma * (1.0 + u_pre * (1.0 - sigma)))).astype(jnp.bfloat16)
            do = (dg * u).astype(jnp.bfloat16)
            q = silu(q_pre).astype(jnp.bfloat16)
            k = (silu(k_pre) * live).astype(jnp.bfloat16)
            v = (silu(v_pre) * live).astype(jnp.bfloat16)
            scores = (product_right(k, q) * table[j]).astype(jnp.bfloat16)
            dv = product(scores, do)
            d_scores = (product_right(v, do) * table[j]).astype(jnp.bfloat16)
            dk = product(d_scores, q)
            dq = product_left(d_scores, k)
            dz[0, at_b(b), lanes] = (dq * slope(pre[j, 0])).astype(jnp.bfloat16)
            dz[1, at_b(b), lanes] = (dk * live * slope(pre[j, 1])).astype(jnp.bfloat16)
            dz[2, at_b(b), lanes] = (dv * live * slope(pre[j, 2])).astype(jnp.bfloat16)
            if b == 0:
                load_pre(1, j, j)

        def body(at, i):
            value = product_right(dz[0, at_b(b)], wa_v[0, at])
            for n in range(1, 4):
                value = value + product_right(dz[n, at_b(b)], wa_v[n, at])
            part[b, :, at] = value.astype(jnp.bfloat16)

        tiles_of(width, body)
        fourth[b].begin()
        if b == 0:
            fourth[0].start(0)
        else:
            fourth[0].start(1)
            fourth[0].hop(0)
    sum_third()
    fourth[0].start(2)
    fourth[0].hop(1)
    fourth[0].hop(2)
    fourth[1].start(0)

    for b in range(2):
        local(n1_all.at[b], b_v.at[at_b(b)], load.at[2 + b])
    turn(turned, lambda t: nat_v[t], tokens // 128, 2 * head)

    def body_o(at, i):
        go_v[:, at] = product(turned[pl.ds(0, 2 * head)], a_v[:, at]).astype(jnp.bfloat16)

    tiles_of(width, body_o)
    for r, o in enumerate(others):
        last.remote(go_v.at[:, aligned(o, wide, 128)], in_o.at[r], xy_o.at[r], o, s)
    fourth[1].start(1)
    fourth[1].hop(0)
    for b in range(2):
        arrived(b_v.at[at_b(b)], load.at[2 + b])
    half = width // 2
    for n in range(4):
        turn(turned, lambda t: dz[n, t], tokens // 128, 2 * head)
        grad = grads_h.at[n]

        def body_h(at, i):
            place = pl.ds(pl.multiple_of((i % 2) * half + (i // 2) * 256, 256), 256)
            grad[:, place] = product(turned[pl.ds(0, 2 * head)], b_v[:, at]).astype(jnp.bfloat16)

        tiles_of(width, body_h)
        for r, o in enumerate(others + (g,)):
            holds = o // 2 == c
            for e in range(2):
                src = grad.at[aligned(o % 2, head, head), pl.ds(e * half, half)]
                dst = in_h.at[n, r]
                if r < 3:
                    last.remote(src, dst, xy_h.at[n, r], o, 2 * z + e, holds)
                else:
                    last.remote(src, dst, xy_h.at[n, r], g, 2 * z + e, jnp.logical_and(holds, c != e))
                    local(src, dst, xy_h.at[n, r], jnp.logical_and(holds, c == e))
        if n == 0:
            fourth[1].start(2)
            fourth[1].hop(1)
        if n == 1:
            fourth[1].hop(2)
    for b in range(2):
        fourth[b].receive()
        scatter = fourth[b]

        def finish_x(i, carry):
            piece = aligned(i, 16, 16)
            at = aligned(b * (rows // 16) + i, 16, 16)
            v = x[b, piece].astype(jnp.float32)
            scale_x = lax.rsqrt(mean_square(v) + EPS)
            normed = v * scale_x
            grad = scatter.total(piece)
            along = jnp.mean(normed * grad, axis=-1, keepdims=True)
            grad_x[at] = grad_x[at] + scale_x * (grad - normed * along)
            return carry

        lax.fori_loop(0, rows // 16, finish_x, 0)

    for r in range(3):
        arrived(in_o.at[r], xy_o.at[r])
        local(in_o.at[r], b_v.at[pl.ds(0, 2 * head), pl.ds(r * wide, wide)], load.at[13 + r])

    def held(n, r):
        return a_v.at[pl.ds((2 * n + r // 2) * head, head), pl.ds((r % 2) * half, half)]

    for n in range(4):
        for r in range(4):
            arrived(in_h.at[n, r], xy_h.at[n, r])
            local(in_h.at[n, r], held(n, r), load.at[18 + 4 * n + r])
    for r in range(3):
        arrived(b_v.at[pl.ds(0, 2 * head), pl.ds(r * wide, wide)], load.at[13 + r])
    mine_o = go_v.at[:, aligned(g, wide, 128)]

    def read_o(at):
        value = mine_o[at].astype(jnp.float32)
        for r in range(3):
            value = value + b_v[at, pl.ds(r * wide, wide)].astype(jnp.float32)
        return value

    def write_o(at, value):
        mine_o[at] = value.astype(jnp.bfloat16)

    pour(read_o, write_o, 2 * head // 16)
    for j in range(2):
        to = 2 * (2 * c + j) + z // 2
        src = mine_o.at[pl.ds(j * head, head)]
        dst = fo.at[aligned(z % 2, head, head)]
        last.remote(src, dst, z_o.at[z % 2], g, to, to != s)
        local(src, dst, z_o.at[z % 2], to == s)
    for n, result in enumerate((fq, fk, fv, fu)):
        for r in range(4):
            arrived(held(n, r), load.at[18 + 4 * n + r])

        def read_h(at):
            value = held(n, 0)[at].astype(jnp.float32)
            for r in range(1, 4):
                value = value + held(n, r)[at].astype(jnp.float32)
            return value

        def write_h(at, value):
            held(n, 0)[at] = value.astype(jnp.bfloat16)

        pour(read_h, write_h, head // 16)
        for d in (2, 1, 3, 0):
            chip = (z + d) % 4
            src = held(n, 0).at[:, aligned(chip, depth, 128)]
            dst = result.at[aligned(z, head, head)]
            if d:
                last.remote(src, dst, z_h.at[n, d], g, 2 * chip + c)
            else:
                local(src, dst, z_h.at[n, d])

    for n, result in enumerate((ff_, fs)):
        for d in range(8):
            arrived(result.at[pl.ds(0, ff)], z_f.at[n, d])
    for d in range(4):
        arrived(ft.at[pl.ds(0, ff)], z_t.at[d])
    for j in range(2):
        arrived(fo.at[pl.ds(0, head)], z_o.at[j])
    for n, result in enumerate((fq, fk, fv, fu)):
        for d in range(4):
            arrived(result.at[pl.ds(0, head)], z_h.at[n, d])
    early.finish()
    bulk.finish()
    last.finish()


def call(kernel, number, ins, outs, scratch, name):
    return pl.pallas_call(
        kernel,
        out_shape=[shape for shape, _ in outs],
        in_specs=[spec for _, spec in ins],
        out_specs=[spec for _, spec in outs],
        scratch_shapes=scratch,
        compiler_params=pltpu.CompilerParams(
            collective_id=number, has_side_effects=True, vmem_limit_bytes=63 * 2**20
        ),
        name=name,
    )(*[value for value, _ in ins])


def low_array(*shape):
    return jax.ShapeDtypeStruct(shape, jnp.bfloat16)


def wide_array(*shape):
    return jax.ShapeDtypeStruct(shape, jnp.float32)


def dma(*shape):
    return pltpu.SemaphoreType.DMA(shape)


def scatter_scratch(rows, width):
    return [
        pltpu.VMEM((2, 4, rows, width), jnp.bfloat16),
        pltpu.VMEM((2, 2, 3, rows, width), jnp.bfloat16),
        dma(2, 4),
        dma(2, 2, 3),
    ]


def line_shards(
    tokens, cotangent, lengths, decay_rate,
    w_query, w_key, w_value, w_gate, w_out, w_first, w_second, w_third,
):
    bf16, f32 = jnp.bfloat16, jnp.float32
    rows, width = tokens.shape[2], tokens.shape[3]
    depth, wide = w_query.shape
    head = width // decay_rate.shape[0]
    hidden = w_third.shape[0]
    length = 8 * rows
    s = lax.axis_index("seq")
    z, c = s // 2, s % 2
    x_low = tokens[:, 0]
    x = x_low.astype(f32).reshape(2 * rows, width)
    in_smem = pl.BlockSpec(memory_space=pltpu.SMEM)

    (n1_all, dm_all, n2_all, q_w, k_w, v_w, u_w, o_w, f_w, s_w, t_w, pre_all, h, scale_all) = call(
        forward_part,
        0,
        [(lengths.T, in_smem), (decay_rate, in_smem), (x_low, VMEM), (cotangent[:, 0], VMEM)]
        + [(v, ANY) for v in (w_query, w_key, w_value, w_gate, w_out)]
        + [(w_first, VMEM), (w_second, VMEM), (w_third, ANY)],
        [(low_array(2, length, width), ANY)] * 3
        + [(low_array(width, 2 * head), ANY)] * 4
        + [(low_array(2 * head, width), ANY)]
        + [(low_array(hidden, width), ANY)] * 3
        + [(wide_array(5, 2, length, 2 * head), ANY), (wide_array(2 * rows, width), VMEM), (wide_array(2, 8, 8, 128), ANY)],
        [pltpu.VMEM((2 * hidden, depth), bf16), pltpu.VMEM((2 * hidden, depth), bf16), dma(280), dma(3, 2), dma(2, 2, 3), dma(2, 7), dma(2, 2, 3), dma(2, 7), dma(2, 2, 3), dma(2, 7),
         dma(4, 4), dma(2), dma(3, 4), dma(4, 3, 4), dma(3), dma(3, 3, 4),
         pltpu.VMEM((2, rows, width), bf16), pltpu.VMEM((2, rows, width), bf16), pltpu.VMEM((2, rows, width), bf16),
         pltpu.VMEM((2, length, width), bf16), pltpu.VMEM((4, width, 2 * head), bf16), pltpu.VMEM((2 * head, width), bf16), dma(7),
         pltpu.VMEM((5, 2, length, 2 * head), f32), dma(),
         pltpu.VMEM((2, length, width), bf16)] + scatter_scratch(rows, width) + [
         pltpu.VMEM((2, length, length), f32), pltpu.VMEM((2, 8, 8, 128), f32), pltpu.VMEM((2, 8, 8, 128), f32),
         pltpu.VMEM((2, 8, 128), f32), dma(2, 8), dma(2, 8), pltpu.VMEM((2, 128, 128), f32)],
        "forward_part",
    )
    da_all, mix_all, out, grad_x, fq, fk, fv, fu, fo, ff, fs, ft, _, _, _, _ = call(
        backward_part,
        1,
        [(lengths.T, in_smem), (decay_rate, in_smem), (x_low, VMEM), (cotangent[:, 0], VMEM), (h, VMEM)]
        + [(v, ANY) for v in (n1_all, dm_all, n2_all, q_w, k_w, v_w, u_w, o_w, f_w, s_w, t_w, pre_all, scale_all)],
        [(low_array(2, length, width), ANY), (wide_array(8, 128), VMEM), (low_array(2 * rows, width), VMEM),
         (wide_array(2 * rows, width), VMEM)]
        + [(low_array(wide, depth), ANY)] * 4 + [(low_array(depth, wide), ANY)]
        + [(low_array(2 * hidden, depth), ANY)] * 2 + [(low_array(hidden, wide), ANY)]
        + [(low_array(2, 3, hidden // 4, width), ANY), (low_array(3, hidden, wide), ANY), (low_array(3, 2 * head, wide), ANY),
           (low_array(4, 4, head, width // 2), ANY)],
        [dma(40), dma(12), dma(120), dma(70), dma(40), dma(2), dma(2, 2, 3), dma(2, 7),
         pltpu.VMEM((2 * length, width), bf16), pltpu.VMEM((2 * length, width), bf16), pltpu.VMEM((3 * hidden, width), bf16),
         pltpu.VMEM((4, width, 2 * head), bf16), pltpu.VMEM((2 * head, width), bf16),
         pltpu.VMEM((3, 2 * length, hidden), bf16), pltpu.VMEM((hidden, 2 * length), bf16),
         pltpu.VMEM((2, length, width), bf16)]
        + scatter_scratch(rows, width) + scatter_scratch(rows, width)
        + [pltpu.VMEM((2, 8, 8, 128), f32), pltpu.VMEM((2, 8, 128), f32), pltpu.VMEM((2, 8, 8, 128), f32), dma(2, 8),
           pltpu.VMEM((2, 128, 128), f32), pltpu.VMEM((2 * length, 128), f32), pltpu.VMEM((length, 128), f32),
           pltpu.VMEM((2, rows, width), bf16), pltpu.VMEM((2, length, length), f32), pltpu.VMEM((2, 5, length, head), f32),
           pltpu.VMEM((4, 2 * length, 2 * head), bf16), pltpu.VMEM((2 * length, 2 * head), bf16),
           pltpu.VMEM((2 * head, width), bf16), pltpu.VMEM((4, 2 * head, width), bf16),
           dma(2, 3), dma(3), dma(3), dma(4, 4), dma(2, 8), dma(4), dma(2), dma(4, 4)],
        "backward_part",
    )
    return (
        out.reshape(2, 1, rows, width),
        grad_x.reshape(2, 1, rows, width),
        fq.T.astype(f32), fk.T.astype(f32), fv.T.astype(f32), fu.T.astype(f32), fo.astype(f32),
        ff.T.astype(f32), fs.T.astype(f32), ft.astype(f32),
    )


def solution(mesh):
    in_specs = (
        P(None, "grp", "seq", None),
        P(None, "grp", "seq", None),
        P(None, "grp"),
        P(),
        P("seq", "grp"),
        P("seq", "grp"),
        P("seq", "grp"),
        P("seq", "grp"),
        P("seq", "grp"),
        P("seq", "grp"),
        P("seq", "grp"),
        P("seq", "grp"),
    )
    out_specs = (
        P(None, "grp", "seq", None),
        P(None, "grp", "seq", None),
        P("seq", "grp"),
        P("seq", "grp"),
        P("seq", "grp"),
        P("seq", "grp"),
        P("seq", "grp"),
        P("seq", "grp"),
        P("seq", "grp"),
        P("seq", "grp"),
    )
    fast = mesh.shape["grp"] == 4 and mesh.shape["seq"] == 8
    return jax.shard_map(line_shards if fast else shards, mesh=mesh, in_specs=in_specs, out_specs=out_specs, check_vma=False)
```

```python
import functools

import jax
import jax.numpy as jnp
from jax import lax
from jax.experimental import pallas as pl
from jax.experimental.pallas import tpu as pltpu
from jax.sharding import PartitionSpec as P

EPS = 1e-06
HIGH = lax.Precision.HIGHEST
MESH = pl.DeviceIdType.MESH
ANY = pl.BlockSpec(memory_space=pl.ANY)
VMEM = pl.BlockSpec(memory_space=pltpu.VMEM)


def prefix(value, axis, join, neutral, backward):
    count, mine = (lax.axis_size(axis), lax.axis_index(axis))
    pieces = jax.tree.map(lambda part: lax.all_gather(part, axis), value)
    if backward:
        pieces = jax.tree.map(lambda part: part[::-1], pieces)
        mine = count - 1 - mine
    subtotal = jax.tree.map(
        lambda part, zero: jnp.full_like(part, 0) + jnp.asarray(zero, part.dtype), value, neutral
    )

    def step(position, subtotal):
        longer = join(subtotal, jax.tree.map(lambda part: part[position], pieces))
        return jax.tree.map(lambda new, old: jnp.where(position < mine, new, old), longer, subtotal)

    return lax.fori_loop(0, count - 1, step, subtotal)


def norm_rows(values):
    return values * lax.rsqrt(jnp.mean(values * values, axis=-1, keepdims=True) + EPS)


def norm_back(values, gradient):
    _, pull = jax.vjp(norm_rows, values)
    return pull(gradient)[0]


def silu_slope(values):
    sigma = jax.nn.sigmoid(values)
    return sigma * (1.0 + values * (1.0 - sigma))


def product(left, right):
    return jnp.dot(left, right, preferred_element_type=jnp.float32)


def product_left(left, right):
    return lax.dot_general(
        left, right, (((0,), (0,)), ((), ())), preferred_element_type=jnp.float32
    )


def product_right(left, right):
    return lax.dot_general(
        left, right, (((1,), (1,)), ((), ())), preferred_element_type=jnp.float32
    )


def combine_state(earlier, later):
    return (later[1][:, None, None] * earlier[0] + later[0], earlier[1] * later[1])


def shards(
    tokens,
    cotangent,
    lengths,
    decay_rate,
    w_query,
    w_key,
    w_value,
    w_gate,
    w_out,
    w_first,
    w_second,
    w_third,
):
    micro = tokens.shape[0]
    block_rows = tokens.shape[2]
    width = tokens.shape[3]
    heads = decay_rate.shape[0]
    head_dim = width // heads
    hidden_width = w_third.shape[0] * lax.axis_size("seq")
    places = jnp.arange(block_rows).astype(jnp.float32)
    slot_index = lax.axis_index("seq") * block_rows + jnp.arange(block_rows)
    offset = places[:, None] - places[None, :]
    weight = jnp.where(
        offset[None] >= 0, jnp.exp(-decay_rate[:, None, None] * jnp.maximum(offset, 0.0)[None]), 0.0
    )
    query_fac = jnp.exp(-decay_rate[None, :] * (places[:, None] + 1.0))[:, :, None]
    key_fac = jnp.exp(-decay_rate[None, :] * (block_rows - 1.0 - places[:, None]))[:, :, None]
    step_decay = jnp.exp(-decay_rate * block_rows)
    empty_state = jnp.zeros((heads, head_dim, head_dim), jnp.float32)
    unit_decay = jnp.ones((heads,), jnp.float32)
    partial_rows = (
        lax.all_gather(w_query, "grp", axis=1, tiled=True),
        lax.all_gather(w_key, "grp", axis=1, tiled=True),
        lax.all_gather(w_value, "grp", axis=1, tiled=True),
        lax.all_gather(w_gate, "grp", axis=1, tiled=True),
        lax.all_gather(w_out, "grp", axis=1, tiled=True),
        lax.all_gather(w_first, "grp", axis=1, tiled=True),
        lax.all_gather(w_second, "grp", axis=1, tiled=True),
        lax.all_gather(w_third, "grp", axis=1, tiled=True),
    )
    gathered = (
        lax.all_gather(partial_rows[0], "seq", axis=0, tiled=True),
        lax.all_gather(partial_rows[1], "seq", axis=0, tiled=True),
        lax.all_gather(partial_rows[2], "seq", axis=0, tiled=True),
        lax.all_gather(partial_rows[3], "seq", axis=0, tiled=True),
        lax.all_gather(partial_rows[4], "seq", axis=0, tiled=True),
        lax.all_gather(partial_rows[5], "seq", axis=0, tiled=True),
        lax.all_gather(partial_rows[6], "seq", axis=0, tiled=True),
        lax.all_gather(partial_rows[7], "seq", axis=0, tiled=True),
    )
    outputs = []
    input_grads = []
    first_norms = []
    attn_rows = []
    normed_rows = []
    branch_rows = []
    second_norms = []
    ffn_rows = []
    mixed_rows = []
    upstream_rows = []
    for batch_idx in range(micro):
        wq_full, wk_full, wv_full, wu_full, wo_full, first_full, second_full, third_full = gathered
        inputs = tokens[batch_idx, 0].astype(jnp.float32)
        live = (slot_index < lengths[batch_idx, 0]).astype(jnp.float32)[:, None]
        live_low = live.astype(jnp.bfloat16)
        first_norm = norm_rows(inputs).astype(jnp.bfloat16)
        query_pre = product(first_norm, wq_full)
        key_pre = product(first_norm, wk_full)
        value_pre = product(first_norm, wv_full)
        gate_pre = product(first_norm, wu_full)
        queries = jax.nn.silu(query_pre).astype(jnp.bfloat16).reshape(block_rows, heads, head_dim)
        key_heads = (jax.nn.silu(key_pre).astype(jnp.bfloat16) * live_low).reshape(
            block_rows, heads, head_dim
        )
        value_heads = (jax.nn.silu(value_pre).astype(jnp.bfloat16) * live_low).reshape(
            block_rows, heads, head_dim
        )
        query_wide = queries.astype(jnp.float32)
        key_wide = key_heads.astype(jnp.float32)
        value_wide = value_heads.astype(jnp.float32)
        local_state = jnp.einsum("jhd,jhe->hde", key_wide * key_fac, value_wide, precision=HIGH)
        prior_state, _ = prefix(
            (local_state, step_decay), "seq", combine_state, (empty_state, unit_decay), False
        )
        scores = (
            jnp.einsum("ihd,jhd->hij", queries, key_heads, preferred_element_type=jnp.float32)
            * weight
        )
        intra = jnp.einsum("hij,jhe->ihe", scores, value_wide, precision=HIGH)
        inter = jnp.einsum("ihd,hde->ihe", query_wide * query_fac, prior_state, precision=HIGH)
        attended = (intra + inter).reshape(block_rows, width)
        gate_act = jax.nn.silu(gate_pre)
        gated = gate_act * attended
        normed = norm_rows(gated).astype(jnp.bfloat16)
        hidden = inputs + product(normed, wo_full)
        second_norm = norm_rows(hidden).astype(jnp.bfloat16)
        first_proj = product(second_norm, first_full)
        second_proj = product(second_norm, second_full)
        mixed_in = (first_proj * second_proj).astype(jnp.bfloat16)
        result = hidden + product(mixed_in, third_full)
        outputs.append(result.astype(jnp.bfloat16))
        upstream = cotangent[batch_idx, 0].astype(jnp.float32) * live
        upstream_low = upstream.astype(jnp.bfloat16)
        grad_mixed = product_right(upstream_low, third_full)
        grad_first_proj = (grad_mixed * second_proj).astype(jnp.bfloat16)
        grad_second_proj = (grad_mixed * first_proj).astype(jnp.bfloat16)
        grad_norm_two = product_right(grad_first_proj, first_full) + product_right(
            grad_second_proj, second_full
        )
        grad_hidden = upstream + norm_back(hidden, grad_norm_two)
        grad_branch = grad_hidden.astype(jnp.bfloat16)
        grad_gated = norm_back(gated, product_right(grad_branch, wo_full))
        grad_attended = (grad_gated * gate_act).astype(jnp.bfloat16)
        grad_gate_pre = (grad_gated * attended * silu_slope(gate_pre)).astype(jnp.bfloat16)
        grad_heads = grad_attended.reshape(block_rows, heads, head_dim)
        grad_wide = grad_heads.astype(jnp.float32)
        local_grad = jnp.einsum("ihd,ihe->hde", query_wide * query_fac, grad_wide, precision=HIGH)
        later_grad, _ = prefix(
            (local_grad, step_decay), "seq", combine_state, (empty_state, unit_decay), True
        )
        grad_scores = (
            jnp.einsum("ihe,jhe->hij", grad_heads, value_heads, preferred_element_type=jnp.float32)
            * weight
        )
        grad_queries = jnp.einsum("hij,jhd->ihd", grad_scores, key_wide, precision=HIGH)
        grad_queries = (
            grad_queries
            + jnp.einsum("ihe,hde->ihd", grad_wide, prior_state, precision=HIGH) * query_fac
        )
        grad_keys = jnp.einsum("hij,ihd->jhd", grad_scores, query_wide, precision=HIGH)
        grad_keys = (
            grad_keys + jnp.einsum("hde,jhe->jhd", later_grad, value_wide, precision=HIGH) * key_fac
        )
        grad_values = jnp.einsum("hij,ihe->jhe", scores, grad_wide, precision=HIGH)
        grad_values = (
            grad_values + jnp.einsum("jhd,hde->jhe", key_wide, later_grad, precision=HIGH) * key_fac
        )
        grad_query_pre = (grad_queries.reshape(block_rows, width) * silu_slope(query_pre)).astype(
            jnp.bfloat16
        )
        grad_key_pre = (grad_keys.reshape(block_rows, width) * live * silu_slope(key_pre)).astype(
            jnp.bfloat16
        )
        grad_value_pre = (
            grad_values.reshape(block_rows, width) * live * silu_slope(value_pre)
        ).astype(jnp.bfloat16)
        grad_norm_one = product_right(grad_query_pre, wq_full) + product_right(
            grad_key_pre, wk_full
        )
        grad_norm_one = (
            grad_norm_one
            + product_right(grad_value_pre, wv_full)
            + product_right(grad_gate_pre, wu_full)
        )
        input_grads.append(grad_hidden + norm_back(inputs, grad_norm_one))
        first_norms.append(first_norm)
        attn_rows.append(
            jnp.concatenate([grad_query_pre, grad_key_pre, grad_value_pre, grad_gate_pre], axis=1)
        )
        normed_rows.append(normed)
        branch_rows.append(grad_branch)
        second_norms.append(second_norm)
        ffn_rows.append(jnp.concatenate([grad_first_proj, grad_second_proj], axis=1))
        mixed_rows.append(mixed_in)
        upstream_rows.append(upstream_low)
    first_all = jnp.concatenate(first_norms, axis=0)
    attn_all = jnp.concatenate(attn_rows, axis=0)
    normed_all = jnp.concatenate(normed_rows, axis=0)
    branch_all = jnp.concatenate(branch_rows, axis=0)
    second_all = jnp.concatenate(second_norms, axis=0)
    ffn_all = jnp.concatenate(ffn_rows, axis=0)
    mixed_all = jnp.concatenate(mixed_rows, axis=0)
    upstream_all = jnp.concatenate(upstream_rows, axis=0)
    proj_rows = lax.psum_scatter(
        product_left(first_all, attn_all), "seq", scatter_dimension=0, tiled=True
    )
    outproj_rows = lax.psum_scatter(
        product_left(normed_all, branch_all), "seq", scatter_dimension=0, tiled=True
    )
    ffn_part = lax.psum_scatter(
        product_left(second_all, ffn_all), "seq", scatter_dimension=0, tiled=True
    )
    down_rows = lax.psum_scatter(
        product_left(mixed_all, upstream_all), "seq", scatter_dimension=0, tiled=True
    )
    summed = (
        lax.psum_scatter(proj_rows[:, :width], "grp", scatter_dimension=1, tiled=True),
        lax.psum_scatter(proj_rows[:, width : 2 * width], "grp", scatter_dimension=1, tiled=True),
        lax.psum_scatter(
            proj_rows[:, 2 * width : 3 * width], "grp", scatter_dimension=1, tiled=True
        ),
        lax.psum_scatter(proj_rows[:, 3 * width :], "grp", scatter_dimension=1, tiled=True),
        lax.psum_scatter(outproj_rows, "grp", scatter_dimension=1, tiled=True),
        lax.psum_scatter(ffn_part[:, :hidden_width], "grp", scatter_dimension=1, tiled=True),
        lax.psum_scatter(ffn_part[:, hidden_width:], "grp", scatter_dimension=1, tiled=True),
        lax.psum_scatter(down_rows, "grp", scatter_dimension=1, tiled=True),
    )
    layer_out = jnp.stack(outputs)[:, None]
    grad_tokens = jnp.stack(input_grads)[:, None]
    return (
        layer_out,
        grad_tokens,
        summed[0],
        summed[1],
        summed[2],
        summed[3],
        summed[4],
        summed[5],
        summed[6],
        summed[7],
    )


class Spare:
    def __init__(self, sems):
        self.sems, self.free = sems, list(range(sems.shape[0]))


class Copies:
    def __init__(self, spare):
        self.spare = spare
        self.pending = []

    def remote(self, src, dst, recv_sem, group, place, when=None):
        number = self.spare.free.pop(0)
        copy = pltpu.make_async_remote_copy(
            src_ref=src,
            dst_ref=dst,
            send_sem=self.spare.sems.at[number],
            recv_sem=recv_sem,
            device_id=(group, place),
            device_id_type=MESH,
        )
        self.pending.append((copy, when, number))
        if when is None:
            copy.start()
        else:
            pl.when(when)(copy.start)
        return self.pending[-1]

    def settle(self, entry):
        if not any(other is entry for other in self.pending):
            return
        self.pending = [other for other in self.pending if other is not entry]
        copy, when, number = entry
        if when is None:
            copy.wait_send()
        else:
            pl.when(when)(copy.wait_send)
        self.spare.free.append(number)

    def finish(self):
        while self.pending:
            self.settle(self.pending[0])


def local(src, dst, sem, when=None):
    copy = pltpu.make_async_copy(src, dst, sem)
    if when is None:
        copy.start()
    else:
        pl.when(when)(copy.start)


def arrived(ref, sem, when=None):
    copy = pltpu.make_async_copy(ref, ref, sem)
    if when is None:
        copy.wait()
    else:
        pl.when(when)(copy.wait)


def where_am_i():
    g, s = lax.axis_index("grp"), lax.axis_index("seq")
    return g, s, g // 2, g % 2, s // 2, s % 2


def across(y, x):
    return (y * 2 + 1 - x, (1 - y) * 2 + x, (1 - y) * 2 + 1 - x)


def greet(partners):
    barrier = pltpu.get_barrier_semaphore()
    for partner in partners:
        pl.semaphore_signal(barrier, inc=1, device_id=partner, device_id_type=MESH)
    pl.semaphore_wait(barrier, len(partners))


def aligned(index, unit, step):
    return pl.ds(pl.multiple_of(index * unit, step), unit)


class Gather:
    def __init__(self, copies, out, rows, hop_sem, side_sem):
        self.copies, self.out, self.rows = copies, out, rows
        self.hop_sem, self.side_sem = hop_sem, side_sem
        self.g, self.s, _, _, self.z, self.c = where_am_i()

    def block(self, b, z, core):
        return self.out.at[b, aligned(2 * z + core, self.rows, 16)]

    def spread(self, src, b, z_of, k, right, left):
        g, s, z, c = self.g, self.s, self.z, self.c
        dst = self.block(b, z_of, c)
        if right is not None:
            self.copies.remote(src, dst, self.hop_sem.at[b, 0, k], g, (s + 2) % 8, right)
        if left is not None:
            self.copies.remote(src, dst, self.hop_sem.at[b, 1, k], g, (s + 6) % 8, left)

    def begin(self, src, own_sem, b):
        g, s, z, c = self.g, self.s, self.z, self.c
        self.spread(src, b, z, 0, z < 3, z > 0)
        self.copies.remote(src, self.block(b, z, c), self.side_sem.at[b, 0], g, s + 1 - 2 * c)
        local(src, self.block(b, z, c), own_sem)

    def step(self, b, k):
        g, s, z, c = self.g, self.s, self.z, self.c
        side = s + 1 - 2 * c
        has = z >= k
        at = jnp.maximum(z - k, 0)
        ref = self.block(b, at, c)
        arrived(ref, self.hop_sem.at[b, 0, k - 1], has)
        if k < 3:
            self.spread(ref, b, at, k, jnp.logical_and(has, z < 3), None)
        self.copies.remote(ref, ref, self.side_sem.at[b, k], g, side, has)
        has = z + k <= 3
        at = jnp.minimum(z + k, 3)
        ref = self.block(b, at, c)
        arrived(ref, self.hop_sem.at[b, 1, k - 1], has)
        if k < 3:
            self.spread(ref, b, at, k, None, jnp.logical_and(has, z > 0))
        self.copies.remote(ref, ref, self.side_sem.at[b, 3 + k], g, side, has)

    def finish(self, own_sem, b):
        z, c = self.z, self.c
        arrived(self.block(b, z, c), own_sem)
        arrived(self.block(b, z, 1 - c), self.side_sem.at[b, 0])
        for k in (1, 2, 3):
            arrived(self.block(b, jnp.maximum(z - k, 0), 1 - c), self.side_sem.at[b, k], z >= k)
            arrived(self.block(b, jnp.minimum(z + k, 3), 1 - c), self.side_sem.at[b, 3 + k], z + k <= 3)


def line_partners(g, s):
    return [(g, (s + d) % 8) for d in range(1, 8)]


def everyone_on_line(copies, src, dst, sem, g, s, to_rows):
    for d in range(1, 8):
        to = (s + d) % 8
        copies.remote(to_rows(to), dst.at[s], sem.at[d - 1], g, to)


def mean_square(values):
    return jnp.mean(values * values, axis=-1, keepdims=True)


def pour(read, write, count):
    def piece(i, carry):
        at = aligned(i, 16, 16)
        write(at, read(at))
        return carry

    lax.fori_loop(0, count, piece, 0)


class LineScatter:
    def __init__(self, copies, part, rows, side, inbox, side_sem, line_sem, queue):
        self.copies, self.part, self.rows, self.queue = copies, part, rows, queue
        self.side, self.inbox, self.side_sem, self.line_sem = side, inbox, side_sem, line_sem
        self.g, self.s, _, _, self.z, self.c = where_am_i()

    def mine(self, chip):
        return self.part.at[aligned(2 * chip + self.c, self.rows, 16)]

    def begin(self):
        for chip in (3, 0, 2, 1):
            theirs = aligned(2 * chip + 1 - self.c, self.rows, 16)
            self.copies.remote(
                self.part.at[theirs], self.side.at[chip], self.side_sem.at[chip], self.g, self.s + 1 - 2 * self.c
            )

    def add_on(self, chip, way):
        own, side = self.mine(chip), self.side.at[chip]
        slot = chip - 1 if way == 0 else chip
        come = self.inbox.at[way, slot]
        arrived(side, self.side_sem.at[chip])
        arrived(come, self.line_sem.at[way, slot])

        def three(at):
            return own[at].astype(jnp.float32) + side[at].astype(jnp.float32) + come[at].astype(jnp.float32)

        def write(at, value):
            own[at] = value.astype(jnp.bfloat16)

        pour(three, write, self.rows // 16)

    def push(self, chip, way, when):
        slot = chip - 1 if way == 0 else chip
        to = (self.s + 2) % 8 if way == 0 else (self.s + 6) % 8
        return self.copies.remote(
            self.mine(chip), self.inbox.at[way, slot], self.line_sem.at[way, slot], self.g, to, when
        )

    def pass_on(self, chip, way):
        end = self.z == (0 if way == 0 else 3)
        own, side = self.mine(chip), self.side.at[chip]

        def two(at):
            return own[at].astype(jnp.float32) + side[at].astype(jnp.float32)

        def write(at, value):
            own[at] = value.astype(jnp.bfloat16)

        @pl.when(end)
        def _():
            arrived(side, self.side_sem.at[chip])
            pour(two, write, self.rows // 16)

        if way in self.queue:
            copies, entry = self.queue.pop(way)
            copies.settle(entry)
        self.queue[way] = (self.copies, self.push(chip, way, end))

    def start(self, i):
        self.pass_on(3 - i, 0)
        self.pass_on(i, 1)

    def hop(self, i):
        z = self.z
        for inner in (1, 2):

            @pl.when(z == inner)
            def _():
                near = inner == 1
                if i < 2:
                    self.add_on(3 - i if near else i, 0 if near else 1)
                else:
                    self.add_on(0 if near else 3, 1 if near else 0)

        for inner in (1, 2):
            near = inner == 1
            if i < 2:
                self.push(3 - i if near else i, 0 if near else 1, z == inner)
            else:
                self.push(0 if near else 3, 1 if near else 0, z == inner)

    def receive(self):
        z = self.z
        arrived(self.side.at[z], self.side_sem.at[z])
        left, right = jnp.maximum(z - 1, 0), jnp.minimum(z, 2)
        arrived(self.inbox.at[0, left], self.line_sem.at[0, left], z > 0)
        arrived(self.inbox.at[1, right], self.line_sem.at[1, right], z < 3)

    def total(self, at):
        z = self.z
        value = self.mine(z)[at].astype(jnp.float32) + self.side[z, at].astype(jnp.float32)
        from_left = self.inbox[0, jnp.maximum(z - 1, 0), at].astype(jnp.float32)
        from_right = self.inbox[1, jnp.minimum(z, 2), at].astype(jnp.float32)
        return value + jnp.where(z > 0, from_left, 0.0) + jnp.where(z < 3, from_right, 0.0)


def silu(values):
    return values / (1.0 + jnp.exp(-values))


def decay_table(rate, length):
    offset = lax.broadcasted_iota(jnp.int32, (length, length), 0) - lax.broadcasted_iota(jnp.int32, (length, length), 1)
    steps = jnp.maximum(offset, 0).astype(jnp.float32)
    return jnp.where(offset >= 0, jnp.exp(-rate * steps), 0.0)


def live_rows(first, count, length):
    return ((first + lax.broadcasted_iota(jnp.int32, (count, 1), 0)) < length).astype(jnp.float32)


def slope(values):
    sigma = 1.0 / (1.0 + jnp.exp(-values))
    return sigma * (1.0 + values * (1.0 - sigma))


def turned_table(rate, length):
    offset = lax.broadcasted_iota(jnp.int32, (length, length), 1) - lax.broadcasted_iota(jnp.int32, (length, length), 0)
    steps = jnp.maximum(offset, 0).astype(jnp.float32)
    return jnp.where(offset >= 0, jnp.exp(-rate * steps), 0.0)


def columns_of(out, tiles, b, rows):
    for owner in range(8):
        out[pl.ds(owner * rows, rows)] = jnp.broadcast_to(tiles[b, owner, :1], (128, 128)).T[:rows]


def turn(dst, read, count, columns):
    def block(i, carry):
        dst[pl.ds(0, columns), aligned(i, 128, 128)] = read(aligned(i, 128, 128)).T
        return carry

    lax.fori_loop(0, count, block, 0)


def tiles_of(width, body):
    def tile(i, carry):
        body(aligned(i, 256, 256), i)
        return carry

    lax.fori_loop(0, width // 256, tile, 0)


def layer_part(
    lengths, decay, x, cot, wq, wk, wv, wu, wo, w1, w2, w3,
    out, grad_x, fq, fk, fv, fu, fo, ff_, fs, ft,
    n1_all, dm_all, n2_all, da_all, q_all, k_all, v_all, u_all, o_all, f_all, s_all, t_all, pre_all, in_f, in_t, in_o, in_h,
    send, load, own, hop_n, side_n, hop_d, side_d, hop_m, side_m_, hop_a, side_a, z_head, z_out, z_ff, xy_head, xy_out, xy_ff,
    n1, dm, n2, da, h, a_v, b_v, w_v, wa_v, wo_v, p_v, turned, part, side, inbox, side_sem, line_sem,
    side_m, inbox_m, side_sem_m, line_sem_m, table, squares, inbox_sq, scale, scale_in, sq_sem, sc_sem, column,
    mix, mix_in, mix_sem, inverse, mixed, pre, pre_sem, go_v, grads_h,
    xy_f, xy_t, xy_o, xy_h, z_f, z_t, z_o, z_h,
):
    g, s, y, x_, z, c = where_am_i()
    others = across(y, x_)
    plane = [(o, 2 * z + e) for o in others for e in range(2)]
    rows, width = x.shape[1], x.shape[2]
    length = 8 * rows
    tokens = 2 * length
    depth, wide = wq.shape
    head = q_all.shape[1] // 2
    ff = f_all.shape[0] // 4
    hidden = 4 * ff
    half = length // 2
    target = g // 2
    mine = aligned(g % 2, head, head)
    here = c == target
    order = [(z + d) % 4 for d in (0, 1, 3, 2)]
    spare = Spare(send)
    copies, turned_out, bulk, last = [Copies(spare) for _ in range(4)]
    early, sums = [[Copies(spare) for _ in range(2)] for _ in range(2)]
    gather_n = Gather(copies, n1_all, rows, hop_n, side_n)
    gather_d = Gather(copies, dm_all, rows, hop_d, side_d)
    gather_m = Gather(copies, n2_all, rows, hop_m, side_m_)
    gather_a = Gather(last, da_all, rows, hop_a, side_a)
    heads = list(zip((wq, wk, wv, wu), (q_all, k_all, v_all, u_all)))
    w1_f, w2_f, w3_f = [w_v.at[pl.ds(n * hidden, hidden)] for n in range(3)]
    w1_in, w2_in = [w_v.at[pl.ds(n * depth, depth), pl.ds(512, 2 * hidden)] for n in range(2)]
    w1_t, w2_t = [w_v.at[pl.ds(0, 2 * hidden), pl.ds(n * depth, depth)] for n in range(2)]
    low_v = p_v.at[2, pl.ds(0, length), pl.ds(0, 2 * head)]

    def at_b(b):
        return pl.ds(b * length, length)

    def dz(n, at):
        return p_v.at[n // 2, at, pl.ds((n % 2) * 2 * head, 2 * head)]

    def nat_v(at):
        return p_v.at[2, at, pl.ds(0, 2 * head)]

    local(w1, w1_in, load.at[0])
    local(w2, w2_in, load.at[1])
    greet(line_partners(g, s) + plane)

    def send_heads(n):
        src, dst = heads[n]
        for d in (2, 1, 3, 0):
            to = (z + d) % 4
            a, b = src.at[:, aligned(to, head, head)], dst.at[aligned(s, depth, 16), mine]
            if d:
                copies.remote(a, b, z_head.at[n, z], g, 2 * to + target)
            else:
                copies.remote(a, b, z_head.at[n, z], g, 2 * to + target, c != target)
                local(a, b, z_head.at[n, z], here)

    def pass_heads(n):
        dst = heads[n][1]
        for zs in order:
            block = dst.at[aligned(zs, 2 * depth, 16), mine]
            arrived(block, z_head.at[n, zs], here)
            for r, o in enumerate(others):
                copies.remote(block, block, xy_head.at[n, r, zs], o, s, here)

    def send_out():
        for i in range(2):
            to = 2 * c + i
            a = wo.at[pl.ds(i * head, head)]
            b = o_all.at[aligned(z % 2, head, head), aligned(g, wide, 128)]
            self_ = jnp.logical_and(to == z, c == z // 2)
            copies.remote(a, b, z_out.at[z % 2], g, 2 * to + z // 2, jnp.logical_not(self_))
            local(a, b, z_out.at[z % 2], self_)

    def pass_out():
        for j in range(2):
            arrived(o_all.at[pl.ds(j * head, head), aligned(g, wide, 128)], z_out.at[j])
        block = o_all.at[:, aligned(g, wide, 128)]
        for r, o in enumerate(others):
            copies.remote(block, block, xy_out.at[r], o, s)

    def send_ff(n):
        src, dst = ((w1_t, f_all), (w2_t, s_all))[n]
        for d in (4, 3, 5, 2, 6, 1, 7, 0):
            to = (s + d) % 8
            a = src.at[aligned(to, ff, 16)]
            b = dst.at[aligned(g, ff, 16), aligned(s, depth, 128)]
            if d:
                turned_out.remote(a, b, z_ff.at[n, z], g, to)
            else:
                local(a, b, z_ff.at[n, z])

    def arrive_ff(n):
        dst = (f_all, s_all)[n]
        for zs in order:
            arrived(dst.at[aligned(g, ff, 16), aligned(zs, 2 * depth, 128)], z_ff.at[n, zs])

    def pass_ff(n):
        dst = (f_all, s_all)[n]
        for zs in order:
            block = dst.at[aligned(g, ff, 16), aligned(zs, 2 * depth, 128)]
            for r, o in enumerate(others):
                copies.remote(block, block, xy_ff.at[n, r, zs], o, s)

    def send_third():
        for d in (2, 1, 3, 0):
            to = 4 * c + (s + d) % 4
            a = w3.at[aligned(to % 4, ff, 16)]
            b = t_all.at[aligned(z, ff, 16), aligned(g, wide, 128)]
            if d:
                copies.remote(a, b, z_ff.at[2, z], g, to)
            else:
                self_ = s // 4 == c
                copies.remote(a, b, z_ff.at[2, z], g, to, jnp.logical_not(self_))
                local(a, b, z_ff.at[2, z], self_)

    def pass_third():
        for zs in order:
            block = t_all.at[aligned(zs, ff, 16), aligned(g, wide, 128)]
            arrived(block, z_ff.at[2, zs])
            for r, o in enumerate(others):
                copies.remote(block, block, xy_ff.at[2, r, zs], o, s)

    send_heads(0)
    send_heads(1)
    for b in range(2):

        def norm(at):
            v = x[b, at].astype(jnp.float32)
            return v * lax.rsqrt(mean_square(v) + EPS)

        def keep(at, value):
            n1[b, at] = value.astype(jnp.bfloat16)

        pour(norm, keep, rows // 16)
        first = s * rows

        def masked(i, carry):
            at = aligned(i, 16, 16)
            live = live_rows(first + i * 16, 16, lengths[0, b])
            dm[b, at] = (cot[b, at].astype(jnp.float32) * live).astype(jnp.bfloat16)
            return carry

        lax.fori_loop(0, rows // 16, masked, 0)
    for n, (src, dst) in enumerate(((w1_in, w1_t), (w2_in, w2_t))):
        arrived(src, load.at[n])
        dst[...] = src[...].T
    pass_heads(0)
    send_heads(2)
    pass_heads(1)
    send_heads(3)
    send_ff(0)
    pass_heads(2)
    pass_heads(3)
    send_out()
    send_ff(1)
    for n in range(2):
        arrive_ff(n)
        if n == 0:
            for b in range(2):
                gather_n.begin(n1.at[b], own.at[0, b], b)
            pass_out()
    gather_n.step(0, 1)
    gather_n.step(1, 1)
    pass_ff(0)
    gather_n.step(0, 2)
    gather_n.step(1, 2)
    pass_ff(1)
    gather_n.step(0, 3)
    gather_n.step(1, 3)
    send_third()
    for r, o in enumerate(others):
        from_here = (o // 2) == c
        for n, (_, dst) in enumerate(heads):
            for zs in range(4):
                block = dst.at[pl.ds(zs * 2 * depth, 2 * depth), aligned(o % 2, head, head)]
                arrived(block, xy_head.at[n, r, zs], from_here)
        arrived(o_all.at[:, aligned(o, wide, 128)], xy_out.at[r])
    for n, (_, dst) in enumerate(heads):
        local(dst, wa_v.at[n], load.at[n])
    local(o_all, wo_v, load.at[4])
    for b in range(2):
        gather_n.finish(own.at[0, b], b)
        local(n1_all.at[b], a_v.at[at_b(b)], load.at[5 + b])
    for j in range(2):
        table[j] = decay_table(decay[4 * (2 * c + j) + z], length)
    for n in range(4):
        arrived(wa_v.at[n], load.at[n])
    arrived(wo_v, load.at[4])

    def scatters_of(copies, first, queue):
        kept = (side, inbox, side_sem, line_sem) if first else (side_m, inbox_m, side_sem_m, line_sem_m)
        return [LineScatter(copies[b], part.at[b], rows, *[k.at[b] for k in kept], queue) for b in range(2)]

    scatters = scatters_of(early, True, {})
    for b in range(2):
        arrived(a_v.at[at_b(b)], load.at[5 + b])
        if b == 1:
            for j in range(2):
                arrived(pre.at[j], pre_sem.at[j])

        def project(i, carry):
            at = aligned(i, half, 16)
            from_ = aligned(2 * b + i, half, 16)
            for n in range(4):
                value = product(a_v[from_], wa_v[n])
                for j in range(2):
                    pre[j, n, at] = value[:, j * head : (j + 1) * head]
            return carry

        lax.fori_loop(0, 2, project, 0)
        if b == 1:
            scatters[0].start(1)
        live = live_rows(0, length, lengths[0, b])
        square = 0.0
        for j in range(2):
            q = silu(pre[j, 0]).astype(jnp.bfloat16)
            k = (silu(pre[j, 1]) * live).astype(jnp.bfloat16)
            v = (silu(pre[j, 2]) * live).astype(jnp.bfloat16)
            scores = (product_right(q, k) * table[j]).astype(jnp.bfloat16)
            attended = product(scores, v)
            pre[j, 4] = attended
            gated = silu(pre[j, 3]) * attended
            square = square + jnp.sum(gated * gated, axis=-1, keepdims=True)
            low_v[:, pl.ds(j * head, head)] = gated.astype(jnp.bfloat16)
            local(pre.at[j], pre_all.at[b, j], pre_sem.at[j])
        row = jnp.broadcast_to(square, (length, 128)).T[:8]
        for to in range(8):
            squares[b, to, :, :rows] = row[:, to * rows : (to + 1) * rows]
        everyone_on_line(copies, squares, inbox_sq.at[b], sq_sem.at[b], g, s, lambda to: squares.at[b, to])
        local(squares.at[b, s], inbox_sq.at[b, s], sq_sem.at[b, 7])

        def out_part(i, carry):
            at = aligned(i, 256, 256)
            part[b, :, at] = product(low_v[...], wo_v[:, at]).astype(jnp.bfloat16)
            return carry

        lax.fori_loop(0, width // 256, out_part, 0)
        scatters[b].begin()
        if b == 0:
            scatters[0].start(0)

    def hidden_state(b):
        for d in range(8):
            arrived(inbox_sq.at[b, 0], sq_sem.at[b, d])
        total = inbox_sq[b, 0]
        for d in range(1, 8):
            total = total + inbox_sq[b, d]
        row = lax.rsqrt(total / width + EPS)
        scale[b] = row
        column[b] = jnp.broadcast_to(row[:1], (128, 128)).T
        scatter = scatters[b]
        scatter.receive()

        def finish(i, carry):
            piece = aligned(i, 16, 16)
            at = aligned(b * (rows // 16) + i, 16, 16)
            a = scatter.total(piece) * column[b, piece, :1]
            value = x[b, piece].astype(jnp.float32) + a
            h[at] = value
            n2[b, piece] = (value * lax.rsqrt(mean_square(value) + EPS)).astype(jnp.bfloat16)
            return carry

        lax.fori_loop(0, rows // 16, finish, 0)
        gather_m.begin(n2.at[b], own.at[2, b], b)

    gather_d.begin(dm.at[0], own.at[1, 0], 0)
    scatters[0].hop(0)
    scatters[0].start(2)
    scatters[0].hop(1)
    scatters[1].start(0)
    scatters[0].hop(2)
    gather_d.step(0, 1)
    hidden_state(0)
    scatters[1].start(1)
    scatters[1].hop(0)
    pass_third()
    gather_d.step(0, 2)
    scatters[1].start(2)
    scatters[1].hop(1)
    gather_m.step(0, 1)
    scatters[1].hop(2)
    gather_d.step(0, 3)
    gather_m.step(0, 2)
    gather_d.begin(dm.at[1], own.at[1, 1], 1)
    hidden_state(1)
    gather_m.step(0, 3)
    gather_d.finish(own.at[1, 0], 0)
    local(dm_all.at[0], b_v.at[at_b(0)], load.at[2])
    gather_m.finish(own.at[2, 0], 0)
    local(n2_all.at[0], a_v.at[at_b(0)], load.at[0])
    gather_d.step(1, 1)
    gather_m.step(1, 1)
    turned_out.finish()
    for n, (dst, room) in enumerate(((f_all, w1_f), (s_all, w2_f), (t_all, w3_f))):
        for r, o in enumerate(others):
            for zs in range(4):
                if n < 2:
                    block = dst.at[aligned(o, ff, 16), pl.ds(zs * 2 * depth, 2 * depth)]
                else:
                    block = dst.at[pl.ds(zs * ff, ff), aligned(o, wide, 128)]
                arrived(block, xy_ff.at[n, r, zs])
        local(dst, room, load.at[4 + n])
    for b in range(2):
        early[b].finish()

    def feed_forward(b):
        def tile(i, carry):
            at = aligned(b * 2 + i, half, 16)
            first = product_right(a_v[at], w1_f[...])
            second = product_right(a_v[at], w2_f[...])
            back = product_right(b_v[at], w3_f[...])
            p_v[0, at] = (back * second).astype(jnp.bfloat16)
            p_v[1, at] = (back * first).astype(jnp.bfloat16)
            p_v[2, at] = (first * second).astype(jnp.bfloat16)
            return carry

        lax.fori_loop(0, 2, tile, 0)

    def norm_part(b):
        def body(at, i):
            value = product(p_v[0, at_b(b)], w1_f[:, at]) + product(p_v[1, at_b(b)], w2_f[:, at])
            part[b, :, at] = value.astype(jnp.bfloat16)

        tiles_of(width, body)

    def mixed_part(b):
        def body(at, i):
            part[b, :, at] = product(p_v[2, at_b(b)], w3_f[:, at]).astype(jnp.bfloat16)

        tiles_of(width, body)

    def weight_part(n, operand):
        turn(turned, lambda t: p_v[n, t], tokens // 128, hidden)

        def body(at, i):
            w_v[pl.ds(n * hidden, hidden), at] = product(turned[...], operand[:, at]).astype(jnp.bfloat16)

        tiles_of(width, body)
        for r, o in enumerate(others):
            if n < 2:
                bulk.remote(w_v.at[aligned(4 * n + o, ff, 16)], in_f.at[n, r], xy_f.at[n, r], o, s)
            else:
                bulk.remote(w_v.at[pl.ds(n * hidden, hidden), aligned(o, wide, 128)], in_t.at[r], xy_t.at[r], o, s)

    def hidden_gradient(b):
        scatter = second[b]
        scatter.receive()

        def finish(i, carry):
            piece = aligned(i, 16, 16)
            at = aligned(b * (rows // 16) + i, 16, 16)
            value = h[at]
            scale_h = lax.rsqrt(mean_square(value) + EPS)
            normed = value * scale_h
            grad = scatter.total(piece)
            along = jnp.mean(normed * grad, axis=-1, keepdims=True)
            live = live_rows(s * rows + i * 16, 16, lengths[0, b])
            upstream = cot[b, piece].astype(jnp.float32) * live
            grad_hidden = upstream + scale_h * (grad - normed * along)
            grad_x[at] = grad_hidden
            low = grad_hidden.astype(jnp.bfloat16)
            da[b, piece] = low
            dot = jnp.mean(low.astype(jnp.float32) * (value - x[b, piece].astype(jnp.float32)), axis=-1, keepdims=True)
            column[b, piece] = jnp.broadcast_to(dot, (16, 128))
            return carry

        lax.fori_loop(0, rows // 16, finish, 0)
        gather_a.begin(da.at[b], own.at[3, b], b)
        mix[b, :, :rows] = column[b].T[:8, :rows]
        for d in range(1, 8):
            last.remote(mix.at[b], mix_in.at[b, s], mix_sem.at[b, d - 1], g, (s + d) % 8)
        local(mix.at[b], mix_in.at[b, s], mix_sem.at[b, 7])

    second = scatters_of(early, True, {})
    for n in (0, 4, 5, 2, 6):
        ref = {0: a_v.at[at_b(0)], 2: b_v.at[at_b(0)], 4: w1_f, 5: w2_f, 6: w3_f}[n]
        arrived(ref, load.at[n])
    feed_forward(0)
    gather_m.step(1, 2)
    gather_d.step(1, 2)
    norm_part(0)
    second[0].begin()
    second[0].start(0)
    gather_m.step(1, 3)
    gather_d.step(1, 3)
    gather_d.finish(own.at[1, 1], 1)
    local(dm_all.at[1], b_v.at[at_b(1)], load.at[3])
    gather_m.finish(own.at[2, 1], 1)
    local(n2_all.at[1], a_v.at[at_b(1)], load.at[1])
    for b in range(2):
        for d in range(1, 8):
            copies.remote(scale.at[b], scale_in.at[b, s], sc_sem.at[b, d - 1], g, (s + d) % 8)
        local(scale.at[b], scale_in.at[b, s], sc_sem.at[b, 7])
    second[0].start(1)
    second[0].hop(0)
    arrived(a_v.at[at_b(1)], load.at[1])
    arrived(b_v.at[at_b(1)], load.at[3])
    feed_forward(1)
    second[0].start(2)
    second[0].hop(1)
    second[0].hop(2)
    norm_part(1)
    def load_pre(b, j):
        local(pre_all.at[b, j], pre.at[j], pre_sem.at[j])

    def attention_back(b):
        gather_a.finish(own.at[3, b], b)
        local(da_all.at[b], a_v.at[at_b(b)], load.at[b])
        for d in range(8):
            arrived(mix_in.at[b, 0], mix_sem.at[b, d])
        columns_of(mixed, mix_in, b, rows)
        live = live_rows(0, length, lengths[0, b])
        arrived(a_v.at[at_b(b)], load.at[b])
        for j in range(2):
            arrived(pre.at[j], pre_sem.at[j])
            lanes = pl.ds(j * head, head)
            error = product_right(a_v[at_b(b)], wo_v[pl.ds(j * head, head)])
            q_pre, k_pre, v_pre, u_pre, o = [pre[j, n] for n in range(5)]
            sigma = 1.0 / (1.0 + jnp.exp(-u_pre))
            u = u_pre * sigma
            scale_g = inverse[at_b(b), :1]
            nat = u * o * scale_g
            nat_v(at_b(b))[:, lanes] = nat.astype(jnp.bfloat16)
            dg = scale_g * (error - nat * mixed[:, :1])
            dz(3, at_b(b))[:, lanes] = (dg * o * (sigma * (1.0 + u_pre * (1.0 - sigma)))).astype(jnp.bfloat16)
            do = (dg * u).astype(jnp.bfloat16)
            q = silu(q_pre).astype(jnp.bfloat16)
            k = (silu(k_pre) * live).astype(jnp.bfloat16)
            v = (silu(v_pre) * live).astype(jnp.bfloat16)
            scores = (product_right(k, q) * table[j]).astype(jnp.bfloat16)
            dv = product(scores, do)
            d_scores = (product_right(v, do) * table[j]).astype(jnp.bfloat16)
            dk = product(d_scores, q)
            dq = product_left(d_scores, k)
            dz(0, at_b(b))[:, lanes] = (dq * slope(pre[j, 0])).astype(jnp.bfloat16)
            dz(1, at_b(b))[:, lanes] = (dk * live * slope(pre[j, 1])).astype(jnp.bfloat16)
            dz(2, at_b(b))[:, lanes] = (dv * live * slope(pre[j, 2])).astype(jnp.bfloat16)
            if b == 0:
                load_pre(1, j)

    def first_part(b):
        def body(at, i):
            value = product_right(dz(0, at_b(b))[...], wa_v[0, at])
            for n in range(1, 4):
                value = value + product_right(dz(n, at_b(b))[...], wa_v[n, at])
            part[b, :, at] = value.astype(jnp.bfloat16)

        tiles_of(width, body)

    second[1].begin()
    second[1].start(0)
    hidden_gradient(0)
    weight_part(0, a_v)
    second[1].start(1)
    second[1].hop(0)
    gather_a.step(0, 1)
    third = scatters_of(sums, False, {})
    early[0].finish()
    mixed_part(0)
    third[0].begin()
    third[0].start(0)
    second[1].start(2)
    second[1].hop(1)
    second[1].hop(2)
    third[0].start(1)
    third[0].hop(0)
    gather_a.step(0, 2)
    weight_part(1, a_v)
    hidden_gradient(1)
    third[0].start(2)
    third[0].hop(1)
    gather_a.step(0, 3)
    third[0].hop(2)
    early[1].finish()
    mixed_part(1)
    third[1].begin()
    third[1].start(0)
    for j in range(2):
        table[j] = turned_table(decay[4 * (2 * c + j) + z], length)
    for b in range(2):
        for d in range(8):
            arrived(scale.at[b], sc_sem.at[b, d])
        columns_of(inverse.at[at_b(b)], scale_in, b, rows)

    for j in range(2):
        arrived(pre.at[j], pre_sem.at[j])
        load_pre(0, j)
    gather_a.step(1, 1)
    third[1].start(1)
    third[1].hop(0)
    weight_part(2, b_v)
    gather_a.step(1, 2)
    third[1].start(2)
    third[1].hop(1)
    third[1].hop(2)
    attention_back(0)
    gather_a.step(1, 3)
    for b in range(2):
        third[b].receive()
        scatter = third[b]

        def result(i, carry):
            piece = aligned(i, 16, 16)
            at = aligned(b * (rows // 16) + i, 16, 16)
            out[at] = (h[at] + scatter.total(piece)).astype(jnp.bfloat16)
            return carry

        lax.fori_loop(0, rows // 16, result, 0)
    def sum_ff(n, result):
        for r in range(3):
            arrived(in_f.at[n, r], xy_f.at[n, r])
            local(in_f.at[n, r], b_v.at[pl.ds(r * ff, ff)], load.at[13 + r])
        for r in range(3):
            arrived(b_v.at[pl.ds(r * ff, ff)], load.at[13 + r])
        mine = w_v.at[aligned(4 * n + g, ff, 16)]

        def read(at):
            value = mine[at].astype(jnp.float32)
            for r in range(3):
                value = value + b_v.at[pl.ds(r * ff, ff)][at].astype(jnp.float32)
            return value

        def write(at, value):
            mine[at] = value.astype(jnp.bfloat16)

        pour(read, write, ff // 16)
        for d in (4, 3, 5, 2, 6, 1, 7, 0):
            to = (s + d) % 8
            src = mine.at[:, aligned(to, depth, 128)]
            dst = result.at[aligned(s, ff, 16)]
            if d:
                last.remote(src, dst, z_f.at[n, d], g, to)
            else:
                local(src, dst, z_f.at[n, d])

    def sum_third():
        for r in range(3):
            arrived(in_t.at[r], xy_t.at[r])
            local(in_t.at[r], b_v.at[pl.ds(0, hidden), pl.ds(r * wide, wide)], load.at[13 + r])
        for r in range(3):
            arrived(b_v.at[pl.ds(0, hidden), pl.ds(r * wide, wide)], load.at[13 + r])
        mine = w_v.at[pl.ds(2 * hidden, hidden), aligned(g, wide, 128)]

        def read(at):
            value = mine[at].astype(jnp.float32)
            for r in range(3):
                value = value + b_v[at, pl.ds(r * wide, wide)].astype(jnp.float32)
            return value

        def write(at, value):
            mine[at] = value.astype(jnp.bfloat16)

        pour(read, write, hidden // 16)
        for d in (2, 1, 3, 0):
            chip = (z + d) % 4
            to = 2 * chip + s // 4
            src = mine.at[aligned(chip, ff, 16)]
            dst = ft.at[aligned(s % 4, ff, 16)]
            if d:
                last.remote(src, dst, z_t.at[s % 4], g, to)
            else:
                last.remote(src, dst, z_t.at[s % 4], g, to, to != s)
                local(src, dst, z_t.at[s % 4], to == s)

    for b in range(2):
        sums[b].finish()
    fourth = scatters_of(early, True, {})
    first_part(0)
    fourth[0].begin()
    fourth[0].start(0)
    sum_ff(0, ff_)
    fourth[0].start(1)
    fourth[0].hop(0)
    attention_back(1)
    sum_ff(1, fs)
    first_part(1)
    fourth[1].begin()

    for b in range(2):
        local(n1_all.at[b], b_v.at[at_b(b)], load.at[2 + b])
    for b in range(2):
        arrived(b_v.at[at_b(b)], load.at[2 + b])
    half = width // 2
    for n in range(4):
        turn(turned, lambda t: dz(n, t)[...], tokens // 128, 2 * head)
        grad = grads_h.at[n]

        def body_h(at, i):
            place = pl.ds(pl.multiple_of((i % 2) * half + (i // 2) * 256, 256), 256)
            grad[:, place] = product(turned[pl.ds(0, 2 * head)], b_v[:, at]).astype(jnp.bfloat16)

        tiles_of(width, body_h)
        for r, o in enumerate(others + (g,)):
            holds = o // 2 == c
            for e in range(2):
                src = grad.at[aligned(o % 2, head, head), pl.ds(e * half, half)]
                dst = in_h.at[n, r]
                if r < 3:
                    last.remote(src, dst, xy_h.at[n, r], o, 2 * z + e, holds)
                else:
                    last.remote(src, dst, xy_h.at[n, r], g, 2 * z + e, jnp.logical_and(holds, c != e))
                    local(src, dst, xy_h.at[n, r], jnp.logical_and(holds, c == e))
        if n == 2:
            fourth[0].start(2)
            fourth[0].hop(1)
    turn(turned, lambda t: nat_v(t)[...], tokens // 128, 2 * head)

    def body_o(at, i):
        go_v[:, at] = product(turned[pl.ds(0, 2 * head)], a_v[:, at]).astype(jnp.bfloat16)

    tiles_of(width, body_o)
    for r, o in enumerate(others):
        last.remote(go_v.at[:, aligned(o, wide, 128)], in_o.at[r], xy_o.at[r], o, s)
    fourth[0].hop(2)
    fourth[1].start(0)
    fourth[1].start(1)
    fourth[1].hop(0)
    sum_third()
    fourth[1].start(2)
    fourth[1].hop(1)
    fourth[1].hop(2)
    for b in range(2):
        fourth[b].receive()
        scatter = fourth[b]

        def finish_x(i, carry):
            piece = aligned(i, 16, 16)
            at = aligned(b * (rows // 16) + i, 16, 16)
            v = x[b, piece].astype(jnp.float32)
            scale_x = lax.rsqrt(mean_square(v) + EPS)
            normed = v * scale_x
            grad = scatter.total(piece)
            along = jnp.mean(normed * grad, axis=-1, keepdims=True)
            grad_x[at] = grad_x[at] + scale_x * (grad - normed * along)
            return carry

        lax.fori_loop(0, rows // 16, finish_x, 0)

    for r in range(3):
        arrived(in_o.at[r], xy_o.at[r])
        local(in_o.at[r], b_v.at[pl.ds(0, 2 * head), pl.ds(r * wide, wide)], load.at[13 + r])

    def held(n, r):
        return a_v.at[pl.ds((2 * n + r // 2) * head, head), pl.ds((r % 2) * half, half)]

    for n in range(4):
        for r in range(4):
            arrived(in_h.at[n, r], xy_h.at[n, r])
            local(in_h.at[n, r], held(n, r), load.at[18 + 4 * n + r])
    for r in range(3):
        arrived(b_v.at[pl.ds(0, 2 * head), pl.ds(r * wide, wide)], load.at[13 + r])
    mine_o = go_v.at[:, aligned(g, wide, 128)]

    def read_o(at):
        value = mine_o[at].astype(jnp.float32)
        for r in range(3):
            value = value + b_v[at, pl.ds(r * wide, wide)].astype(jnp.float32)
        return value

    def write_o(at, value):
        mine_o[at] = value.astype(jnp.bfloat16)

    pour(read_o, write_o, 2 * head // 16)
    for j in range(2):
        to = 2 * (2 * c + j) + z // 2
        src = mine_o.at[pl.ds(j * head, head)]
        dst = fo.at[aligned(z % 2, head, head)]
        last.remote(src, dst, z_o.at[z % 2], g, to, to != s)
        local(src, dst, z_o.at[z % 2], to == s)
    for n, result in enumerate((fq, fk, fv, fu)):
        for r in range(4):
            arrived(held(n, r), load.at[18 + 4 * n + r])

        def read_h(at):
            value = held(n, 0)[at].astype(jnp.float32)
            for r in range(1, 4):
                value = value + held(n, r)[at].astype(jnp.float32)
            return value

        def write_h(at, value):
            held(n, 0)[at] = value.astype(jnp.bfloat16)

        pour(read_h, write_h, head // 16)
        for d in (2, 1, 3, 0):
            chip = (z + d) % 4
            src = held(n, 0).at[:, aligned(chip, depth, 128)]
            dst = result.at[aligned(z, head, head)]
            if d:
                last.remote(src, dst, z_h.at[n, d], g, 2 * chip + c)
            else:
                local(src, dst, z_h.at[n, d])

    for n, result in enumerate((ff_, fs)):
        for d in range(8):
            arrived(result.at[pl.ds(0, ff)], z_f.at[n, d])
    for d in range(4):
        arrived(ft.at[pl.ds(0, ff)], z_t.at[d])
    for j in range(2):
        arrived(fo.at[pl.ds(0, head)], z_o.at[j])
    for n, result in enumerate((fq, fk, fv, fu)):
        for d in range(4):
            arrived(result.at[pl.ds(0, head)], z_h.at[n, d])
    for b in range(2):
        early[b].finish()
    bulk.finish()
    last.finish()
    copies.finish()


def call(kernel, number, ins, outs, scratch, name):
    return pl.pallas_call(
        kernel,
        out_shape=[shape for shape, _ in outs],
        in_specs=[spec for _, spec in ins],
        out_specs=[spec for _, spec in outs],
        scratch_shapes=scratch,
        compiler_params=pltpu.CompilerParams(
            collective_id=number, has_side_effects=True, vmem_limit_bytes=64 * 2**20 - 2**17
        ),
        name=name,
    )(*[value for value, _ in ins])


def finish_arrays(count, turned_count, *refs):
    ins, outs, held, done = refs[:count], refs[count : 2 * count], refs[2 * count : 3 * count], refs[3 * count : 4 * count]
    in_sem, out_sem = refs[4 * count :]
    for i in range(count):
        local(ins[i], held[i], in_sem.at[i])
    for i in range(count):
        arrived(held[i], in_sem.at[i])
        if i < 2:
            local(held[i], outs[i], out_sem.at[i])
            continue
        if i < 2 + turned_count:
            done[i][...] = held[i][...].T.astype(jnp.float32)
        else:

            def write(at, value):
                done[i][at] = value

            pour(lambda at: held[i][at].astype(jnp.float32), write, held[i].shape[0] // 16)
        local(done[i], outs[i], out_sem.at[i])
    for i in range(count):
        arrived(outs[i], out_sem.at[i])


def finished(out, grad_x, turned, straight):
    arrays = [out, grad_x] + turned + straight
    shapes = [jax.ShapeDtypeStruct(v.shape, v.dtype) for v in (out, grad_x)]
    shapes += [wide_array(*v.shape[::-1]) for v in turned] + [wide_array(*v.shape) for v in straight]
    count = len(arrays)
    small = jax.ShapeDtypeStruct((8, 128), jnp.float32)
    done = [small, small] + shapes[2:]
    return pl.pallas_call(
        functools.partial(finish_arrays, count, len(turned)),
        out_shape=shapes,
        in_specs=[ANY] * count,
        out_specs=[ANY] * count,
        scratch_shapes=[pltpu.VMEM(v.shape, v.dtype) for v in arrays] + [pltpu.VMEM(v.shape, v.dtype) for v in done]
        + [dma(count), dma(count)],
        compiler_params=pltpu.CompilerParams(vmem_limit_bytes=62 * 2**20),
        name="finish_arrays",
    )(*arrays)


def low_array(*shape):
    return jax.ShapeDtypeStruct(shape, jnp.bfloat16)


def wide_array(*shape):
    return jax.ShapeDtypeStruct(shape, jnp.float32)


def dma(*shape):
    return pltpu.SemaphoreType.DMA(shape)


def scatter_scratch(rows, width):
    return [
        pltpu.VMEM((2, 4, rows, width), jnp.bfloat16),
        pltpu.VMEM((2, 2, 3, rows, width), jnp.bfloat16),
        dma(2, 4),
        dma(2, 2, 3),
    ]


def line_shards(
    tokens, cotangent, lengths, decay_rate,
    w_query, w_key, w_value, w_gate, w_out, w_first, w_second, w_third,
):
    bf16, f32 = jnp.bfloat16, jnp.float32
    rows, width = tokens.shape[2], tokens.shape[3]
    depth, wide = w_query.shape
    head = width // decay_rate.shape[0]
    hidden = w_third.shape[0]
    length = 8 * rows
    x_low = tokens[:, 0]
    in_smem = pl.BlockSpec(memory_space=pltpu.SMEM)
    gathered = low_array(2, length, width)
    out, grad_x, fq, fk, fv, fu, fo, ff, fs, ft = call(
        layer_part,
        0,
        [(lengths.T, in_smem), (decay_rate, in_smem), (x_low, VMEM), (cotangent[:, 0], VMEM)]
        + [(v, ANY) for v in (w_query, w_key, w_value, w_gate, w_out, w_first, w_second, w_third)],
        [(low_array(2 * rows, width), VMEM), (wide_array(2 * rows, width), VMEM)]
        + [(low_array(wide, depth), ANY)] * 4 + [(low_array(depth, wide), ANY)]
        + [(low_array(2 * hidden, depth), ANY)] * 2 + [(low_array(hidden, wide), ANY)]
        + [(gathered, ANY)] * 4
        + [(low_array(width, 2 * head), ANY)] * 4
        + [(low_array(2 * head, width), ANY)]
        + [(low_array(hidden, width), ANY)] * 3
        + [(wide_array(2, 2, 5, length, head), ANY)]
        + [(low_array(2, 3, hidden // 4, width), ANY), (low_array(3, hidden, wide), ANY), (low_array(3, 2 * head, wide), ANY),
           (low_array(4, 4, head, width // 2), ANY)],
        [dma(360), dma(40), dma(4, 2)] + [dma(2, 2, 3), dma(2, 7)] * 4
        + [dma(4, 4), dma(2), dma(3, 4), dma(4, 3, 4), dma(3), dma(3, 3, 4)]
        + [pltpu.VMEM((2, rows, width), bf16)] * 4
        + [pltpu.VMEM((2 * rows, width), f32),
           pltpu.VMEM((2 * length, width), bf16), pltpu.VMEM((2 * length, width), bf16), pltpu.VMEM((3 * hidden, width), bf16),
           pltpu.VMEM((4, width, 2 * head), bf16), pltpu.VMEM((2 * head, width), bf16),
           pltpu.VMEM((3, 2 * length, hidden), bf16), pltpu.VMEM((hidden, 2 * length), bf16),
           pltpu.VMEM((2, length, width), bf16)]
        + scatter_scratch(rows, width) + scatter_scratch(rows, width)
        + [pltpu.VMEM((2, length, length), f32), pltpu.VMEM((2, 8, 8, 128), f32), pltpu.VMEM((2, 8, 8, 128), f32),
           pltpu.VMEM((2, 8, 128), f32), pltpu.VMEM((2, 8, 8, 128), f32), dma(2, 8), dma(2, 8), pltpu.VMEM((2, 128, 128), f32),
           pltpu.VMEM((2, 8, 128), f32), pltpu.VMEM((2, 8, 8, 128), f32), dma(2, 8),
           pltpu.VMEM((2 * length, 128), f32), pltpu.VMEM((length, 128), f32),
           pltpu.VMEM((2, 5, length, head), f32), dma(2),
           pltpu.VMEM((2 * head, width), bf16), pltpu.VMEM((4, 2 * head, width), bf16),
           dma(2, 3), dma(3), dma(3), dma(4, 4), dma(2, 8), dma(4), dma(2), dma(4, 4)],
        "layer_part",
    )[:10]
    results = finished(out, grad_x, [fq, fk, fv, fu, ff, fs], [fo, ft])
    out, grad_x, fq, fk, fv, fu, ff, fs, fo, ft = results
    return (out.reshape(2, 1, rows, width), grad_x.reshape(2, 1, rows, width), fq, fk, fv, fu, fo, ff, fs, ft)


def solution(mesh):
    in_specs = (
        P(None, "grp", "seq", None),
        P(None, "grp", "seq", None),
        P(None, "grp"),
        P(),
        P("seq", "grp"),
        P("seq", "grp"),
        P("seq", "grp"),
        P("seq", "grp"),
        P("seq", "grp"),
        P("seq", "grp"),
        P("seq", "grp"),
        P("seq", "grp"),
    )
    out_specs = (
        P(None, "grp", "seq", None),
        P(None, "grp", "seq", None),
        P("seq", "grp"),
        P("seq", "grp"),
        P("seq", "grp"),
        P("seq", "grp"),
        P("seq", "grp"),
        P("seq", "grp"),
        P("seq", "grp"),
        P("seq", "grp"),
    )
    fast = mesh.shape["grp"] == 4 and mesh.shape["seq"] == 8
    return jax.shard_map(line_shards if fast else shards, mesh=mesh, in_specs=in_specs, out_specs=out_specs, check_vma=False)
```

```python
import functools

import jax
import jax.numpy as jnp
from jax import lax
from jax.experimental import pallas as pl
from jax.experimental.pallas import tpu as pltpu
from jax.sharding import PartitionSpec as P

EPS = 1e-06
HIGH = lax.Precision.HIGHEST
MESH = pl.DeviceIdType.MESH
ANY = pl.BlockSpec(memory_space=pl.ANY)
VMEM = pl.BlockSpec(memory_space=pltpu.VMEM)


def prefix(value, axis, join, neutral, backward):
    count, mine = (lax.axis_size(axis), lax.axis_index(axis))
    pieces = jax.tree.map(lambda part: lax.all_gather(part, axis), value)
    if backward:
        pieces = jax.tree.map(lambda part: part[::-1], pieces)
        mine = count - 1 - mine
    subtotal = jax.tree.map(
        lambda part, zero: jnp.full_like(part, 0) + jnp.asarray(zero, part.dtype), value, neutral
    )

    def step(position, subtotal):
        longer = join(subtotal, jax.tree.map(lambda part: part[position], pieces))
        return jax.tree.map(lambda new, old: jnp.where(position < mine, new, old), longer, subtotal)

    return lax.fori_loop(0, count - 1, step, subtotal)


def norm_rows(values):
    return values * lax.rsqrt(jnp.mean(values * values, axis=-1, keepdims=True) + EPS)


def norm_back(values, gradient):
    _, pull = jax.vjp(norm_rows, values)
    return pull(gradient)[0]


def silu_slope(values):
    sigma = jax.nn.sigmoid(values)
    return sigma * (1.0 + values * (1.0 - sigma))


def product(left, right):
    return jnp.dot(left, right, preferred_element_type=jnp.float32)


def product_left(left, right):
    return lax.dot_general(
        left, right, (((0,), (0,)), ((), ())), preferred_element_type=jnp.float32
    )


def product_right(left, right):
    return lax.dot_general(
        left, right, (((1,), (1,)), ((), ())), preferred_element_type=jnp.float32
    )


def combine_state(earlier, later):
    return (later[1][:, None, None] * earlier[0] + later[0], earlier[1] * later[1])


def shards(
    tokens,
    cotangent,
    lengths,
    decay_rate,
    w_query,
    w_key,
    w_value,
    w_gate,
    w_out,
    w_first,
    w_second,
    w_third,
):
    micro = tokens.shape[0]
    block_rows = tokens.shape[2]
    width = tokens.shape[3]
    heads = decay_rate.shape[0]
    head_dim = width // heads
    hidden_width = w_third.shape[0] * lax.axis_size("seq")
    places = jnp.arange(block_rows).astype(jnp.float32)
    slot_index = lax.axis_index("seq") * block_rows + jnp.arange(block_rows)
    offset = places[:, None] - places[None, :]
    weight = jnp.where(
        offset[None] >= 0, jnp.exp(-decay_rate[:, None, None] * jnp.maximum(offset, 0.0)[None]), 0.0
    )
    query_fac = jnp.exp(-decay_rate[None, :] * (places[:, None] + 1.0))[:, :, None]
    key_fac = jnp.exp(-decay_rate[None, :] * (block_rows - 1.0 - places[:, None]))[:, :, None]
    step_decay = jnp.exp(-decay_rate * block_rows)
    empty_state = jnp.zeros((heads, head_dim, head_dim), jnp.float32)
    unit_decay = jnp.ones((heads,), jnp.float32)
    partial_rows = (
        lax.all_gather(w_query, "grp", axis=1, tiled=True),
        lax.all_gather(w_key, "grp", axis=1, tiled=True),
        lax.all_gather(w_value, "grp", axis=1, tiled=True),
        lax.all_gather(w_gate, "grp", axis=1, tiled=True),
        lax.all_gather(w_out, "grp", axis=1, tiled=True),
        lax.all_gather(w_first, "grp", axis=1, tiled=True),
        lax.all_gather(w_second, "grp", axis=1, tiled=True),
        lax.all_gather(w_third, "grp", axis=1, tiled=True),
    )
    gathered = (
        lax.all_gather(partial_rows[0], "seq", axis=0, tiled=True),
        lax.all_gather(partial_rows[1], "seq", axis=0, tiled=True),
        lax.all_gather(partial_rows[2], "seq", axis=0, tiled=True),
        lax.all_gather(partial_rows[3], "seq", axis=0, tiled=True),
        lax.all_gather(partial_rows[4], "seq", axis=0, tiled=True),
        lax.all_gather(partial_rows[5], "seq", axis=0, tiled=True),
        lax.all_gather(partial_rows[6], "seq", axis=0, tiled=True),
        lax.all_gather(partial_rows[7], "seq", axis=0, tiled=True),
    )
    outputs = []
    input_grads = []
    first_norms = []
    attn_rows = []
    normed_rows = []
    branch_rows = []
    second_norms = []
    ffn_rows = []
    mixed_rows = []
    upstream_rows = []
    for batch_idx in range(micro):
        wq_full, wk_full, wv_full, wu_full, wo_full, first_full, second_full, third_full = gathered
        inputs = tokens[batch_idx, 0].astype(jnp.float32)
        live = (slot_index < lengths[batch_idx, 0]).astype(jnp.float32)[:, None]
        live_low = live.astype(jnp.bfloat16)
        first_norm = norm_rows(inputs).astype(jnp.bfloat16)
        query_pre = product(first_norm, wq_full)
        key_pre = product(first_norm, wk_full)
        value_pre = product(first_norm, wv_full)
        gate_pre = product(first_norm, wu_full)
        queries = jax.nn.silu(query_pre).astype(jnp.bfloat16).reshape(block_rows, heads, head_dim)
        key_heads = (jax.nn.silu(key_pre).astype(jnp.bfloat16) * live_low).reshape(
            block_rows, heads, head_dim
        )
        value_heads = (jax.nn.silu(value_pre).astype(jnp.bfloat16) * live_low).reshape(
            block_rows, heads, head_dim
        )
        query_wide = queries.astype(jnp.float32)
        key_wide = key_heads.astype(jnp.float32)
        value_wide = value_heads.astype(jnp.float32)
        local_state = jnp.einsum("jhd,jhe->hde", key_wide * key_fac, value_wide, precision=HIGH)
        prior_state, _ = prefix(
            (local_state, step_decay), "seq", combine_state, (empty_state, unit_decay), False
        )
        scores = (
            jnp.einsum("ihd,jhd->hij", queries, key_heads, preferred_element_type=jnp.float32)
            * weight
        )
        intra = jnp.einsum("hij,jhe->ihe", scores, value_wide, precision=HIGH)
        inter = jnp.einsum("ihd,hde->ihe", query_wide * query_fac, prior_state, precision=HIGH)
        attended = (intra + inter).reshape(block_rows, width)
        gate_act = jax.nn.silu(gate_pre)
        gated = gate_act * attended
        normed = norm_rows(gated).astype(jnp.bfloat16)
        hidden = inputs + product(normed, wo_full)
        second_norm = norm_rows(hidden).astype(jnp.bfloat16)
        first_proj = product(second_norm, first_full)
        second_proj = product(second_norm, second_full)
        mixed_in = (first_proj * second_proj).astype(jnp.bfloat16)
        result = hidden + product(mixed_in, third_full)
        outputs.append(result.astype(jnp.bfloat16))
        upstream = cotangent[batch_idx, 0].astype(jnp.float32) * live
        upstream_low = upstream.astype(jnp.bfloat16)
        grad_mixed = product_right(upstream_low, third_full)
        grad_first_proj = (grad_mixed * second_proj).astype(jnp.bfloat16)
        grad_second_proj = (grad_mixed * first_proj).astype(jnp.bfloat16)
        grad_norm_two = product_right(grad_first_proj, first_full) + product_right(
            grad_second_proj, second_full
        )
        grad_hidden = upstream + norm_back(hidden, grad_norm_two)
        grad_branch = grad_hidden.astype(jnp.bfloat16)
        grad_gated = norm_back(gated, product_right(grad_branch, wo_full))
        grad_attended = (grad_gated * gate_act).astype(jnp.bfloat16)
        grad_gate_pre = (grad_gated * attended * silu_slope(gate_pre)).astype(jnp.bfloat16)
        grad_heads = grad_attended.reshape(block_rows, heads, head_dim)
        grad_wide = grad_heads.astype(jnp.float32)
        local_grad = jnp.einsum("ihd,ihe->hde", query_wide * query_fac, grad_wide, precision=HIGH)
        later_grad, _ = prefix(
            (local_grad, step_decay), "seq", combine_state, (empty_state, unit_decay), True
        )
        grad_scores = (
            jnp.einsum("ihe,jhe->hij", grad_heads, value_heads, preferred_element_type=jnp.float32)
            * weight
        )
        grad_queries = jnp.einsum("hij,jhd->ihd", grad_scores, key_wide, precision=HIGH)
        grad_queries = (
            grad_queries
            + jnp.einsum("ihe,hde->ihd", grad_wide, prior_state, precision=HIGH) * query_fac
        )
        grad_keys = jnp.einsum("hij,ihd->jhd", grad_scores, query_wide, precision=HIGH)
        grad_keys = (
            grad_keys + jnp.einsum("hde,jhe->jhd", later_grad, value_wide, precision=HIGH) * key_fac
        )
        grad_values = jnp.einsum("hij,ihe->jhe", scores, grad_wide, precision=HIGH)
        grad_values = (
            grad_values + jnp.einsum("jhd,hde->jhe", key_wide, later_grad, precision=HIGH) * key_fac
        )
        grad_query_pre = (grad_queries.reshape(block_rows, width) * silu_slope(query_pre)).astype(
            jnp.bfloat16
        )
        grad_key_pre = (grad_keys.reshape(block_rows, width) * live * silu_slope(key_pre)).astype(
            jnp.bfloat16
        )
        grad_value_pre = (
            grad_values.reshape(block_rows, width) * live * silu_slope(value_pre)
        ).astype(jnp.bfloat16)
        grad_norm_one = product_right(grad_query_pre, wq_full) + product_right(
            grad_key_pre, wk_full
        )
        grad_norm_one = (
            grad_norm_one
            + product_right(grad_value_pre, wv_full)
            + product_right(grad_gate_pre, wu_full)
        )
        input_grads.append(grad_hidden + norm_back(inputs, grad_norm_one))
        first_norms.append(first_norm)
        attn_rows.append(
            jnp.concatenate([grad_query_pre, grad_key_pre, grad_value_pre, grad_gate_pre], axis=1)
        )
        normed_rows.append(normed)
        branch_rows.append(grad_branch)
        second_norms.append(second_norm)
        ffn_rows.append(jnp.concatenate([grad_first_proj, grad_second_proj], axis=1))
        mixed_rows.append(mixed_in)
        upstream_rows.append(upstream_low)
    first_all = jnp.concatenate(first_norms, axis=0)
    attn_all = jnp.concatenate(attn_rows, axis=0)
    normed_all = jnp.concatenate(normed_rows, axis=0)
    branch_all = jnp.concatenate(branch_rows, axis=0)
    second_all = jnp.concatenate(second_norms, axis=0)
    ffn_all = jnp.concatenate(ffn_rows, axis=0)
    mixed_all = jnp.concatenate(mixed_rows, axis=0)
    upstream_all = jnp.concatenate(upstream_rows, axis=0)
    proj_rows = lax.psum_scatter(
        product_left(first_all, attn_all), "seq", scatter_dimension=0, tiled=True
    )
    outproj_rows = lax.psum_scatter(
        product_left(normed_all, branch_all), "seq", scatter_dimension=0, tiled=True
    )
    ffn_part = lax.psum_scatter(
        product_left(second_all, ffn_all), "seq", scatter_dimension=0, tiled=True
    )
    down_rows = lax.psum_scatter(
        product_left(mixed_all, upstream_all), "seq", scatter_dimension=0, tiled=True
    )
    summed = (
        lax.psum_scatter(proj_rows[:, :width], "grp", scatter_dimension=1, tiled=True),
        lax.psum_scatter(proj_rows[:, width : 2 * width], "grp", scatter_dimension=1, tiled=True),
        lax.psum_scatter(
            proj_rows[:, 2 * width : 3 * width], "grp", scatter_dimension=1, tiled=True
        ),
        lax.psum_scatter(proj_rows[:, 3 * width :], "grp", scatter_dimension=1, tiled=True),
        lax.psum_scatter(outproj_rows, "grp", scatter_dimension=1, tiled=True),
        lax.psum_scatter(ffn_part[:, :hidden_width], "grp", scatter_dimension=1, tiled=True),
        lax.psum_scatter(ffn_part[:, hidden_width:], "grp", scatter_dimension=1, tiled=True),
        lax.psum_scatter(down_rows, "grp", scatter_dimension=1, tiled=True),
    )
    layer_out = jnp.stack(outputs)[:, None]
    grad_tokens = jnp.stack(input_grads)[:, None]
    return (
        layer_out,
        grad_tokens,
        summed[0],
        summed[1],
        summed[2],
        summed[3],
        summed[4],
        summed[5],
        summed[6],
        summed[7],
    )


class Spare:
    def __init__(self, sems):
        self.sems, self.free = sems, list(range(sems.shape[0]))


class Copies:
    def __init__(self, spare):
        self.spare = spare
        self.pending = []

    def remote(self, src, dst, recv_sem, group, place, when=None):
        number = self.spare.free.pop(0)
        copy = pltpu.make_async_remote_copy(
            src_ref=src,
            dst_ref=dst,
            send_sem=self.spare.sems.at[number],
            recv_sem=recv_sem,
            device_id=(group, place),
            device_id_type=MESH,
        )
        self.pending.append((copy, when, number))
        if when is None:
            copy.start()
        else:
            pl.when(when)(copy.start)
        return self.pending[-1]

    def settle(self, entry):
        if not any(other is entry for other in self.pending):
            return
        self.pending = [other for other in self.pending if other is not entry]
        copy, when, number = entry
        if when is None:
            copy.wait_send()
        else:
            pl.when(when)(copy.wait_send)
        self.spare.free.append(number)

    def finish(self):
        while self.pending:
            self.settle(self.pending[0])


def local(src, dst, sem, when=None):
    copy = pltpu.make_async_copy(src, dst, sem)
    if when is None:
        copy.start()
    else:
        pl.when(when)(copy.start)


def arrived(ref, sem, when=None):
    copy = pltpu.make_async_copy(ref, ref, sem)
    if when is None:
        copy.wait()
    else:
        pl.when(when)(copy.wait)


def where_am_i():
    g, s = lax.axis_index("grp"), lax.axis_index("seq")
    return g, s, g // 2, g % 2, s // 2, s % 2


def across(y, x):
    return (y * 2 + 1 - x, (1 - y) * 2 + x, (1 - y) * 2 + 1 - x)


def greet(partners):
    barrier = pltpu.get_barrier_semaphore()
    for partner in partners:
        pl.semaphore_signal(barrier, inc=1, device_id=partner, device_id_type=MESH)
    pl.semaphore_wait(barrier, len(partners))


def aligned(index, unit, step):
    return pl.ds(pl.multiple_of(index * unit, step), unit)


class Gather:
    def __init__(self, copies, out, rows, hop_sem, side_sem):
        self.copies, self.out, self.rows = copies, out, rows
        self.hop_sem, self.side_sem = hop_sem, side_sem
        self.g, self.s, _, _, self.z, self.c = where_am_i()

    def block(self, b, z, core):
        return self.out.at[b, aligned(2 * z + core, self.rows, 16)]

    def spread(self, src, b, z_of, k, right, left):
        g, s, z, c = self.g, self.s, self.z, self.c
        dst = self.block(b, z_of, c)
        if right is not None:
            self.copies.remote(src, dst, self.hop_sem.at[b, 0, k], g, (s + 2) % 8, right)
        if left is not None:
            self.copies.remote(src, dst, self.hop_sem.at[b, 1, k], g, (s + 6) % 8, left)

    def begin(self, src, own_sem, b):
        g, s, z, c = self.g, self.s, self.z, self.c
        self.spread(src, b, z, 0, z < 3, z > 0)
        self.copies.remote(src, self.block(b, z, c), self.side_sem.at[b, 0], g, s + 1 - 2 * c)
        local(src, self.block(b, z, c), own_sem)

    def step(self, b, k):
        g, s, z, c = self.g, self.s, self.z, self.c
        side = s + 1 - 2 * c
        has = z >= k
        at = jnp.maximum(z - k, 0)
        ref = self.block(b, at, c)
        arrived(ref, self.hop_sem.at[b, 0, k - 1], has)
        if k < 3:
            self.spread(ref, b, at, k, jnp.logical_and(has, z < 3), None)
        self.copies.remote(ref, ref, self.side_sem.at[b, k], g, side, has)
        has = z + k <= 3
        at = jnp.minimum(z + k, 3)
        ref = self.block(b, at, c)
        arrived(ref, self.hop_sem.at[b, 1, k - 1], has)
        if k < 3:
            self.spread(ref, b, at, k, None, jnp.logical_and(has, z > 0))
        self.copies.remote(ref, ref, self.side_sem.at[b, 3 + k], g, side, has)

    def finish(self, own_sem, b):
        z, c = self.z, self.c
        arrived(self.block(b, z, c), own_sem)
        arrived(self.block(b, z, 1 - c), self.side_sem.at[b, 0])
        for k in (1, 2, 3):
            arrived(self.block(b, jnp.maximum(z - k, 0), 1 - c), self.side_sem.at[b, k], z >= k)
            arrived(self.block(b, jnp.minimum(z + k, 3), 1 - c), self.side_sem.at[b, 3 + k], z + k <= 3)


def line_partners(g, s):
    return [(g, (s + d) % 8) for d in range(1, 8)]


def everyone_on_line(copies, src, dst, sem, g, s, to_rows):
    for d in range(1, 8):
        to = (s + d) % 8
        copies.remote(to_rows(to), dst.at[s], sem.at[d - 1], g, to)


def mean_square(values):
    return jnp.mean(values * values, axis=-1, keepdims=True)


def pour(read, write, count):
    def piece(i, carry):
        at = aligned(i, 16, 16)
        write(at, read(at))
        return carry

    lax.fori_loop(0, count, piece, 0)


class LineScatter:
    def __init__(self, copies, part, rows, side, inbox, side_sem, line_sem, queue):
        self.copies, self.part, self.rows, self.queue = copies, part, rows, queue
        self.side, self.inbox, self.side_sem, self.line_sem = side, inbox, side_sem, line_sem
        self.g, self.s, _, _, self.z, self.c = where_am_i()

    def mine(self, chip):
        return self.part.at[aligned(2 * chip + self.c, self.rows, 16)]

    def begin(self):
        for chip in (3, 0, 2, 1):
            theirs = aligned(2 * chip + 1 - self.c, self.rows, 16)
            self.copies.remote(
                self.part.at[theirs], self.side.at[chip], self.side_sem.at[chip], self.g, self.s + 1 - 2 * self.c
            )

    def add_on(self, chip, way):
        own, side = self.mine(chip), self.side.at[chip]
        slot = chip - 1 if way == 0 else chip
        come = self.inbox.at[way, slot]
        arrived(side, self.side_sem.at[chip])
        arrived(come, self.line_sem.at[way, slot])

        def three(at):
            return own[at].astype(jnp.float32) + side[at].astype(jnp.float32) + come[at].astype(jnp.float32)

        def write(at, value):
            own[at] = value.astype(jnp.bfloat16)

        pour(three, write, self.rows // 16)

    def push(self, chip, way, when):
        slot = chip - 1 if way == 0 else chip
        to = (self.s + 2) % 8 if way == 0 else (self.s + 6) % 8
        return self.copies.remote(
            self.mine(chip), self.inbox.at[way, slot], self.line_sem.at[way, slot], self.g, to, when
        )

    def pass_on(self, chip, way):
        end = self.z == (0 if way == 0 else 3)
        own, side = self.mine(chip), self.side.at[chip]

        def two(at):
            return own[at].astype(jnp.float32) + side[at].astype(jnp.float32)

        def write(at, value):
            own[at] = value.astype(jnp.bfloat16)

        @pl.when(end)
        def _():
            arrived(side, self.side_sem.at[chip])
            pour(two, write, self.rows // 16)

        if way in self.queue:
            copies, entry = self.queue.pop(way)
            copies.settle(entry)
        self.queue[way] = (self.copies, self.push(chip, way, end))

    def start(self, i):
        self.pass_on(3 - i, 0)
        self.pass_on(i, 1)

    def hop(self, i):
        z = self.z
        for inner in (1, 2):

            @pl.when(z == inner)
            def _():
                near = inner == 1
                if i < 2:
                    self.add_on(3 - i if near else i, 0 if near else 1)
                else:
                    self.add_on(0 if near else 3, 1 if near else 0)

        for inner in (1, 2):
            near = inner == 1
            if i < 2:
                self.push(3 - i if near else i, 0 if near else 1, z == inner)
            else:
                self.push(0 if near else 3, 1 if near else 0, z == inner)

    def receive(self):
        z = self.z
        arrived(self.side.at[z], self.side_sem.at[z])
        left, right = jnp.maximum(z - 1, 0), jnp.minimum(z, 2)
        arrived(self.inbox.at[0, left], self.line_sem.at[0, left], z > 0)
        arrived(self.inbox.at[1, right], self.line_sem.at[1, right], z < 3)

    def total(self, at):
        z = self.z
        value = self.mine(z)[at].astype(jnp.float32) + self.side[z, at].astype(jnp.float32)
        from_left = self.inbox[0, jnp.maximum(z - 1, 0), at].astype(jnp.float32)
        from_right = self.inbox[1, jnp.minimum(z, 2), at].astype(jnp.float32)
        return value + jnp.where(z > 0, from_left, 0.0) + jnp.where(z < 3, from_right, 0.0)


def silu(values):
    return values / (1.0 + jnp.exp(-values))


def decay_table(rate, length):
    offset = lax.broadcasted_iota(jnp.int32, (length, length), 0) - lax.broadcasted_iota(jnp.int32, (length, length), 1)
    steps = jnp.maximum(offset, 0).astype(jnp.float32)
    return jnp.where(offset >= 0, jnp.exp(-rate * steps), 0.0)


def live_rows(first, count, length):
    return ((first + lax.broadcasted_iota(jnp.int32, (count, 1), 0)) < length).astype(jnp.float32)


def slope(values):
    sigma = 1.0 / (1.0 + jnp.exp(-values))
    return sigma * (1.0 + values * (1.0 - sigma))


def turned_table(rate, length):
    offset = lax.broadcasted_iota(jnp.int32, (length, length), 1) - lax.broadcasted_iota(jnp.int32, (length, length), 0)
    steps = jnp.maximum(offset, 0).astype(jnp.float32)
    return jnp.where(offset >= 0, jnp.exp(-rate * steps), 0.0)


def columns_of(out, tiles, b, rows):
    for owner in range(8):
        out[pl.ds(owner * rows, rows)] = jnp.broadcast_to(tiles[b, owner, :1], (128, 128)).T[:rows]


def turn(dst, read, count, columns):
    def block(i, carry):
        dst[pl.ds(0, columns), aligned(i, 128, 128)] = read(aligned(i, 128, 128)).T
        return carry

    lax.fori_loop(0, count, block, 0)


def tiles_of(width, body):
    def tile(i, carry):
        body(aligned(i, 256, 256), i)
        return carry

    lax.fori_loop(0, width // 256, tile, 0)


def layer_part(
    lengths, decay, x, cot, wq, wk, wv, wu, wo, w1, w2, w3,
    out, grad_x, fq, fk, fv, fu, fo, ff_, fs, ft,
    n1_all, dm_all, n2_all, da_all, q_all, k_all, v_all, u_all, o_all, f_all, s_all, t_all, pre_all, in_f, in_t, in_o, in_h, x_f, y_f,
    send, load, own, hop_n, side_n, hop_d, side_d, hop_m, side_m_, hop_a, side_a, z_head, z_out, z_ff, xy_head, xy_out, xy_ff, spread_f, join_f,
    n1, dm, n2, da, h, a_v, b_v, w_v, wa_v, wo_v, p_v, turned, part, side, inbox, side_sem, line_sem,
    side_m, inbox_m, side_sem_m, line_sem_m, table, squares, inbox_sq, scale, scale_in, sq_sem, sc_sem, column,
    mix, mix_in, mix_sem, inverse, mixed, pre, pre_sem, go_v, grads_h,
    xy_f, xy_t, xy_o, xy_h, z_f, z_t, z_o, z_h,
):
    g, s, y, x_, z, c = where_am_i()
    others = across(y, x_)
    plane = [(o, 2 * z + e) for o in others for e in range(2)]
    rows, width = x.shape[1], x.shape[2]
    length = 8 * rows
    tokens = 2 * length
    depth, wide = wq.shape
    head = q_all.shape[1] // 2
    hidden = f_all.shape[0]
    quarter = hidden // 2
    half = length // 2
    target = g // 2
    mine = aligned(g % 2, head, head)
    here = c == target
    order = [(z + d) % 4 for d in (0, 1, 3, 2)]
    spare = Spare(send)
    copies, turned_out, bulk, last = [Copies(spare) for _ in range(4)]
    early, sums = [[Copies(spare) for _ in range(2)] for _ in range(2)]
    gather_n = Gather(copies, n1_all, rows, hop_n, side_n)
    gather_d = Gather(copies, dm_all, rows, hop_d, side_d)
    gather_m = Gather(copies, n2_all, rows, hop_m, side_m_)
    gather_a = Gather(last, da_all, rows, hop_a, side_a)
    heads = list(zip((wq, wk, wv, wu), (q_all, k_all, v_all, u_all)))
    w1_f, w2_f, w3_f = [w_v.at[pl.ds(n * hidden, hidden)] for n in range(3)]
    w1_in, w2_in = [w_v.at[pl.ds(n * depth, depth), pl.ds(512, 2 * hidden)] for n in range(2)]
    w1_t, w2_t = [w_v.at[pl.ds(0, 2 * hidden), pl.ds(n * depth, depth)] for n in range(2)]
    low_v = p_v.at[2, pl.ds(0, length), pl.ds(0, 2 * head)]

    def at_b(b):
        return pl.ds(b * length, length)

    def dz(n, at):
        return p_v.at[n // 2, at, pl.ds((n % 2) * 2 * head, 2 * head)]

    def nat_v(at):
        return p_v.at[2, at, pl.ds(0, 2 * head)]

    local(w1, w1_in, load.at[0])
    local(w2, w2_in, load.at[1])
    greet(line_partners(g, s) + plane)

    def send_heads(n):
        src, dst = heads[n]
        for d in (2, 1, 3, 0):
            to = (z + d) % 4
            a, b = src.at[:, aligned(to, head, head)], dst.at[aligned(s, depth, 16), mine]
            if d:
                copies.remote(a, b, z_head.at[n, z], g, 2 * to + target)
            else:
                copies.remote(a, b, z_head.at[n, z], g, 2 * to + target, c != target)
                local(a, b, z_head.at[n, z], here)

    def pass_heads(n):
        dst = heads[n][1]
        for zs in order:
            block = dst.at[aligned(zs, 2 * depth, 16), mine]
            arrived(block, z_head.at[n, zs], here)
            for r, o in enumerate(others[:2]):
                copies.remote(block, block, xy_head.at[n, r, zs], o, s, here)

    def relay_heads(n):
        dst = heads[n][1]
        for zs in order:
            for r, when in ((0, here), (1, jnp.logical_not(here))):
                lanes = aligned(others[r] % 2, head, head)
                arrived(dst.at[aligned(zs, 2 * depth, 16), lanes], xy_head.at[n, r, zs], when)
                part_ = dst.at[aligned(2 * zs + r, depth, 16), lanes]
                copies.remote(part_, part_, xy_head.at[n, 2, zs], others[1 - r], s, when)

    def send_out():
        for i in range(2):
            to = 2 * c + i
            a = wo.at[pl.ds(i * head, head)]
            b = o_all.at[aligned(z % 2, head, head), aligned(g, wide, 128)]
            self_ = jnp.logical_and(to == z, c == z // 2)
            copies.remote(a, b, z_out.at[z % 2], g, 2 * to + z // 2, jnp.logical_not(self_))
            local(a, b, z_out.at[z % 2], self_)

    def pass_out():
        for j in range(2):
            arrived(o_all.at[pl.ds(j * head, head), aligned(g, wide, 128)], z_out.at[j])
        block = o_all.at[:, aligned(g, wide, 128)]
        for r, o in enumerate(others[:2]):
            copies.remote(block, block, xy_out.at[r], o, s)

    def relay_out():
        for r in range(2):
            lanes = aligned(others[r], wide, 128)
            arrived(o_all.at[:, lanes], xy_out.at[r])
            part_ = o_all.at[pl.ds(r * head, head), lanes]
            copies.remote(part_, part_, xy_out.at[2], others[1 - r], s)

    def spread_ff():
        for n, src in enumerate((w1_t, w2_t)):
            for r, o in enumerate(others):
                turned_out.remote(src.at[aligned(o, quarter, 16)], x_f.at[n, g], spread_f.at[n, r], o, s)
            local(src.at[aligned(g, quarter, 16)], x_f.at[n, g], spread_f.at[n, 3])

    def ff_block(n, group, zs):
        return (f_all, s_all)[n].at[aligned(group % 2, quarter, 16), aligned(zs, 2 * depth, 128)]

    def send_ff(n):
        for r, o in enumerate(others):
            arrived(x_f.at[n, o], spread_f.at[n, r])
        arrived(x_f.at[n, g], spread_f.at[n, 3])
        b = (f_all, s_all)[n].at[aligned(g % 2, quarter, 16), aligned(s, depth, 128)]
        for d in (2, 1, 3, 0):
            to = (z + d) % 4
            a = x_f.at[n, to]
            if d:
                copies.remote(a, b, z_ff.at[n, z], g, 2 * to + target)
            else:
                copies.remote(a, b, z_ff.at[n, z], g, 2 * to + target, c != target)
                local(a, b, z_ff.at[n, z], here)

    def pass_ff(n):
        for zs in order:
            block = ff_block(n, g, zs)
            arrived(block, z_ff.at[n, zs], here)
            for r, o in enumerate(others[:2]):
                copies.remote(block, block, xy_ff.at[n, r, zs], o, s, here)

    def relay_ff(n):
        for zs in order:
            for r, when in ((0, here), (1, jnp.logical_not(here))):
                arrived(ff_block(n, others[r], zs), xy_ff.at[n, r, zs], when)
                part_ = (f_all, s_all)[n].at[aligned(others[r] % 2, quarter, 16), aligned(2 * zs + r, depth, 128)]
                copies.remote(part_, part_, xy_ff.at[n, 2, zs], others[1 - r], s, when)

    def send_third():
        block = t_all.at[:, aligned(g, wide, 128)]
        for r, o in enumerate(others[:2]):
            copies.remote(w3, block, xy_ff.at[2, r, 0], o, s)
        local(w3, block, z_ff.at[2, 0])

    def relay_third():
        for r in range(2):
            lanes = aligned(others[r], wide, 128)
            arrived(t_all.at[:, lanes], xy_ff.at[2, r, 0])
            part_ = t_all.at[pl.ds(r * quarter, quarter), lanes]
            copies.remote(part_, part_, xy_ff.at[2, 2, 0], others[1 - r], s)

    send_heads(0)
    send_heads(1)
    for b in range(2):

        def norm(at):
            v = x[b, at].astype(jnp.float32)
            return v * lax.rsqrt(mean_square(v) + EPS)

        def keep(at, value):
            n1[b, at] = value.astype(jnp.bfloat16)

        pour(norm, keep, rows // 16)
        first = s * rows

        def masked(i, carry):
            at = aligned(i, 16, 16)
            live = live_rows(first + i * 16, 16, lengths[0, b])
            dm[b, at] = (cot[b, at].astype(jnp.float32) * live).astype(jnp.bfloat16)
            return carry

        lax.fori_loop(0, rows // 16, masked, 0)
    for n, (src, dst) in enumerate(((w1_in, w1_t), (w2_in, w2_t))):
        arrived(src, load.at[n])
        dst[...] = src[...].T
    spread_ff()
    pass_heads(0)
    send_heads(2)
    pass_heads(1)
    send_heads(3)
    for b in range(2):
        gather_n.begin(n1.at[b], own.at[0, b], b)
    pass_heads(2)
    relay_heads(0)
    pass_heads(3)
    send_out()
    relay_heads(1)
    gather_n.step(0, 1)
    gather_n.step(1, 1)
    pass_out()
    relay_heads(2)
    gather_n.step(0, 2)
    gather_n.step(1, 2)
    relay_heads(3)
    relay_out()
    gather_n.step(0, 3)
    gather_n.step(1, 3)
    send_ff(0)
    send_ff(1)
    send_third()
    over = others[2]
    for n, (_, dst) in enumerate(heads):
        for zs in range(4):
            block = dst.at[pl.ds(zs * 2 * depth, 2 * depth), aligned(over % 2, head, head)]
            arrived(block, xy_head.at[n, 2, zs], over // 2 == c)
    arrived(o_all.at[:, aligned(over, wide, 128)], xy_out.at[2])
    for n, (_, dst) in enumerate(heads):
        local(dst, wa_v.at[n], load.at[n])
    local(o_all, wo_v, load.at[4])
    for b in range(2):
        gather_n.finish(own.at[0, b], b)
        local(n1_all.at[b], a_v.at[at_b(b)], load.at[5 + b])
    for j in range(2):
        table[j] = decay_table(decay[4 * (2 * c + j) + z], length)
    for n in range(4):
        arrived(wa_v.at[n], load.at[n])
    arrived(wo_v, load.at[4])

    def scatters_of(copies, first, queue):
        kept = (side, inbox, side_sem, line_sem) if first else (side_m, inbox_m, side_sem_m, line_sem_m)
        return [LineScatter(copies[b], part.at[b], rows, *[k.at[b] for k in kept], queue) for b in range(2)]

    scatters = scatters_of(early, True, {})
    for b in range(2):
        arrived(a_v.at[at_b(b)], load.at[5 + b])
        if b == 1:
            for j in range(2):
                arrived(pre.at[j], pre_sem.at[j])

        def project(i, carry):
            at = aligned(i, half, 16)
            from_ = aligned(2 * b + i, half, 16)
            for n in range(4):
                value = product(a_v[from_], wa_v[n])
                for j in range(2):
                    pre[j, n, at] = value[:, j * head : (j + 1) * head]
            return carry

        lax.fori_loop(0, 2, project, 0)
        if b == 1:
            scatters[0].start(1)
        live = live_rows(0, length, lengths[0, b])
        square = 0.0
        for j in range(2):
            q = silu(pre[j, 0]).astype(jnp.bfloat16)
            k = (silu(pre[j, 1]) * live).astype(jnp.bfloat16)
            v = (silu(pre[j, 2]) * live).astype(jnp.bfloat16)
            scores = (product_right(q, k) * table[j]).astype(jnp.bfloat16)
            attended = product(scores, v)
            pre[j, 4] = attended
            gated = silu(pre[j, 3]) * attended
            square = square + jnp.sum(gated * gated, axis=-1, keepdims=True)
            low_v[:, pl.ds(j * head, head)] = gated.astype(jnp.bfloat16)
            local(pre.at[j], pre_all.at[b, j], pre_sem.at[j])
        row = jnp.broadcast_to(square, (length, 128)).T[:8]
        for to in range(8):
            squares[b, to, :, :rows] = row[:, to * rows : (to + 1) * rows]
        everyone_on_line(copies, squares, inbox_sq.at[b], sq_sem.at[b], g, s, lambda to: squares.at[b, to])
        local(squares.at[b, s], inbox_sq.at[b, s], sq_sem.at[b, 7])

        def out_part(i, carry):
            at = aligned(i, 256, 256)
            part[b, :, at] = product(low_v[...], wo_v[:, at]).astype(jnp.bfloat16)
            return carry

        lax.fori_loop(0, width // 256, out_part, 0)
        scatters[b].begin()
        if b == 0:
            scatters[0].start(0)

    def hidden_state(b):
        for d in range(8):
            arrived(inbox_sq.at[b, 0], sq_sem.at[b, d])
        total = inbox_sq[b, 0]
        for d in range(1, 8):
            total = total + inbox_sq[b, d]
        row = lax.rsqrt(total / width + EPS)
        scale[b] = row
        column[b] = jnp.broadcast_to(row[:1], (128, 128)).T
        scatter = scatters[b]
        scatter.receive()

        def finish(i, carry):
            piece = aligned(i, 16, 16)
            at = aligned(b * (rows // 16) + i, 16, 16)
            a = scatter.total(piece) * column[b, piece, :1]
            value = x[b, piece].astype(jnp.float32) + a
            h[at] = value
            n2[b, piece] = (value * lax.rsqrt(mean_square(value) + EPS)).astype(jnp.bfloat16)
            return carry

        lax.fori_loop(0, rows // 16, finish, 0)
        gather_m.begin(n2.at[b], own.at[2, b], b)

    gather_d.begin(dm.at[0], own.at[1, 0], 0)
    scatters[0].hop(0)
    relay_third()
    scatters[0].start(2)
    scatters[0].hop(1)
    pass_ff(0)
    scatters[1].start(0)
    scatters[0].hop(2)
    pass_ff(1)
    gather_d.step(0, 1)
    hidden_state(0)
    scatters[1].start(1)
    scatters[1].hop(0)
    relay_ff(0)
    gather_d.step(0, 2)
    scatters[1].start(2)
    scatters[1].hop(1)
    gather_m.step(0, 1)
    scatters[1].hop(2)
    gather_d.step(0, 3)
    gather_m.step(0, 2)
    gather_d.begin(dm.at[1], own.at[1, 1], 1)
    hidden_state(1)
    gather_m.step(0, 3)
    relay_ff(1)
    gather_d.finish(own.at[1, 0], 0)
    local(dm_all.at[0], b_v.at[at_b(0)], load.at[2])
    gather_m.finish(own.at[2, 0], 0)
    local(n2_all.at[0], a_v.at[at_b(0)], load.at[0])
    gather_d.step(1, 1)
    gather_m.step(1, 1)
    turned_out.finish()
    for n, (dst, room) in enumerate(((f_all, w1_f), (s_all, w2_f), (t_all, w3_f))):
        if n < 2:
            for zs in range(4):
                arrived(ff_block(n, over, zs), xy_ff.at[n, 2, zs], over // 2 == c)
        else:
            arrived(dst.at[:, aligned(over, wide, 128)], xy_ff.at[2, 2, 0])
        if n == 2:
            arrived(dst.at[:, aligned(g, wide, 128)], z_ff.at[2, 0])
        local(dst, room, load.at[4 + n])
    for b in range(2):
        early[b].finish()

    def feed_forward(b):
        def tile(i, carry):
            at = aligned(b * 2 + i, half, 16)
            first = product_right(a_v[at], w1_f[...])
            second = product_right(a_v[at], w2_f[...])
            back = product_right(b_v[at], w3_f[...])
            p_v[0, at] = (back * second).astype(jnp.bfloat16)
            p_v[1, at] = (back * first).astype(jnp.bfloat16)
            p_v[2, at] = (first * second).astype(jnp.bfloat16)
            return carry

        lax.fori_loop(0, 2, tile, 0)

    def norm_part(b):
        def body(at, i):
            value = product(p_v[0, at_b(b)], w1_f[:, at]) + product(p_v[1, at_b(b)], w2_f[:, at])
            part[b, :, at] = value.astype(jnp.bfloat16)

        tiles_of(width, body)

    def mixed_part(b):
        def body(at, i):
            part[b, :, at] = product(p_v[2, at_b(b)], w3_f[:, at]).astype(jnp.bfloat16)

        tiles_of(width, body)

    half_w = width // 2
    sent_f = [[], []]

    def spread_place(i):
        return pl.ds(pl.multiple_of((i % 2) * half_w + (i // 2) * 256, 256), 256)

    def to_groups(copies, block, inbox_ref, sem):
        entries = []
        for r, o in enumerate(others + (g,)):
            holds = o // 2 == c
            for e in range(2):
                src = block(o).at[:, pl.ds(e * half_w, half_w)]
                if r < 3:
                    entries.append(copies.remote(src, inbox_ref.at[r], sem.at[r], o, 2 * z + e, holds))
                else:
                    entries.append(copies.remote(src, inbox_ref.at[r], sem.at[r], g, 2 * z + e, jnp.logical_and(holds, c != e)))
                    local(src, inbox_ref.at[r], sem.at[r], jnp.logical_and(holds, c == e))
        return entries

    def weight_part(n, operand):
        turn(turned, lambda t: p_v[n, t], tokens // 128, hidden)

        def body(at, i):
            place = spread_place(i) if n < 2 else at
            w_v[pl.ds(n * hidden, hidden), place] = product(turned[...], operand[:, at]).astype(jnp.bfloat16)

        tiles_of(width, body)
        if n < 2:
            sent_f[n] = to_groups(bulk, lambda o: w_v.at[aligned(2 * n + o % 2, quarter, 16)], in_f.at[n], xy_f.at[n])
        else:
            for r, o in enumerate(others):
                bulk.remote(w_v.at[pl.ds(n * hidden, hidden), aligned(o, wide, 128)], in_t.at[r], xy_t.at[r], o, s)

    def hidden_gradient(b):
        scatter = second[b]
        scatter.receive()

        def finish(i, carry):
            piece = aligned(i, 16, 16)
            at = aligned(b * (rows // 16) + i, 16, 16)
            value = h[at]
            scale_h = lax.rsqrt(mean_square(value) + EPS)
            normed = value * scale_h
            grad = scatter.total(piece)
            along = jnp.mean(normed * grad, axis=-1, keepdims=True)
            live = live_rows(s * rows + i * 16, 16, lengths[0, b])
            upstream = cot[b, piece].astype(jnp.float32) * live
            grad_hidden = upstream + scale_h * (grad - normed * along)
            grad_x[at] = grad_hidden
            low = grad_hidden.astype(jnp.bfloat16)
            da[b, piece] = low
            dot = jnp.mean(low.astype(jnp.float32) * (value - x[b, piece].astype(jnp.float32)), axis=-1, keepdims=True)
            column[b, piece] = jnp.broadcast_to(dot, (16, 128))
            return carry

        lax.fori_loop(0, rows // 16, finish, 0)
        gather_a.begin(da.at[b], own.at[3, b], b)
        mix[b, :, :rows] = column[b].T[:8, :rows]
        for d in range(1, 8):
            last.remote(mix.at[b], mix_in.at[b, s], mix_sem.at[b, d - 1], g, (s + d) % 8)
        local(mix.at[b], mix_in.at[b, s], mix_sem.at[b, 7])

    second = scatters_of(early, True, {})
    for n in (0, 4, 5, 2, 6):
        ref = {0: a_v.at[at_b(0)], 2: b_v.at[at_b(0)], 4: w1_f, 5: w2_f, 6: w3_f}[n]
        arrived(ref, load.at[n])
    feed_forward(0)
    gather_m.step(1, 2)
    gather_d.step(1, 2)
    norm_part(0)
    second[0].begin()
    second[0].start(0)
    gather_m.step(1, 3)
    gather_d.step(1, 3)
    gather_d.finish(own.at[1, 1], 1)
    local(dm_all.at[1], b_v.at[at_b(1)], load.at[3])
    gather_m.finish(own.at[2, 1], 1)
    local(n2_all.at[1], a_v.at[at_b(1)], load.at[1])
    for b in range(2):
        for d in range(1, 8):
            copies.remote(scale.at[b], scale_in.at[b, s], sc_sem.at[b, d - 1], g, (s + d) % 8)
        local(scale.at[b], scale_in.at[b, s], sc_sem.at[b, 7])
    second[0].start(1)
    second[0].hop(0)
    arrived(a_v.at[at_b(1)], load.at[1])
    arrived(b_v.at[at_b(1)], load.at[3])
    feed_forward(1)
    second[0].start(2)
    second[0].hop(1)
    second[0].hop(2)
    norm_part(1)
    def load_pre(b, j):
        local(pre_all.at[b, j], pre.at[j], pre_sem.at[j])

    def attention_back(b):
        gather_a.finish(own.at[3, b], b)
        local(da_all.at[b], a_v.at[at_b(b)], load.at[b])
        for d in range(8):
            arrived(mix_in.at[b, 0], mix_sem.at[b, d])
        columns_of(mixed, mix_in, b, rows)
        live = live_rows(0, length, lengths[0, b])
        arrived(a_v.at[at_b(b)], load.at[b])
        for j in range(2):
            arrived(pre.at[j], pre_sem.at[j])
            lanes = pl.ds(j * head, head)
            error = product_right(a_v[at_b(b)], wo_v[pl.ds(j * head, head)])
            q_pre, k_pre, v_pre, u_pre, o = [pre[j, n] for n in range(5)]
            sigma = 1.0 / (1.0 + jnp.exp(-u_pre))
            u = u_pre * sigma
            scale_g = inverse[at_b(b), :1]
            nat = u * o * scale_g
            nat_v(at_b(b))[:, lanes] = nat.astype(jnp.bfloat16)
            dg = scale_g * (error - nat * mixed[:, :1])
            dz(3, at_b(b))[:, lanes] = (dg * o * (sigma * (1.0 + u_pre * (1.0 - sigma)))).astype(jnp.bfloat16)
            do = (dg * u).astype(jnp.bfloat16)
            q = silu(q_pre).astype(jnp.bfloat16)
            k = (silu(k_pre) * live).astype(jnp.bfloat16)
            v = (silu(v_pre) * live).astype(jnp.bfloat16)
            scores = (product_right(k, q) * table[j]).astype(jnp.bfloat16)
            dv = product(scores, do)
            d_scores = (product_right(v, do) * table[j]).astype(jnp.bfloat16)
            dk = product(d_scores, q)
            dq = product_left(d_scores, k)
            dz(0, at_b(b))[:, lanes] = (dq * slope(pre[j, 0])).astype(jnp.bfloat16)
            dz(1, at_b(b))[:, lanes] = (dk * live * slope(pre[j, 1])).astype(jnp.bfloat16)
            dz(2, at_b(b))[:, lanes] = (dv * live * slope(pre[j, 2])).astype(jnp.bfloat16)
            if b == 0:
                load_pre(1, j)

    def first_part(b):
        def body(at, i):
            value = product_right(dz(0, at_b(b))[...], wa_v[0, at])
            for n in range(1, 4):
                value = value + product_right(dz(n, at_b(b))[...], wa_v[n, at])
            part[b, :, at] = value.astype(jnp.bfloat16)

        tiles_of(width, body)

    second[1].begin()
    second[1].start(0)
    hidden_gradient(0)
    weight_part(0, a_v)
    second[1].start(1)
    second[1].hop(0)
    gather_a.step(0, 1)
    third = scatters_of(sums, False, {})
    early[0].finish()
    mixed_part(0)
    third[0].begin()
    third[0].start(0)
    second[1].start(2)
    second[1].hop(1)
    second[1].hop(2)
    third[0].start(1)
    third[0].hop(0)
    gather_a.step(0, 2)
    weight_part(1, a_v)
    hidden_gradient(1)
    third[0].start(2)
    third[0].hop(1)
    gather_a.step(0, 3)
    third[0].hop(2)
    early[1].finish()
    mixed_part(1)
    third[1].begin()
    third[1].start(0)
    for j in range(2):
        table[j] = turned_table(decay[4 * (2 * c + j) + z], length)
    for b in range(2):
        for d in range(8):
            arrived(scale.at[b], sc_sem.at[b, d])
        columns_of(inverse.at[at_b(b)], scale_in, b, rows)

    for j in range(2):
        arrived(pre.at[j], pre_sem.at[j])
        load_pre(0, j)
    gather_a.step(1, 1)
    third[1].start(1)
    third[1].hop(0)
    weight_part(2, b_v)
    gather_a.step(1, 2)
    third[1].start(2)
    third[1].hop(1)
    third[1].hop(2)
    attention_back(0)
    gather_a.step(1, 3)
    for b in range(2):
        third[b].receive()
        scatter = third[b]

        def result(i, carry):
            piece = aligned(i, 16, 16)
            at = aligned(b * (rows // 16) + i, 16, 16)
            out[at] = (h[at] + scatter.total(piece)).astype(jnp.bfloat16)
            return carry

        lax.fori_loop(0, rows // 16, result, 0)
    def sum_ff(n):
        def room(r):
            return b_v.at[pl.ds((r // 2) * quarter, quarter), pl.ds((r % 2) * half_w, half_w)]

        for r in range(4):
            arrived(in_f.at[n, r], xy_f.at[n, r])
            local(in_f.at[n, r], room(r), load.at[13 + r])
        for entry in sent_f[n]:
            bulk.settle(entry)
        for r in range(4):
            arrived(room(r), load.at[13 + r])
        total = w_v.at[pl.ds(n * hidden, quarter), pl.ds(0, half_w)]

        def read(at):
            value = room(0)[at].astype(jnp.float32)
            for r in range(1, 4):
                value = value + room(r)[at].astype(jnp.float32)
            return value

        def write(at, value):
            total[at] = value.astype(jnp.bfloat16)

        pour(read, write, quarter // 16)
        for d in (2, 1, 3, 0):
            chip = (z + d) % 4
            src = total.at[:, aligned(chip, depth, 128)]
            if d:
                last.remote(src, y_f.at[n, z], z_f.at[n, z], g, 2 * chip + c)
            else:
                local(src, y_f.at[n, z], z_f.at[n, z])

    def join_ff(n, result):
        for r, o in enumerate(others + (g,)):
            arrived(y_f.at[n, o], z_f.at[n, o])
            dst = result.at[aligned(g, quarter, 16)]
            if r < 3:
                last.remote(y_f.at[n, o], dst, join_f.at[n, r], o, s)
            else:
                local(y_f.at[n, o], dst, join_f.at[n, r])

    def sum_third():
        for r in range(3):
            arrived(in_t.at[r], xy_t.at[r])
            local(in_t.at[r], b_v.at[pl.ds(0, hidden), pl.ds(r * wide, wide)], load.at[13 + r])
        for r in range(3):
            arrived(b_v.at[pl.ds(0, hidden), pl.ds(r * wide, wide)], load.at[13 + r])
        mine = w_v.at[pl.ds(2 * hidden, hidden), aligned(g, wide, 128)]

        def read(at):
            value = mine[at].astype(jnp.float32)
            for r in range(3):
                value = value + b_v[at, pl.ds(r * wide, wide)].astype(jnp.float32)
            return value

        def write(at, value):
            mine[at] = value.astype(jnp.bfloat16)

        pour(read, write, hidden // 16)
        local(mine, ft, z_t)

    for b in range(2):
        sums[b].finish()
    fourth = scatters_of(early, True, {})
    first_part(0)
    fourth[0].begin()
    fourth[0].start(0)
    sum_ff(0)
    fourth[0].start(1)
    fourth[0].hop(0)
    attention_back(1)
    sum_ff(1)
    first_part(1)
    fourth[1].begin()

    for b in range(2):
        local(n1_all.at[b], b_v.at[at_b(b)], load.at[2 + b])
    for b in range(2):
        arrived(b_v.at[at_b(b)], load.at[2 + b])
    sent_h = []

    def head_part(n):
        turn(turned, lambda t: dz(n, t)[...], tokens // 128, 2 * head)

        def body(at, i):
            grads_h[n, :, spread_place(i)] = product(turned[pl.ds(0, 2 * head)], b_v[:, at]).astype(jnp.bfloat16)

        tiles_of(width, body)

    def send_head(n):
        if n >= 2:
            for entry in sent_h[n - 2]:
                last.settle(entry)
        grad = grads_h.at[n]
        sent_h.append(to_groups(last, lambda o: grad.at[aligned(o % 2, head, head)], in_h.at[n], xy_h.at[n]))

    def out_weight():
        turn(turned, lambda t: nat_v(t)[...], tokens // 128, 2 * head)

        def body(at, i):
            go_v[:, at] = product(turned[pl.ds(0, 2 * head)], a_v[:, at]).astype(jnp.bfloat16)

        tiles_of(width, body)

    head_part(0)
    send_head(0)
    head_part(1)
    send_head(1)
    head_part(2)
    fourth[0].start(2)
    fourth[0].hop(1)
    send_head(2)
    head_part(3)
    fourth[0].hop(2)
    fourth[1].start(0)
    send_head(3)
    out_weight()
    fourth[1].start(1)
    fourth[1].hop(0)
    for entry in sent_h[2]:
        last.settle(entry)
    for r, o in enumerate(others):
        last.remote(go_v.at[:, aligned(o, wide, 128)], in_o.at[r], xy_o.at[r], o, s)
    sum_third()
    fourth[1].start(2)
    fourth[1].hop(1)
    fourth[1].hop(2)

    def held(n, r):
        return a_v.at[pl.ds((2 * n + r // 2) * head, head), pl.ds((r % 2) * half_w, half_w)]

    def sum_head(n, result):
        for r in range(4):
            arrived(in_h.at[n, r], xy_h.at[n, r])
            local(in_h.at[n, r], held(n, r), load.at[18 + 4 * n + r])
        for r in range(4):
            arrived(held(n, r), load.at[18 + 4 * n + r])

        def read(at):
            value = held(n, 0)[at].astype(jnp.float32)
            for r in range(1, 4):
                value = value + held(n, r)[at].astype(jnp.float32)
            return value

        def write(at, value):
            held(n, 0)[at] = value.astype(jnp.bfloat16)

        pour(read, write, head // 16)
        for d in (2, 1, 3, 0):
            chip = (z + d) % 4
            src = held(n, 0).at[:, aligned(chip, depth, 128)]
            dst = result.at[aligned(z, head, head)]
            if d:
                last.remote(src, dst, z_h.at[n, d], g, 2 * chip + c)
            else:
                local(src, dst, z_h.at[n, d])

    def sum_out():
        for r in range(3):
            arrived(in_o.at[r], xy_o.at[r])
            local(in_o.at[r], b_v.at[pl.ds(0, 2 * head), pl.ds(r * wide, wide)], load.at[13 + r])
        for r in range(3):
            arrived(b_v.at[pl.ds(0, 2 * head), pl.ds(r * wide, wide)], load.at[13 + r])
        mine_o = go_v.at[:, aligned(g, wide, 128)]

        def read(at):
            value = mine_o[at].astype(jnp.float32)
            for r in range(3):
                value = value + b_v[at, pl.ds(r * wide, wide)].astype(jnp.float32)
            return value

        def write(at, value):
            mine_o[at] = value.astype(jnp.bfloat16)

        pour(read, write, 2 * head // 16)
        for j in range(2):
            to = 2 * (2 * c + j) + z // 2
            src = mine_o.at[pl.ds(j * head, head)]
            dst = fo.at[aligned(z % 2, head, head)]
            last.remote(src, dst, z_o.at[z % 2], g, to, to != s)
            local(src, dst, z_o.at[z % 2], to == s)

    sum_head(0, fq)
    sum_head(1, fk)
    for b in range(2):
        fourth[b].receive()
        scatter = fourth[b]

        def finish_x(i, carry):
            piece = aligned(i, 16, 16)
            at = aligned(b * (rows // 16) + i, 16, 16)
            v = x[b, piece].astype(jnp.float32)
            scale_x = lax.rsqrt(mean_square(v) + EPS)
            normed = v * scale_x
            grad = scatter.total(piece)
            along = jnp.mean(normed * grad, axis=-1, keepdims=True)
            grad_x[at] = grad_x[at] + scale_x * (grad - normed * along)
            return carry

        lax.fori_loop(0, rows // 16, finish_x, 0)

    sum_head(2, fv)
    join_ff(0, ff_)
    join_ff(1, fs)
    sum_head(3, fu)
    sum_out()

    for n, result in enumerate((ff_, fs)):
        for r in range(4):
            arrived(result.at[pl.ds(0, quarter)], join_f.at[n, r])
    arrived(ft, z_t)
    for j in range(2):
        arrived(fo.at[pl.ds(0, head)], z_o.at[j])
    for n, result in enumerate((fq, fk, fv, fu)):
        for d in range(4):
            arrived(result.at[pl.ds(0, head)], z_h.at[n, d])
    for b in range(2):
        early[b].finish()
    bulk.finish()
    last.finish()
    copies.finish()


def call(kernel, number, ins, outs, scratch, name):
    return pl.pallas_call(
        kernel,
        out_shape=[shape for shape, _ in outs],
        in_specs=[spec for _, spec in ins],
        out_specs=[spec for _, spec in outs],
        scratch_shapes=scratch,
        compiler_params=pltpu.CompilerParams(
            collective_id=number, has_side_effects=True, vmem_limit_bytes=64 * 2**20 - 2**17
        ),
        name=name,
    )(*[value for value, _ in ins])


def finish_arrays(count, turned_count, *refs):
    ins, outs, held, done = refs[:count], refs[count : 2 * count], refs[2 * count : 3 * count], refs[3 * count : 4 * count]
    in_sem, out_sem = refs[4 * count :]
    for i in range(count):
        local(ins[i], held[i], in_sem.at[i])
    for i in range(count):
        arrived(held[i], in_sem.at[i])
        if i < 2:
            local(held[i], outs[i], out_sem.at[i])
            continue
        if i < 2 + turned_count:
            done[i][...] = held[i][...].T.astype(jnp.float32)
        else:

            def write(at, value):
                done[i][at] = value

            pour(lambda at: held[i][at].astype(jnp.float32), write, held[i].shape[0] // 16)
        local(done[i], outs[i], out_sem.at[i])
    for i in range(count):
        arrived(outs[i], out_sem.at[i])


def finished(out, grad_x, turned, straight):
    arrays = [out, grad_x] + turned + straight
    shapes = [jax.ShapeDtypeStruct(v.shape, v.dtype) for v in (out, grad_x)]
    shapes += [wide_array(*v.shape[::-1]) for v in turned] + [wide_array(*v.shape) for v in straight]
    count = len(arrays)
    small = jax.ShapeDtypeStruct((8, 128), jnp.float32)
    done = [small, small] + shapes[2:]
    return pl.pallas_call(
        functools.partial(finish_arrays, count, len(turned)),
        out_shape=shapes,
        in_specs=[ANY] * count,
        out_specs=[ANY] * count,
        scratch_shapes=[pltpu.VMEM(v.shape, v.dtype) for v in arrays] + [pltpu.VMEM(v.shape, v.dtype) for v in done]
        + [dma(count), dma(count)],
        compiler_params=pltpu.CompilerParams(vmem_limit_bytes=62 * 2**20),
        name="finish_arrays",
    )(*arrays)


def low_array(*shape):
    return jax.ShapeDtypeStruct(shape, jnp.bfloat16)


def wide_array(*shape):
    return jax.ShapeDtypeStruct(shape, jnp.float32)


def dma(*shape):
    return pltpu.SemaphoreType.DMA(shape)


def scatter_scratch(rows, width):
    return [
        pltpu.VMEM((2, 4, rows, width), jnp.bfloat16),
        pltpu.VMEM((2, 2, 3, rows, width), jnp.bfloat16),
        dma(2, 4),
        dma(2, 2, 3),
    ]


def line_shards(
    tokens, cotangent, lengths, decay_rate,
    w_query, w_key, w_value, w_gate, w_out, w_first, w_second, w_third,
):
    bf16, f32 = jnp.bfloat16, jnp.float32
    rows, width = tokens.shape[2], tokens.shape[3]
    depth, wide = w_query.shape
    head = width // decay_rate.shape[0]
    hidden = w_third.shape[0]
    length = 8 * rows
    x_low = tokens[:, 0]
    in_smem = pl.BlockSpec(memory_space=pltpu.SMEM)
    gathered = low_array(2, length, width)
    out, grad_x, fq, fk, fv, fu, fo, ff, fs, ft = call(
        layer_part,
        0,
        [(lengths.T, in_smem), (decay_rate, in_smem), (x_low, VMEM), (cotangent[:, 0], VMEM)]
        + [(v, ANY) for v in (w_query, w_key, w_value, w_gate, w_out, w_first, w_second, w_third)],
        [(low_array(2 * rows, width), VMEM), (wide_array(2 * rows, width), VMEM)]
        + [(low_array(wide, depth), ANY)] * 4 + [(low_array(depth, wide), ANY)]
        + [(low_array(2 * hidden, depth), ANY)] * 2 + [(low_array(hidden, wide), ANY)]
        + [(gathered, ANY)] * 4
        + [(low_array(width, 2 * head), ANY)] * 4
        + [(low_array(2 * head, width), ANY)]
        + [(low_array(hidden, width), ANY)] * 3
        + [(wide_array(2, 2, 5, length, head), ANY)]
        + [(low_array(2, 4, hidden // 2, width // 2), ANY), (low_array(3, hidden, wide), ANY), (low_array(3, 2 * head, wide), ANY),
           (low_array(4, 4, head, width // 2), ANY)]
        + [(low_array(2, 4, hidden // 2, depth), ANY)] * 2,
        [dma(480), dma(40), dma(4, 2)] + [dma(2, 2, 3), dma(2, 7)] * 4
        + [dma(4, 4), dma(2), dma(3, 4), dma(4, 3, 4), dma(3), dma(3, 3, 4), dma(2, 4), dma(2, 4)]
        + [pltpu.VMEM((2, rows, width), bf16)] * 4
        + [pltpu.VMEM((2 * rows, width), f32),
           pltpu.VMEM((2 * length, width), bf16), pltpu.VMEM((2 * length, width), bf16), pltpu.VMEM((3 * hidden, width), bf16),
           pltpu.VMEM((4, width, 2 * head), bf16), pltpu.VMEM((2 * head, width), bf16),
           pltpu.VMEM((3, 2 * length, hidden), bf16), pltpu.VMEM((hidden, 2 * length), bf16),
           pltpu.VMEM((2, length, width), bf16)]
        + scatter_scratch(rows, width) + scatter_scratch(rows, width)
        + [pltpu.VMEM((2, length, length), f32), pltpu.VMEM((2, 8, 8, 128), f32), pltpu.VMEM((2, 8, 8, 128), f32),
           pltpu.VMEM((2, 8, 128), f32), pltpu.VMEM((2, 8, 8, 128), f32), dma(2, 8), dma(2, 8), pltpu.VMEM((2, 128, 128), f32),
           pltpu.VMEM((2, 8, 128), f32), pltpu.VMEM((2, 8, 8, 128), f32), dma(2, 8),
           pltpu.VMEM((2 * length, 128), f32), pltpu.VMEM((length, 128), f32),
           pltpu.VMEM((2, 5, length, head), f32), dma(2),
           pltpu.VMEM((2 * head, width), bf16), pltpu.VMEM((4, 2 * head, width), bf16),
           dma(2, 4), dma(3), dma(3), dma(4, 4), dma(2, 4), dma(), dma(2), dma(4, 4)],
        "layer_part",
    )[:10]
    results = finished(out, grad_x, [fq, fk, fv, fu, ff, fs], [fo, ft])
    out, grad_x, fq, fk, fv, fu, ff, fs, fo, ft = results
    return (out.reshape(2, 1, rows, width), grad_x.reshape(2, 1, rows, width), fq, fk, fv, fu, fo, ff, fs, ft)


def solution(mesh):
    in_specs = (
        P(None, "grp", "seq", None),
        P(None, "grp", "seq", None),
        P(None, "grp"),
        P(),
        P("seq", "grp"),
        P("seq", "grp"),
        P("seq", "grp"),
        P("seq", "grp"),
        P("seq", "grp"),
        P("seq", "grp"),
        P("seq", "grp"),
        P("seq", "grp"),
    )
    out_specs = (
        P(None, "grp", "seq", None),
        P(None, "grp", "seq", None),
        P("seq", "grp"),
        P("seq", "grp"),
        P("seq", "grp"),
        P("seq", "grp"),
        P("seq", "grp"),
        P("seq", "grp"),
        P("seq", "grp"),
        P("seq", "grp"),
    )
    fast = mesh.shape["grp"] == 4 and mesh.shape["seq"] == 8
    return jax.shard_map(line_shards if fast else shards, mesh=mesh, in_specs=in_specs, out_specs=out_specs, check_vma=False)
```

```python
import functools

import jax
import jax.numpy as jnp
from jax import lax
from jax.experimental import pallas as pl
from jax.experimental.pallas import tpu as pltpu
from jax.sharding import PartitionSpec as P

EPS = 1e-06
HIGH = lax.Precision.HIGHEST
MESH = pl.DeviceIdType.MESH
ANY = pl.BlockSpec(memory_space=pl.ANY)
VMEM = pl.BlockSpec(memory_space=pltpu.VMEM)


def prefix(value, axis, join, neutral, backward):
    count, mine = (lax.axis_size(axis), lax.axis_index(axis))
    pieces = jax.tree.map(lambda part: lax.all_gather(part, axis), value)
    if backward:
        pieces = jax.tree.map(lambda part: part[::-1], pieces)
        mine = count - 1 - mine
    subtotal = jax.tree.map(
        lambda part, zero: jnp.full_like(part, 0) + jnp.asarray(zero, part.dtype), value, neutral
    )

    def step(position, subtotal):
        longer = join(subtotal, jax.tree.map(lambda part: part[position], pieces))
        return jax.tree.map(lambda new, old: jnp.where(position < mine, new, old), longer, subtotal)

    return lax.fori_loop(0, count - 1, step, subtotal)


def norm_rows(values):
    return values * lax.rsqrt(jnp.mean(values * values, axis=-1, keepdims=True) + EPS)


def norm_back(values, gradient):
    _, pull = jax.vjp(norm_rows, values)
    return pull(gradient)[0]


def silu_slope(values):
    sigma = jax.nn.sigmoid(values)
    return sigma * (1.0 + values * (1.0 - sigma))


def product(left, right):
    return jnp.dot(left, right, preferred_element_type=jnp.float32)


def product_left(left, right):
    return lax.dot_general(
        left, right, (((0,), (0,)), ((), ())), preferred_element_type=jnp.float32
    )


def product_right(left, right):
    return lax.dot_general(
        left, right, (((1,), (1,)), ((), ())), preferred_element_type=jnp.float32
    )


def combine_state(earlier, later):
    return (later[1][:, None, None] * earlier[0] + later[0], earlier[1] * later[1])


def shards(
    tokens,
    cotangent,
    lengths,
    decay_rate,
    w_query,
    w_key,
    w_value,
    w_gate,
    w_out,
    w_first,
    w_second,
    w_third,
):
    micro = tokens.shape[0]
    block_rows = tokens.shape[2]
    width = tokens.shape[3]
    heads = decay_rate.shape[0]
    head_dim = width // heads
    hidden_width = w_third.shape[0] * lax.axis_size("seq")
    places = jnp.arange(block_rows).astype(jnp.float32)
    slot_index = lax.axis_index("seq") * block_rows + jnp.arange(block_rows)
    offset = places[:, None] - places[None, :]
    weight = jnp.where(
        offset[None] >= 0, jnp.exp(-decay_rate[:, None, None] * jnp.maximum(offset, 0.0)[None]), 0.0
    )
    query_fac = jnp.exp(-decay_rate[None, :] * (places[:, None] + 1.0))[:, :, None]
    key_fac = jnp.exp(-decay_rate[None, :] * (block_rows - 1.0 - places[:, None]))[:, :, None]
    step_decay = jnp.exp(-decay_rate * block_rows)
    empty_state = jnp.zeros((heads, head_dim, head_dim), jnp.float32)
    unit_decay = jnp.ones((heads,), jnp.float32)
    partial_rows = (
        lax.all_gather(w_query, "grp", axis=1, tiled=True),
        lax.all_gather(w_key, "grp", axis=1, tiled=True),
        lax.all_gather(w_value, "grp", axis=1, tiled=True),
        lax.all_gather(w_gate, "grp", axis=1, tiled=True),
        lax.all_gather(w_out, "grp", axis=1, tiled=True),
        lax.all_gather(w_first, "grp", axis=1, tiled=True),
        lax.all_gather(w_second, "grp", axis=1, tiled=True),
        lax.all_gather(w_third, "grp", axis=1, tiled=True),
    )
    gathered = (
        lax.all_gather(partial_rows[0], "seq", axis=0, tiled=True),
        lax.all_gather(partial_rows[1], "seq", axis=0, tiled=True),
        lax.all_gather(partial_rows[2], "seq", axis=0, tiled=True),
        lax.all_gather(partial_rows[3], "seq", axis=0, tiled=True),
        lax.all_gather(partial_rows[4], "seq", axis=0, tiled=True),
        lax.all_gather(partial_rows[5], "seq", axis=0, tiled=True),
        lax.all_gather(partial_rows[6], "seq", axis=0, tiled=True),
        lax.all_gather(partial_rows[7], "seq", axis=0, tiled=True),
    )
    outputs = []
    input_grads = []
    first_norms = []
    attn_rows = []
    normed_rows = []
    branch_rows = []
    second_norms = []
    ffn_rows = []
    mixed_rows = []
    upstream_rows = []
    for batch_idx in range(micro):
        wq_full, wk_full, wv_full, wu_full, wo_full, first_full, second_full, third_full = gathered
        inputs = tokens[batch_idx, 0].astype(jnp.float32)
        live = (slot_index < lengths[batch_idx, 0]).astype(jnp.float32)[:, None]
        live_low = live.astype(jnp.bfloat16)
        first_norm = norm_rows(inputs).astype(jnp.bfloat16)
        query_pre = product(first_norm, wq_full)
        key_pre = product(first_norm, wk_full)
        value_pre = product(first_norm, wv_full)
        gate_pre = product(first_norm, wu_full)
        queries = jax.nn.silu(query_pre).astype(jnp.bfloat16).reshape(block_rows, heads, head_dim)
        key_heads = (jax.nn.silu(key_pre).astype(jnp.bfloat16) * live_low).reshape(
            block_rows, heads, head_dim
        )
        value_heads = (jax.nn.silu(value_pre).astype(jnp.bfloat16) * live_low).reshape(
            block_rows, heads, head_dim
        )
        query_wide = queries.astype(jnp.float32)
        key_wide = key_heads.astype(jnp.float32)
        value_wide = value_heads.astype(jnp.float32)
        local_state = jnp.einsum("jhd,jhe->hde", key_wide * key_fac, value_wide, precision=HIGH)
        prior_state, _ = prefix(
            (local_state, step_decay), "seq", combine_state, (empty_state, unit_decay), False
        )
        scores = (
            jnp.einsum("ihd,jhd->hij", queries, key_heads, preferred_element_type=jnp.float32)
            * weight
        )
        intra = jnp.einsum("hij,jhe->ihe", scores, value_wide, precision=HIGH)
        inter = jnp.einsum("ihd,hde->ihe", query_wide * query_fac, prior_state, precision=HIGH)
        attended = (intra + inter).reshape(block_rows, width)
        gate_act = jax.nn.silu(gate_pre)
        gated = gate_act * attended
        normed = norm_rows(gated).astype(jnp.bfloat16)
        hidden = inputs + product(normed, wo_full)
        second_norm = norm_rows(hidden).astype(jnp.bfloat16)
        first_proj = product(second_norm, first_full)
        second_proj = product(second_norm, second_full)
        mixed_in = (first_proj * second_proj).astype(jnp.bfloat16)
        result = hidden + product(mixed_in, third_full)
        outputs.append(result.astype(jnp.bfloat16))
        upstream = cotangent[batch_idx, 0].astype(jnp.float32) * live
        upstream_low = upstream.astype(jnp.bfloat16)
        grad_mixed = product_right(upstream_low, third_full)
        grad_first_proj = (grad_mixed * second_proj).astype(jnp.bfloat16)
        grad_second_proj = (grad_mixed * first_proj).astype(jnp.bfloat16)
        grad_norm_two = product_right(grad_first_proj, first_full) + product_right(
            grad_second_proj, second_full
        )
        grad_hidden = upstream + norm_back(hidden, grad_norm_two)
        grad_branch = grad_hidden.astype(jnp.bfloat16)
        grad_gated = norm_back(gated, product_right(grad_branch, wo_full))
        grad_attended = (grad_gated * gate_act).astype(jnp.bfloat16)
        grad_gate_pre = (grad_gated * attended * silu_slope(gate_pre)).astype(jnp.bfloat16)
        grad_heads = grad_attended.reshape(block_rows, heads, head_dim)
        grad_wide = grad_heads.astype(jnp.float32)
        local_grad = jnp.einsum("ihd,ihe->hde", query_wide * query_fac, grad_wide, precision=HIGH)
        later_grad, _ = prefix(
            (local_grad, step_decay), "seq", combine_state, (empty_state, unit_decay), True
        )
        grad_scores = (
            jnp.einsum("ihe,jhe->hij", grad_heads, value_heads, preferred_element_type=jnp.float32)
            * weight
        )
        grad_queries = jnp.einsum("hij,jhd->ihd", grad_scores, key_wide, precision=HIGH)
        grad_queries = (
            grad_queries
            + jnp.einsum("ihe,hde->ihd", grad_wide, prior_state, precision=HIGH) * query_fac
        )
        grad_keys = jnp.einsum("hij,ihd->jhd", grad_scores, query_wide, precision=HIGH)
        grad_keys = (
            grad_keys + jnp.einsum("hde,jhe->jhd", later_grad, value_wide, precision=HIGH) * key_fac
        )
        grad_values = jnp.einsum("hij,ihe->jhe", scores, grad_wide, precision=HIGH)
        grad_values = (
            grad_values + jnp.einsum("jhd,hde->jhe", key_wide, later_grad, precision=HIGH) * key_fac
        )
        grad_query_pre = (grad_queries.reshape(block_rows, width) * silu_slope(query_pre)).astype(
            jnp.bfloat16
        )
        grad_key_pre = (grad_keys.reshape(block_rows, width) * live * silu_slope(key_pre)).astype(
            jnp.bfloat16
        )
        grad_value_pre = (
            grad_values.reshape(block_rows, width) * live * silu_slope(value_pre)
        ).astype(jnp.bfloat16)
        grad_norm_one = product_right(grad_query_pre, wq_full) + product_right(
            grad_key_pre, wk_full
        )
        grad_norm_one = (
            grad_norm_one
            + product_right(grad_value_pre, wv_full)
            + product_right(grad_gate_pre, wu_full)
        )
        input_grads.append(grad_hidden + norm_back(inputs, grad_norm_one))
        first_norms.append(first_norm)
        attn_rows.append(
            jnp.concatenate([grad_query_pre, grad_key_pre, grad_value_pre, grad_gate_pre], axis=1)
        )
        normed_rows.append(normed)
        branch_rows.append(grad_branch)
        second_norms.append(second_norm)
        ffn_rows.append(jnp.concatenate([grad_first_proj, grad_second_proj], axis=1))
        mixed_rows.append(mixed_in)
        upstream_rows.append(upstream_low)
    first_all = jnp.concatenate(first_norms, axis=0)
    attn_all = jnp.concatenate(attn_rows, axis=0)
    normed_all = jnp.concatenate(normed_rows, axis=0)
    branch_all = jnp.concatenate(branch_rows, axis=0)
    second_all = jnp.concatenate(second_norms, axis=0)
    ffn_all = jnp.concatenate(ffn_rows, axis=0)
    mixed_all = jnp.concatenate(mixed_rows, axis=0)
    upstream_all = jnp.concatenate(upstream_rows, axis=0)
    proj_rows = lax.psum_scatter(
        product_left(first_all, attn_all), "seq", scatter_dimension=0, tiled=True
    )
    outproj_rows = lax.psum_scatter(
        product_left(normed_all, branch_all), "seq", scatter_dimension=0, tiled=True
    )
    ffn_part = lax.psum_scatter(
        product_left(second_all, ffn_all), "seq", scatter_dimension=0, tiled=True
    )
    down_rows = lax.psum_scatter(
        product_left(mixed_all, upstream_all), "seq", scatter_dimension=0, tiled=True
    )
    summed = (
        lax.psum_scatter(proj_rows[:, :width], "grp", scatter_dimension=1, tiled=True),
        lax.psum_scatter(proj_rows[:, width : 2 * width], "grp", scatter_dimension=1, tiled=True),
        lax.psum_scatter(
            proj_rows[:, 2 * width : 3 * width], "grp", scatter_dimension=1, tiled=True
        ),
        lax.psum_scatter(proj_rows[:, 3 * width :], "grp", scatter_dimension=1, tiled=True),
        lax.psum_scatter(outproj_rows, "grp", scatter_dimension=1, tiled=True),
        lax.psum_scatter(ffn_part[:, :hidden_width], "grp", scatter_dimension=1, tiled=True),
        lax.psum_scatter(ffn_part[:, hidden_width:], "grp", scatter_dimension=1, tiled=True),
        lax.psum_scatter(down_rows, "grp", scatter_dimension=1, tiled=True),
    )
    layer_out = jnp.stack(outputs)[:, None]
    grad_tokens = jnp.stack(input_grads)[:, None]
    return (
        layer_out,
        grad_tokens,
        summed[0],
        summed[1],
        summed[2],
        summed[3],
        summed[4],
        summed[5],
        summed[6],
        summed[7],
    )


class Spare:
    def __init__(self, sems):
        self.sems, self.free = sems, list(range(sems.shape[0]))


class Copies:
    def __init__(self, spare):
        self.spare = spare
        self.pending = []

    def remote(self, src, dst, recv_sem, group, place, when=None):
        number = self.spare.free.pop(0)
        copy = pltpu.make_async_remote_copy(
            src_ref=src,
            dst_ref=dst,
            send_sem=self.spare.sems.at[number],
            recv_sem=recv_sem,
            device_id=(group, place),
            device_id_type=MESH,
        )
        self.pending.append((copy, when, number))
        if when is None:
            copy.start()
        else:
            pl.when(when)(copy.start)
        return self.pending[-1]

    def settle(self, entry):
        if not any(other is entry for other in self.pending):
            return
        self.pending = [other for other in self.pending if other is not entry]
        copy, when, number = entry
        if when is None:
            copy.wait_send()
        else:
            pl.when(when)(copy.wait_send)
        self.spare.free.append(number)

    def finish(self):
        while self.pending:
            self.settle(self.pending[0])


def local(src, dst, sem, when=None):
    copy = pltpu.make_async_copy(src, dst, sem)
    if when is None:
        copy.start()
    else:
        pl.when(when)(copy.start)


def arrived(ref, sem, when=None):
    copy = pltpu.make_async_copy(ref, ref, sem)
    if when is None:
        copy.wait()
    else:
        pl.when(when)(copy.wait)


def where_am_i():
    g, s = lax.axis_index("grp"), lax.axis_index("seq")
    return g, s, g // 2, g % 2, s // 2, s % 2


def across(y, x):
    return (y * 2 + 1 - x, (1 - y) * 2 + x, (1 - y) * 2 + 1 - x)


def greet(partners):
    barrier = pltpu.get_barrier_semaphore()
    for partner in partners:
        pl.semaphore_signal(barrier, inc=1, device_id=partner, device_id_type=MESH)
    pl.semaphore_wait(barrier, len(partners))


def aligned(index, unit, step):
    return pl.ds(pl.multiple_of(index * unit, step), unit)


class Gather:
    def __init__(self, copies, out, rows, hop_sem, side_sem):
        self.copies, self.out, self.rows = copies, out, rows
        self.hop_sem, self.side_sem = hop_sem, side_sem
        self.g, self.s, _, _, self.z, self.c = where_am_i()

    def block(self, b, z, core):
        return self.out.at[b, aligned(2 * z + core, self.rows, 16)]

    def spread(self, src, b, z_of, k, right, left):
        g, s, z, c = self.g, self.s, self.z, self.c
        dst = self.block(b, z_of, c)
        if right is not None:
            self.copies.remote(src, dst, self.hop_sem.at[b, 0, k], g, (s + 2) % 8, right)
        if left is not None:
            self.copies.remote(src, dst, self.hop_sem.at[b, 1, k], g, (s + 6) % 8, left)

    def begin(self, src, own_sem, b):
        g, s, z, c = self.g, self.s, self.z, self.c
        self.spread(src, b, z, 0, z < 3, z > 0)
        self.copies.remote(src, self.block(b, z, c), self.side_sem.at[b, 0], g, s + 1 - 2 * c)
        local(src, self.block(b, z, c), own_sem)

    def step(self, b, k):
        g, s, z, c = self.g, self.s, self.z, self.c
        side = s + 1 - 2 * c
        has = z >= k
        at = jnp.maximum(z - k, 0)
        ref = self.block(b, at, c)
        arrived(ref, self.hop_sem.at[b, 0, k - 1], has)
        if k < 3:
            self.spread(ref, b, at, k, jnp.logical_and(has, z < 3), None)
        self.copies.remote(ref, ref, self.side_sem.at[b, k], g, side, has)
        has = z + k <= 3
        at = jnp.minimum(z + k, 3)
        ref = self.block(b, at, c)
        arrived(ref, self.hop_sem.at[b, 1, k - 1], has)
        if k < 3:
            self.spread(ref, b, at, k, None, jnp.logical_and(has, z > 0))
        self.copies.remote(ref, ref, self.side_sem.at[b, 3 + k], g, side, has)

    def finish(self, own_sem, b):
        z, c = self.z, self.c
        arrived(self.block(b, z, c), own_sem)
        arrived(self.block(b, z, 1 - c), self.side_sem.at[b, 0])
        for k in (1, 2, 3):
            arrived(self.block(b, jnp.maximum(z - k, 0), 1 - c), self.side_sem.at[b, k], z >= k)
            arrived(self.block(b, jnp.minimum(z + k, 3), 1 - c), self.side_sem.at[b, 3 + k], z + k <= 3)


def line_partners(g, s):
    return [(g, (s + d) % 8) for d in range(1, 8)]


def add_rows(target, room):
    def write(at, value):
        target[at] = value.astype(jnp.bfloat16)

    pour(lambda at: target[at].astype(jnp.float32) + room[at].astype(jnp.float32), write, target.shape[0] // 16)


class GroupSum:
    def __init__(self, copies, grad, inbox, sem):
        self.copies, self.grad, self.inbox, self.sem = copies, grad, inbox, sem
        self.g, self.s, self.y, self.x, self.z, self.c = where_am_i()
        self.rows, self.half = grad.shape[0] // 2, grad.shape[1] // 2
        self.entries = []

    def block(self, x, core):
        return self.grad.at[aligned(x, self.rows, 16), pl.ds(core * self.half, self.half)]

    def slot(self, first, count=1):
        return self.inbox.at[pl.ds(first * self.rows, count * self.rows)]

    def remote(self, *args):
        self.entries.append(self.copies.remote(*args))

    def depart(self):
        gx, gy, _ = across(self.y, self.x)
        self.remote(self.grad.at[:, pl.ds(0, self.half)], self.slot(0, 2), self.sem.at[0], gy, self.s, self.c != self.y)
        self.remote(self.block(1 - self.x, 1), self.slot(2), self.sem.at[1], gx, self.s)

    def middle(self, room, small, load):
        gx, gy, _ = across(self.y, self.x)
        mine = self.c == self.y
        arrived(self.slot(0, 2), self.sem.at[0], mine)
        local(self.slot(0, 2), room, load.at[0], mine)
        arrived(self.slot(2), self.sem.at[1])
        local(self.slot(2), small, load.at[1])
        arrived(room, load.at[0], mine)

        @pl.when(mine)
        def _():
            add_rows(self.grad.at[:, pl.ds(0, self.half)], room)

        arrived(small, load.at[1])
        add_rows(self.block(self.x, 1), small)
        for core in range(2):
            block = self.block(self.x, core)
            self.remote(
                block, self.slot(3), self.sem.at[2], self.g, 2 * self.z + core, jnp.logical_and(mine, self.c != core)
            )
            local(block, self.slot(3), self.sem.at[2], jnp.logical_and(mine, self.c == core))
        self.remote(self.block(1 - self.x, 0), self.slot(4), self.sem.at[3], gx, 2 * self.z, mine)
        self.remote(self.block(self.x, 1), self.slot(4), self.sem.at[3], gy, 2 * self.z + 1, jnp.logical_not(mine))

    def final(self, room, small, load):
        for i, ref in enumerate((room, small)):
            arrived(self.slot(3 + i), self.sem.at[2 + i])
            local(self.slot(3 + i), ref, load.at[i])
        for i, ref in enumerate((room, small)):
            arrived(ref, load.at[i])
        add_rows(room, small)

    def settle(self):
        for entry in self.entries:
            self.copies.settle(entry)


class ColumnSum:
    def __init__(self, copies, grad, inbox, sem):
        self.copies, self.grad, self.inbox, self.sem = copies, grad, inbox, sem
        self.g, self.s, y, x, _, _ = where_am_i()
        self.others = across(y, x)
        self.rows, self.wide = grad.shape[0] // 2, grad.shape[1] // 4

    def block(self, group, i):
        return self.grad.at[pl.ds(i * self.rows, self.rows), aligned(group, self.wide, 128)]

    def depart(self):
        for i in range(2):
            to = self.others[i]
            for k, group in enumerate((to, self.others[2])):
                self.copies.remote(self.block(group, i), self.inbox.at[i, k], self.sem.at[i, k], to, self.s)

    def middle(self, rooms, load):
        for i in range(2):
            arrived(self.inbox.at[i, 1], self.sem.at[i, 1])
            local(self.inbox.at[i, 1], rooms[i], load.at[i])
        for i in range(2):
            arrived(rooms[i], load.at[i])
            to = self.others[1 - i]
            add_rows(self.block(to, i), rooms[i])
            self.copies.remote(self.block(to, i), self.inbox.at[i, 2], self.sem.at[i, 2], to, self.s)

    def final(self, rooms, load):
        for i in range(2):
            for k in range(2):
                arrived(self.inbox.at[i, 2 * k], self.sem.at[i, 2 * k])
                local(self.inbox.at[i, 2 * k], rooms[2 * i + k], load.at[2 * i + k])
        for i in range(2):
            for k in range(2):
                arrived(rooms[2 * i + k], load.at[2 * i + k])
            mine, first, second = self.block(self.g, i), rooms[2 * i], rooms[2 * i + 1]

            def read(at):
                return mine[at].astype(jnp.float32) + first[at].astype(jnp.float32) + second[at].astype(jnp.float32)

            def write(at, value):
                mine[at] = value.astype(jnp.bfloat16)

            pour(read, write, self.rows // 16)


def everyone_on_line(copies, src, dst, sem, g, s, to_rows):
    for d in range(1, 8):
        to = (s + d) % 8
        copies.remote(to_rows(to), dst.at[s], sem.at[d - 1], g, to)


def mean_square(values):
    return jnp.mean(values * values, axis=-1, keepdims=True)


def pour(read, write, count):
    def piece(i, carry):
        at = aligned(i, 16, 16)
        write(at, read(at))
        return carry

    lax.fori_loop(0, count, piece, 0)


class LineScatter:
    def __init__(self, copies, part, rows, side, inbox, side_sem, line_sem, queue):
        self.copies, self.part, self.rows, self.queue = copies, part, rows, queue
        self.side, self.inbox, self.side_sem, self.line_sem = side, inbox, side_sem, line_sem
        self.g, self.s, _, _, self.z, self.c = where_am_i()

    def mine(self, chip):
        return self.part.at[aligned(2 * chip + self.c, self.rows, 16)]

    def begin(self):
        for chip in (3, 0, 2, 1):
            theirs = aligned(2 * chip + 1 - self.c, self.rows, 16)
            self.copies.remote(
                self.part.at[theirs], self.side.at[chip], self.side_sem.at[chip], self.g, self.s + 1 - 2 * self.c
            )

    def add_on(self, chip, way):
        own, side = self.mine(chip), self.side.at[chip]
        slot = chip - 1 if way == 0 else chip
        come = self.inbox.at[way, slot]
        arrived(side, self.side_sem.at[chip])
        arrived(come, self.line_sem.at[way, slot])

        def three(at):
            return own[at].astype(jnp.float32) + side[at].astype(jnp.float32) + come[at].astype(jnp.float32)

        def write(at, value):
            own[at] = value.astype(jnp.bfloat16)

        pour(three, write, self.rows // 16)

    def push(self, chip, way, when):
        slot = chip - 1 if way == 0 else chip
        to = (self.s + 2) % 8 if way == 0 else (self.s + 6) % 8
        return self.copies.remote(
            self.mine(chip), self.inbox.at[way, slot], self.line_sem.at[way, slot], self.g, to, when
        )

    def pass_on(self, chip, way):
        end = self.z == (0 if way == 0 else 3)
        own, side = self.mine(chip), self.side.at[chip]

        def two(at):
            return own[at].astype(jnp.float32) + side[at].astype(jnp.float32)

        def write(at, value):
            own[at] = value.astype(jnp.bfloat16)

        @pl.when(end)
        def _():
            arrived(side, self.side_sem.at[chip])
            pour(two, write, self.rows // 16)

        if way in self.queue:
            copies, entry = self.queue.pop(way)
            copies.settle(entry)
        self.queue[way] = (self.copies, self.push(chip, way, end))

    def start(self, i):
        self.pass_on(3 - i, 0)
        self.pass_on(i, 1)

    def hop(self, i):
        z = self.z
        for inner in (1, 2):

            @pl.when(z == inner)
            def _():
                near = inner == 1
                if i < 2:
                    self.add_on(3 - i if near else i, 0 if near else 1)
                else:
                    self.add_on(0 if near else 3, 1 if near else 0)

        for inner in (1, 2):
            near = inner == 1
            if i < 2:
                self.push(3 - i if near else i, 0 if near else 1, z == inner)
            else:
                self.push(0 if near else 3, 1 if near else 0, z == inner)

    def receive(self):
        z = self.z
        arrived(self.side.at[z], self.side_sem.at[z])
        left, right = jnp.maximum(z - 1, 0), jnp.minimum(z, 2)
        arrived(self.inbox.at[0, left], self.line_sem.at[0, left], z > 0)
        arrived(self.inbox.at[1, right], self.line_sem.at[1, right], z < 3)

    def total(self, at):
        z = self.z
        value = self.mine(z)[at].astype(jnp.float32) + self.side[z, at].astype(jnp.float32)
        from_left = self.inbox[0, jnp.maximum(z - 1, 0), at].astype(jnp.float32)
        from_right = self.inbox[1, jnp.minimum(z, 2), at].astype(jnp.float32)
        return value + jnp.where(z > 0, from_left, 0.0) + jnp.where(z < 3, from_right, 0.0)


def silu(values):
    return values / (1.0 + jnp.exp(-values))


def decay_table(rate, length):
    offset = lax.broadcasted_iota(jnp.int32, (length, length), 0) - lax.broadcasted_iota(jnp.int32, (length, length), 1)
    steps = jnp.maximum(offset, 0).astype(jnp.float32)
    return jnp.where(offset >= 0, jnp.exp(-rate * steps), 0.0)


def live_rows(first, count, length):
    return ((first + lax.broadcasted_iota(jnp.int32, (count, 1), 0)) < length).astype(jnp.float32)


def slope(values):
    sigma = 1.0 / (1.0 + jnp.exp(-values))
    return sigma * (1.0 + values * (1.0 - sigma))


def turned_table(rate, length):
    offset = lax.broadcasted_iota(jnp.int32, (length, length), 1) - lax.broadcasted_iota(jnp.int32, (length, length), 0)
    steps = jnp.maximum(offset, 0).astype(jnp.float32)
    return jnp.where(offset >= 0, jnp.exp(-rate * steps), 0.0)


def columns_of(out, tiles, b, rows):
    for owner in range(8):
        out[pl.ds(owner * rows, rows)] = jnp.broadcast_to(tiles[b, owner, :1], (128, 128)).T[:rows]


def turn(dst, read, count, columns):
    def block(i, carry):
        dst[pl.ds(0, columns), aligned(i, 128, 128)] = read(aligned(i, 128, 128)).T
        return carry

    lax.fori_loop(0, count, block, 0)


def tiles_of(width, body):
    def tile(i, carry):
        body(aligned(i, 256, 256), i)
        return carry

    lax.fori_loop(0, width // 256, tile, 0)


def layer_part(
    lengths, decay, x, cot, wq, wk, wv, wu, wo, w1, w2, w3,
    out, grad_x, fq, fk, fv, fu, fo, ff_, fs, ft,
    n1_all, dm_all, n2_all, da_all, q_all, k_all, v_all, u_all, o_all, f_all, s_all, t_all, pre_all, in_f, in_t, in_o, in_h, x_f, y_f,
    send, load, own, hop_n, side_n, hop_d, side_d, hop_m, side_m_, hop_a, side_a, z_head, z_out, z_ff, xy_head, xy_out, xy_ff, spread_f, join_f,
    n1, dm, n2, da, h, a_v, b_v, w_v, wa_v, wo_v, p_v, turned, part, side, inbox, side_sem, line_sem,
    side_m, inbox_m, side_sem_m, line_sem_m, table, squares, inbox_sq, scale, scale_in, sq_sem, sc_sem, column,
    mix, mix_in, mix_sem, inverse, mixed, pre, pre_sem, go_v, grads_h,
    xy_f, xy_t, xy_o, xy_h, z_f, z_t, z_o, z_h,
):
    g, s, y, x_, z, c = where_am_i()
    others = across(y, x_)
    plane = [(o, 2 * z + e) for o in others for e in range(2)]
    rows, width = x.shape[1], x.shape[2]
    length = 8 * rows
    tokens = 2 * length
    depth, wide = wq.shape
    head = q_all.shape[1] // 2
    hidden = f_all.shape[0]
    quarter = hidden // 2
    half = length // 2
    target = g // 2
    mine = aligned(g % 2, head, head)
    here = c == target
    order = [(z + d) % 4 for d in (0, 1, 3, 2)]
    spare = Spare(send)
    copies, later, turned_out, bulk, last = [Copies(spare) for _ in range(5)]
    early, sums = [[Copies(spare) for _ in range(2)] for _ in range(2)]
    gather_n = Gather(copies, n1_all, rows, hop_n, side_n)
    gather_d = Gather(later, dm_all, rows, hop_d, side_d)
    gather_m = Gather(later, n2_all, rows, hop_m, side_m_)
    gather_a = Gather(last, da_all, rows, hop_a, side_a)
    heads = list(zip((wq, wk, wv, wu), (q_all, k_all, v_all, u_all)))
    w1_f, w2_f, w3_f = [w_v.at[pl.ds(n * hidden, hidden)] for n in range(3)]
    w1_in, w2_in = [w_v.at[pl.ds(n * depth, depth), pl.ds(512, 2 * hidden)] for n in range(2)]
    w1_t, w2_t = [w_v.at[pl.ds(0, 2 * hidden), pl.ds(n * depth, depth)] for n in range(2)]
    low_v = p_v.at[2, pl.ds(0, length), pl.ds(0, 2 * head)]

    def at_b(b):
        return pl.ds(b * length, length)

    def dz(n, at):
        return p_v.at[n // 2, at, pl.ds((n % 2) * 2 * head, 2 * head)]

    def nat_v(at):
        return p_v.at[2, at, pl.ds(0, 2 * head)]

    local(w1, w1_in, load.at[0])
    local(w2, w2_in, load.at[1])
    greet(line_partners(g, s) + plane)

    def send_heads(n):
        src, dst = heads[n]
        for d in (2, 1, 3, 0):
            to = (z + d) % 4
            a, b = src.at[:, aligned(to, head, head)], dst.at[aligned(s, depth, 16), mine]
            if d:
                copies.remote(a, b, z_head.at[n, z], g, 2 * to + target)
            else:
                copies.remote(a, b, z_head.at[n, z], g, 2 * to + target, c != target)
                local(a, b, z_head.at[n, z], here)

    def pass_heads(n):
        dst = heads[n][1]
        for zs in order:
            block = dst.at[aligned(zs, 2 * depth, 16), mine]
            arrived(block, z_head.at[n, zs], here)
            for r, o in enumerate(others[:2]):
                copies.remote(block, block, xy_head.at[n, r, zs], o, s, here)

    def relay_heads(n):
        dst = heads[n][1]
        for zs in order:
            for r, when in ((0, here), (1, jnp.logical_not(here))):
                lanes = aligned(others[r] % 2, head, head)
                arrived(dst.at[aligned(zs, 2 * depth, 16), lanes], xy_head.at[n, r, zs], when)
                part_ = dst.at[aligned(2 * zs + r, depth, 16), lanes]
                copies.remote(part_, part_, xy_head.at[n, 2, zs], others[1 - r], s, when)

    def send_out():
        for i in range(2):
            to = 2 * c + i
            a = wo.at[pl.ds(i * head, head)]
            b = o_all.at[aligned(z % 2, head, head), aligned(g, wide, 128)]
            self_ = jnp.logical_and(to == z, c == z // 2)
            copies.remote(a, b, z_out.at[z % 2], g, 2 * to + z // 2, jnp.logical_not(self_))
            local(a, b, z_out.at[z % 2], self_)

    def pass_out():
        for j in range(2):
            arrived(o_all.at[pl.ds(j * head, head), aligned(g, wide, 128)], z_out.at[j])
        block = o_all.at[:, aligned(g, wide, 128)]
        for r, o in enumerate(others[:2]):
            copies.remote(block, block, xy_out.at[r], o, s)

    def relay_out():
        for r in range(2):
            lanes = aligned(others[r], wide, 128)
            arrived(o_all.at[:, lanes], xy_out.at[r])
            part_ = o_all.at[pl.ds(r * head, head), lanes]
            copies.remote(part_, part_, xy_out.at[2], others[1 - r], s)

    def spread_ff():
        for n, src in enumerate((w1_t, w2_t)):
            for r, o in enumerate(others):
                turned_out.remote(src.at[aligned(o, quarter, 16)], x_f.at[n, g], spread_f.at[n, r], o, s)
            local(src.at[aligned(g, quarter, 16)], x_f.at[n, g], spread_f.at[n, 3])

    def ff_block(n, group, zs):
        return (f_all, s_all)[n].at[aligned(group % 2, quarter, 16), aligned(zs, 2 * depth, 128)]

    def send_ff(n):
        for r, o in enumerate(others):
            arrived(x_f.at[n, o], spread_f.at[n, r])
        arrived(x_f.at[n, g], spread_f.at[n, 3])
        b = (f_all, s_all)[n].at[aligned(g % 2, quarter, 16), aligned(s, depth, 128)]
        for d in (2, 1, 3, 0):
            to = (z + d) % 4
            a = x_f.at[n, to]
            if d:
                later.remote(a, b, z_ff.at[n, z], g, 2 * to + target)
            else:
                later.remote(a, b, z_ff.at[n, z], g, 2 * to + target, c != target)
                local(a, b, z_ff.at[n, z], here)

    def pass_ff(n):
        for zs in order:
            block = ff_block(n, g, zs)
            arrived(block, z_ff.at[n, zs], here)
            for r, o in enumerate(others[:2]):
                later.remote(block, block, xy_ff.at[n, r, zs], o, s, here)

    def relay_ff(n):
        for zs in order:
            for r, when in ((0, here), (1, jnp.logical_not(here))):
                arrived(ff_block(n, others[r], zs), xy_ff.at[n, r, zs], when)
                part_ = (f_all, s_all)[n].at[aligned(others[r] % 2, quarter, 16), aligned(2 * zs + r, depth, 128)]
                later.remote(part_, part_, xy_ff.at[n, 2, zs], others[1 - r], s, when)

    def send_third():
        block = t_all.at[:, aligned(g, wide, 128)]
        for r, o in enumerate(others[:2]):
            later.remote(w3, block, xy_ff.at[2, r, 0], o, s)
        local(w3, block, z_ff.at[2, 0])

    def relay_third():
        for r in range(2):
            lanes = aligned(others[r], wide, 128)
            arrived(t_all.at[:, lanes], xy_ff.at[2, r, 0])
            part_ = t_all.at[pl.ds(r * quarter, quarter), lanes]
            later.remote(part_, part_, xy_ff.at[2, 2, 0], others[1 - r], s)

    send_heads(0)
    send_heads(1)
    for b in range(2):

        def norm(at):
            v = x[b, at].astype(jnp.float32)
            return v * lax.rsqrt(mean_square(v) + EPS)

        def keep(at, value):
            n1[b, at] = value.astype(jnp.bfloat16)

        pour(norm, keep, rows // 16)
        first = s * rows

        def masked(i, carry):
            at = aligned(i, 16, 16)
            live = live_rows(first + i * 16, 16, lengths[0, b])
            dm[b, at] = (cot[b, at].astype(jnp.float32) * live).astype(jnp.bfloat16)
            return carry

        lax.fori_loop(0, rows // 16, masked, 0)
    for n, (src, dst) in enumerate(((w1_in, w1_t), (w2_in, w2_t))):
        arrived(src, load.at[n])
        dst[...] = src[...].T
    spread_ff()
    pass_heads(0)
    send_heads(2)
    pass_heads(1)
    send_heads(3)
    for b in range(2):
        gather_n.begin(n1.at[b], own.at[0, b], b)
    pass_heads(2)
    relay_heads(0)
    pass_heads(3)
    send_out()
    relay_heads(1)
    gather_n.step(0, 1)
    gather_n.step(1, 1)
    pass_out()
    relay_heads(2)
    gather_n.step(0, 2)
    gather_n.step(1, 2)
    relay_heads(3)
    relay_out()
    gather_n.step(0, 3)
    gather_n.step(1, 3)
    send_ff(0)
    send_ff(1)
    send_third()
    over = others[2]
    for n, (_, dst) in enumerate(heads):
        for zs in range(4):
            block = dst.at[pl.ds(zs * 2 * depth, 2 * depth), aligned(over % 2, head, head)]
            arrived(block, xy_head.at[n, 2, zs], over // 2 == c)
    arrived(o_all.at[:, aligned(over, wide, 128)], xy_out.at[2])
    for n, (_, dst) in enumerate(heads):
        local(dst, wa_v.at[n], load.at[n])
    local(o_all, wo_v, load.at[4])
    for b in range(2):
        gather_n.finish(own.at[0, b], b)
        local(n1_all.at[b], a_v.at[at_b(b)], load.at[5 + b])
    for j in range(2):
        table[j] = decay_table(decay[4 * (2 * c + j) + z], length)
    for n in range(4):
        arrived(wa_v.at[n], load.at[n])
    arrived(wo_v, load.at[4])

    def scatters_of(copies, first, queue):
        kept = (side, inbox, side_sem, line_sem) if first else (side_m, inbox_m, side_sem_m, line_sem_m)
        return [LineScatter(copies[b], part.at[b], rows, *[k.at[b] for k in kept], queue) for b in range(2)]

    copies.finish()
    scatters = scatters_of(early, True, {})
    for b in range(2):
        arrived(a_v.at[at_b(b)], load.at[5 + b])
        if b == 1:
            for j in range(2):
                arrived(pre.at[j], pre_sem.at[j])

        def project(i, carry):
            at = aligned(i, half, 16)
            from_ = aligned(2 * b + i, half, 16)
            for n in range(4):
                value = product(a_v[from_], wa_v[n])
                for j in range(2):
                    pre[j, n, at] = value[:, j * head : (j + 1) * head]
            return carry

        lax.fori_loop(0, 2, project, 0)
        if b == 1:
            scatters[0].start(1)
        live = live_rows(0, length, lengths[0, b])
        square = 0.0
        for j in range(2):
            q = silu(pre[j, 0]).astype(jnp.bfloat16)
            k = (silu(pre[j, 1]) * live).astype(jnp.bfloat16)
            v = (silu(pre[j, 2]) * live).astype(jnp.bfloat16)
            scores = (product_right(q, k) * table[j]).astype(jnp.bfloat16)
            attended = product(scores, v)
            pre[j, 4] = attended
            gated = silu(pre[j, 3]) * attended
            square = square + jnp.sum(gated * gated, axis=-1, keepdims=True)
            low_v[:, pl.ds(j * head, head)] = gated.astype(jnp.bfloat16)
            local(pre.at[j], pre_all.at[b, j], pre_sem.at[j])
        row = jnp.broadcast_to(square, (length, 128)).T[:8]
        for to in range(8):
            squares[b, to, :, :rows] = row[:, to * rows : (to + 1) * rows]
        everyone_on_line(later, squares, inbox_sq.at[b], sq_sem.at[b], g, s, lambda to: squares.at[b, to])
        local(squares.at[b, s], inbox_sq.at[b, s], sq_sem.at[b, 7])

        def out_part(i, carry):
            at = aligned(i, 256, 256)
            part[b, :, at] = product(low_v[...], wo_v[:, at]).astype(jnp.bfloat16)
            return carry

        lax.fori_loop(0, width // 256, out_part, 0)
        scatters[b].begin()
        if b == 0:
            scatters[0].start(0)

    def hidden_state(b):
        for d in range(8):
            arrived(inbox_sq.at[b, 0], sq_sem.at[b, d])
        total = inbox_sq[b, 0]
        for d in range(1, 8):
            total = total + inbox_sq[b, d]
        row = lax.rsqrt(total / width + EPS)
        scale[b] = row
        column[b] = jnp.broadcast_to(row[:1], (128, 128)).T
        scatter = scatters[b]
        scatter.receive()

        def finish(i, carry):
            piece = aligned(i, 16, 16)
            at = aligned(b * (rows // 16) + i, 16, 16)
            a = scatter.total(piece) * column[b, piece, :1]
            value = x[b, piece].astype(jnp.float32) + a
            h[at] = value
            n2[b, piece] = (value * lax.rsqrt(mean_square(value) + EPS)).astype(jnp.bfloat16)
            return carry

        lax.fori_loop(0, rows // 16, finish, 0)
        gather_m.begin(n2.at[b], own.at[2, b], b)

    gather_d.begin(dm.at[0], own.at[1, 0], 0)
    scatters[0].hop(0)
    relay_third()
    scatters[0].start(2)
    scatters[0].hop(1)
    pass_ff(0)
    scatters[1].start(0)
    scatters[0].hop(2)
    pass_ff(1)
    gather_d.step(0, 1)
    hidden_state(0)
    scatters[1].start(1)
    scatters[1].hop(0)
    relay_ff(0)
    gather_d.step(0, 2)
    scatters[1].start(2)
    scatters[1].hop(1)
    gather_m.step(0, 1)
    scatters[1].hop(2)
    gather_d.step(0, 3)
    gather_m.step(0, 2)
    gather_d.begin(dm.at[1], own.at[1, 1], 1)
    hidden_state(1)
    gather_m.step(0, 3)
    relay_ff(1)
    gather_d.finish(own.at[1, 0], 0)
    local(dm_all.at[0], b_v.at[at_b(0)], load.at[2])
    gather_m.finish(own.at[2, 0], 0)
    local(n2_all.at[0], a_v.at[at_b(0)], load.at[0])
    gather_d.step(1, 1)
    gather_m.step(1, 1)
    turned_out.finish()
    for n, (dst, room) in enumerate(((f_all, w1_f), (s_all, w2_f), (t_all, w3_f))):
        if n < 2:
            for zs in range(4):
                arrived(ff_block(n, over, zs), xy_ff.at[n, 2, zs], over // 2 == c)
        else:
            arrived(dst.at[:, aligned(over, wide, 128)], xy_ff.at[2, 2, 0])
        if n == 2:
            arrived(dst.at[:, aligned(g, wide, 128)], z_ff.at[2, 0])
        local(dst, room, load.at[4 + n])
    for b in range(2):
        early[b].finish()

    def feed_forward(b):
        def tile(i, carry):
            at = aligned(b * 2 + i, half, 16)
            first = product_right(a_v[at], w1_f[...])
            second = product_right(a_v[at], w2_f[...])
            back = product_right(b_v[at], w3_f[...])
            p_v[0, at] = (back * second).astype(jnp.bfloat16)
            p_v[1, at] = (back * first).astype(jnp.bfloat16)
            p_v[2, at] = (first * second).astype(jnp.bfloat16)
            return carry

        lax.fori_loop(0, 2, tile, 0)

    def norm_part(b):
        def body(at, i):
            value = product(p_v[0, at_b(b)], w1_f[:, at]) + product(p_v[1, at_b(b)], w2_f[:, at])
            part[b, :, at] = value.astype(jnp.bfloat16)

        tiles_of(width, body)

    def mixed_part(b):
        def body(at, i):
            part[b, :, at] = product(p_v[2, at_b(b)], w3_f[:, at]).astype(jnp.bfloat16)

        tiles_of(width, body)

    half_w = width // 2
    groups_f = [GroupSum(bulk, w_v.at[pl.ds(n * hidden, hidden)], in_f.at[n], xy_f.at[n]) for n in range(2)]
    groups_t = ColumnSum(bulk, w_v.at[pl.ds(2 * hidden, hidden)], in_t, xy_t)

    def rooms_ff(ref):
        return ref.at[pl.ds(0, hidden), pl.ds(0, half_w)], ref.at[pl.ds(0, quarter), pl.ds(half_w, half_w)]

    def spread_place(i):
        return pl.ds(pl.multiple_of((i % 2) * half_w + (i // 2) * 256, 256), 256)

    def weight_part(n, operand):
        turn(turned, lambda t: p_v[n, t], tokens // 128, hidden)

        def body(at, i):
            place = spread_place(i) if n < 2 else at
            w_v[pl.ds(n * hidden, hidden), place] = product(turned[...], operand[:, at]).astype(jnp.bfloat16)

        tiles_of(width, body)
        if n < 2:
            groups_f[n].depart()
        else:
            groups_t.depart()

    def hidden_gradient(b):
        scatter = second[b]
        scatter.receive()

        def finish(i, carry):
            piece = aligned(i, 16, 16)
            at = aligned(b * (rows // 16) + i, 16, 16)
            value = h[at]
            scale_h = lax.rsqrt(mean_square(value) + EPS)
            normed = value * scale_h
            grad = scatter.total(piece)
            along = jnp.mean(normed * grad, axis=-1, keepdims=True)
            live = live_rows(s * rows + i * 16, 16, lengths[0, b])
            upstream = cot[b, piece].astype(jnp.float32) * live
            grad_hidden = upstream + scale_h * (grad - normed * along)
            grad_x[at] = grad_hidden
            low = grad_hidden.astype(jnp.bfloat16)
            da[b, piece] = low
            dot = jnp.mean(low.astype(jnp.float32) * (value - x[b, piece].astype(jnp.float32)), axis=-1, keepdims=True)
            column[b, piece] = jnp.broadcast_to(dot, (16, 128))
            return carry

        lax.fori_loop(0, rows // 16, finish, 0)
        gather_a.begin(da.at[b], own.at[3, b], b)
        mix[b, :, :rows] = column[b].T[:8, :rows]
        for d in range(1, 8):
            last.remote(mix.at[b], mix_in.at[b, s], mix_sem.at[b, d - 1], g, (s + d) % 8)
        local(mix.at[b], mix_in.at[b, s], mix_sem.at[b, 7])

    second = scatters_of(early, True, {})
    for n in (0, 4, 5, 2, 6):
        ref = {0: a_v.at[at_b(0)], 2: b_v.at[at_b(0)], 4: w1_f, 5: w2_f, 6: w3_f}[n]
        arrived(ref, load.at[n])
    feed_forward(0)
    gather_m.step(1, 2)
    gather_d.step(1, 2)
    norm_part(0)
    second[0].begin()
    second[0].start(0)
    gather_m.step(1, 3)
    gather_d.step(1, 3)
    gather_d.finish(own.at[1, 1], 1)
    local(dm_all.at[1], b_v.at[at_b(1)], load.at[3])
    gather_m.finish(own.at[2, 1], 1)
    local(n2_all.at[1], a_v.at[at_b(1)], load.at[1])
    for b in range(2):
        for d in range(1, 8):
            later.remote(scale.at[b], scale_in.at[b, s], sc_sem.at[b, d - 1], g, (s + d) % 8)
        local(scale.at[b], scale_in.at[b, s], sc_sem.at[b, 7])
    second[0].start(1)
    second[0].hop(0)
    arrived(a_v.at[at_b(1)], load.at[1])
    arrived(b_v.at[at_b(1)], load.at[3])
    feed_forward(1)
    second[0].start(2)
    second[0].hop(1)
    second[0].hop(2)
    norm_part(1)
    def load_pre(b, j):
        local(pre_all.at[b, j], pre.at[j], pre_sem.at[j])

    def attention_back(b):
        gather_a.finish(own.at[3, b], b)
        local(da_all.at[b], a_v.at[at_b(b)], load.at[b])
        for d in range(8):
            arrived(mix_in.at[b, 0], mix_sem.at[b, d])
        columns_of(mixed, mix_in, b, rows)
        live = live_rows(0, length, lengths[0, b])
        arrived(a_v.at[at_b(b)], load.at[b])
        for j in range(2):
            arrived(pre.at[j], pre_sem.at[j])
            lanes = pl.ds(j * head, head)
            error = product_right(a_v[at_b(b)], wo_v[pl.ds(j * head, head)])
            q_pre, k_pre, v_pre, u_pre, o = [pre[j, n] for n in range(5)]
            sigma = 1.0 / (1.0 + jnp.exp(-u_pre))
            u = u_pre * sigma
            scale_g = inverse[at_b(b), :1]
            nat = u * o * scale_g
            nat_v(at_b(b))[:, lanes] = nat.astype(jnp.bfloat16)
            dg = scale_g * (error - nat * mixed[:, :1])
            dz(3, at_b(b))[:, lanes] = (dg * o * (sigma * (1.0 + u_pre * (1.0 - sigma)))).astype(jnp.bfloat16)
            do = (dg * u).astype(jnp.bfloat16)
            q = silu(q_pre).astype(jnp.bfloat16)
            k = (silu(k_pre) * live).astype(jnp.bfloat16)
            v = (silu(v_pre) * live).astype(jnp.bfloat16)
            scores = (product_right(k, q) * table[j]).astype(jnp.bfloat16)
            dv = product(scores, do)
            d_scores = (product_right(v, do) * table[j]).astype(jnp.bfloat16)
            dk = product(d_scores, q)
            dq = product_left(d_scores, k)
            dz(0, at_b(b))[:, lanes] = (dq * slope(pre[j, 0])).astype(jnp.bfloat16)
            dz(1, at_b(b))[:, lanes] = (dk * live * slope(pre[j, 1])).astype(jnp.bfloat16)
            dz(2, at_b(b))[:, lanes] = (dv * live * slope(pre[j, 2])).astype(jnp.bfloat16)
            if b == 0:
                load_pre(1, j)

    def first_part(b):
        def body(at, i):
            value = product_right(dz(0, at_b(b))[...], wa_v[0, at])
            for n in range(1, 4):
                value = value + product_right(dz(n, at_b(b))[...], wa_v[n, at])
            part[b, :, at] = value.astype(jnp.bfloat16)

        tiles_of(width, body)

    second[1].begin()
    second[1].start(0)
    hidden_gradient(0)
    weight_part(0, a_v)
    second[1].start(1)
    second[1].hop(0)
    gather_a.step(0, 1)
    third = scatters_of(sums, False, {})
    early[0].finish()
    mixed_part(0)
    third[0].begin()
    third[0].start(0)
    second[1].start(2)
    second[1].hop(1)
    second[1].hop(2)
    third[0].start(1)
    third[0].hop(0)
    gather_a.step(0, 2)
    weight_part(1, a_v)
    hidden_gradient(1)
    third[0].start(2)
    third[0].hop(1)
    groups_f[0].middle(*rooms_ff(a_v), load.at[pl.ds(13, 2)])
    gather_a.step(0, 3)
    third[0].hop(2)
    early[1].finish()
    mixed_part(1)
    third[1].begin()
    third[1].start(0)
    for j in range(2):
        table[j] = turned_table(decay[4 * (2 * c + j) + z], length)
    for b in range(2):
        for d in range(8):
            arrived(scale.at[b], sc_sem.at[b, d])
        columns_of(inverse.at[at_b(b)], scale_in, b, rows)

    for j in range(2):
        arrived(pre.at[j], pre_sem.at[j])
        load_pre(0, j)
    gather_a.step(1, 1)
    third[1].start(1)
    third[1].hop(0)
    weight_part(2, b_v)
    gather_a.step(1, 2)
    third[1].start(2)
    third[1].hop(1)
    third[1].hop(2)
    groups_f[1].middle(*rooms_ff(b_v), load.at[pl.ds(13, 2)])
    for b in range(2):
        local(n1_all.at[b], b_v.at[at_b(b)], load.at[2 + b])
    later.finish()
    attention_back(0)
    gather_a.step(1, 3)
    def sum_ff(n):
        small = w_v.at[pl.ds(n * hidden, quarter), pl.ds(half_w, half_w)]
        groups_f[n].settle()
        total = w_v.at[pl.ds(n * hidden, quarter), pl.ds(0, half_w)]
        groups_f[n].final(total, small, load.at[pl.ds(13, 2)])
        for d in (2, 1, 3, 0):
            chip = (z + d) % 4
            src = total.at[:, aligned(chip, depth, 128)]
            if d:
                last.remote(src, y_f.at[n, z], z_f.at[n, z], g, 2 * chip + c)
            else:
                local(src, y_f.at[n, z], z_f.at[n, z])

    def join_ff(n, result):
        for r, o in enumerate(others + (g,)):
            arrived(y_f.at[n, o], z_f.at[n, o])
            dst = result.at[aligned(g, quarter, 16)]
            if r < 3:
                last.remote(y_f.at[n, o], dst, join_f.at[n, r], o, s)
            else:
                local(y_f.at[n, o], dst, join_f.at[n, r])

    def rooms_column(rows):
        return [b_v.at[pl.ds(0, rows), pl.ds(i * wide, wide)] for i in range(4)]

    def sum_third():
        groups_t.final(rooms_column(quarter), load.at[pl.ds(13, 4)])
        local(w_v.at[pl.ds(2 * hidden, hidden), aligned(g, wide, 128)], ft, z_t)

    groups_h = [GroupSum(last, grads_h.at[n], in_h.at[n], xy_h.at[n]) for n in range(4)]
    groups_o = ColumnSum(last, go_v, in_o, xy_o)

    def room_h(first, count):
        return w_v.at[pl.ds(first * head, count * head), pl.ds(half_w, half_w)]

    def middle_head(n):
        groups_h[n].middle(room_h(3 * (n % 2), 2), room_h(3 * (n % 2) + 2, 1), load.at[pl.ds(18, 2)])

    def head_part(n):
        turn(turned, lambda t: dz(n, t)[...], tokens // 128, 2 * head)

        def body(at, i):
            grads_h[n, :, spread_place(i)] = product(turned[pl.ds(0, 2 * head)], b_v[:, at]).astype(jnp.bfloat16)

        tiles_of(width, body)

    def out_weight():
        turn(turned, lambda t: nat_v(t)[...], tokens // 128, 2 * head)

        def body(at, i):
            go_v[:, at] = product(turned[pl.ds(0, 2 * head)], a_v[:, at]).astype(jnp.bfloat16)

        tiles_of(width, body)

    def sum_head(n, result):
        total = room_h(6 + n, 1)
        groups_h[n].final(total, room_h(10, 1), load.at[pl.ds(18, 2)])
        for d in (2, 1, 3, 0):
            chip = (z + d) % 4
            src = total.at[:, aligned(chip, depth, 128)]
            dst = result.at[aligned(z, head, head)]
            if d:
                last.remote(src, dst, z_h.at[n, d], g, 2 * chip + c)
            else:
                local(src, dst, z_h.at[n, d])

    def sum_out():
        groups_o.final(rooms_column(head), load.at[pl.ds(13, 4)])
        mine_o = go_v.at[:, aligned(g, wide, 128)]
        for j in range(2):
            to = 2 * (2 * c + j) + z // 2
            src = mine_o.at[pl.ds(j * head, head)]
            dst = fo.at[aligned(z % 2, head, head)]
            last.remote(src, dst, z_o.at[z % 2], g, to, to != s)
            local(src, dst, z_o.at[z % 2], to == s)

    sum_ff(0)
    attention_back(1)
    for b in range(2):
        arrived(b_v.at[at_b(b)], load.at[2 + b])
    head_part(0)
    groups_h[0].depart()
    for b in range(2):
        third[b].receive()
        scatter = third[b]

        def result(i, carry):
            piece = aligned(i, 16, 16)
            at = aligned(b * (rows // 16) + i, 16, 16)
            out[at] = (h[at] + scatter.total(piece)).astype(jnp.bfloat16)
            return carry

        lax.fori_loop(0, rows // 16, result, 0)
    for b in range(2):
        sums[b].finish()
    fourth = scatters_of(early, True, {})
    first_part(0)
    fourth[0].begin()
    fourth[0].start(0)
    head_part(1)
    groups_h[1].depart()
    sum_ff(1)
    groups_t.middle(
        [w_v.at[pl.ds(0, quarter), pl.ds(half_w + k * wide, wide)] for k in range(2)], load.at[pl.ds(13, 2)]
    )
    first_part(1)
    fourth[0].start(1)
    fourth[0].hop(0)
    fourth[1].begin()
    head_part(2)
    fourth[0].start(2)
    fourth[0].hop(1)
    middle_head(0)
    groups_h[2].depart()
    head_part(3)
    middle_head(1)
    groups_h[3].depart()
    fourth[0].hop(2)
    fourth[1].start(0)
    out_weight()
    groups_o.depart()
    middle_head(2)
    fourth[1].start(1)
    fourth[1].hop(0)
    middle_head(3)
    sum_head(0, fq)
    groups_o.middle(rooms_column(head), load.at[pl.ds(13, 2)])
    join_ff(0, ff_)
    join_ff(1, fs)
    sum_head(1, fk)
    fourth[1].start(2)
    fourth[1].hop(1)
    fourth[1].hop(2)
    sum_third()
    sum_head(2, fv)
    sum_head(3, fu)
    for b in range(2):
        fourth[b].receive()
        scatter = fourth[b]

        def finish_x(i, carry):
            piece = aligned(i, 16, 16)
            at = aligned(b * (rows // 16) + i, 16, 16)
            v = x[b, piece].astype(jnp.float32)
            scale_x = lax.rsqrt(mean_square(v) + EPS)
            normed = v * scale_x
            grad = scatter.total(piece)
            along = jnp.mean(normed * grad, axis=-1, keepdims=True)
            grad_x[at] = grad_x[at] + scale_x * (grad - normed * along)
            return carry

        lax.fori_loop(0, rows // 16, finish_x, 0)

    sum_out()

    for n, result in enumerate((ff_, fs)):
        for r in range(4):
            arrived(result.at[pl.ds(0, quarter)], join_f.at[n, r])
    arrived(ft, z_t)
    for j in range(2):
        arrived(fo.at[pl.ds(0, head)], z_o.at[j])
    for n, result in enumerate((fq, fk, fv, fu)):
        for d in range(4):
            arrived(result.at[pl.ds(0, head)], z_h.at[n, d])
    for b in range(2):
        early[b].finish()
    bulk.finish()
    last.finish()
    copies.finish()


def call(kernel, number, ins, outs, scratch, name):
    return pl.pallas_call(
        kernel,
        out_shape=[shape for shape, _ in outs],
        in_specs=[spec for _, spec in ins],
        out_specs=[spec for _, spec in outs],
        scratch_shapes=scratch,
        compiler_params=pltpu.CompilerParams(
            collective_id=number, has_side_effects=True, vmem_limit_bytes=64 * 2**20 - 2**17
        ),
        name=name,
    )(*[value for value, _ in ins])


def finish_arrays(count, turned_count, *refs):
    ins, outs, held, done = refs[:count], refs[count : 2 * count], refs[2 * count : 3 * count], refs[3 * count : 4 * count]
    in_sem, out_sem = refs[4 * count :]
    for i in range(count):
        local(ins[i], held[i], in_sem.at[i])
    for i in range(count):
        arrived(held[i], in_sem.at[i])
        if i < 2:
            local(held[i], outs[i], out_sem.at[i])
            continue
        if i < 2 + turned_count:
            done[i][...] = held[i][...].T.astype(jnp.float32)
        else:

            def write(at, value):
                done[i][at] = value

            pour(lambda at: held[i][at].astype(jnp.float32), write, held[i].shape[0] // 16)
        local(done[i], outs[i], out_sem.at[i])
    for i in range(count):
        arrived(outs[i], out_sem.at[i])


def finished(out, grad_x, turned, straight):
    arrays = [out, grad_x] + turned + straight
    shapes = [jax.ShapeDtypeStruct(v.shape, v.dtype) for v in (out, grad_x)]
    shapes += [wide_array(*v.shape[::-1]) for v in turned] + [wide_array(*v.shape) for v in straight]
    count = len(arrays)
    small = jax.ShapeDtypeStruct((8, 128), jnp.float32)
    done = [small, small] + shapes[2:]
    return pl.pallas_call(
        functools.partial(finish_arrays, count, len(turned)),
        out_shape=shapes,
        in_specs=[ANY] * count,
        out_specs=[ANY] * count,
        scratch_shapes=[pltpu.VMEM(v.shape, v.dtype) for v in arrays] + [pltpu.VMEM(v.shape, v.dtype) for v in done]
        + [dma(count), dma(count)],
        compiler_params=pltpu.CompilerParams(vmem_limit_bytes=62 * 2**20),
        name="finish_arrays",
    )(*arrays)


def low_array(*shape):
    return jax.ShapeDtypeStruct(shape, jnp.bfloat16)


def wide_array(*shape):
    return jax.ShapeDtypeStruct(shape, jnp.float32)


def dma(*shape):
    return pltpu.SemaphoreType.DMA(shape)


def scatter_scratch(rows, width):
    return [
        pltpu.VMEM((2, 4, rows, width), jnp.bfloat16),
        pltpu.VMEM((2, 2, 3, rows, width), jnp.bfloat16),
        dma(2, 4),
        dma(2, 2, 3),
    ]


def line_shards(
    tokens, cotangent, lengths, decay_rate,
    w_query, w_key, w_value, w_gate, w_out, w_first, w_second, w_third,
):
    bf16, f32 = jnp.bfloat16, jnp.float32
    rows, width = tokens.shape[2], tokens.shape[3]
    depth, wide = w_query.shape
    head = width // decay_rate.shape[0]
    hidden = w_third.shape[0]
    length = 8 * rows
    x_low = tokens[:, 0]
    in_smem = pl.BlockSpec(memory_space=pltpu.SMEM)
    gathered = low_array(2, length, width)
    out, grad_x, fq, fk, fv, fu, fo, ff, fs, ft = call(
        layer_part,
        0,
        [(lengths.T, in_smem), (decay_rate, in_smem), (x_low, VMEM), (cotangent[:, 0], VMEM)]
        + [(v, ANY) for v in (w_query, w_key, w_value, w_gate, w_out, w_first, w_second, w_third)],
        [(low_array(2 * rows, width), VMEM), (wide_array(2 * rows, width), VMEM)]
        + [(low_array(wide, depth), ANY)] * 4 + [(low_array(depth, wide), ANY)]
        + [(low_array(2 * hidden, depth), ANY)] * 2 + [(low_array(hidden, wide), ANY)]
        + [(gathered, ANY)] * 4
        + [(low_array(width, 2 * head), ANY)] * 4
        + [(low_array(2 * head, width), ANY)]
        + [(low_array(hidden, width), ANY)] * 3
        + [(wide_array(2, 2, 5, length, head), ANY)]
        + [(low_array(2, 5 * hidden // 2, width // 2), ANY), (low_array(2, 3, hidden // 2, wide), ANY), (low_array(2, 3, head, wide), ANY),
           (low_array(4, 5 * head, width // 2), ANY)]
        + [(low_array(2, 4, hidden // 2, depth), ANY)] * 2,
        [dma(200), dma(26), dma(4, 2)] + [dma(2, 2, 3), dma(2, 7)] * 4
        + [dma(4, 4), dma(2), dma(3, 4), dma(4, 3, 4), dma(3), dma(3, 3, 4), dma(2, 4), dma(2, 4)]
        + [pltpu.VMEM((2, rows, width), bf16)] * 4
        + [pltpu.VMEM((2 * rows, width), f32),
           pltpu.VMEM((2 * length, width), bf16), pltpu.VMEM((2 * length, width), bf16), pltpu.VMEM((3 * hidden, width), bf16),
           pltpu.VMEM((4, width, 2 * head), bf16), pltpu.VMEM((2 * head, width), bf16),
           pltpu.VMEM((3, 2 * length, hidden), bf16), pltpu.VMEM((hidden, 2 * length), bf16),
           pltpu.VMEM((2, length, width), bf16)]
        + scatter_scratch(rows, width) + scatter_scratch(rows, width)
        + [pltpu.VMEM((2, length, length), f32), pltpu.VMEM((2, 8, 8, 128), f32), pltpu.VMEM((2, 8, 8, 128), f32),
           pltpu.VMEM((2, 8, 128), f32), pltpu.VMEM((2, 8, 8, 128), f32), dma(2, 8), dma(2, 8), pltpu.VMEM((2, 128, 128), f32),
           pltpu.VMEM((2, 8, 128), f32), pltpu.VMEM((2, 8, 8, 128), f32), dma(2, 8),
           pltpu.VMEM((2 * length, 128), f32), pltpu.VMEM((length, 128), f32),
           pltpu.VMEM((2, 5, length, head), f32), dma(2),
           pltpu.VMEM((2 * head, width), bf16), pltpu.VMEM((4, 2 * head, width), bf16),
           dma(2, 4), dma(2, 3), dma(2, 3), dma(4, 4), dma(2, 4), dma(), dma(2), dma(4, 4)],
        "layer_part",
    )[:10]
    results = finished(out, grad_x, [fq, fk, fv, fu, ff, fs], [fo, ft])
    out, grad_x, fq, fk, fv, fu, ff, fs, fo, ft = results
    return (out.reshape(2, 1, rows, width), grad_x.reshape(2, 1, rows, width), fq, fk, fv, fu, fo, ff, fs, ft)


def solution(mesh):
    in_specs = (
        P(None, "grp", "seq", None),
        P(None, "grp", "seq", None),
        P(None, "grp"),
        P(),
        P("seq", "grp"),
        P("seq", "grp"),
        P("seq", "grp"),
        P("seq", "grp"),
        P("seq", "grp"),
        P("seq", "grp"),
        P("seq", "grp"),
        P("seq", "grp"),
    )
    out_specs = (
        P(None, "grp", "seq", None),
        P(None, "grp", "seq", None),
        P("seq", "grp"),
        P("seq", "grp"),
        P("seq", "grp"),
        P("seq", "grp"),
        P("seq", "grp"),
        P("seq", "grp"),
        P("seq", "grp"),
        P("seq", "grp"),
    )
    fast = mesh.shape["grp"] == 4 and mesh.shape["seq"] == 8
    return jax.shard_map(line_shards if fast else shards, mesh=mesh, in_specs=in_specs, out_specs=out_specs, check_vma=False)
```

```python
import functools

import jax
import jax.numpy as jnp
from jax import lax
from jax.experimental import pallas as pl
from jax.experimental.pallas import tpu as pltpu
from jax.sharding import PartitionSpec as P

EPS = 1e-06
HIGH = lax.Precision.HIGHEST
MESH = pl.DeviceIdType.MESH
ANY = pl.BlockSpec(memory_space=pl.ANY)
VMEM = pl.BlockSpec(memory_space=pltpu.VMEM)


def prefix(value, axis, join, neutral, backward):
    count, mine = (lax.axis_size(axis), lax.axis_index(axis))
    pieces = jax.tree.map(lambda part: lax.all_gather(part, axis), value)
    if backward:
        pieces = jax.tree.map(lambda part: part[::-1], pieces)
        mine = count - 1 - mine
    subtotal = jax.tree.map(
        lambda part, zero: jnp.full_like(part, 0) + jnp.asarray(zero, part.dtype), value, neutral
    )

    def step(position, subtotal):
        longer = join(subtotal, jax.tree.map(lambda part: part[position], pieces))
        return jax.tree.map(lambda new, old: jnp.where(position < mine, new, old), longer, subtotal)

    return lax.fori_loop(0, count - 1, step, subtotal)


def norm_rows(values):
    return values * lax.rsqrt(jnp.mean(values * values, axis=-1, keepdims=True) + EPS)


def norm_back(values, gradient):
    _, pull = jax.vjp(norm_rows, values)
    return pull(gradient)[0]


def silu_slope(values):
    sigma = jax.nn.sigmoid(values)
    return sigma * (1.0 + values * (1.0 - sigma))


def product(left, right):
    return jnp.dot(left, right, preferred_element_type=jnp.float32)


def product_left(left, right):
    return lax.dot_general(
        left, right, (((0,), (0,)), ((), ())), preferred_element_type=jnp.float32
    )


def product_right(left, right):
    return lax.dot_general(
        left, right, (((1,), (1,)), ((), ())), preferred_element_type=jnp.float32
    )


def combine_state(earlier, later):
    return (later[1][:, None, None] * earlier[0] + later[0], earlier[1] * later[1])


def shards(
    tokens,
    cotangent,
    lengths,
    decay_rate,
    w_query,
    w_key,
    w_value,
    w_gate,
    w_out,
    w_first,
    w_second,
    w_third,
):
    micro = tokens.shape[0]
    block_rows = tokens.shape[2]
    width = tokens.shape[3]
    heads = decay_rate.shape[0]
    head_dim = width // heads
    hidden_width = w_third.shape[0] * lax.axis_size("seq")
    places = jnp.arange(block_rows).astype(jnp.float32)
    slot_index = lax.axis_index("seq") * block_rows + jnp.arange(block_rows)
    offset = places[:, None] - places[None, :]
    weight = jnp.where(
        offset[None] >= 0, jnp.exp(-decay_rate[:, None, None] * jnp.maximum(offset, 0.0)[None]), 0.0
    )
    query_fac = jnp.exp(-decay_rate[None, :] * (places[:, None] + 1.0))[:, :, None]
    key_fac = jnp.exp(-decay_rate[None, :] * (block_rows - 1.0 - places[:, None]))[:, :, None]
    step_decay = jnp.exp(-decay_rate * block_rows)
    empty_state = jnp.zeros((heads, head_dim, head_dim), jnp.float32)
    unit_decay = jnp.ones((heads,), jnp.float32)
    partial_rows = (
        lax.all_gather(w_query, "grp", axis=1, tiled=True),
        lax.all_gather(w_key, "grp", axis=1, tiled=True),
        lax.all_gather(w_value, "grp", axis=1, tiled=True),
        lax.all_gather(w_gate, "grp", axis=1, tiled=True),
        lax.all_gather(w_out, "grp", axis=1, tiled=True),
        lax.all_gather(w_first, "grp", axis=1, tiled=True),
        lax.all_gather(w_second, "grp", axis=1, tiled=True),
        lax.all_gather(w_third, "grp", axis=1, tiled=True),
    )
    gathered = (
        lax.all_gather(partial_rows[0], "seq", axis=0, tiled=True),
        lax.all_gather(partial_rows[1], "seq", axis=0, tiled=True),
        lax.all_gather(partial_rows[2], "seq", axis=0, tiled=True),
        lax.all_gather(partial_rows[3], "seq", axis=0, tiled=True),
        lax.all_gather(partial_rows[4], "seq", axis=0, tiled=True),
        lax.all_gather(partial_rows[5], "seq", axis=0, tiled=True),
        lax.all_gather(partial_rows[6], "seq", axis=0, tiled=True),
        lax.all_gather(partial_rows[7], "seq", axis=0, tiled=True),
    )
    outputs = []
    input_grads = []
    first_norms = []
    attn_rows = []
    normed_rows = []
    branch_rows = []
    second_norms = []
    ffn_rows = []
    mixed_rows = []
    upstream_rows = []
    for batch_idx in range(micro):
        wq_full, wk_full, wv_full, wu_full, wo_full, first_full, second_full, third_full = gathered
        inputs = tokens[batch_idx, 0].astype(jnp.float32)
        live = (slot_index < lengths[batch_idx, 0]).astype(jnp.float32)[:, None]
        live_low = live.astype(jnp.bfloat16)
        first_norm = norm_rows(inputs).astype(jnp.bfloat16)
        query_pre = product(first_norm, wq_full)
        key_pre = product(first_norm, wk_full)
        value_pre = product(first_norm, wv_full)
        gate_pre = product(first_norm, wu_full)
        queries = jax.nn.silu(query_pre).astype(jnp.bfloat16).reshape(block_rows, heads, head_dim)
        key_heads = (jax.nn.silu(key_pre).astype(jnp.bfloat16) * live_low).reshape(
            block_rows, heads, head_dim
        )
        value_heads = (jax.nn.silu(value_pre).astype(jnp.bfloat16) * live_low).reshape(
            block_rows, heads, head_dim
        )
        query_wide = queries.astype(jnp.float32)
        key_wide = key_heads.astype(jnp.float32)
        value_wide = value_heads.astype(jnp.float32)
        local_state = jnp.einsum("jhd,jhe->hde", key_wide * key_fac, value_wide, precision=HIGH)
        prior_state, _ = prefix(
            (local_state, step_decay), "seq", combine_state, (empty_state, unit_decay), False
        )
        scores = (
            jnp.einsum("ihd,jhd->hij", queries, key_heads, preferred_element_type=jnp.float32)
            * weight
        )
        intra = jnp.einsum("hij,jhe->ihe", scores, value_wide, precision=HIGH)
        inter = jnp.einsum("ihd,hde->ihe", query_wide * query_fac, prior_state, precision=HIGH)
        attended = (intra + inter).reshape(block_rows, width)
        gate_act = jax.nn.silu(gate_pre)
        gated = gate_act * attended
        normed = norm_rows(gated).astype(jnp.bfloat16)
        hidden = inputs + product(normed, wo_full)
        second_norm = norm_rows(hidden).astype(jnp.bfloat16)
        first_proj = product(second_norm, first_full)
        second_proj = product(second_norm, second_full)
        mixed_in = (first_proj * second_proj).astype(jnp.bfloat16)
        result = hidden + product(mixed_in, third_full)
        outputs.append(result.astype(jnp.bfloat16))
        upstream = cotangent[batch_idx, 0].astype(jnp.float32) * live
        upstream_low = upstream.astype(jnp.bfloat16)
        grad_mixed = product_right(upstream_low, third_full)
        grad_first_proj = (grad_mixed * second_proj).astype(jnp.bfloat16)
        grad_second_proj = (grad_mixed * first_proj).astype(jnp.bfloat16)
        grad_norm_two = product_right(grad_first_proj, first_full) + product_right(
            grad_second_proj, second_full
        )
        grad_hidden = upstream + norm_back(hidden, grad_norm_two)
        grad_branch = grad_hidden.astype(jnp.bfloat16)
        grad_gated = norm_back(gated, product_right(grad_branch, wo_full))
        grad_attended = (grad_gated * gate_act).astype(jnp.bfloat16)
        grad_gate_pre = (grad_gated * attended * silu_slope(gate_pre)).astype(jnp.bfloat16)
        grad_heads = grad_attended.reshape(block_rows, heads, head_dim)
        grad_wide = grad_heads.astype(jnp.float32)
        local_grad = jnp.einsum("ihd,ihe->hde", query_wide * query_fac, grad_wide, precision=HIGH)
        later_grad, _ = prefix(
            (local_grad, step_decay), "seq", combine_state, (empty_state, unit_decay), True
        )
        grad_scores = (
            jnp.einsum("ihe,jhe->hij", grad_heads, value_heads, preferred_element_type=jnp.float32)
            * weight
        )
        grad_queries = jnp.einsum("hij,jhd->ihd", grad_scores, key_wide, precision=HIGH)
        grad_queries = (
            grad_queries
            + jnp.einsum("ihe,hde->ihd", grad_wide, prior_state, precision=HIGH) * query_fac
        )
        grad_keys = jnp.einsum("hij,ihd->jhd", grad_scores, query_wide, precision=HIGH)
        grad_keys = (
            grad_keys + jnp.einsum("hde,jhe->jhd", later_grad, value_wide, precision=HIGH) * key_fac
        )
        grad_values = jnp.einsum("hij,ihe->jhe", scores, grad_wide, precision=HIGH)
        grad_values = (
            grad_values + jnp.einsum("jhd,hde->jhe", key_wide, later_grad, precision=HIGH) * key_fac
        )
        grad_query_pre = (grad_queries.reshape(block_rows, width) * silu_slope(query_pre)).astype(
            jnp.bfloat16
        )
        grad_key_pre = (grad_keys.reshape(block_rows, width) * live * silu_slope(key_pre)).astype(
            jnp.bfloat16
        )
        grad_value_pre = (
            grad_values.reshape(block_rows, width) * live * silu_slope(value_pre)
        ).astype(jnp.bfloat16)
        grad_norm_one = product_right(grad_query_pre, wq_full) + product_right(
            grad_key_pre, wk_full
        )
        grad_norm_one = (
            grad_norm_one
            + product_right(grad_value_pre, wv_full)
            + product_right(grad_gate_pre, wu_full)
        )
        input_grads.append(grad_hidden + norm_back(inputs, grad_norm_one))
        first_norms.append(first_norm)
        attn_rows.append(
            jnp.concatenate([grad_query_pre, grad_key_pre, grad_value_pre, grad_gate_pre], axis=1)
        )
        normed_rows.append(normed)
        branch_rows.append(grad_branch)
        second_norms.append(second_norm)
        ffn_rows.append(jnp.concatenate([grad_first_proj, grad_second_proj], axis=1))
        mixed_rows.append(mixed_in)
        upstream_rows.append(upstream_low)
    first_all = jnp.concatenate(first_norms, axis=0)
    attn_all = jnp.concatenate(attn_rows, axis=0)
    normed_all = jnp.concatenate(normed_rows, axis=0)
    branch_all = jnp.concatenate(branch_rows, axis=0)
    second_all = jnp.concatenate(second_norms, axis=0)
    ffn_all = jnp.concatenate(ffn_rows, axis=0)
    mixed_all = jnp.concatenate(mixed_rows, axis=0)
    upstream_all = jnp.concatenate(upstream_rows, axis=0)
    proj_rows = lax.psum_scatter(
        product_left(first_all, attn_all), "seq", scatter_dimension=0, tiled=True
    )
    outproj_rows = lax.psum_scatter(
        product_left(normed_all, branch_all), "seq", scatter_dimension=0, tiled=True
    )
    ffn_part = lax.psum_scatter(
        product_left(second_all, ffn_all), "seq", scatter_dimension=0, tiled=True
    )
    down_rows = lax.psum_scatter(
        product_left(mixed_all, upstream_all), "seq", scatter_dimension=0, tiled=True
    )
    summed = (
        lax.psum_scatter(proj_rows[:, :width], "grp", scatter_dimension=1, tiled=True),
        lax.psum_scatter(proj_rows[:, width : 2 * width], "grp", scatter_dimension=1, tiled=True),
        lax.psum_scatter(
            proj_rows[:, 2 * width : 3 * width], "grp", scatter_dimension=1, tiled=True
        ),
        lax.psum_scatter(proj_rows[:, 3 * width :], "grp", scatter_dimension=1, tiled=True),
        lax.psum_scatter(outproj_rows, "grp", scatter_dimension=1, tiled=True),
        lax.psum_scatter(ffn_part[:, :hidden_width], "grp", scatter_dimension=1, tiled=True),
        lax.psum_scatter(ffn_part[:, hidden_width:], "grp", scatter_dimension=1, tiled=True),
        lax.psum_scatter(down_rows, "grp", scatter_dimension=1, tiled=True),
    )
    layer_out = jnp.stack(outputs)[:, None]
    grad_tokens = jnp.stack(input_grads)[:, None]
    return (
        layer_out,
        grad_tokens,
        summed[0],
        summed[1],
        summed[2],
        summed[3],
        summed[4],
        summed[5],
        summed[6],
        summed[7],
    )


class Spare:
    def __init__(self, sems):
        self.sems, self.free, self.order = sems, list(range(sems.shape[0])), []


class Copies:
    def __init__(self, spare):
        self.spare = spare
        self.pending = []

    def remote(self, src, dst, recv_sem, group, place, when=None):
        while not self.spare.free:
            owner, entry = self.spare.order.pop(0)
            owner.settle(entry)
        number = self.spare.free.pop(0)
        copy = pltpu.make_async_remote_copy(
            src_ref=src,
            dst_ref=dst,
            send_sem=self.spare.sems.at[number],
            recv_sem=recv_sem,
            device_id=(group, place),
            device_id_type=MESH,
        )
        self.pending.append((copy, when, number))
        self.spare.order.append((self, self.pending[-1]))
        if when is None:
            copy.start()
        else:
            pl.when(when)(copy.start)
        return self.pending[-1]

    def settle(self, entry):
        if not any(other is entry for other in self.pending):
            return
        self.pending = [other for other in self.pending if other is not entry]
        copy, when, number = entry
        if when is None:
            copy.wait_send()
        else:
            pl.when(when)(copy.wait_send)
        self.spare.free.append(number)

    def finish(self):
        while self.pending:
            self.settle(self.pending[0])


def local(src, dst, sem, when=None):
    copy = pltpu.make_async_copy(src, dst, sem)
    if when is None:
        copy.start()
    else:
        pl.when(when)(copy.start)


def arrived(ref, sem, when=None):
    copy = pltpu.make_async_copy(ref, ref, sem)
    if when is None:
        copy.wait()
    else:
        pl.when(when)(copy.wait)


def where_am_i():
    g, s = lax.axis_index("grp"), lax.axis_index("seq")
    return g, s, g // 2, g % 2, s // 2, s % 2


def across(y, x):
    return (y * 2 + 1 - x, (1 - y) * 2 + x, (1 - y) * 2 + 1 - x)


def greet(partners):
    barrier = pltpu.get_barrier_semaphore()
    for partner in partners:
        pl.semaphore_signal(barrier, inc=1, device_id=partner, device_id_type=MESH)
    pl.semaphore_wait(barrier, len(partners))


def aligned(index, unit, step):
    return pl.ds(pl.multiple_of(index * unit, step), unit)


class Gather:
    def __init__(self, copies, out, rows, hop_sem, side_sem):
        self.copies, self.out, self.rows = copies, out, rows
        self.hop_sem, self.side_sem = hop_sem, side_sem
        self.g, self.s, _, _, self.z, self.c = where_am_i()

    def block(self, b, z, core):
        return self.out.at[b, aligned(2 * z + core, self.rows, 16)]

    def spread(self, src, b, z_of, k, right, left):
        g, s, z, c = self.g, self.s, self.z, self.c
        dst = self.block(b, z_of, c)
        if right is not None:
            self.copies.remote(src, dst, self.hop_sem.at[b, 0, k], g, (s + 2) % 8, right)
        if left is not None:
            self.copies.remote(src, dst, self.hop_sem.at[b, 1, k], g, (s + 6) % 8, left)

    def begin(self, src, own_sem, b):
        g, s, z, c = self.g, self.s, self.z, self.c
        self.spread(src, b, z, 0, z < 3, z > 0)
        self.copies.remote(src, self.block(b, z, c), self.side_sem.at[b, 0], g, s + 1 - 2 * c)
        local(src, self.block(b, z, c), own_sem)

    def step(self, b, k):
        g, s, z, c = self.g, self.s, self.z, self.c
        side = s + 1 - 2 * c
        has = z >= k
        at = jnp.maximum(z - k, 0)
        ref = self.block(b, at, c)
        arrived(ref, self.hop_sem.at[b, 0, k - 1], has)
        if k < 3:
            self.spread(ref, b, at, k, jnp.logical_and(has, z < 3), None)
        self.copies.remote(ref, ref, self.side_sem.at[b, k], g, side, has)
        has = z + k <= 3
        at = jnp.minimum(z + k, 3)
        ref = self.block(b, at, c)
        arrived(ref, self.hop_sem.at[b, 1, k - 1], has)
        if k < 3:
            self.spread(ref, b, at, k, None, jnp.logical_and(has, z > 0))
        self.copies.remote(ref, ref, self.side_sem.at[b, 3 + k], g, side, has)

    def finish(self, own_sem, b):
        z, c = self.z, self.c
        arrived(self.block(b, z, c), own_sem)
        arrived(self.block(b, z, 1 - c), self.side_sem.at[b, 0])
        for k in (1, 2, 3):
            arrived(self.block(b, jnp.maximum(z - k, 0), 1 - c), self.side_sem.at[b, k], z >= k)
            arrived(self.block(b, jnp.minimum(z + k, 3), 1 - c), self.side_sem.at[b, 3 + k], z + k <= 3)


def line_partners(g, s):
    return [(g, (s + d) % 8) for d in range(1, 8)]


def add_rows(target, room):
    def write(at, value):
        target[at] = value.astype(jnp.bfloat16)

    pour(lambda at: target[at].astype(jnp.float32) + room[at].astype(jnp.float32), write, target.shape[0] // 16)


class GroupSum:
    def __init__(self, copies, grad, inbox, sem):
        self.copies, self.grad, self.inbox, self.sem = copies, grad, inbox, sem
        self.g, self.s, self.y, self.x, self.z, self.c = where_am_i()
        self.rows, self.half = grad.shape[0] // 2, grad.shape[1] // 2
        self.entries = []

    def block(self, x, core):
        return self.grad.at[aligned(x, self.rows, 16), pl.ds(core * self.half, self.half)]

    def slot(self, first, count=1):
        return self.inbox.at[pl.ds(first * self.rows, count * self.rows)]

    def remote(self, *args):
        self.entries.append(self.copies.remote(*args))

    def depart(self):
        gx, gy, _ = across(self.y, self.x)
        self.remote(self.grad.at[:, pl.ds(0, self.half)], self.slot(0, 2), self.sem.at[0], gy, self.s, self.c != self.y)
        self.remote(self.block(1 - self.x, 1), self.slot(2), self.sem.at[1], gx, self.s)

    def middle(self, room, small, load):
        gx, gy, _ = across(self.y, self.x)
        mine = self.c == self.y
        arrived(self.slot(0, 2), self.sem.at[0], mine)
        local(self.slot(0, 2), room, load.at[0], mine)
        arrived(self.slot(2), self.sem.at[1])
        local(self.slot(2), small, load.at[1])
        arrived(room, load.at[0], mine)

        @pl.when(mine)
        def _():
            add_rows(self.grad.at[:, pl.ds(0, self.half)], room)

        arrived(small, load.at[1])
        add_rows(self.block(self.x, 1), small)
        for core in range(2):
            block = self.block(self.x, core)
            self.remote(
                block, self.slot(3), self.sem.at[2], self.g, 2 * self.z + core, jnp.logical_and(mine, self.c != core)
            )
            local(block, self.slot(3), self.sem.at[2], jnp.logical_and(mine, self.c == core))
        self.remote(self.block(1 - self.x, 0), self.slot(4), self.sem.at[3], gx, 2 * self.z, mine)
        self.remote(self.block(self.x, 1), self.slot(4), self.sem.at[3], gy, 2 * self.z + 1, jnp.logical_not(mine))

    def final(self, room, small, load):
        for i, ref in enumerate((room, small)):
            arrived(self.slot(3 + i), self.sem.at[2 + i])
            local(self.slot(3 + i), ref, load.at[i])
        for i, ref in enumerate((room, small)):
            arrived(ref, load.at[i])
        add_rows(room, small)

    def settle(self):
        for entry in self.entries:
            self.copies.settle(entry)


class ColumnSum:
    def __init__(self, copies, grad, inbox, sem):
        self.copies, self.grad, self.inbox, self.sem = copies, grad, inbox, sem
        self.g, self.s, y, x, _, _ = where_am_i()
        self.others = across(y, x)
        self.rows, self.wide = grad.shape[0] // 2, grad.shape[1] // 4

    def block(self, group, i):
        return self.grad.at[pl.ds(i * self.rows, self.rows), aligned(group, self.wide, 128)]

    def depart(self):
        for i in range(2):
            to = self.others[i]
            for k, group in enumerate((to, self.others[2])):
                self.copies.remote(self.block(group, i), self.inbox.at[i, k], self.sem.at[i, k], to, self.s)

    def middle(self, rooms, load):
        for i in range(2):
            arrived(self.inbox.at[i, 1], self.sem.at[i, 1])
            local(self.inbox.at[i, 1], rooms[i], load.at[i])
        for i in range(2):
            arrived(rooms[i], load.at[i])
            to = self.others[1 - i]
            add_rows(self.block(to, i), rooms[i])
            self.copies.remote(self.block(to, i), self.inbox.at[i, 2], self.sem.at[i, 2], to, self.s)

    def final(self, rooms, load):
        for i in range(2):
            for k in range(2):
                arrived(self.inbox.at[i, 2 * k], self.sem.at[i, 2 * k])
                local(self.inbox.at[i, 2 * k], rooms[2 * i + k], load.at[2 * i + k])
        for i in range(2):
            for k in range(2):
                arrived(rooms[2 * i + k], load.at[2 * i + k])
            mine, first, second = self.block(self.g, i), rooms[2 * i], rooms[2 * i + 1]

            def read(at):
                return mine[at].astype(jnp.float32) + first[at].astype(jnp.float32) + second[at].astype(jnp.float32)

            def write(at, value):
                mine[at] = value.astype(jnp.bfloat16)

            pour(read, write, self.rows // 16)


def everyone_on_line(copies, src, dst, sem, g, s, to_rows):
    for d in range(1, 8):
        to = (s + d) % 8
        copies.remote(to_rows(to), dst.at[s], sem, g, to)


def mean_square(values):
    return jnp.mean(values * values, axis=-1, keepdims=True)


def pour(read, write, count):
    def piece(i, carry):
        at = aligned(i, 16, 16)
        write(at, read(at))
        return carry

    lax.fori_loop(0, count, piece, 0)


class LineScatter:
    def __init__(self, copies, part, rows, side, inbox, side_sem, line_sem, queue):
        self.copies, self.part, self.rows, self.queue = copies, part, rows, queue
        self.side, self.inbox, self.side_sem, self.line_sem = side, inbox, side_sem, line_sem
        self.g, self.s, _, _, self.z, self.c = where_am_i()

    def mine(self, chip):
        return self.part.at[aligned(2 * chip + self.c, self.rows, 16)]

    def begin(self):
        for chip in (3, 0, 2, 1):
            theirs = aligned(2 * chip + 1 - self.c, self.rows, 16)
            self.copies.remote(
                self.part.at[theirs], self.side.at[chip], self.side_sem.at[chip], self.g, self.s + 1 - 2 * self.c
            )

    def add_on(self, chip, way):
        own, side = self.mine(chip), self.side.at[chip]
        slot = chip - 1 if way == 0 else chip
        come = self.inbox.at[way, slot]
        arrived(side, self.side_sem.at[chip])
        arrived(come, self.line_sem.at[way, slot])

        def three(at):
            return own[at].astype(jnp.float32) + side[at].astype(jnp.float32) + come[at].astype(jnp.float32)

        def write(at, value):
            own[at] = value.astype(jnp.bfloat16)

        pour(three, write, self.rows // 16)

    def push(self, chip, way, when):
        slot = chip - 1 if way == 0 else chip
        to = (self.s + 2) % 8 if way == 0 else (self.s + 6) % 8
        return self.copies.remote(
            self.mine(chip), self.inbox.at[way, slot], self.line_sem.at[way, slot], self.g, to, when
        )

    def pass_on(self, chip, way):
        end = self.z == (0 if way == 0 else 3)
        own, side = self.mine(chip), self.side.at[chip]

        def two(at):
            return own[at].astype(jnp.float32) + side[at].astype(jnp.float32)

        def write(at, value):
            own[at] = value.astype(jnp.bfloat16)

        @pl.when(end)
        def _():
            arrived(side, self.side_sem.at[chip])
            pour(two, write, self.rows // 16)

        if way in self.queue:
            copies, entry = self.queue.pop(way)
            copies.settle(entry)
        self.queue[way] = (self.copies, self.push(chip, way, end))

    def start(self, i):
        self.pass_on(3 - i, 0)
        self.pass_on(i, 1)

    def hop(self, i):
        z = self.z
        for inner in (1, 2):

            @pl.when(z == inner)
            def _():
                near = inner == 1
                if i < 2:
                    self.add_on(3 - i if near else i, 0 if near else 1)
                else:
                    self.add_on(0 if near else 3, 1 if near else 0)

        for inner in (1, 2):
            near = inner == 1
            if i < 2:
                self.push(3 - i if near else i, 0 if near else 1, z == inner)
            else:
                self.push(0 if near else 3, 1 if near else 0, z == inner)

    def receive(self):
        z = self.z
        arrived(self.side.at[z], self.side_sem.at[z])
        left, right = jnp.maximum(z - 1, 0), jnp.minimum(z, 2)
        arrived(self.inbox.at[0, left], self.line_sem.at[0, left], z > 0)
        arrived(self.inbox.at[1, right], self.line_sem.at[1, right], z < 3)

    def total(self, at):
        z = self.z
        value = self.mine(z)[at].astype(jnp.float32) + self.side[z, at].astype(jnp.float32)
        from_left = self.inbox[0, jnp.maximum(z - 1, 0), at].astype(jnp.float32)
        from_right = self.inbox[1, jnp.minimum(z, 2), at].astype(jnp.float32)
        return value + jnp.where(z > 0, from_left, 0.0) + jnp.where(z < 3, from_right, 0.0)


def silu(values):
    return values / (1.0 + jnp.exp(-values))


def decay_table(rate, length):
    offset = lax.broadcasted_iota(jnp.int32, (length, length), 0) - lax.broadcasted_iota(jnp.int32, (length, length), 1)
    steps = jnp.maximum(offset, 0).astype(jnp.float32)
    return jnp.where(offset >= 0, jnp.exp(-rate * steps), 0.0)


def live_rows(first, count, length):
    return ((first + lax.broadcasted_iota(jnp.int32, (count, 1), 0)) < length).astype(jnp.float32)


def slope(values):
    sigma = 1.0 / (1.0 + jnp.exp(-values))
    return sigma * (1.0 + values * (1.0 - sigma))


def turned_table(rate, length):
    offset = lax.broadcasted_iota(jnp.int32, (length, length), 1) - lax.broadcasted_iota(jnp.int32, (length, length), 0)
    steps = jnp.maximum(offset, 0).astype(jnp.float32)
    return jnp.where(offset >= 0, jnp.exp(-rate * steps), 0.0)


def columns_of(out, tiles, b, rows):
    for owner in range(8):
        out[pl.ds(owner * rows, rows)] = jnp.broadcast_to(tiles[b, owner, :1], (128, 128)).T[:rows]


def turn(dst, read, count, columns):
    def block(i, carry):
        dst[pl.ds(0, columns), aligned(i, 128, 128)] = read(aligned(i, 128, 128)).T
        return carry

    lax.fori_loop(0, count, block, 0)


def tiles_of(width, body):
    def tile(i, carry):
        body(aligned(i, 256, 256), i)
        return carry

    lax.fori_loop(0, width // 256, tile, 0)


def layer_part(
    lengths, decay, x, cot, wq, wk, wv, wu, wo, w1, w2, w3,
    out, grad_x, fq, fk, fv, fu, fo, ff_, fs, ft,
    n1_all, dm_all, n2_all, da_all, q_all, k_all, v_all, u_all, o_all, f_all, s_all, t_all, pre_all, in_f, in_t, in_o, in_h, x_f, y_f,
    send, load, own, hop_n, side_n, hop_d, side_d, z_head, z_out, z_ff, xy_head, xy_out, xy_ff, spread_f, join_f,
    n1, dm, n2, da, h, a_v, b_v, w_v, wa_v, wo_v, p_v, turned, part, side, inbox, side_sem, line_sem,
    side_m, inbox_m, side_sem_m, line_sem_m, table, squares, inbox_sq, scale, scale_in, sq_sem, sc_sem, column,
    mix, mix_in, mix_sem, inverse, mixed, pre, pre_sem, go_v, grads_h,
    xy_f, xy_t, xy_o, xy_h, z_f, z_t, z_o, z_h,
):
    g, s, y, x_, z, c = where_am_i()
    others = across(y, x_)
    plane = [(o, 2 * z + e) for o in others for e in range(2)]
    rows, width = x.shape[1], x.shape[2]
    length = 8 * rows
    tokens = 2 * length
    depth, wide = wq.shape
    head = q_all.shape[1] // 2
    hidden = f_all.shape[0]
    quarter = hidden // 2
    half = length // 2
    target = g // 2
    mine = aligned(g % 2, head, head)
    here = c == target
    order = [(z + d) % 4 for d in (0, 1, 3, 2)]
    spare = Spare(send)
    copies, later, turned_out, bulk, last = [Copies(spare) for _ in range(5)]
    early, sums = [[Copies(spare) for _ in range(2)] for _ in range(2)]
    gather_n = Gather(copies, n1_all, rows, hop_n, side_n)
    gather_d = Gather(later, dm_all, rows, hop_d, side_d)
    gather_m = Gather(later, n2_all, rows, hop_n, side_n)
    gather_a = Gather(last, da_all, rows, hop_d, side_d)
    heads = list(zip((wq, wk, wv, wu), (q_all, k_all, v_all, u_all)))
    w1_f, w2_f, w3_f = [w_v.at[pl.ds(n * hidden, hidden)] for n in range(3)]
    w1_in, w2_in = [w_v.at[pl.ds(n * depth, depth), pl.ds(512, 2 * hidden)] for n in range(2)]
    w1_t, w2_t = [w_v.at[pl.ds(0, 2 * hidden), pl.ds(n * depth, depth)] for n in range(2)]
    low_v = p_v.at[2, pl.ds(0, length), pl.ds(0, 2 * head)]

    def at_b(b):
        return pl.ds(b * length, length)

    def dz(n, at):
        return p_v.at[n // 2, at, pl.ds((n % 2) * 2 * head, 2 * head)]

    def nat_v(at):
        return p_v.at[2, at, pl.ds(0, 2 * head)]

    local(w1, w1_in, load.at[0])
    local(w2, w2_in, load.at[1])
    greet(line_partners(g, s) + plane)

    def send_heads(n):
        src, dst = heads[n]
        for d in (2, 1, 3, 0):
            to = (z + d) % 4
            a, b = src.at[:, aligned(to, head, head)], dst.at[aligned(s, depth, 16), mine]
            if d:
                copies.remote(a, b, z_head.at[n, z], g, 2 * to + target)
            else:
                copies.remote(a, b, z_head.at[n, z], g, 2 * to + target, c != target)
                local(a, b, z_head.at[n, z], here)

    def pass_heads(n):
        dst = heads[n][1]
        for zs in order:
            block = dst.at[aligned(zs, 2 * depth, 16), mine]
            arrived(block, z_head.at[n, zs], here)
            for r, o in enumerate(others[:2]):
                copies.remote(block, block, xy_head.at[n, r, zs], o, s, here)

    def relay_heads(n):
        dst = heads[n][1]
        for zs in order:
            for r, when in ((0, here), (1, jnp.logical_not(here))):
                lanes = aligned(others[r] % 2, head, head)
                arrived(dst.at[aligned(zs, 2 * depth, 16), lanes], xy_head.at[n, r, zs], when)
                part_ = dst.at[aligned(2 * zs + r, depth, 16), lanes]
                copies.remote(part_, part_, xy_head.at[n, 2, zs], others[1 - r], s, when)

    def send_out():
        for i in range(2):
            to = 2 * c + i
            a = wo.at[pl.ds(i * head, head)]
            b = o_all.at[aligned(z % 2, head, head), aligned(g, wide, 128)]
            self_ = jnp.logical_and(to == z, c == z // 2)
            copies.remote(a, b, z_out.at[z % 2], g, 2 * to + z // 2, jnp.logical_not(self_))
            local(a, b, z_out.at[z % 2], self_)

    def pass_out():
        for j in range(2):
            arrived(o_all.at[pl.ds(j * head, head), aligned(g, wide, 128)], z_out.at[j])
        block = o_all.at[:, aligned(g, wide, 128)]
        for r, o in enumerate(others[:2]):
            copies.remote(block, block, xy_out.at[r], o, s)

    def relay_out():
        for r in range(2):
            lanes = aligned(others[r], wide, 128)
            arrived(o_all.at[:, lanes], xy_out.at[r])
            part_ = o_all.at[pl.ds(r * head, head), lanes]
            copies.remote(part_, part_, xy_out.at[2], others[1 - r], s)

    def spread_ff():
        for n, src in enumerate((w1_t, w2_t)):
            for r, o in enumerate(others):
                turned_out.remote(src.at[aligned(o, quarter, 16)], x_f.at[n, g], spread_f.at[n, r], o, s)
            local(src.at[aligned(g, quarter, 16)], x_f.at[n, g], spread_f.at[n, 3])

    def ff_block(n, group, zs):
        return (f_all, s_all)[n].at[aligned(group % 2, quarter, 16), aligned(zs, 2 * depth, 128)]

    def send_ff(n):
        for r, o in enumerate(others):
            arrived(x_f.at[n, o], spread_f.at[n, r])
        arrived(x_f.at[n, g], spread_f.at[n, 3])
        b = (f_all, s_all)[n].at[aligned(g % 2, quarter, 16), aligned(s, depth, 128)]
        for d in (2, 1, 3, 0):
            to = (z + d) % 4
            a = x_f.at[n, to]
            if d:
                later.remote(a, b, z_ff.at[n, z], g, 2 * to + target)
            else:
                later.remote(a, b, z_ff.at[n, z], g, 2 * to + target, c != target)
                local(a, b, z_ff.at[n, z], here)

    def pass_ff(n):
        for zs in order:
            block = ff_block(n, g, zs)
            arrived(block, z_ff.at[n, zs], here)
            for r, o in enumerate(others[:2]):
                later.remote(block, block, xy_ff.at[n, r, zs], o, s, here)

    def relay_ff(n):
        for zs in order:
            for r, when in ((0, here), (1, jnp.logical_not(here))):
                arrived(ff_block(n, others[r], zs), xy_ff.at[n, r, zs], when)
                part_ = (f_all, s_all)[n].at[aligned(others[r] % 2, quarter, 16), aligned(2 * zs + r, depth, 128)]
                later.remote(part_, part_, xy_ff.at[n, 2, zs], others[1 - r], s, when)

    def send_third():
        block = t_all.at[:, aligned(g, wide, 128)]
        for r, o in enumerate(others[:2]):
            later.remote(w3, block, xy_ff.at[2, r, 0], o, s)
        local(w3, block, z_ff.at[2, 0])

    def relay_third():
        for r in range(2):
            lanes = aligned(others[r], wide, 128)
            arrived(t_all.at[:, lanes], xy_ff.at[2, r, 0])
            part_ = t_all.at[pl.ds(r * quarter, quarter), lanes]
            later.remote(part_, part_, xy_ff.at[2, 2, 0], others[1 - r], s)

    send_heads(0)
    send_heads(1)
    for b in range(2):

        def norm(at):
            v = x[b, at].astype(jnp.float32)
            return v * lax.rsqrt(mean_square(v) + EPS)

        def keep(at, value):
            n1[b, at] = value.astype(jnp.bfloat16)

        pour(norm, keep, rows // 16)
        first = s * rows

        def masked(i, carry):
            at = aligned(i, 16, 16)
            live = live_rows(first + i * 16, 16, lengths[0, b])
            dm[b, at] = (cot[b, at].astype(jnp.float32) * live).astype(jnp.bfloat16)
            return carry

        lax.fori_loop(0, rows // 16, masked, 0)
    for n, (src, dst) in enumerate(((w1_in, w1_t), (w2_in, w2_t))):
        arrived(src, load.at[n])
        dst[...] = src[...].T
    spread_ff()
    pass_heads(0)
    send_heads(2)
    pass_heads(1)
    send_heads(3)
    for b in range(2):
        gather_n.begin(n1.at[b], own.at[0, b], b)
    pass_heads(2)
    relay_heads(0)
    pass_heads(3)
    send_out()
    relay_heads(1)
    gather_n.step(0, 1)
    gather_n.step(1, 1)
    pass_out()
    relay_heads(2)
    gather_n.step(0, 2)
    gather_n.step(1, 2)
    relay_heads(3)
    relay_out()
    gather_n.step(0, 3)
    send_ff(0)
    send_ff(1)
    send_third()
    over = others[2]
    for n, (_, dst) in enumerate(heads):
        for zs in range(4):
            block = dst.at[pl.ds(zs * 2 * depth, 2 * depth), aligned(over % 2, head, head)]
            arrived(block, xy_head.at[n, 2, zs], over // 2 == c)
    arrived(o_all.at[:, aligned(over, wide, 128)], xy_out.at[2])
    for n, (_, dst) in enumerate(heads):
        local(dst, wa_v.at[n], load.at[n])
    local(o_all, wo_v, load.at[4])
    gather_n.finish(own.at[0, 0], 0)
    local(n1_all.at[0], a_v.at[at_b(0)], load.at[5])
    for j in range(2):
        table[j] = decay_table(decay[4 * (2 * c + j) + z], length)
    for n in range(4):
        arrived(wa_v.at[n], load.at[n])
    arrived(wo_v, load.at[4])

    def scatters_of(copies, first, queue):
        kept = (side, inbox, side_sem, line_sem) if first else (side_m, inbox_m, side_sem_m, line_sem_m)
        return [LineScatter(copies[b], part.at[b], rows, *[k.at[b] for k in kept], queue) for b in range(2)]

    scatters = scatters_of(early, True, {})
    for b in range(2):
        if b == 1:
            gather_n.step(1, 3)
            gather_n.finish(own.at[0, 1], 1)
            local(n1_all.at[1], a_v.at[at_b(1)], load.at[6])
        arrived(a_v.at[at_b(b)], load.at[5 + b])
        if b == 1:
            for j in range(2):
                arrived(pre.at[j], pre_sem.at[j])

        def project(i, carry):
            at = aligned(i, half, 16)
            from_ = aligned(2 * b + i, half, 16)
            for n in range(4):
                value = product(a_v[from_], wa_v[n])
                for j in range(2):
                    pre[j, n, at] = value[:, j * head : (j + 1) * head]
            return carry

        lax.fori_loop(0, 2, project, 0)
        if b == 1:
            scatters[0].start(1)
        live = live_rows(0, length, lengths[0, b])
        square = 0.0
        for j in range(2):
            q = silu(pre[j, 0]).astype(jnp.bfloat16)
            k = (silu(pre[j, 1]) * live).astype(jnp.bfloat16)
            v = (silu(pre[j, 2]) * live).astype(jnp.bfloat16)
            scores = (product_right(q, k) * table[j]).astype(jnp.bfloat16)
            attended = product(scores, v)
            pre[j, 4] = attended
            gated = silu(pre[j, 3]) * attended
            square = square + jnp.sum(gated * gated, axis=-1, keepdims=True)
            low_v[:, pl.ds(j * head, head)] = gated.astype(jnp.bfloat16)
            local(pre.at[j], pre_all.at[b, j], pre_sem.at[j])
        row = jnp.broadcast_to(square, (length, 128)).T[:8]
        for to in range(8):
            squares[b, to, :, :rows] = row[:, to * rows : (to + 1) * rows]
        everyone_on_line(later, squares, inbox_sq.at[b], sq_sem.at[b], g, s, lambda to: squares.at[b, to])
        local(squares.at[b, s], inbox_sq.at[b, s], sq_sem.at[b])

        def out_part(i, carry):
            at = aligned(i, 256, 256)
            part[b, :, at] = product(low_v[...], wo_v[:, at]).astype(jnp.bfloat16)
            return carry

        lax.fori_loop(0, width // 256, out_part, 0)
        scatters[b].begin()
        if b == 0:
            scatters[0].start(0)

    def hidden_state(b):
        arrived(inbox_sq.at[b], sq_sem.at[b])
        total = inbox_sq[b, 0]
        for d in range(1, 8):
            total = total + inbox_sq[b, d]
        row = lax.rsqrt(total / width + EPS)
        scale[b] = row
        column[b] = jnp.broadcast_to(row[:1], (128, 128)).T
        scatter = scatters[b]
        scatter.receive()

        def finish(i, carry):
            piece = aligned(i, 16, 16)
            at = aligned(b * (rows // 16) + i, 16, 16)
            a = scatter.total(piece) * column[b, piece, :1]
            value = x[b, piece].astype(jnp.float32) + a
            h[at] = value
            n2[b, piece] = (value * lax.rsqrt(mean_square(value) + EPS)).astype(jnp.bfloat16)
            return carry

        lax.fori_loop(0, rows // 16, finish, 0)
        gather_m.begin(n2.at[b], own.at[2, b], b)

    gather_d.begin(dm.at[0], own.at[1, 0], 0)
    scatters[0].hop(0)
    relay_third()
    scatters[0].start(2)
    scatters[0].hop(1)
    pass_ff(0)
    scatters[1].start(0)
    scatters[0].hop(2)
    pass_ff(1)
    gather_d.step(0, 1)
    hidden_state(0)
    scatters[1].start(1)
    scatters[1].hop(0)
    gather_d.step(0, 2)
    scatters[1].start(2)
    scatters[1].hop(1)
    gather_m.step(0, 1)
    scatters[1].hop(2)
    relay_ff(0)
    gather_d.step(0, 3)
    gather_m.step(0, 2)
    gather_d.begin(dm.at[1], own.at[1, 1], 1)
    hidden_state(1)
    gather_m.step(0, 3)
    relay_ff(1)
    gather_d.finish(own.at[1, 0], 0)
    local(dm_all.at[0], b_v.at[at_b(0)], load.at[2])
    gather_m.finish(own.at[2, 0], 0)
    local(n2_all.at[0], a_v.at[at_b(0)], load.at[0])
    gather_d.step(1, 1)
    gather_m.step(1, 1)
    turned_out.finish()
    for n, (dst, room) in enumerate(((f_all, w1_f), (s_all, w2_f), (t_all, w3_f))):
        if n < 2:
            for zs in range(4):
                arrived(ff_block(n, over, zs), xy_ff.at[n, 2, zs], over // 2 == c)
        else:
            arrived(dst.at[:, aligned(over, wide, 128)], xy_ff.at[2, 2, 0])
        if n == 2:
            arrived(dst.at[:, aligned(g, wide, 128)], z_ff.at[2, 0])
        local(dst, room, load.at[4 + n])
    for b in range(2):
        early[b].finish()

    def feed_forward(b):
        def tile(i, carry):
            at = aligned(b * 2 + i, half, 16)
            first = product_right(a_v[at], w1_f[...])
            second = product_right(a_v[at], w2_f[...])
            back = product_right(b_v[at], w3_f[...])
            p_v[0, at] = (back * second).astype(jnp.bfloat16)
            p_v[1, at] = (back * first).astype(jnp.bfloat16)
            p_v[2, at] = (first * second).astype(jnp.bfloat16)
            return carry

        lax.fori_loop(0, 2, tile, 0)

    def norm_part(b):
        def body(at, i):
            value = product(p_v[0, at_b(b)], w1_f[:, at]) + product(p_v[1, at_b(b)], w2_f[:, at])
            part[b, :, at] = value.astype(jnp.bfloat16)

        tiles_of(width, body)

    def mixed_part(b):
        def body(at, i):
            part[b, :, at] = product(p_v[2, at_b(b)], w3_f[:, at]).astype(jnp.bfloat16)

        tiles_of(width, body)

    half_w = width // 2
    groups_f = [GroupSum(bulk, w_v.at[pl.ds(n * hidden, hidden)], in_f.at[n], xy_f.at[n]) for n in range(2)]
    groups_t = ColumnSum(bulk, w_v.at[pl.ds(2 * hidden, hidden)], in_t, xy_t)

    def rooms_ff(ref):
        return ref.at[pl.ds(0, hidden), pl.ds(0, half_w)], ref.at[pl.ds(0, quarter), pl.ds(half_w, half_w)]

    def spread_place(i):
        return pl.ds(pl.multiple_of((i % 2) * half_w + (i // 2) * 256, 256), 256)

    def weight_part(n, operand):
        turn(turned, lambda t: p_v[n, t], tokens // 128, hidden)

        def body(at, i):
            place = spread_place(i) if n < 2 else at
            w_v[pl.ds(n * hidden, hidden), place] = product(turned[...], operand[:, at]).astype(jnp.bfloat16)

        tiles_of(width, body)
        if n < 2:
            groups_f[n].depart()
        else:
            groups_t.depart()

    def hidden_gradient(b):
        scatter = second[b]
        scatter.receive()

        def finish(i, carry):
            piece = aligned(i, 16, 16)
            at = aligned(b * (rows // 16) + i, 16, 16)
            value = h[at]
            scale_h = lax.rsqrt(mean_square(value) + EPS)
            normed = value * scale_h
            grad = scatter.total(piece)
            along = jnp.mean(normed * grad, axis=-1, keepdims=True)
            live = live_rows(s * rows + i * 16, 16, lengths[0, b])
            upstream = cot[b, piece].astype(jnp.float32) * live
            grad_hidden = upstream + scale_h * (grad - normed * along)
            grad_x[at] = grad_hidden
            low = grad_hidden.astype(jnp.bfloat16)
            da[b, piece] = low
            dot = jnp.mean(low.astype(jnp.float32) * (value - x[b, piece].astype(jnp.float32)), axis=-1, keepdims=True)
            column[b, piece] = jnp.broadcast_to(dot, (16, 128))
            return carry

        lax.fori_loop(0, rows // 16, finish, 0)
        gather_a.begin(da.at[b], own.at[3, b], b)
        mix[b, :, :rows] = column[b].T[:8, :rows]
        for d in range(1, 8):
            last.remote(mix.at[b], mix_in.at[b, s], mix_sem.at[b], g, (s + d) % 8)
        local(mix.at[b], mix_in.at[b, s], mix_sem.at[b])

    second = scatters_of(early, True, {})
    for n in (0, 4, 5, 2, 6):
        ref = {0: a_v.at[at_b(0)], 2: b_v.at[at_b(0)], 4: w1_f, 5: w2_f, 6: w3_f}[n]
        arrived(ref, load.at[n])
    feed_forward(0)
    gather_m.step(1, 2)
    gather_d.step(1, 2)
    norm_part(0)
    second[0].begin()
    second[0].start(0)
    gather_m.step(1, 3)
    gather_d.step(1, 3)
    gather_d.finish(own.at[1, 1], 1)
    local(dm_all.at[1], b_v.at[at_b(1)], load.at[3])
    gather_m.finish(own.at[2, 1], 1)
    local(n2_all.at[1], a_v.at[at_b(1)], load.at[1])
    for b in range(2):
        for d in range(1, 8):
            later.remote(scale.at[b], scale_in.at[b, s], sc_sem.at[b], g, (s + d) % 8)
        local(scale.at[b], scale_in.at[b, s], sc_sem.at[b])
    second[0].start(1)
    second[0].hop(0)
    arrived(a_v.at[at_b(1)], load.at[1])
    arrived(b_v.at[at_b(1)], load.at[3])
    feed_forward(1)
    second[0].start(2)
    second[0].hop(1)
    second[0].hop(2)
    norm_part(1)
    def load_pre(b, j):
        local(pre_all.at[b, j], pre.at[j], pre_sem.at[j])

    def attention_back(b):
        gather_a.finish(own.at[3, b], b)
        local(da_all.at[b], a_v.at[at_b(b)], load.at[b])
        arrived(mix_in.at[b], mix_sem.at[b])
        columns_of(mixed, mix_in, b, rows)
        live = live_rows(0, length, lengths[0, b])
        arrived(a_v.at[at_b(b)], load.at[b])
        for j in range(2):
            arrived(pre.at[j], pre_sem.at[j])
            lanes = pl.ds(j * head, head)
            error = product_right(a_v[at_b(b)], wo_v[pl.ds(j * head, head)])
            q_pre, k_pre, v_pre, u_pre, o = [pre[j, n] for n in range(5)]
            sigma = 1.0 / (1.0 + jnp.exp(-u_pre))
            u = u_pre * sigma
            scale_g = inverse[at_b(b), :1]
            nat = u * o * scale_g
            nat_v(at_b(b))[:, lanes] = nat.astype(jnp.bfloat16)
            dg = scale_g * (error - nat * mixed[:, :1])
            dz(3, at_b(b))[:, lanes] = (dg * o * (sigma * (1.0 + u_pre * (1.0 - sigma)))).astype(jnp.bfloat16)
            do = (dg * u).astype(jnp.bfloat16)
            q = silu(q_pre).astype(jnp.bfloat16)
            k = (silu(k_pre) * live).astype(jnp.bfloat16)
            v = (silu(v_pre) * live).astype(jnp.bfloat16)
            scores = (product_right(k, q) * table[j]).astype(jnp.bfloat16)
            dv = product(scores, do)
            d_scores = (product_right(v, do) * table[j]).astype(jnp.bfloat16)
            dk = product(d_scores, q)
            dq = product_left(d_scores, k)
            dz(0, at_b(b))[:, lanes] = (dq * slope(pre[j, 0])).astype(jnp.bfloat16)
            dz(1, at_b(b))[:, lanes] = (dk * live * slope(pre[j, 1])).astype(jnp.bfloat16)
            dz(2, at_b(b))[:, lanes] = (dv * live * slope(pre[j, 2])).astype(jnp.bfloat16)
            if b == 0:
                load_pre(1, j)

    def first_part(b):
        def body(at, i):
            value = product_right(dz(0, at_b(b))[...], wa_v[0, at])
            for n in range(1, 4):
                value = value + product_right(dz(n, at_b(b))[...], wa_v[n, at])
            part[b, :, at] = value.astype(jnp.bfloat16)

        tiles_of(width, body)

    second[1].begin()
    second[1].start(0)
    hidden_gradient(0)
    weight_part(0, a_v)
    second[1].start(1)
    second[1].hop(0)
    gather_a.step(0, 1)
    third = scatters_of(sums, False, {})
    early[0].finish()
    mixed_part(0)
    third[0].begin()
    third[0].start(0)
    second[1].start(2)
    second[1].hop(1)
    second[1].hop(2)
    third[0].start(1)
    third[0].hop(0)
    gather_a.step(0, 2)
    weight_part(1, a_v)
    hidden_gradient(1)
    third[0].start(2)
    third[0].hop(1)
    groups_f[0].middle(*rooms_ff(a_v), load.at[pl.ds(13, 2)])
    gather_a.step(0, 3)
    third[0].hop(2)
    early[1].finish()
    mixed_part(1)
    third[1].begin()
    third[1].start(0)
    for j in range(2):
        table[j] = turned_table(decay[4 * (2 * c + j) + z], length)
    for b in range(2):
        arrived(scale_in.at[b], sc_sem.at[b])
        columns_of(inverse.at[at_b(b)], scale_in, b, rows)

    for j in range(2):
        arrived(pre.at[j], pre_sem.at[j])
        load_pre(0, j)
    gather_a.step(1, 1)
    third[1].start(1)
    third[1].hop(0)
    weight_part(2, b_v)
    gather_a.step(1, 2)
    third[1].start(2)
    third[1].hop(1)
    third[1].hop(2)
    groups_f[1].middle(*rooms_ff(b_v), load.at[pl.ds(13, 2)])
    for b in range(2):
        local(n1_all.at[b], b_v.at[at_b(b)], load.at[2 + b])
    later.finish()
    attention_back(0)
    gather_a.step(1, 3)
    def sum_ff(n):
        small = w_v.at[pl.ds(n * hidden, quarter), pl.ds(half_w, half_w)]
        groups_f[n].settle()
        total = w_v.at[pl.ds(n * hidden, quarter), pl.ds(0, half_w)]
        groups_f[n].final(total, small, load.at[pl.ds(13, 2)])
        for d in (2, 1, 3, 0):
            chip = (z + d) % 4
            src = total.at[:, aligned(chip, depth, 128)]
            if d:
                last.remote(src, y_f.at[n, z], z_f.at[n, z], g, 2 * chip + c)
            else:
                local(src, y_f.at[n, z], z_f.at[n, z])

    def join_ff(n, result):
        for r, o in enumerate(others + (g,)):
            arrived(y_f.at[n, o], z_f.at[n, o])
            dst = result.at[aligned(g, quarter, 16)]
            if r < 3:
                last.remote(y_f.at[n, o], dst, join_f.at[n, r], o, s)
            else:
                local(y_f.at[n, o], dst, join_f.at[n, r])

    def rooms_column(rows):
        return [b_v.at[pl.ds(0, rows), pl.ds(i * wide, wide)] for i in range(4)]

    def sum_third():
        groups_t.final(rooms_column(quarter), load.at[pl.ds(13, 4)])
        local(w_v.at[pl.ds(2 * hidden, hidden), aligned(g, wide, 128)], ft, z_t)

    groups_h = [GroupSum(last, grads_h.at[n], in_h.at[n], xy_h.at[n]) for n in range(4)]
    groups_o = ColumnSum(last, go_v, in_o, xy_o)

    def room_h(first, count):
        return w_v.at[pl.ds(first * head, count * head), pl.ds(half_w, half_w)]

    def middle_head(n):
        groups_h[n].middle(room_h(3 * (n % 2), 2), room_h(3 * (n % 2) + 2, 1), load.at[pl.ds(18, 2)])

    def head_part(n):
        turn(turned, lambda t: dz(n, t)[...], tokens // 128, 2 * head)

        def body(at, i):
            grads_h[n, :, spread_place(i)] = product(turned[pl.ds(0, 2 * head)], b_v[:, at]).astype(jnp.bfloat16)

        tiles_of(width, body)

    def out_weight():
        turn(turned, lambda t: nat_v(t)[...], tokens // 128, 2 * head)

        def body(at, i):
            go_v[:, at] = product(turned[pl.ds(0, 2 * head)], a_v[:, at]).astype(jnp.bfloat16)

        tiles_of(width, body)

    def sum_head(n, result):
        total = room_h(6 + n, 1)
        groups_h[n].final(total, room_h(10, 1), load.at[pl.ds(18, 2)])
        for d in (2, 1, 3, 0):
            chip = (z + d) % 4
            src = total.at[:, aligned(chip, depth, 128)]
            dst = result.at[aligned(z, head, head)]
            if d:
                last.remote(src, dst, z_h.at[n, d], g, 2 * chip + c)
            else:
                local(src, dst, z_h.at[n, d])

    def sum_out():
        groups_o.final(rooms_column(head), load.at[pl.ds(13, 4)])
        mine_o = go_v.at[:, aligned(g, wide, 128)]
        for j in range(2):
            to = 2 * (2 * c + j) + z // 2
            src = mine_o.at[pl.ds(j * head, head)]
            dst = fo.at[aligned(z % 2, head, head)]
            last.remote(src, dst, z_o.at[z % 2], g, to, to != s)
            local(src, dst, z_o.at[z % 2], to == s)

    sum_ff(0)
    attention_back(1)
    for b in range(2):
        arrived(b_v.at[at_b(b)], load.at[2 + b])
    head_part(0)
    groups_h[0].depart()
    for b in range(2):
        third[b].receive()
        scatter = third[b]

        def result(i, carry):
            piece = aligned(i, 16, 16)
            at = aligned(b * (rows // 16) + i, 16, 16)
            out[at] = (h[at] + scatter.total(piece)).astype(jnp.bfloat16)
            return carry

        lax.fori_loop(0, rows // 16, result, 0)
    for b in range(2):
        sums[b].finish()
    fourth = scatters_of(early, True, {})
    first_part(0)
    fourth[0].begin()
    fourth[0].start(0)
    head_part(1)
    groups_h[1].depart()
    sum_ff(1)
    groups_t.middle(
        [w_v.at[pl.ds(0, quarter), pl.ds(half_w + k * wide, wide)] for k in range(2)], load.at[pl.ds(13, 2)]
    )
    first_part(1)
    fourth[0].start(1)
    fourth[0].hop(0)
    fourth[1].begin()
    head_part(2)
    groups_h[2].depart()
    middle_head(0)
    head_part(3)
    groups_h[3].depart()
    middle_head(1)
    fourth[0].start(2)
    fourth[0].hop(1)
    out_weight()
    groups_o.depart()
    middle_head(2)
    fourth[0].hop(2)
    fourth[1].start(0)
    middle_head(3)
    sum_head(0, fq)
    fourth[1].start(1)
    fourth[1].hop(0)
    groups_o.middle(rooms_column(head), load.at[pl.ds(13, 2)])
    sum_head(1, fk)
    join_ff(0, ff_)
    join_ff(1, fs)
    fourth[1].start(2)
    fourth[1].hop(1)
    sum_head(2, fv)
    fourth[1].hop(2)
    sum_head(3, fu)
    sum_out()
    sum_third()
    for b in range(2):
        fourth[b].receive()
        scatter = fourth[b]

        def finish_x(i, carry):
            piece = aligned(i, 16, 16)
            at = aligned(b * (rows // 16) + i, 16, 16)
            v = x[b, piece].astype(jnp.float32)
            scale_x = lax.rsqrt(mean_square(v) + EPS)
            normed = v * scale_x
            grad = scatter.total(piece)
            along = jnp.mean(normed * grad, axis=-1, keepdims=True)
            grad_x[at] = grad_x[at] + scale_x * (grad - normed * along)
            return carry

        lax.fori_loop(0, rows // 16, finish_x, 0)


    for n, result in enumerate((ff_, fs)):
        for r in range(4):
            arrived(result.at[pl.ds(0, quarter)], join_f.at[n, r])
    arrived(ft, z_t)
    for j in range(2):
        arrived(fo.at[pl.ds(0, head)], z_o.at[j])
    for n, result in enumerate((fq, fk, fv, fu)):
        for d in range(4):
            arrived(result.at[pl.ds(0, head)], z_h.at[n, d])
    for b in range(2):
        early[b].finish()
    bulk.finish()
    last.finish()
    copies.finish()


def call(kernel, number, ins, outs, scratch, name):
    return pl.pallas_call(
        kernel,
        out_shape=[shape for shape, _ in outs],
        in_specs=[spec for _, spec in ins],
        out_specs=[spec for _, spec in outs],
        scratch_shapes=scratch,
        compiler_params=pltpu.CompilerParams(
            collective_id=number, has_side_effects=True, vmem_limit_bytes=64 * 2**20 - 2**17
        ),
        name=name,
    )(*[value for value, _ in ins])


def finish_arrays(count, turned_count, *refs):
    ins, outs, held, done = refs[:count], refs[count : 2 * count], refs[2 * count : 3 * count], refs[3 * count : 4 * count]
    in_sem, out_sem = refs[4 * count :]
    for i in range(count):
        local(ins[i], held[i], in_sem.at[i])
    for i in range(count):
        arrived(held[i], in_sem.at[i])
        if i < 2:
            local(held[i], outs[i], out_sem.at[i])
            continue
        if i < 2 + turned_count:
            done[i][...] = held[i][...].T.astype(jnp.float32)
        else:

            def write(at, value):
                done[i][at] = value

            pour(lambda at: held[i][at].astype(jnp.float32), write, held[i].shape[0] // 16)
        local(done[i], outs[i], out_sem.at[i])
    for i in range(count):
        arrived(outs[i], out_sem.at[i])


def finished(out, grad_x, turned, straight):
    arrays = [out, grad_x] + turned + straight
    shapes = [jax.ShapeDtypeStruct(v.shape, v.dtype) for v in (out, grad_x)]
    shapes += [wide_array(*v.shape[::-1]) for v in turned] + [wide_array(*v.shape) for v in straight]
    count = len(arrays)
    small = jax.ShapeDtypeStruct((8, 128), jnp.float32)
    done = [small, small] + shapes[2:]
    return pl.pallas_call(
        functools.partial(finish_arrays, count, len(turned)),
        out_shape=shapes,
        in_specs=[ANY] * count,
        out_specs=[ANY] * count,
        scratch_shapes=[pltpu.VMEM(v.shape, v.dtype) for v in arrays] + [pltpu.VMEM(v.shape, v.dtype) for v in done]
        + [dma(count), dma(count)],
        compiler_params=pltpu.CompilerParams(vmem_limit_bytes=62 * 2**20),
        name="finish_arrays",
    )(*arrays)


def low_array(*shape):
    return jax.ShapeDtypeStruct(shape, jnp.bfloat16)


def wide_array(*shape):
    return jax.ShapeDtypeStruct(shape, jnp.float32)


def dma(*shape):
    return pltpu.SemaphoreType.DMA(shape)


def scatter_scratch(rows, width):
    return [
        pltpu.VMEM((2, 4, rows, width), jnp.bfloat16),
        pltpu.VMEM((2, 2, 3, rows, width), jnp.bfloat16),
        dma(2, 4),
        dma(2, 2, 3),
    ]


def line_shards(
    tokens, cotangent, lengths, decay_rate,
    w_query, w_key, w_value, w_gate, w_out, w_first, w_second, w_third,
):
    bf16, f32 = jnp.bfloat16, jnp.float32
    rows, width = tokens.shape[2], tokens.shape[3]
    depth, wide = w_query.shape
    head = width // decay_rate.shape[0]
    hidden = w_third.shape[0]
    length = 8 * rows
    x_low = tokens[:, 0]
    in_smem = pl.BlockSpec(memory_space=pltpu.SMEM)
    gathered = low_array(2, length, width)
    out, grad_x, fq, fk, fv, fu, fo, ff, fs, ft = call(
        layer_part,
        0,
        [(lengths.T, in_smem), (decay_rate, in_smem), (x_low, VMEM), (cotangent[:, 0], VMEM)]
        + [(v, ANY) for v in (w_query, w_key, w_value, w_gate, w_out, w_first, w_second, w_third)],
        [(low_array(2 * rows, width), VMEM), (wide_array(2 * rows, width), VMEM)]
        + [(low_array(wide, depth), ANY)] * 4 + [(low_array(depth, wide), ANY)]
        + [(low_array(2 * hidden, depth), ANY)] * 2 + [(low_array(hidden, wide), ANY)]
        + [(gathered, ANY)] * 4
        + [(low_array(width, 2 * head), ANY)] * 4
        + [(low_array(2 * head, width), ANY)]
        + [(low_array(hidden, width), ANY)] * 3
        + [(wide_array(2, 2, 5, length, head), ANY)]
        + [(low_array(2, 5 * hidden // 2, width // 2), ANY), (low_array(2, 3, hidden // 2, wide), ANY), (low_array(2, 3, head, wide), ANY),
           (low_array(4, 5 * head, width // 2), ANY)]
        + [(low_array(2, 4, hidden // 2, depth), ANY)] * 2,
        [dma(176), dma(26), dma(4, 2)] + [dma(2, 2, 3), dma(2, 7)] * 2
        + [dma(4, 4), dma(2), dma(3, 4), dma(4, 3, 4), dma(3), dma(3, 3, 4), dma(2, 4), dma(2, 4)]
        + [pltpu.VMEM((2, rows, width), bf16)] * 4
        + [pltpu.VMEM((2 * rows, width), f32),
           pltpu.VMEM((2 * length, width), bf16), pltpu.VMEM((2 * length, width), bf16), pltpu.VMEM((3 * hidden, width), bf16),
           pltpu.VMEM((4, width, 2 * head), bf16), pltpu.VMEM((2 * head, width), bf16),
           pltpu.VMEM((3, 2 * length, hidden), bf16), pltpu.VMEM((hidden, 2 * length), bf16),
           pltpu.VMEM((2, length, width), bf16)]
        + scatter_scratch(rows, width) + scatter_scratch(rows, width)
        + [pltpu.VMEM((2, length, length), f32), pltpu.VMEM((2, 8, 8, 128), f32), pltpu.VMEM((2, 8, 8, 128), f32),
           pltpu.VMEM((2, 8, 128), f32), pltpu.VMEM((2, 8, 8, 128), f32), dma(2), dma(2), pltpu.VMEM((2, 128, 128), f32),
           pltpu.VMEM((2, 8, 128), f32), pltpu.VMEM((2, 8, 8, 128), f32), dma(2),
           pltpu.VMEM((2 * length, 128), f32), pltpu.VMEM((length, 128), f32),
           pltpu.VMEM((2, 5, length, head), f32), dma(2),
           pltpu.VMEM((2 * head, width), bf16), pltpu.VMEM((4, 2 * head, width), bf16),
           dma(2, 4), dma(2, 3), dma(2, 3), dma(4, 4), dma(2, 4), dma(), dma(2), dma(4, 4)],
        "layer_part",
    )[:10]
    results = finished(out, grad_x, [fq, fk, fv, fu, ff, fs], [fo, ft])
    out, grad_x, fq, fk, fv, fu, ff, fs, fo, ft = results
    return (out.reshape(2, 1, rows, width), grad_x.reshape(2, 1, rows, width), fq, fk, fv, fu, fo, ff, fs, ft)


def solution(mesh):
    in_specs = (
        P(None, "grp", "seq", None),
        P(None, "grp", "seq", None),
        P(None, "grp"),
        P(),
        P("seq", "grp"),
        P("seq", "grp"),
        P("seq", "grp"),
        P("seq", "grp"),
        P("seq", "grp"),
        P("seq", "grp"),
        P("seq", "grp"),
        P("seq", "grp"),
    )
    out_specs = (
        P(None, "grp", "seq", None),
        P(None, "grp", "seq", None),
        P("seq", "grp"),
        P("seq", "grp"),
        P("seq", "grp"),
        P("seq", "grp"),
        P("seq", "grp"),
        P("seq", "grp"),
        P("seq", "grp"),
        P("seq", "grp"),
    )
    fast = mesh.shape["grp"] == 4 and mesh.shape["seq"] == 8
    return jax.shard_map(line_shards if fast else shards, mesh=mesh, in_specs=in_specs, out_specs=out_specs, check_vma=False)
```

```python
import functools

import jax
import jax.numpy as jnp
from jax import lax
from jax.experimental import pallas as pl
from jax.experimental.pallas import tpu as pltpu
from jax.sharding import PartitionSpec as P

EPS = 1e-06
HIGH = lax.Precision.HIGHEST
MESH = pl.DeviceIdType.MESH
ANY = pl.BlockSpec(memory_space=pl.ANY)
VMEM = pl.BlockSpec(memory_space=pltpu.VMEM)


def prefix(value, axis, join, neutral, backward):
    count, mine = (lax.axis_size(axis), lax.axis_index(axis))
    pieces = jax.tree.map(lambda part: lax.all_gather(part, axis), value)
    if backward:
        pieces = jax.tree.map(lambda part: part[::-1], pieces)
        mine = count - 1 - mine
    subtotal = jax.tree.map(
        lambda part, zero: jnp.full_like(part, 0) + jnp.asarray(zero, part.dtype), value, neutral
    )

    def step(position, subtotal):
        longer = join(subtotal, jax.tree.map(lambda part: part[position], pieces))
        return jax.tree.map(lambda new, old: jnp.where(position < mine, new, old), longer, subtotal)

    return lax.fori_loop(0, count - 1, step, subtotal)


def norm_rows(values):
    return values * lax.rsqrt(jnp.mean(values * values, axis=-1, keepdims=True) + EPS)


def norm_back(values, gradient):
    _, pull = jax.vjp(norm_rows, values)
    return pull(gradient)[0]


def silu_slope(values):
    sigma = jax.nn.sigmoid(values)
    return sigma * (1.0 + values * (1.0 - sigma))


def product(left, right):
    return jnp.dot(left, right, preferred_element_type=jnp.float32)


def product_left(left, right):
    return lax.dot_general(
        left, right, (((0,), (0,)), ((), ())), preferred_element_type=jnp.float32
    )


def product_right(left, right):
    return lax.dot_general(
        left, right, (((1,), (1,)), ((), ())), preferred_element_type=jnp.float32
    )


def combine_state(earlier, later):
    return (later[1][:, None, None] * earlier[0] + later[0], earlier[1] * later[1])


def shards(
    tokens,
    cotangent,
    lengths,
    decay_rate,
    w_query,
    w_key,
    w_value,
    w_gate,
    w_out,
    w_first,
    w_second,
    w_third,
):
    micro = tokens.shape[0]
    block_rows = tokens.shape[2]
    width = tokens.shape[3]
    heads = decay_rate.shape[0]
    head_dim = width // heads
    hidden_width = w_third.shape[0] * lax.axis_size("seq")
    places = jnp.arange(block_rows).astype(jnp.float32)
    slot_index = lax.axis_index("seq") * block_rows + jnp.arange(block_rows)
    offset = places[:, None] - places[None, :]
    weight = jnp.where(
        offset[None] >= 0, jnp.exp(-decay_rate[:, None, None] * jnp.maximum(offset, 0.0)[None]), 0.0
    )
    query_fac = jnp.exp(-decay_rate[None, :] * (places[:, None] + 1.0))[:, :, None]
    key_fac = jnp.exp(-decay_rate[None, :] * (block_rows - 1.0 - places[:, None]))[:, :, None]
    step_decay = jnp.exp(-decay_rate * block_rows)
    empty_state = jnp.zeros((heads, head_dim, head_dim), jnp.float32)
    unit_decay = jnp.ones((heads,), jnp.float32)
    partial_rows = (
        lax.all_gather(w_query, "grp", axis=1, tiled=True),
        lax.all_gather(w_key, "grp", axis=1, tiled=True),
        lax.all_gather(w_value, "grp", axis=1, tiled=True),
        lax.all_gather(w_gate, "grp", axis=1, tiled=True),
        lax.all_gather(w_out, "grp", axis=1, tiled=True),
        lax.all_gather(w_first, "grp", axis=1, tiled=True),
        lax.all_gather(w_second, "grp", axis=1, tiled=True),
        lax.all_gather(w_third, "grp", axis=1, tiled=True),
    )
    gathered = (
        lax.all_gather(partial_rows[0], "seq", axis=0, tiled=True),
        lax.all_gather(partial_rows[1], "seq", axis=0, tiled=True),
        lax.all_gather(partial_rows[2], "seq", axis=0, tiled=True),
        lax.all_gather(partial_rows[3], "seq", axis=0, tiled=True),
        lax.all_gather(partial_rows[4], "seq", axis=0, tiled=True),
        lax.all_gather(partial_rows[5], "seq", axis=0, tiled=True),
        lax.all_gather(partial_rows[6], "seq", axis=0, tiled=True),
        lax.all_gather(partial_rows[7], "seq", axis=0, tiled=True),
    )
    outputs = []
    input_grads = []
    first_norms = []
    attn_rows = []
    normed_rows = []
    branch_rows = []
    second_norms = []
    ffn_rows = []
    mixed_rows = []
    upstream_rows = []
    for batch_idx in range(micro):
        wq_full, wk_full, wv_full, wu_full, wo_full, first_full, second_full, third_full = gathered
        inputs = tokens[batch_idx, 0].astype(jnp.float32)
        live = (slot_index < lengths[batch_idx, 0]).astype(jnp.float32)[:, None]
        live_low = live.astype(jnp.bfloat16)
        first_norm = norm_rows(inputs).astype(jnp.bfloat16)
        query_pre = product(first_norm, wq_full)
        key_pre = product(first_norm, wk_full)
        value_pre = product(first_norm, wv_full)
        gate_pre = product(first_norm, wu_full)
        queries = jax.nn.silu(query_pre).astype(jnp.bfloat16).reshape(block_rows, heads, head_dim)
        key_heads = (jax.nn.silu(key_pre).astype(jnp.bfloat16) * live_low).reshape(
            block_rows, heads, head_dim
        )
        value_heads = (jax.nn.silu(value_pre).astype(jnp.bfloat16) * live_low).reshape(
            block_rows, heads, head_dim
        )
        query_wide = queries.astype(jnp.float32)
        key_wide = key_heads.astype(jnp.float32)
        value_wide = value_heads.astype(jnp.float32)
        local_state = jnp.einsum("jhd,jhe->hde", key_wide * key_fac, value_wide, precision=HIGH)
        prior_state, _ = prefix(
            (local_state, step_decay), "seq", combine_state, (empty_state, unit_decay), False
        )
        scores = (
            jnp.einsum("ihd,jhd->hij", queries, key_heads, preferred_element_type=jnp.float32)
            * weight
        )
        intra = jnp.einsum("hij,jhe->ihe", scores, value_wide, precision=HIGH)
        inter = jnp.einsum("ihd,hde->ihe", query_wide * query_fac, prior_state, precision=HIGH)
        attended = (intra + inter).reshape(block_rows, width)
        gate_act = jax.nn.silu(gate_pre)
        gated = gate_act * attended
        normed = norm_rows(gated).astype(jnp.bfloat16)
        hidden = inputs + product(normed, wo_full)
        second_norm = norm_rows(hidden).astype(jnp.bfloat16)
        first_proj = product(second_norm, first_full)
        second_proj = product(second_norm, second_full)
        mixed_in = (first_proj * second_proj).astype(jnp.bfloat16)
        result = hidden + product(mixed_in, third_full)
        outputs.append(result.astype(jnp.bfloat16))
        upstream = cotangent[batch_idx, 0].astype(jnp.float32) * live
        upstream_low = upstream.astype(jnp.bfloat16)
        grad_mixed = product_right(upstream_low, third_full)
        grad_first_proj = (grad_mixed * second_proj).astype(jnp.bfloat16)
        grad_second_proj = (grad_mixed * first_proj).astype(jnp.bfloat16)
        grad_norm_two = product_right(grad_first_proj, first_full) + product_right(
            grad_second_proj, second_full
        )
        grad_hidden = upstream + norm_back(hidden, grad_norm_two)
        grad_branch = grad_hidden.astype(jnp.bfloat16)
        grad_gated = norm_back(gated, product_right(grad_branch, wo_full))
        grad_attended = (grad_gated * gate_act).astype(jnp.bfloat16)
        grad_gate_pre = (grad_gated * attended * silu_slope(gate_pre)).astype(jnp.bfloat16)
        grad_heads = grad_attended.reshape(block_rows, heads, head_dim)
        grad_wide = grad_heads.astype(jnp.float32)
        local_grad = jnp.einsum("ihd,ihe->hde", query_wide * query_fac, grad_wide, precision=HIGH)
        later_grad, _ = prefix(
            (local_grad, step_decay), "seq", combine_state, (empty_state, unit_decay), True
        )
        grad_scores = (
            jnp.einsum("ihe,jhe->hij", grad_heads, value_heads, preferred_element_type=jnp.float32)
            * weight
        )
        grad_queries = jnp.einsum("hij,jhd->ihd", grad_scores, key_wide, precision=HIGH)
        grad_queries = (
            grad_queries
            + jnp.einsum("ihe,hde->ihd", grad_wide, prior_state, precision=HIGH) * query_fac
        )
        grad_keys = jnp.einsum("hij,ihd->jhd", grad_scores, query_wide, precision=HIGH)
        grad_keys = (
            grad_keys + jnp.einsum("hde,jhe->jhd", later_grad, value_wide, precision=HIGH) * key_fac
        )
        grad_values = jnp.einsum("hij,ihe->jhe", scores, grad_wide, precision=HIGH)
        grad_values = (
            grad_values + jnp.einsum("jhd,hde->jhe", key_wide, later_grad, precision=HIGH) * key_fac
        )
        grad_query_pre = (grad_queries.reshape(block_rows, width) * silu_slope(query_pre)).astype(
            jnp.bfloat16
        )
        grad_key_pre = (grad_keys.reshape(block_rows, width) * live * silu_slope(key_pre)).astype(
            jnp.bfloat16
        )
        grad_value_pre = (
            grad_values.reshape(block_rows, width) * live * silu_slope(value_pre)
        ).astype(jnp.bfloat16)
        grad_norm_one = product_right(grad_query_pre, wq_full) + product_right(
            grad_key_pre, wk_full
        )
        grad_norm_one = (
            grad_norm_one
            + product_right(grad_value_pre, wv_full)
            + product_right(grad_gate_pre, wu_full)
        )
        input_grads.append(grad_hidden + norm_back(inputs, grad_norm_one))
        first_norms.append(first_norm)
        attn_rows.append(
            jnp.concatenate([grad_query_pre, grad_key_pre, grad_value_pre, grad_gate_pre], axis=1)
        )
        normed_rows.append(normed)
        branch_rows.append(grad_branch)
        second_norms.append(second_norm)
        ffn_rows.append(jnp.concatenate([grad_first_proj, grad_second_proj], axis=1))
        mixed_rows.append(mixed_in)
        upstream_rows.append(upstream_low)
    first_all = jnp.concatenate(first_norms, axis=0)
    attn_all = jnp.concatenate(attn_rows, axis=0)
    normed_all = jnp.concatenate(normed_rows, axis=0)
    branch_all = jnp.concatenate(branch_rows, axis=0)
    second_all = jnp.concatenate(second_norms, axis=0)
    ffn_all = jnp.concatenate(ffn_rows, axis=0)
    mixed_all = jnp.concatenate(mixed_rows, axis=0)
    upstream_all = jnp.concatenate(upstream_rows, axis=0)
    proj_rows = lax.psum_scatter(
        product_left(first_all, attn_all), "seq", scatter_dimension=0, tiled=True
    )
    outproj_rows = lax.psum_scatter(
        product_left(normed_all, branch_all), "seq", scatter_dimension=0, tiled=True
    )
    ffn_part = lax.psum_scatter(
        product_left(second_all, ffn_all), "seq", scatter_dimension=0, tiled=True
    )
    down_rows = lax.psum_scatter(
        product_left(mixed_all, upstream_all), "seq", scatter_dimension=0, tiled=True
    )
    summed = (
        lax.psum_scatter(proj_rows[:, :width], "grp", scatter_dimension=1, tiled=True),
        lax.psum_scatter(proj_rows[:, width : 2 * width], "grp", scatter_dimension=1, tiled=True),
        lax.psum_scatter(
            proj_rows[:, 2 * width : 3 * width], "grp", scatter_dimension=1, tiled=True
        ),
        lax.psum_scatter(proj_rows[:, 3 * width :], "grp", scatter_dimension=1, tiled=True),
        lax.psum_scatter(outproj_rows, "grp", scatter_dimension=1, tiled=True),
        lax.psum_scatter(ffn_part[:, :hidden_width], "grp", scatter_dimension=1, tiled=True),
        lax.psum_scatter(ffn_part[:, hidden_width:], "grp", scatter_dimension=1, tiled=True),
        lax.psum_scatter(down_rows, "grp", scatter_dimension=1, tiled=True),
    )
    layer_out = jnp.stack(outputs)[:, None]
    grad_tokens = jnp.stack(input_grads)[:, None]
    return (
        layer_out,
        grad_tokens,
        summed[0],
        summed[1],
        summed[2],
        summed[3],
        summed[4],
        summed[5],
        summed[6],
        summed[7],
    )


class Spare:
    def __init__(self, sems):
        self.sems, self.free, self.order = sems, list(range(sems.shape[0])), []


class Copies:
    def __init__(self, spare):
        self.spare = spare
        self.pending = []

    def remote(self, src, dst, recv_sem, group, place, when=None):
        while not self.spare.free:
            owner, entry = self.spare.order.pop(0)
            owner.settle(entry)
        number = self.spare.free.pop(0)
        copy = pltpu.make_async_remote_copy(
            src_ref=src,
            dst_ref=dst,
            send_sem=self.spare.sems.at[number],
            recv_sem=recv_sem,
            device_id=(group, place),
            device_id_type=MESH,
        )
        self.pending.append((copy, when, number))
        self.spare.order.append((self, self.pending[-1]))
        if when is None:
            copy.start()
        else:
            pl.when(when)(copy.start)
        return self.pending[-1]

    def settle(self, entry):
        if not any(other is entry for other in self.pending):
            return
        self.pending = [other for other in self.pending if other is not entry]
        copy, when, number = entry
        if when is None:
            copy.wait_send()
        else:
            pl.when(when)(copy.wait_send)
        self.spare.free.append(number)

    def finish(self):
        while self.pending:
            self.settle(self.pending[0])


def local(src, dst, sem, when=None):
    copy = pltpu.make_async_copy(src, dst, sem)
    if when is None:
        copy.start()
    else:
        pl.when(when)(copy.start)


def arrived(ref, sem, when=None):
    copy = pltpu.make_async_copy(ref, ref, sem)
    if when is None:
        copy.wait()
    else:
        pl.when(when)(copy.wait)


def where_am_i():
    g, s = lax.axis_index("grp"), lax.axis_index("seq")
    return g, s, g // 2, g % 2, s // 2, s % 2


def across(y, x):
    return (y * 2 + 1 - x, (1 - y) * 2 + x, (1 - y) * 2 + 1 - x)


def greet(partners):
    barrier = pltpu.get_barrier_semaphore()
    for partner in partners:
        pl.semaphore_signal(barrier, inc=1, device_id=partner, device_id_type=MESH)
    pl.semaphore_wait(barrier, len(partners))


def aligned(index, unit, step):
    return pl.ds(pl.multiple_of(index * unit, step), unit)


class Gather:
    def __init__(self, copies, out, rows, hop_sem, side_sem):
        self.copies, self.out, self.rows = copies, out, rows
        self.hop_sem, self.side_sem = hop_sem, side_sem
        self.g, self.s, _, _, self.z, self.c = where_am_i()

    def block(self, b, z, core):
        return self.out.at[b, aligned(2 * z + core, self.rows, 16)]

    def spread(self, src, b, z_of, k, right, left):
        g, s, z, c = self.g, self.s, self.z, self.c
        dst = self.block(b, z_of, c)
        if right is not None:
            self.copies.remote(src, dst, self.hop_sem.at[b, 0, k], g, (s + 2) % 8, right)
        if left is not None:
            self.copies.remote(src, dst, self.hop_sem.at[b, 1, k], g, (s + 6) % 8, left)

    def begin(self, src, own_sem, b):
        g, s, z, c = self.g, self.s, self.z, self.c
        self.spread(src, b, z, 0, z < 3, z > 0)
        self.copies.remote(src, self.block(b, z, c), self.side_sem.at[b, 0], g, s + 1 - 2 * c)
        local(src, self.block(b, z, c), own_sem)

    def step(self, b, k, inner=None):
        g, s, z, c = self.g, self.s, self.z, self.c
        side = s + 1 - 2 * c
        ends = jnp.logical_or(z == 0, z == 3)

        def these(has):
            if inner is None:
                return has
            return jnp.logical_and(has, jnp.logical_not(ends) if inner else ends)

        has = these(z >= k)
        at = jnp.maximum(z - k, 0)
        ref = self.block(b, at, c)
        arrived(ref, self.hop_sem.at[b, 0, k - 1], has)
        if k < 3:
            self.spread(ref, b, at, k, jnp.logical_and(has, z < 3), None)
        self.copies.remote(ref, ref, self.side_sem.at[b, k], g, side, has)
        has = these(z + k <= 3)
        at = jnp.minimum(z + k, 3)
        ref = self.block(b, at, c)
        arrived(ref, self.hop_sem.at[b, 1, k - 1], has)
        if k < 3:
            self.spread(ref, b, at, k, None, jnp.logical_and(has, z > 0))
        self.copies.remote(ref, ref, self.side_sem.at[b, 3 + k], g, side, has)

    def finish(self, own_sem, b):
        z, c = self.z, self.c
        arrived(self.block(b, z, c), own_sem)
        arrived(self.block(b, z, 1 - c), self.side_sem.at[b, 0])
        for k in (1, 2, 3):
            arrived(self.block(b, jnp.maximum(z - k, 0), 1 - c), self.side_sem.at[b, k], z >= k)
            arrived(self.block(b, jnp.minimum(z + k, 3), 1 - c), self.side_sem.at[b, 3 + k], z + k <= 3)


def line_partners(g, s):
    return [(g, (s + d) % 8) for d in range(1, 8)]


def add_rows(target, room):
    def write(at, value):
        target[at] = value.astype(jnp.bfloat16)

    pour(lambda at: target[at].astype(jnp.float32) + room[at].astype(jnp.float32), write, target.shape[0] // 16)


class GroupSum:
    def __init__(self, copies, grad, inbox, sem):
        self.copies, self.grad, self.inbox, self.sem = copies, grad, inbox, sem
        self.g, self.s, self.y, self.x, self.z, self.c = where_am_i()
        self.rows, self.half = grad.shape[0] // 2, grad.shape[1] // 2
        self.entries = []

    def block(self, x, core):
        return self.grad.at[aligned(x, self.rows, 16), pl.ds(core * self.half, self.half)]

    def slot(self, first, count=1):
        return self.inbox.at[pl.ds(first * self.rows, count * self.rows)]

    def remote(self, *args):
        self.entries.append(self.copies.remote(*args))

    def depart(self):
        gx, gy, _ = across(self.y, self.x)
        self.remote(self.grad.at[:, pl.ds(0, self.half)], self.slot(0, 2), self.sem.at[0], gy, self.s, self.c != self.y)
        self.remote(self.block(1 - self.x, 1), self.slot(2), self.sem.at[1], gx, self.s)

    def middle(self, room, small, load):
        gx, gy, _ = across(self.y, self.x)
        mine = self.c == self.y
        arrived(self.slot(0, 2), self.sem.at[0], mine)
        local(self.slot(0, 2), room, load.at[0], mine)
        arrived(self.slot(2), self.sem.at[1])
        local(self.slot(2), small, load.at[1])
        arrived(room, load.at[0], mine)

        @pl.when(mine)
        def _():
            add_rows(self.grad.at[:, pl.ds(0, self.half)], room)

        arrived(small, load.at[1])
        add_rows(self.block(self.x, 1), small)
        for core in range(2):
            block = self.block(self.x, core)
            self.remote(
                block, self.slot(3), self.sem.at[2], self.g, 2 * self.z + core, jnp.logical_and(mine, self.c != core)
            )
            local(block, self.slot(3), self.sem.at[2], jnp.logical_and(mine, self.c == core))
        self.remote(self.block(1 - self.x, 0), self.slot(4), self.sem.at[3], gx, 2 * self.z, mine)
        self.remote(self.block(self.x, 1), self.slot(4), self.sem.at[3], gy, 2 * self.z + 1, jnp.logical_not(mine))

    def final(self, room, small, load):
        for i, ref in enumerate((room, small)):
            arrived(self.slot(3 + i), self.sem.at[2 + i])
            local(self.slot(3 + i), ref, load.at[i])
        for i, ref in enumerate((room, small)):
            arrived(ref, load.at[i])
        add_rows(room, small)

    def settle(self):
        for entry in self.entries:
            self.copies.settle(entry)


class ColumnSum:
    def __init__(self, copies, grad, inbox, sem):
        self.copies, self.grad, self.inbox, self.sem = copies, grad, inbox, sem
        self.g, self.s, y, x, _, _ = where_am_i()
        self.others = across(y, x)
        self.rows, self.wide = grad.shape[0] // 2, grad.shape[1] // 4

    def block(self, group, i):
        return self.grad.at[pl.ds(i * self.rows, self.rows), aligned(group, self.wide, 128)]

    def depart(self):
        for i in range(2):
            to = self.others[i]
            for k, group in enumerate((to, self.others[2])):
                self.copies.remote(self.block(group, i), self.inbox.at[i, k], self.sem.at[i, k], to, self.s)

    def middle(self, rooms, load):
        for i in range(2):
            arrived(self.inbox.at[i, 1], self.sem.at[i, 1])
            local(self.inbox.at[i, 1], rooms[i], load.at[i])
        for i in range(2):
            arrived(rooms[i], load.at[i])
            to = self.others[1 - i]
            add_rows(self.block(to, i), rooms[i])
            self.copies.remote(self.block(to, i), self.inbox.at[i, 2], self.sem.at[i, 2], to, self.s)

    def final(self, rooms, load):
        for i in range(2):
            for k in range(2):
                arrived(self.inbox.at[i, 2 * k], self.sem.at[i, 2 * k])
                local(self.inbox.at[i, 2 * k], rooms[2 * i + k], load.at[2 * i + k])
        for i in range(2):
            for k in range(2):
                arrived(rooms[2 * i + k], load.at[2 * i + k])
            mine, first, second = self.block(self.g, i), rooms[2 * i], rooms[2 * i + 1]

            def read(at):
                return mine[at].astype(jnp.float32) + first[at].astype(jnp.float32) + second[at].astype(jnp.float32)

            def write(at, value):
                mine[at] = value.astype(jnp.bfloat16)

            pour(read, write, self.rows // 16)


def everyone_on_line(copies, src, dst, sem, g, s, to_rows):
    for d in range(1, 8):
        to = (s + d) % 8
        copies.remote(to_rows(to), dst.at[s], sem, g, to)


def mean_square(values):
    return jnp.mean(values * values, axis=-1, keepdims=True)


def pour(read, write, count):
    def piece(i, carry):
        at = aligned(i, 16, 16)
        write(at, read(at))
        return carry

    lax.fori_loop(0, count, piece, 0)


class LineScatter:
    def __init__(self, copies, part, rows, side, inbox, side_sem, line_sem, queue):
        self.copies, self.part, self.rows, self.queue = copies, part, rows, queue
        self.side, self.inbox, self.side_sem, self.line_sem = side, inbox, side_sem, line_sem
        self.g, self.s, _, _, self.z, self.c = where_am_i()

    def mine(self, chip):
        return self.part.at[aligned(2 * chip + self.c, self.rows, 16)]

    def begin(self):
        for chip in (3, 0, 2, 1):
            theirs = aligned(2 * chip + 1 - self.c, self.rows, 16)
            self.copies.remote(
                self.part.at[theirs], self.side.at[chip], self.side_sem.at[chip], self.g, self.s + 1 - 2 * self.c
            )

    def add_on(self, chip, way):
        own, side = self.mine(chip), self.side.at[chip]
        slot = chip - 1 if way == 0 else chip
        come = self.inbox.at[way, slot]
        arrived(side, self.side_sem.at[chip])
        arrived(come, self.line_sem.at[way, slot])

        def three(at):
            return own[at].astype(jnp.float32) + side[at].astype(jnp.float32) + come[at].astype(jnp.float32)

        def write(at, value):
            own[at] = value.astype(jnp.bfloat16)

        pour(three, write, self.rows // 16)

    def push(self, chip, way, when):
        slot = chip - 1 if way == 0 else chip
        to = (self.s + 2) % 8 if way == 0 else (self.s + 6) % 8
        return self.copies.remote(
            self.mine(chip), self.inbox.at[way, slot], self.line_sem.at[way, slot], self.g, to, when
        )

    def pass_on(self, chip, way):
        end = self.z == (0 if way == 0 else 3)
        own, side = self.mine(chip), self.side.at[chip]

        def two(at):
            return own[at].astype(jnp.float32) + side[at].astype(jnp.float32)

        def write(at, value):
            own[at] = value.astype(jnp.bfloat16)

        @pl.when(end)
        def _():
            arrived(side, self.side_sem.at[chip])
            pour(two, write, self.rows // 16)

        if way in self.queue:
            copies, entry = self.queue.pop(way)
            copies.settle(entry)
        self.queue[way] = (self.copies, self.push(chip, way, end))

    def start(self, i):
        self.pass_on(3 - i, 0)
        self.pass_on(i, 1)

    def hop(self, i):
        z = self.z
        for inner in (1, 2):

            @pl.when(z == inner)
            def _():
                near = inner == 1
                if i < 2:
                    self.add_on(3 - i if near else i, 0 if near else 1)
                else:
                    self.add_on(0 if near else 3, 1 if near else 0)

        for inner in (1, 2):
            near = inner == 1
            if i < 2:
                self.push(3 - i if near else i, 0 if near else 1, z == inner)
            else:
                self.push(0 if near else 3, 1 if near else 0, z == inner)

    def receive(self):
        z = self.z
        arrived(self.side.at[z], self.side_sem.at[z])
        left, right = jnp.maximum(z - 1, 0), jnp.minimum(z, 2)
        arrived(self.inbox.at[0, left], self.line_sem.at[0, left], z > 0)
        arrived(self.inbox.at[1, right], self.line_sem.at[1, right], z < 3)

    def total(self, at):
        z = self.z
        value = self.mine(z)[at].astype(jnp.float32) + self.side[z, at].astype(jnp.float32)
        from_left = self.inbox[0, jnp.maximum(z - 1, 0), at].astype(jnp.float32)
        from_right = self.inbox[1, jnp.minimum(z, 2), at].astype(jnp.float32)
        return value + jnp.where(z > 0, from_left, 0.0) + jnp.where(z < 3, from_right, 0.0)


def silu(values):
    return values / (1.0 + jnp.exp(-values))


def decay_table(rate, length):
    offset = lax.broadcasted_iota(jnp.int32, (length, length), 0) - lax.broadcasted_iota(jnp.int32, (length, length), 1)
    steps = jnp.maximum(offset, 0).astype(jnp.float32)
    return jnp.where(offset >= 0, jnp.exp(-rate * steps), 0.0)


def live_rows(first, count, length):
    return ((first + lax.broadcasted_iota(jnp.int32, (count, 1), 0)) < length).astype(jnp.float32)


def slope(values):
    sigma = 1.0 / (1.0 + jnp.exp(-values))
    return sigma * (1.0 + values * (1.0 - sigma))


def turned_table(rate, length):
    offset = lax.broadcasted_iota(jnp.int32, (length, length), 1) - lax.broadcasted_iota(jnp.int32, (length, length), 0)
    steps = jnp.maximum(offset, 0).astype(jnp.float32)
    return jnp.where(offset >= 0, jnp.exp(-rate * steps), 0.0)


def columns_of(out, tiles, b, rows):
    for owner in range(8):
        out[pl.ds(owner * rows, rows)] = jnp.broadcast_to(tiles[b, owner, :1], (128, 128)).T[:rows]


def turn(dst, read, count, columns):
    def block(i, carry):
        dst[pl.ds(0, columns), aligned(i, 128, 128)] = read(aligned(i, 128, 128)).T
        return carry

    lax.fori_loop(0, count, block, 0)


def tiles_of(width, body):
    def tile(i, carry):
        body(aligned(i, 256, 256), i)
        return carry

    lax.fori_loop(0, width // 256, tile, 0)


def layer_part(
    lengths, decay, x, cot, wq, wk, wv, wu, wo, w1, w2, w3,
    out_all, grad_all, fq, fk, fv, fu, fo, ff_, fs, ft,
    n1_all, dm_all, n2_all, da_all, q_all, k_all, v_all, u_all, o_all, f_all, s_all, t_all, pre_all, in_f, in_t, in_o, in_h, x_f, y_f,
    send, load, own, hop_n, side_n, hop_d, side_d, z_head, z_out, z_ff, xy_head, xy_out, xy_ff, spread_f, join_f,
    out, grad_x, out_sem, n1, dm, n2, da, h, a_v, b_v, w_v, wa_v, wo_v, p_v, turned, part, side, inbox, side_sem, line_sem,
    side_m, inbox_m, side_sem_m, line_sem_m, table, squares, inbox_sq, scale, scale_in, sq_sem, sc_sem, column,
    mix, mix_in, mix_sem, inverse, mixed, pre, pre_sem, go_v, grads_h,
    xy_f, xy_t, xy_o, xy_h, z_f, z_t, z_o, z_h,
):
    g, s, y, x_, z, c = where_am_i()
    others = across(y, x_)
    plane = [(o, 2 * z + e) for o in others for e in range(2)]
    rows, width = x.shape[1], x.shape[2]
    length = 8 * rows
    tokens = 2 * length
    depth, wide = wq.shape
    head = q_all.shape[1] // 2
    hidden = f_all.shape[0]
    quarter = hidden // 2
    half = length // 2
    target = g // 2
    mine = aligned(g % 2, head, head)
    here = c == target
    order = [(z + d) % 4 for d in (0, 1, 3, 2)]
    spare = Spare(send)
    copies, later, turned_out, bulk, last = [Copies(spare) for _ in range(5)]
    early, sums = [[Copies(spare) for _ in range(2)] for _ in range(2)]
    gather_n = Gather(copies, n1_all, rows, hop_n, side_n)
    gather_d = Gather(later, dm_all, rows, hop_d, side_d)
    gather_m = Gather(later, n2_all, rows, hop_n, side_n)
    gather_a = Gather(last, da_all, rows, hop_d, side_d)
    heads = list(zip((wq, wk, wv, wu), (q_all, k_all, v_all, u_all)))
    w1_f, w2_f, w3_f = [w_v.at[pl.ds(n * hidden, hidden)] for n in range(3)]
    w1_in, w2_in = [w_v.at[pl.ds(n * depth, depth), pl.ds(512, 2 * hidden)] for n in range(2)]
    w1_t, w2_t = [w_v.at[pl.ds(0, 2 * hidden), pl.ds(n * depth, depth)] for n in range(2)]
    low_v = p_v.at[2, pl.ds(0, length), pl.ds(0, 2 * head)]

    def at_b(b):
        return pl.ds(b * length, length)

    def dz(n, at):
        return p_v.at[n // 2, at, pl.ds((n % 2) * 2 * head, 2 * head)]

    def nat_v(at):
        return p_v.at[2, at, pl.ds(0, 2 * head)]

    local(w1, w1_in, load.at[0])
    local(w2, w2_in, load.at[1])
    greet(line_partners(g, s) + plane)

    def send_heads(n):
        src, dst = heads[n]
        for d in (2, 1, 3, 0):
            to = (z + d) % 4
            a, b = src.at[:, aligned(to, head, head)], dst.at[aligned(s, depth, 16), mine]
            if d:
                copies.remote(a, b, z_head.at[n, z], g, 2 * to + target)
            else:
                copies.remote(a, b, z_head.at[n, z], g, 2 * to + target, c != target)
                local(a, b, z_head.at[n, z], here)

    def pass_heads(n):
        dst = heads[n][1]
        for zs in order:
            block = dst.at[aligned(zs, 2 * depth, 16), mine]
            arrived(block, z_head.at[n, zs], here)
            for r, o in enumerate(others[:2]):
                copies.remote(block, block, xy_head.at[n, r, zs], o, s, here)

    def relay_heads(n):
        dst = heads[n][1]
        for zs in order:
            for r, when in ((0, here), (1, jnp.logical_not(here))):
                lanes = aligned(others[r] % 2, head, head)
                arrived(dst.at[aligned(zs, 2 * depth, 16), lanes], xy_head.at[n, r, zs], when)
                part_ = dst.at[aligned(2 * zs + r, depth, 16), lanes]
                copies.remote(part_, part_, xy_head.at[n, 2, zs], others[1 - r], s, when)

    def send_out():
        for i in range(2):
            to = 2 * c + i
            a = wo.at[pl.ds(i * head, head)]
            b = o_all.at[aligned(z % 2, head, head), aligned(g, wide, 128)]
            self_ = jnp.logical_and(to == z, c == z // 2)
            copies.remote(a, b, z_out.at[z % 2], g, 2 * to + z // 2, jnp.logical_not(self_))
            local(a, b, z_out.at[z % 2], self_)

    def pass_out():
        for j in range(2):
            arrived(o_all.at[pl.ds(j * head, head), aligned(g, wide, 128)], z_out.at[j])
        block = o_all.at[:, aligned(g, wide, 128)]
        for r, o in enumerate(others[:2]):
            copies.remote(block, block, xy_out.at[r], o, s)

    def relay_out():
        for r in range(2):
            lanes = aligned(others[r], wide, 128)
            arrived(o_all.at[:, lanes], xy_out.at[r])
            part_ = o_all.at[pl.ds(r * head, head), lanes]
            copies.remote(part_, part_, xy_out.at[2], others[1 - r], s)

    def spread_ff():
        for n, src in enumerate((w1_t, w2_t)):
            for r, o in enumerate(others):
                turned_out.remote(src.at[aligned(o, quarter, 16)], x_f.at[n, g], spread_f.at[n, r], o, s)
            local(src.at[aligned(g, quarter, 16)], x_f.at[n, g], spread_f.at[n, 3])

    def ff_block(n, group, zs):
        return (f_all, s_all)[n].at[aligned(group % 2, quarter, 16), aligned(zs, 2 * depth, 128)]

    def send_ff(n):
        for r, o in enumerate(others):
            arrived(x_f.at[n, o], spread_f.at[n, r])
        arrived(x_f.at[n, g], spread_f.at[n, 3])
        b = (f_all, s_all)[n].at[aligned(g % 2, quarter, 16), aligned(s, depth, 128)]
        for d in (2, 1, 3, 0):
            to = (z + d) % 4
            a = x_f.at[n, to]
            if d:
                later.remote(a, b, z_ff.at[n, z], g, 2 * to + target)
            else:
                later.remote(a, b, z_ff.at[n, z], g, 2 * to + target, c != target)
                local(a, b, z_ff.at[n, z], here)

    def pass_ff(n):
        for zs in order:
            block = ff_block(n, g, zs)
            arrived(block, z_ff.at[n, zs], here)
            for r, o in enumerate(others[:2]):
                later.remote(block, block, xy_ff.at[n, r, zs], o, s, here)

    def relay_ff(n):
        for zs in order:
            for r, when in ((0, here), (1, jnp.logical_not(here))):
                arrived(ff_block(n, others[r], zs), xy_ff.at[n, r, zs], when)
                part_ = (f_all, s_all)[n].at[aligned(others[r] % 2, quarter, 16), aligned(2 * zs + r, depth, 128)]
                later.remote(part_, part_, xy_ff.at[n, 2, zs], others[1 - r], s, when)

    def send_third():
        block = t_all.at[:, aligned(g, wide, 128)]
        for r, o in enumerate(others[:2]):
            later.remote(w3, block, xy_ff.at[2, r, 0], o, s)
        local(w3, block, z_ff.at[2, 0])

    def relay_third():
        for r in range(2):
            lanes = aligned(others[r], wide, 128)
            arrived(t_all.at[:, lanes], xy_ff.at[2, r, 0])
            part_ = t_all.at[pl.ds(r * quarter, quarter), lanes]
            later.remote(part_, part_, xy_ff.at[2, 2, 0], others[1 - r], s)

    send_heads(0)
    send_heads(1)
    for b in range(2):

        def norm(at):
            v = x[b, at].astype(jnp.float32)
            return v * lax.rsqrt(mean_square(v) + EPS)

        def keep(at, value):
            n1[b, at] = value.astype(jnp.bfloat16)

        pour(norm, keep, rows // 16)
        first = s * rows

        def masked(i, carry):
            at = aligned(i, 16, 16)
            live = live_rows(first + i * 16, 16, lengths[0, b])
            dm[b, at] = (cot[b, at].astype(jnp.float32) * live).astype(jnp.bfloat16)
            return carry

        lax.fori_loop(0, rows // 16, masked, 0)
    for n, (src, dst) in enumerate(((w1_in, w1_t), (w2_in, w2_t))):
        arrived(src, load.at[n])
        dst[...] = src[...].T
    spread_ff()
    pass_heads(0)
    send_heads(2)
    pass_heads(1)
    send_heads(3)
    for b in range(2):
        gather_n.begin(n1.at[b], own.at[0, b], b)
    pass_heads(2)
    relay_heads(0)
    pass_heads(3)
    send_out()
    relay_heads(1)
    gather_n.step(0, 1)
    gather_n.step(1, 1)
    pass_out()
    relay_heads(2)
    gather_n.step(0, 2)
    gather_n.step(1, 2)
    relay_heads(3)
    relay_out()
    gather_n.step(0, 3)
    send_ff(0)
    send_ff(1)
    send_third()
    over = others[2]
    for n, (_, dst) in enumerate(heads):
        for zs in range(4):
            block = dst.at[pl.ds(zs * 2 * depth, 2 * depth), aligned(over % 2, head, head)]
            arrived(block, xy_head.at[n, 2, zs], over // 2 == c)
    arrived(o_all.at[:, aligned(over, wide, 128)], xy_out.at[2])
    for n, (_, dst) in enumerate(heads):
        local(dst, wa_v.at[n], load.at[n])
    local(o_all, wo_v, load.at[4])
    gather_n.finish(own.at[0, 0], 0)
    local(n1_all.at[0], a_v.at[at_b(0)], load.at[5])
    for j in range(2):
        table[j] = decay_table(decay[4 * (2 * c + j) + z], length)
    for n in range(4):
        arrived(wa_v.at[n], load.at[n])
    arrived(wo_v, load.at[4])

    def scatters_of(copies, first, queue):
        kept = (side, inbox, side_sem, line_sem) if first else (side_m, inbox_m, side_sem_m, line_sem_m)
        return [LineScatter(copies[b], part.at[b], rows, *[k.at[b] for k in kept], queue) for b in range(2)]

    scatters = scatters_of(early, True, {})
    for b in range(2):
        if b == 1:
            gather_n.step(1, 3)
            gather_n.finish(own.at[0, 1], 1)
            local(n1_all.at[1], a_v.at[at_b(1)], load.at[6])
        arrived(a_v.at[at_b(b)], load.at[5 + b])
        if b == 1:
            for j in range(2):
                arrived(pre.at[j], pre_sem.at[j])

        def project(i, carry):
            at = aligned(i, half, 16)
            from_ = aligned(2 * b + i, half, 16)
            for n in range(4):
                value = product(a_v[from_], wa_v[n])
                for j in range(2):
                    pre[j, n, at] = value[:, j * head : (j + 1) * head]
            return carry

        lax.fori_loop(0, 2, project, 0)
        if b == 1:
            scatters[0].start(1)
        live = live_rows(0, length, lengths[0, b])
        square = 0.0
        for j in range(2):
            q = silu(pre[j, 0]).astype(jnp.bfloat16)
            k = (silu(pre[j, 1]) * live).astype(jnp.bfloat16)
            v = (silu(pre[j, 2]) * live).astype(jnp.bfloat16)
            scores = (product_right(q, k) * table[j]).astype(jnp.bfloat16)
            attended = product(scores, v)
            pre[j, 4] = attended
            gated = silu(pre[j, 3]) * attended
            square = square + jnp.sum(gated * gated, axis=-1, keepdims=True)
            low_v[:, pl.ds(j * head, head)] = gated.astype(jnp.bfloat16)
            local(pre.at[j], pre_all.at[b, j], pre_sem.at[j])
        row = jnp.broadcast_to(square, (length, 128)).T[:8]
        for to in range(8):
            squares[b, to, :, :rows] = row[:, to * rows : (to + 1) * rows]
        everyone_on_line(later, squares, inbox_sq.at[b], sq_sem.at[b], g, s, lambda to: squares.at[b, to])
        local(squares.at[b, s], inbox_sq.at[b, s], sq_sem.at[b])

        def out_part(i, carry):
            at = aligned(i, 256, 256)
            part[b, :, at] = product(low_v[...], wo_v[:, at]).astype(jnp.bfloat16)
            return carry

        lax.fori_loop(0, width // 256, out_part, 0)
        scatters[b].begin()
        if b == 0:
            scatters[0].start(0)

    def hidden_state(b):
        arrived(inbox_sq.at[b], sq_sem.at[b])
        total = inbox_sq[b, 0]
        for d in range(1, 8):
            total = total + inbox_sq[b, d]
        row = lax.rsqrt(total / width + EPS)
        scale[b] = row
        column[b] = jnp.broadcast_to(row[:1], (128, 128)).T
        scatter = scatters[b]
        scatter.receive()

        def finish(i, carry):
            piece = aligned(i, 16, 16)
            at = aligned(b * (rows // 16) + i, 16, 16)
            a = scatter.total(piece) * column[b, piece, :1]
            value = x[b, piece].astype(jnp.float32) + a
            h[at] = value
            n2[b, piece] = (value * lax.rsqrt(mean_square(value) + EPS)).astype(jnp.bfloat16)
            return carry

        lax.fori_loop(0, rows // 16, finish, 0)
        gather_m.begin(n2.at[b], own.at[2, b], b)

    gather_d.begin(dm.at[0], own.at[1, 0], 0)
    scatters[0].hop(0)
    relay_third()
    scatters[0].start(2)
    scatters[0].hop(1)
    pass_ff(0)
    scatters[1].start(0)
    scatters[0].hop(2)
    pass_ff(1)
    gather_d.step(0, 1)
    hidden_state(0)
    scatters[1].start(1)
    scatters[1].hop(0)
    gather_d.step(0, 2)
    scatters[1].start(2)
    scatters[1].hop(1)
    gather_m.step(0, 1)
    scatters[1].hop(2)
    relay_ff(0)
    gather_d.step(0, 3)
    gather_m.step(0, 2)
    gather_d.begin(dm.at[1], own.at[1, 1], 1)
    hidden_state(1)
    gather_m.step(0, 3)
    relay_ff(1)
    gather_d.finish(own.at[1, 0], 0)
    local(dm_all.at[0], b_v.at[at_b(0)], load.at[2])
    gather_m.finish(own.at[2, 0], 0)
    local(n2_all.at[0], a_v.at[at_b(0)], load.at[0])
    gather_d.step(1, 1, True)
    gather_m.step(1, 1, True)
    turned_out.finish()
    for n, (dst, room) in enumerate(((f_all, w1_f), (s_all, w2_f), (t_all, w3_f))):
        if n < 2:
            for zs in range(4):
                arrived(ff_block(n, over, zs), xy_ff.at[n, 2, zs], over // 2 == c)
        else:
            arrived(dst.at[:, aligned(over, wide, 128)], xy_ff.at[2, 2, 0])
        if n == 2:
            arrived(dst.at[:, aligned(g, wide, 128)], z_ff.at[2, 0])
        local(dst, room, load.at[4 + n])
    for b in range(2):
        early[b].finish()

    def feed_forward(b):
        def tile(i, carry):
            at = aligned(b * 2 + i, half, 16)
            first = product_right(a_v[at], w1_f[...])
            second = product_right(a_v[at], w2_f[...])
            back = product_right(b_v[at], w3_f[...])
            p_v[0, at] = (back * second).astype(jnp.bfloat16)
            p_v[1, at] = (back * first).astype(jnp.bfloat16)
            p_v[2, at] = (first * second).astype(jnp.bfloat16)
            return carry

        lax.fori_loop(0, 2, tile, 0)

    def norm_part(b):
        def body(at, i):
            value = product(p_v[0, at_b(b)], w1_f[:, at]) + product(p_v[1, at_b(b)], w2_f[:, at])
            part[b, :, at] = value.astype(jnp.bfloat16)

        tiles_of(width, body)

    def mixed_part(b):
        def body(at, i):
            part[b, :, at] = product(p_v[2, at_b(b)], w3_f[:, at]).astype(jnp.bfloat16)

        tiles_of(width, body)

    half_w = width // 2
    groups_f = [GroupSum(bulk, w_v.at[pl.ds(n * hidden, hidden)], in_f.at[n], xy_f.at[n]) for n in range(2)]
    groups_t = ColumnSum(bulk, w_v.at[pl.ds(2 * hidden, hidden)], in_t, xy_t)

    def rooms_ff(ref):
        return ref.at[pl.ds(0, hidden), pl.ds(0, half_w)], ref.at[pl.ds(0, quarter), pl.ds(half_w, half_w)]

    def spread_place(i):
        return pl.ds(pl.multiple_of((i % 2) * half_w + (i // 2) * 256, 256), 256)

    def weight_part(n, operand):
        turn(turned, lambda t: p_v[n, t], tokens // 128, hidden)

        def body(at, i):
            place = spread_place(i) if n < 2 else at
            w_v[pl.ds(n * hidden, hidden), place] = product(turned[...], operand[:, at]).astype(jnp.bfloat16)

        tiles_of(width, body)
        if n < 2:
            groups_f[n].depart()
        else:
            groups_t.depart()

    def hidden_gradient(b):
        scatter = second[b]
        scatter.receive()

        def finish(i, carry):
            piece = aligned(i, 16, 16)
            at = aligned(b * (rows // 16) + i, 16, 16)
            value = h[at]
            scale_h = lax.rsqrt(mean_square(value) + EPS)
            normed = value * scale_h
            grad = scatter.total(piece)
            along = jnp.mean(normed * grad, axis=-1, keepdims=True)
            live = live_rows(s * rows + i * 16, 16, lengths[0, b])
            upstream = cot[b, piece].astype(jnp.float32) * live
            grad_hidden = upstream + scale_h * (grad - normed * along)
            grad_x[at] = grad_hidden
            low = grad_hidden.astype(jnp.bfloat16)
            da[b, piece] = low
            dot = jnp.mean(low.astype(jnp.float32) * (value - x[b, piece].astype(jnp.float32)), axis=-1, keepdims=True)
            column[b, piece] = jnp.broadcast_to(dot, (16, 128))
            return carry

        lax.fori_loop(0, rows // 16, finish, 0)
        gather_a.begin(da.at[b], own.at[3, b], b)
        mix[b, :, :rows] = column[b].T[:8, :rows]
        for d in range(1, 8):
            last.remote(mix.at[b], mix_in.at[b, s], mix_sem.at[b], g, (s + d) % 8)
        local(mix.at[b], mix_in.at[b, s], mix_sem.at[b])

    second = scatters_of(early, True, {})
    for n in (0, 4, 5, 2, 6):
        ref = {0: a_v.at[at_b(0)], 2: b_v.at[at_b(0)], 4: w1_f, 5: w2_f, 6: w3_f}[n]
        arrived(ref, load.at[n])
    feed_forward(0)
    gather_m.step(1, 2, True)
    gather_d.step(1, 2, True)
    norm_part(0)
    second[0].begin()
    second[0].start(0)
    for k in (1, 2):
        gather_d.step(1, k, False)
        gather_m.step(1, k, False)
    gather_m.step(1, 3)
    gather_d.step(1, 3)
    gather_d.finish(own.at[1, 1], 1)
    local(dm_all.at[1], b_v.at[at_b(1)], load.at[3])
    gather_m.finish(own.at[2, 1], 1)
    local(n2_all.at[1], a_v.at[at_b(1)], load.at[1])
    for b in range(2):
        for d in range(1, 8):
            later.remote(scale.at[b], scale_in.at[b, s], sc_sem.at[b], g, (s + d) % 8)
        local(scale.at[b], scale_in.at[b, s], sc_sem.at[b])
    second[0].start(1)
    second[0].hop(0)
    arrived(a_v.at[at_b(1)], load.at[1])
    arrived(b_v.at[at_b(1)], load.at[3])
    feed_forward(1)
    second[0].start(2)
    second[0].hop(1)
    second[0].hop(2)
    norm_part(1)
    def load_pre(b, j):
        local(pre_all.at[b, j], pre.at[j], pre_sem.at[j])

    def attention_back(b):
        gather_a.finish(own.at[3, b], b)
        local(da_all.at[b], a_v.at[at_b(b)], load.at[b])
        arrived(mix_in.at[b], mix_sem.at[b])
        columns_of(mixed, mix_in, b, rows)
        live = live_rows(0, length, lengths[0, b])
        arrived(a_v.at[at_b(b)], load.at[b])
        for j in range(2):
            arrived(pre.at[j], pre_sem.at[j])
            lanes = pl.ds(j * head, head)
            error = product_right(a_v[at_b(b)], wo_v[pl.ds(j * head, head)])
            q_pre, k_pre, v_pre, u_pre, o = [pre[j, n] for n in range(5)]
            sigma = 1.0 / (1.0 + jnp.exp(-u_pre))
            u = u_pre * sigma
            scale_g = inverse[at_b(b), :1]
            nat = u * o * scale_g
            nat_v(at_b(b))[:, lanes] = nat.astype(jnp.bfloat16)
            dg = scale_g * (error - nat * mixed[:, :1])
            dz(3, at_b(b))[:, lanes] = (dg * o * (sigma * (1.0 + u_pre * (1.0 - sigma)))).astype(jnp.bfloat16)
            do = (dg * u).astype(jnp.bfloat16)
            q = silu(q_pre).astype(jnp.bfloat16)
            k = (silu(k_pre) * live).astype(jnp.bfloat16)
            v = (silu(v_pre) * live).astype(jnp.bfloat16)
            scores = (product_right(k, q) * table[j]).astype(jnp.bfloat16)
            dv = product(scores, do)
            d_scores = (product_right(v, do) * table[j]).astype(jnp.bfloat16)
            dk = product(d_scores, q)
            dq = product_left(d_scores, k)
            dz(0, at_b(b))[:, lanes] = (dq * slope(pre[j, 0])).astype(jnp.bfloat16)
            dz(1, at_b(b))[:, lanes] = (dk * live * slope(pre[j, 1])).astype(jnp.bfloat16)
            dz(2, at_b(b))[:, lanes] = (dv * live * slope(pre[j, 2])).astype(jnp.bfloat16)
            if b == 0:
                load_pre(1, j)

    def first_part(b):
        def body(at, i):
            value = product_right(dz(0, at_b(b))[...], wa_v[0, at])
            for n in range(1, 4):
                value = value + product_right(dz(n, at_b(b))[...], wa_v[n, at])
            part[b, :, at] = value.astype(jnp.bfloat16)

        tiles_of(width, body)

    second[1].begin()
    second[1].start(0)
    hidden_gradient(0)
    weight_part(0, a_v)
    second[1].start(1)
    second[1].hop(0)
    gather_a.step(0, 1)
    third = scatters_of(sums, False, {})
    early[0].finish()
    mixed_part(0)
    third[0].begin()
    third[0].start(0)
    second[1].start(2)
    second[1].hop(1)
    second[1].hop(2)
    third[0].start(1)
    third[0].hop(0)
    gather_a.step(0, 2)
    weight_part(1, a_v)
    hidden_gradient(1)
    third[0].start(2)
    third[0].hop(1)
    groups_f[0].middle(*rooms_ff(a_v), load.at[pl.ds(13, 2)])
    gather_a.step(0, 3)
    third[0].hop(2)
    early[1].finish()
    mixed_part(1)
    third[1].begin()
    third[1].start(0)
    for j in range(2):
        table[j] = turned_table(decay[4 * (2 * c + j) + z], length)
    for b in range(2):
        arrived(scale_in.at[b], sc_sem.at[b])
        columns_of(inverse.at[at_b(b)], scale_in, b, rows)

    for j in range(2):
        arrived(pre.at[j], pre_sem.at[j])
        load_pre(0, j)
    gather_a.step(1, 1)
    third[1].start(1)
    third[1].hop(0)
    weight_part(2, b_v)
    gather_a.step(1, 2)
    third[1].start(2)
    third[1].hop(1)
    third[1].hop(2)
    groups_f[1].middle(*rooms_ff(b_v), load.at[pl.ds(13, 2)])
    for b in range(2):
        local(n1_all.at[b], b_v.at[at_b(b)], load.at[2 + b])
    later.finish()
    attention_back(0)
    gather_a.step(1, 3)
    def sum_ff(n):
        small = w_v.at[pl.ds(n * hidden, quarter), pl.ds(half_w, half_w)]
        groups_f[n].settle()
        total = w_v.at[pl.ds(n * hidden, quarter), pl.ds(0, half_w)]
        groups_f[n].final(total, small, load.at[pl.ds(13, 2)])
        for d in (2, 1, 3, 0):
            chip = (z + d) % 4
            src = total.at[:, aligned(chip, depth, 128)]
            if d:
                last.remote(src, y_f.at[n, z], z_f.at[n, z], g, 2 * chip + c)
            else:
                local(src, y_f.at[n, z], z_f.at[n, z])

    def join_ff(n, result):
        for r, o in enumerate(others + (g,)):
            arrived(y_f.at[n, o], z_f.at[n, o])
            dst = result.at[aligned(g, quarter, 16)]
            if r < 3:
                last.remote(y_f.at[n, o], dst, join_f.at[n, r], o, s)
            else:
                local(y_f.at[n, o], dst, join_f.at[n, r])

    def rooms_column(rows):
        return [b_v.at[pl.ds(0, rows), pl.ds(i * wide, wide)] for i in range(4)]

    def sum_third():
        groups_t.final(rooms_column(quarter), load.at[pl.ds(13, 4)])
        local(w_v.at[pl.ds(2 * hidden, hidden), aligned(g, wide, 128)], ft, z_t)

    groups_h = [GroupSum(last, grads_h.at[n], in_h.at[n], xy_h.at[n]) for n in range(4)]
    groups_o = ColumnSum(last, go_v, in_o, xy_o)

    def room_h(first, count):
        return w_v.at[pl.ds(first * head, count * head), pl.ds(half_w, half_w)]

    def middle_head(n):
        groups_h[n].middle(room_h(3 * (n % 2), 2), room_h(3 * (n % 2) + 2, 1), load.at[pl.ds(18, 2)])

    def head_part(n):
        turn(turned, lambda t: dz(n, t)[...], tokens // 128, 2 * head)

        def body(at, i):
            grads_h[n, :, spread_place(i)] = product(turned[pl.ds(0, 2 * head)], b_v[:, at]).astype(jnp.bfloat16)

        tiles_of(width, body)

    def out_weight():
        turn(turned, lambda t: nat_v(t)[...], tokens // 128, 2 * head)

        def body(at, i):
            go_v[:, at] = product(turned[pl.ds(0, 2 * head)], a_v[:, at]).astype(jnp.bfloat16)

        tiles_of(width, body)

    def sum_head(n, result):
        total = room_h(6 + n, 1)
        groups_h[n].final(total, room_h(10, 1), load.at[pl.ds(18, 2)])
        for d in (2, 1, 3, 0):
            chip = (z + d) % 4
            src = total.at[:, aligned(chip, depth, 128)]
            dst = result.at[aligned(z, head, head)]
            if d:
                last.remote(src, dst, z_h.at[n, d], g, 2 * chip + c)
            else:
                local(src, dst, z_h.at[n, d])

    def sum_out():
        groups_o.final(rooms_column(head), load.at[pl.ds(13, 4)])
        mine_o = go_v.at[:, aligned(g, wide, 128)]
        for j in range(2):
            to = 2 * (2 * c + j) + z // 2
            src = mine_o.at[pl.ds(j * head, head)]
            dst = fo.at[aligned(z % 2, head, head)]
            last.remote(src, dst, z_o.at[z % 2], g, to, to != s)
            local(src, dst, z_o.at[z % 2], to == s)

    sum_ff(0)
    attention_back(1)
    for b in range(2):
        arrived(b_v.at[at_b(b)], load.at[2 + b])
    head_part(0)
    groups_h[0].depart()
    for b in range(2):
        third[b].receive()
        scatter = third[b]

        def result(i, carry):
            piece = aligned(i, 16, 16)
            at = aligned(b * (rows // 16) + i, 16, 16)
            out[at] = (h[at] + scatter.total(piece)).astype(jnp.bfloat16)
            return carry

        lax.fori_loop(0, rows // 16, result, 0)
    local(out, out_all, out_sem.at[2])
    for b in range(2):
        sums[b].finish()
    fourth = scatters_of(early, True, {})
    first_part(0)
    fourth[0].begin()
    fourth[0].start(0)
    head_part(1)
    groups_h[1].depart()
    sum_ff(1)
    groups_t.middle(
        [w_v.at[pl.ds(0, quarter), pl.ds(half_w + k * wide, wide)] for k in range(2)], load.at[pl.ds(13, 2)]
    )
    first_part(1)
    fourth[0].start(1)
    fourth[0].hop(0)
    fourth[1].begin()
    head_part(2)
    groups_h[2].depart()
    middle_head(0)
    head_part(3)
    groups_h[3].depart()
    middle_head(1)
    fourth[0].start(2)
    fourth[0].hop(1)
    out_weight()
    groups_o.depart()
    middle_head(2)
    fourth[0].hop(2)
    fourth[1].start(0)
    middle_head(3)
    sum_head(0, fq)
    fourth[1].start(1)
    fourth[1].hop(0)
    groups_o.middle(rooms_column(head), load.at[pl.ds(13, 2)])
    sum_head(1, fk)
    join_ff(0, ff_)
    join_ff(1, fs)
    fourth[1].start(2)
    fourth[1].hop(1)
    sum_head(2, fv)
    fourth[1].hop(2)
    sum_head(3, fu)
    sum_out()
    sum_third()
    for b in range(2):
        fourth[b].receive()
        scatter = fourth[b]

        def finish_x(i, carry):
            piece = aligned(i, 16, 16)
            at = aligned(b * (rows // 16) + i, 16, 16)
            v = x[b, piece].astype(jnp.float32)
            scale_x = lax.rsqrt(mean_square(v) + EPS)
            normed = v * scale_x
            grad = scatter.total(piece)
            along = jnp.mean(normed * grad, axis=-1, keepdims=True)
            grad_x[at] = grad_x[at] + scale_x * (grad - normed * along)
            return carry

        lax.fori_loop(0, rows // 16, finish_x, 0)
        block = pl.ds(b * rows, rows)
        local(grad_x.at[block], grad_all.at[block], out_sem.at[b])


    arrived(out, out_sem.at[2])
    for b in range(2):
        arrived(grad_x.at[pl.ds(b * rows, rows)], out_sem.at[b])
    for n, result in enumerate((ff_, fs)):
        for r in range(4):
            arrived(result.at[pl.ds(0, quarter)], join_f.at[n, r])
    arrived(ft, z_t)
    for j in range(2):
        arrived(fo.at[pl.ds(0, head)], z_o.at[j])
    for n, result in enumerate((fq, fk, fv, fu)):
        for d in range(4):
            arrived(result.at[pl.ds(0, head)], z_h.at[n, d])
    for b in range(2):
        early[b].finish()
    bulk.finish()
    last.finish()
    copies.finish()


def call(kernel, number, ins, outs, scratch, name):
    return pl.pallas_call(
        kernel,
        out_shape=[shape for shape, _ in outs],
        in_specs=[spec for _, spec in ins],
        out_specs=[spec for _, spec in outs],
        scratch_shapes=scratch,
        compiler_params=pltpu.CompilerParams(
            collective_id=number, has_side_effects=True, vmem_limit_bytes=64 * 2**20 - 2**17
        ),
        name=name,
    )(*[value for value, _ in ins])


def finish_arrays(count, turned_count, *refs):
    ins, outs, held, done = refs[:count], refs[count : 2 * count], refs[2 * count : 3 * count], refs[3 * count : 4 * count]
    in_sem, out_sem = refs[4 * count :]
    for i in range(count):
        local(ins[i], held[i], in_sem.at[i])
    for i in range(count):
        arrived(held[i], in_sem.at[i])
        if i < 2:
            local(held[i], outs[i], out_sem.at[i])
            continue
        if i < 2 + turned_count:
            done[i][...] = held[i][...].T.astype(jnp.float32)
        else:

            def write(at, value):
                done[i][at] = value

            pour(lambda at: held[i][at].astype(jnp.float32), write, held[i].shape[0] // 16)
        local(done[i], outs[i], out_sem.at[i])
    for i in range(count):
        arrived(outs[i], out_sem.at[i])


def finished(out, grad_x, turned, straight):
    arrays = [out, grad_x] + turned + straight
    shapes = [jax.ShapeDtypeStruct(v.shape, v.dtype) for v in (out, grad_x)]
    shapes += [wide_array(*v.shape[::-1]) for v in turned] + [wide_array(*v.shape) for v in straight]
    count = len(arrays)
    small = jax.ShapeDtypeStruct((8, 128), jnp.float32)
    done = [small, small] + shapes[2:]
    return pl.pallas_call(
        functools.partial(finish_arrays, count, len(turned)),
        out_shape=shapes,
        in_specs=[ANY] * count,
        out_specs=[ANY] * count,
        scratch_shapes=[pltpu.VMEM(v.shape, v.dtype) for v in arrays] + [pltpu.VMEM(v.shape, v.dtype) for v in done]
        + [dma(count), dma(count)],
        compiler_params=pltpu.CompilerParams(vmem_limit_bytes=62 * 2**20),
        name="finish_arrays",
    )(*arrays)


def low_array(*shape):
    return jax.ShapeDtypeStruct(shape, jnp.bfloat16)


def wide_array(*shape):
    return jax.ShapeDtypeStruct(shape, jnp.float32)


def dma(*shape):
    return pltpu.SemaphoreType.DMA(shape)


def scatter_scratch(rows, width):
    return [
        pltpu.VMEM((2, 4, rows, width), jnp.bfloat16),
        pltpu.VMEM((2, 2, 3, rows, width), jnp.bfloat16),
        dma(2, 4),
        dma(2, 2, 3),
    ]


def line_shards(
    tokens, cotangent, lengths, decay_rate,
    w_query, w_key, w_value, w_gate, w_out, w_first, w_second, w_third,
):
    bf16, f32 = jnp.bfloat16, jnp.float32
    rows, width = tokens.shape[2], tokens.shape[3]
    depth, wide = w_query.shape
    head = width // decay_rate.shape[0]
    hidden = w_third.shape[0]
    length = 8 * rows
    x_low = tokens[:, 0]
    in_smem = pl.BlockSpec(memory_space=pltpu.SMEM)
    gathered = low_array(2, length, width)
    out, grad_x, fq, fk, fv, fu, fo, ff, fs, ft = call(
        layer_part,
        0,
        [(lengths.T, in_smem), (decay_rate, in_smem), (x_low, VMEM), (cotangent[:, 0], VMEM)]
        + [(v, ANY) for v in (w_query, w_key, w_value, w_gate, w_out, w_first, w_second, w_third)],
        [(low_array(2 * rows, width), ANY), (wide_array(2 * rows, width), ANY)]
        + [(low_array(wide, depth), ANY)] * 4 + [(low_array(depth, wide), ANY)]
        + [(low_array(2 * hidden, depth), ANY)] * 2 + [(low_array(hidden, wide), ANY)]
        + [(gathered, ANY)] * 4
        + [(low_array(width, 2 * head), ANY)] * 4
        + [(low_array(2 * head, width), ANY)]
        + [(low_array(hidden, width), ANY)] * 3
        + [(wide_array(2, 2, 5, length, head), ANY)]
        + [(low_array(2, 5 * hidden // 2, width // 2), ANY), (low_array(2, 3, hidden // 2, wide), ANY), (low_array(2, 3, head, wide), ANY),
           (low_array(4, 5 * head, width // 2), ANY)]
        + [(low_array(2, 4, hidden // 2, depth), ANY)] * 2,
        [dma(128), dma(26), dma(4, 2)] + [dma(2, 2, 3), dma(2, 7)] * 2
        + [dma(4, 4), dma(2), dma(3, 4), dma(4, 3, 4), dma(3), dma(3, 3, 4), dma(2, 4), dma(2, 4)]
        + [pltpu.VMEM((2 * rows, width), bf16), pltpu.VMEM((2 * rows, width), f32), dma(3)]
        + [pltpu.VMEM((2, rows, width), bf16)] * 4
        + [pltpu.VMEM((2 * rows, width), f32),
           pltpu.VMEM((2 * length, width), bf16), pltpu.VMEM((2 * length, width), bf16), pltpu.VMEM((3 * hidden, width), bf16),
           pltpu.VMEM((4, width, 2 * head), bf16), pltpu.VMEM((2 * head, width), bf16),
           pltpu.VMEM((3, 2 * length, hidden), bf16), pltpu.VMEM((hidden, 2 * length), bf16),
           pltpu.VMEM((2, length, width), bf16)]
        + scatter_scratch(rows, width) + scatter_scratch(rows, width)
        + [pltpu.VMEM((2, length, length), f32), pltpu.VMEM((2, 8, 8, 128), f32), pltpu.VMEM((2, 8, 8, 128), f32),
           pltpu.VMEM((2, 8, 128), f32), pltpu.VMEM((2, 8, 8, 128), f32), dma(2), dma(2), pltpu.VMEM((2, 128, 128), f32),
           pltpu.VMEM((2, 8, 128), f32), pltpu.VMEM((2, 8, 8, 128), f32), dma(2),
           pltpu.VMEM((2 * length, 128), f32), pltpu.VMEM((length, 128), f32),
           pltpu.VMEM((2, 5, length, head), f32), dma(2),
           pltpu.VMEM((2 * head, width), bf16), pltpu.VMEM((4, 2 * head, width), bf16),
           dma(2, 4), dma(2, 3), dma(2, 3), dma(4, 4), dma(2, 4), dma(), dma(2), dma(4, 4)],
        "layer_part",
    )[:10]
    results = finished(out, grad_x, [fq, fk, fv, fu, ff, fs], [fo, ft])
    out, grad_x, fq, fk, fv, fu, ff, fs, fo, ft = results
    return (out.reshape(2, 1, rows, width), grad_x.reshape(2, 1, rows, width), fq, fk, fv, fu, fo, ff, fs, ft)


def solution(mesh):
    in_specs = (
        P(None, "grp", "seq", None),
        P(None, "grp", "seq", None),
        P(None, "grp"),
        P(),
        P("seq", "grp"),
        P("seq", "grp"),
        P("seq", "grp"),
        P("seq", "grp"),
        P("seq", "grp"),
        P("seq", "grp"),
        P("seq", "grp"),
        P("seq", "grp"),
    )
    out_specs = (
        P(None, "grp", "seq", None),
        P(None, "grp", "seq", None),
        P("seq", "grp"),
        P("seq", "grp"),
        P("seq", "grp"),
        P("seq", "grp"),
        P("seq", "grp"),
        P("seq", "grp"),
        P("seq", "grp"),
        P("seq", "grp"),
    )
    fast = mesh.shape["grp"] == 4 and mesh.shape["seq"] == 8
    return jax.shard_map(line_shards if fast else shards, mesh=mesh, in_specs=in_specs, out_specs=out_specs, check_vma=False)
```

```python
import functools

import jax
import jax.numpy as jnp
from jax import lax
from jax.experimental import pallas as pl
from jax.experimental.pallas import tpu as pltpu
from jax.sharding import PartitionSpec as P

EPS = 1e-06
HIGH = lax.Precision.HIGHEST
MESH = pl.DeviceIdType.MESH
ANY = pl.BlockSpec(memory_space=pl.ANY)
VMEM = pl.BlockSpec(memory_space=pltpu.VMEM)


def prefix(value, axis, join, neutral, backward):
    count, mine = (lax.axis_size(axis), lax.axis_index(axis))
    pieces = jax.tree.map(lambda part: lax.all_gather(part, axis), value)
    if backward:
        pieces = jax.tree.map(lambda part: part[::-1], pieces)
        mine = count - 1 - mine
    subtotal = jax.tree.map(
        lambda part, zero: jnp.full_like(part, 0) + jnp.asarray(zero, part.dtype), value, neutral
    )

    def step(position, subtotal):
        longer = join(subtotal, jax.tree.map(lambda part: part[position], pieces))
        return jax.tree.map(lambda new, old: jnp.where(position < mine, new, old), longer, subtotal)

    return lax.fori_loop(0, count - 1, step, subtotal)


def norm_rows(values):
    return values * lax.rsqrt(jnp.mean(values * values, axis=-1, keepdims=True) + EPS)


def norm_back(values, gradient):
    _, pull = jax.vjp(norm_rows, values)
    return pull(gradient)[0]


def silu_slope(values):
    sigma = jax.nn.sigmoid(values)
    return sigma * (1.0 + values * (1.0 - sigma))


def product(left, right):
    return jnp.dot(left, right, preferred_element_type=jnp.float32)


def product_left(left, right):
    return lax.dot_general(
        left, right, (((0,), (0,)), ((), ())), preferred_element_type=jnp.float32
    )


def product_right(left, right):
    return lax.dot_general(
        left, right, (((1,), (1,)), ((), ())), preferred_element_type=jnp.float32
    )


def combine_state(earlier, later):
    return (later[1][:, None, None] * earlier[0] + later[0], earlier[1] * later[1])


def shards(
    tokens,
    cotangent,
    lengths,
    decay_rate,
    w_query,
    w_key,
    w_value,
    w_gate,
    w_out,
    w_first,
    w_second,
    w_third,
):
    micro = tokens.shape[0]
    block_rows = tokens.shape[2]
    width = tokens.shape[3]
    heads = decay_rate.shape[0]
    head_dim = width // heads
    hidden_width = w_third.shape[0] * lax.axis_size("seq")
    places = jnp.arange(block_rows).astype(jnp.float32)
    slot_index = lax.axis_index("seq") * block_rows + jnp.arange(block_rows)
    offset = places[:, None] - places[None, :]
    weight = jnp.where(
        offset[None] >= 0, jnp.exp(-decay_rate[:, None, None] * jnp.maximum(offset, 0.0)[None]), 0.0
    )
    query_fac = jnp.exp(-decay_rate[None, :] * (places[:, None] + 1.0))[:, :, None]
    key_fac = jnp.exp(-decay_rate[None, :] * (block_rows - 1.0 - places[:, None]))[:, :, None]
    step_decay = jnp.exp(-decay_rate * block_rows)
    empty_state = jnp.zeros((heads, head_dim, head_dim), jnp.float32)
    unit_decay = jnp.ones((heads,), jnp.float32)
    partial_rows = (
        lax.all_gather(w_query, "grp", axis=1, tiled=True),
        lax.all_gather(w_key, "grp", axis=1, tiled=True),
        lax.all_gather(w_value, "grp", axis=1, tiled=True),
        lax.all_gather(w_gate, "grp", axis=1, tiled=True),
        lax.all_gather(w_out, "grp", axis=1, tiled=True),
        lax.all_gather(w_first, "grp", axis=1, tiled=True),
        lax.all_gather(w_second, "grp", axis=1, tiled=True),
        lax.all_gather(w_third, "grp", axis=1, tiled=True),
    )
    gathered = (
        lax.all_gather(partial_rows[0], "seq", axis=0, tiled=True),
        lax.all_gather(partial_rows[1], "seq", axis=0, tiled=True),
        lax.all_gather(partial_rows[2], "seq", axis=0, tiled=True),
        lax.all_gather(partial_rows[3], "seq", axis=0, tiled=True),
        lax.all_gather(partial_rows[4], "seq", axis=0, tiled=True),
        lax.all_gather(partial_rows[5], "seq", axis=0, tiled=True),
        lax.all_gather(partial_rows[6], "seq", axis=0, tiled=True),
        lax.all_gather(partial_rows[7], "seq", axis=0, tiled=True),
    )
    outputs = []
    input_grads = []
    first_norms = []
    attn_rows = []
    normed_rows = []
    branch_rows = []
    second_norms = []
    ffn_rows = []
    mixed_rows = []
    upstream_rows = []
    for batch_idx in range(micro):
        wq_full, wk_full, wv_full, wu_full, wo_full, first_full, second_full, third_full = gathered
        inputs = tokens[batch_idx, 0].astype(jnp.float32)
        live = (slot_index < lengths[batch_idx, 0]).astype(jnp.float32)[:, None]
        live_low = live.astype(jnp.bfloat16)
        first_norm = norm_rows(inputs).astype(jnp.bfloat16)
        query_pre = product(first_norm, wq_full)
        key_pre = product(first_norm, wk_full)
        value_pre = product(first_norm, wv_full)
        gate_pre = product(first_norm, wu_full)
        queries = jax.nn.silu(query_pre).astype(jnp.bfloat16).reshape(block_rows, heads, head_dim)
        key_heads = (jax.nn.silu(key_pre).astype(jnp.bfloat16) * live_low).reshape(
            block_rows, heads, head_dim
        )
        value_heads = (jax.nn.silu(value_pre).astype(jnp.bfloat16) * live_low).reshape(
            block_rows, heads, head_dim
        )
        query_wide = queries.astype(jnp.float32)
        key_wide = key_heads.astype(jnp.float32)
        value_wide = value_heads.astype(jnp.float32)
        local_state = jnp.einsum("jhd,jhe->hde", key_wide * key_fac, value_wide, precision=HIGH)
        prior_state, _ = prefix(
            (local_state, step_decay), "seq", combine_state, (empty_state, unit_decay), False
        )
        scores = (
            jnp.einsum("ihd,jhd->hij", queries, key_heads, preferred_element_type=jnp.float32)
            * weight
        )
        intra = jnp.einsum("hij,jhe->ihe", scores, value_wide, precision=HIGH)
        inter = jnp.einsum("ihd,hde->ihe", query_wide * query_fac, prior_state, precision=HIGH)
        attended = (intra + inter).reshape(block_rows, width)
        gate_act = jax.nn.silu(gate_pre)
        gated = gate_act * attended
        normed = norm_rows(gated).astype(jnp.bfloat16)
        hidden = inputs + product(normed, wo_full)
        second_norm = norm_rows(hidden).astype(jnp.bfloat16)
        first_proj = product(second_norm, first_full)
        second_proj = product(second_norm, second_full)
        mixed_in = (first_proj * second_proj).astype(jnp.bfloat16)
        result = hidden + product(mixed_in, third_full)
        outputs.append(result.astype(jnp.bfloat16))
        upstream = cotangent[batch_idx, 0].astype(jnp.float32) * live
        upstream_low = upstream.astype(jnp.bfloat16)
        grad_mixed = product_right(upstream_low, third_full)
        grad_first_proj = (grad_mixed * second_proj).astype(jnp.bfloat16)
        grad_second_proj = (grad_mixed * first_proj).astype(jnp.bfloat16)
        grad_norm_two = product_right(grad_first_proj, first_full) + product_right(
            grad_second_proj, second_full
        )
        grad_hidden = upstream + norm_back(hidden, grad_norm_two)
        grad_branch = grad_hidden.astype(jnp.bfloat16)
        grad_gated = norm_back(gated, product_right(grad_branch, wo_full))
        grad_attended = (grad_gated * gate_act).astype(jnp.bfloat16)
        grad_gate_pre = (grad_gated * attended * silu_slope(gate_pre)).astype(jnp.bfloat16)
        grad_heads = grad_attended.reshape(block_rows, heads, head_dim)
        grad_wide = grad_heads.astype(jnp.float32)
        local_grad = jnp.einsum("ihd,ihe->hde", query_wide * query_fac, grad_wide, precision=HIGH)
        later_grad, _ = prefix(
            (local_grad, step_decay), "seq", combine_state, (empty_state, unit_decay), True
        )
        grad_scores = (
            jnp.einsum("ihe,jhe->hij", grad_heads, value_heads, preferred_element_type=jnp.float32)
            * weight
        )
        grad_queries = jnp.einsum("hij,jhd->ihd", grad_scores, key_wide, precision=HIGH)
        grad_queries = (
            grad_queries
            + jnp.einsum("ihe,hde->ihd", grad_wide, prior_state, precision=HIGH) * query_fac
        )
        grad_keys = jnp.einsum("hij,ihd->jhd", grad_scores, query_wide, precision=HIGH)
        grad_keys = (
            grad_keys + jnp.einsum("hde,jhe->jhd", later_grad, value_wide, precision=HIGH) * key_fac
        )
        grad_values = jnp.einsum("hij,ihe->jhe", scores, grad_wide, precision=HIGH)
        grad_values = (
            grad_values + jnp.einsum("jhd,hde->jhe", key_wide, later_grad, precision=HIGH) * key_fac
        )
        grad_query_pre = (grad_queries.reshape(block_rows, width) * silu_slope(query_pre)).astype(
            jnp.bfloat16
        )
        grad_key_pre = (grad_keys.reshape(block_rows, width) * live * silu_slope(key_pre)).astype(
            jnp.bfloat16
        )
        grad_value_pre = (
            grad_values.reshape(block_rows, width) * live * silu_slope(value_pre)
        ).astype(jnp.bfloat16)
        grad_norm_one = product_right(grad_query_pre, wq_full) + product_right(
            grad_key_pre, wk_full
        )
        grad_norm_one = (
            grad_norm_one
            + product_right(grad_value_pre, wv_full)
            + product_right(grad_gate_pre, wu_full)
        )
        input_grads.append(grad_hidden + norm_back(inputs, grad_norm_one))
        first_norms.append(first_norm)
        attn_rows.append(
            jnp.concatenate([grad_query_pre, grad_key_pre, grad_value_pre, grad_gate_pre], axis=1)
        )
        normed_rows.append(normed)
        branch_rows.append(grad_branch)
        second_norms.append(second_norm)
        ffn_rows.append(jnp.concatenate([grad_first_proj, grad_second_proj], axis=1))
        mixed_rows.append(mixed_in)
        upstream_rows.append(upstream_low)
    first_all = jnp.concatenate(first_norms, axis=0)
    attn_all = jnp.concatenate(attn_rows, axis=0)
    normed_all = jnp.concatenate(normed_rows, axis=0)
    branch_all = jnp.concatenate(branch_rows, axis=0)
    second_all = jnp.concatenate(second_norms, axis=0)
    ffn_all = jnp.concatenate(ffn_rows, axis=0)
    mixed_all = jnp.concatenate(mixed_rows, axis=0)
    upstream_all = jnp.concatenate(upstream_rows, axis=0)
    proj_rows = lax.psum_scatter(
        product_left(first_all, attn_all), "seq", scatter_dimension=0, tiled=True
    )
    outproj_rows = lax.psum_scatter(
        product_left(normed_all, branch_all), "seq", scatter_dimension=0, tiled=True
    )
    ffn_part = lax.psum_scatter(
        product_left(second_all, ffn_all), "seq", scatter_dimension=0, tiled=True
    )
    down_rows = lax.psum_scatter(
        product_left(mixed_all, upstream_all), "seq", scatter_dimension=0, tiled=True
    )
    summed = (
        lax.psum_scatter(proj_rows[:, :width], "grp", scatter_dimension=1, tiled=True),
        lax.psum_scatter(proj_rows[:, width : 2 * width], "grp", scatter_dimension=1, tiled=True),
        lax.psum_scatter(
            proj_rows[:, 2 * width : 3 * width], "grp", scatter_dimension=1, tiled=True
        ),
        lax.psum_scatter(proj_rows[:, 3 * width :], "grp", scatter_dimension=1, tiled=True),
        lax.psum_scatter(outproj_rows, "grp", scatter_dimension=1, tiled=True),
        lax.psum_scatter(ffn_part[:, :hidden_width], "grp", scatter_dimension=1, tiled=True),
        lax.psum_scatter(ffn_part[:, hidden_width:], "grp", scatter_dimension=1, tiled=True),
        lax.psum_scatter(down_rows, "grp", scatter_dimension=1, tiled=True),
    )
    layer_out = jnp.stack(outputs)[:, None]
    grad_tokens = jnp.stack(input_grads)[:, None]
    return (
        layer_out,
        grad_tokens,
        summed[0],
        summed[1],
        summed[2],
        summed[3],
        summed[4],
        summed[5],
        summed[6],
        summed[7],
    )


class Spare:
    def __init__(self, sems):
        self.sems, self.free, self.order = sems, list(range(sems.shape[0])), []


class Copies:
    def __init__(self, spare):
        self.spare = spare
        self.pending = []

    def remote(self, src, dst, recv_sem, group, place, when=None):
        while not self.spare.free:
            owner, entry = self.spare.order.pop(0)
            owner.settle(entry)
        number = self.spare.free.pop(0)
        copy = pltpu.make_async_remote_copy(
            src_ref=src,
            dst_ref=dst,
            send_sem=self.spare.sems.at[number],
            recv_sem=recv_sem,
            device_id=(group, place),
            device_id_type=MESH,
        )
        self.pending.append((copy, when, number))
        self.spare.order.append((self, self.pending[-1]))
        if when is None:
            copy.start()
        else:
            pl.when(when)(copy.start)
        return self.pending[-1]

    def settle(self, entry):
        if not any(other is entry for other in self.pending):
            return
        self.pending = [other for other in self.pending if other is not entry]
        copy, when, number = entry
        if when is None:
            copy.wait_send()
        else:
            pl.when(when)(copy.wait_send)
        self.spare.free.append(number)

    def finish(self):
        while self.pending:
            self.settle(self.pending[0])


def local(src, dst, sem, when=None):
    copy = pltpu.make_async_copy(src, dst, sem)
    if when is None:
        copy.start()
    else:
        pl.when(when)(copy.start)


def arrived(ref, sem, when=None):
    copy = pltpu.make_async_copy(ref, ref, sem)
    if when is None:
        copy.wait()
    else:
        pl.when(when)(copy.wait)


def where_am_i():
    g, s = lax.axis_index("grp"), lax.axis_index("seq")
    return g, s, g // 2, g % 2, s // 2, s % 2


def across(y, x):
    return (y * 2 + 1 - x, (1 - y) * 2 + x, (1 - y) * 2 + 1 - x)


def greet(partners):
    barrier = pltpu.get_barrier_semaphore()
    for partner in partners:
        pl.semaphore_signal(barrier, inc=1, device_id=partner, device_id_type=MESH)
    pl.semaphore_wait(barrier, len(partners))


def aligned(index, unit, step):
    return pl.ds(pl.multiple_of(index * unit, step), unit)


class Gather:
    def __init__(self, copies, out, rows, hop_sem, side_sem):
        self.copies, self.out, self.rows = copies, out, rows
        self.hop_sem, self.side_sem = hop_sem, side_sem
        self.g, self.s, _, _, self.z, self.c = where_am_i()

    def block(self, b, z, core):
        return self.out.at[b, aligned(2 * z + core, self.rows, 16)]

    def spread(self, src, b, z_of, k, right, left):
        g, s, z, c = self.g, self.s, self.z, self.c
        dst = self.block(b, z_of, c)
        if right is not None:
            self.copies.remote(src, dst, self.hop_sem.at[b, 0, k], g, (s + 2) % 8, right)
        if left is not None:
            self.copies.remote(src, dst, self.hop_sem.at[b, 1, k], g, (s + 6) % 8, left)

    def begin(self, src, own_sem, b):
        g, s, z, c = self.g, self.s, self.z, self.c
        self.spread(src, b, z, 0, z < 3, z > 0)
        self.copies.remote(src, self.block(b, z, c), self.side_sem.at[b, 0], g, s + 1 - 2 * c)
        local(src, self.block(b, z, c), own_sem)

    def step(self, b, k, inner=None):
        g, s, z, c = self.g, self.s, self.z, self.c
        side = s + 1 - 2 * c
        ends = jnp.logical_or(z == 0, z == 3)

        def these(has):
            if inner is None:
                return has
            return jnp.logical_and(has, jnp.logical_not(ends) if inner else ends)

        has = these(z >= k)
        at = jnp.maximum(z - k, 0)
        ref = self.block(b, at, c)
        arrived(ref, self.hop_sem.at[b, 0, k - 1], has)
        if k < 3:
            self.spread(ref, b, at, k, jnp.logical_and(has, z < 3), None)
        self.copies.remote(ref, ref, self.side_sem.at[b, k], g, side, has)
        has = these(z + k <= 3)
        at = jnp.minimum(z + k, 3)
        ref = self.block(b, at, c)
        arrived(ref, self.hop_sem.at[b, 1, k - 1], has)
        if k < 3:
            self.spread(ref, b, at, k, None, jnp.logical_and(has, z > 0))
        self.copies.remote(ref, ref, self.side_sem.at[b, 3 + k], g, side, has)

    def finish(self, own_sem, b):
        z, c = self.z, self.c
        arrived(self.block(b, z, c), own_sem)
        arrived(self.block(b, z, 1 - c), self.side_sem.at[b, 0])
        for k in (1, 2, 3):
            arrived(self.block(b, jnp.maximum(z - k, 0), 1 - c), self.side_sem.at[b, k], z >= k)
            arrived(self.block(b, jnp.minimum(z + k, 3), 1 - c), self.side_sem.at[b, 3 + k], z + k <= 3)


def line_partners(g, s):
    return [(g, (s + d) % 8) for d in range(1, 8)]


def add_rows(target, room):
    def write(at, value):
        target[at] = value.astype(jnp.bfloat16)

    pour(lambda at: target[at].astype(jnp.float32) + room[at].astype(jnp.float32), write, target.shape[0] // 16)


class GroupSum:
    def __init__(self, copies, grad, inbox, sem):
        self.copies, self.grad, self.inbox, self.sem = copies, grad, inbox, sem
        self.g, self.s, self.y, self.x, self.z, self.c = where_am_i()
        self.rows, self.half = grad.shape[0] // 2, grad.shape[1] // 2
        self.entries = []

    def block(self, x, core):
        return self.grad.at[aligned(x, self.rows, 16), pl.ds(core * self.half, self.half)]

    def slot(self, first, count=1):
        return self.inbox.at[pl.ds(first * self.rows, count * self.rows)]

    def remote(self, *args):
        self.entries.append(self.copies.remote(*args))

    def depart(self):
        gx, gy, _ = across(self.y, self.x)
        self.remote(self.grad.at[:, pl.ds(0, self.half)], self.slot(0, 2), self.sem.at[0], gy, self.s, self.c != self.y)
        self.remote(self.block(1 - self.x, 1), self.slot(2), self.sem.at[1], gx, self.s)

    def middle(self, room, small, load):
        gx, gy, _ = across(self.y, self.x)
        mine = self.c == self.y
        arrived(self.slot(0, 2), self.sem.at[0], mine)
        local(self.slot(0, 2), room, load.at[0], mine)
        arrived(self.slot(2), self.sem.at[1])
        local(self.slot(2), small, load.at[1])
        arrived(room, load.at[0], mine)

        @pl.when(mine)
        def _():
            add_rows(self.grad.at[:, pl.ds(0, self.half)], room)

        arrived(small, load.at[1])
        add_rows(self.block(self.x, 1), small)
        for core in range(2):
            block = self.block(self.x, core)
            self.remote(
                block, self.slot(3), self.sem.at[2], self.g, 2 * self.z + core, jnp.logical_and(mine, self.c != core)
            )
            local(block, self.slot(3), self.sem.at[2], jnp.logical_and(mine, self.c == core))
        self.remote(self.block(1 - self.x, 0), self.slot(4), self.sem.at[3], gx, 2 * self.z, mine)
        self.remote(self.block(self.x, 1), self.slot(4), self.sem.at[3], gy, 2 * self.z + 1, jnp.logical_not(mine))

    def final(self, room, small, load):
        for i, ref in enumerate((room, small)):
            arrived(self.slot(3 + i), self.sem.at[2 + i])
            local(self.slot(3 + i), ref, load.at[i])
        for i, ref in enumerate((room, small)):
            arrived(ref, load.at[i])
        add_rows(room, small)

    def settle(self):
        for entry in self.entries:
            self.copies.settle(entry)


class ColumnSum:
    def __init__(self, copies, grad, inbox, sem):
        self.copies, self.grad, self.inbox, self.sem = copies, grad, inbox, sem
        self.g, self.s, y, x, _, _ = where_am_i()
        self.others = across(y, x)
        self.rows, self.wide = grad.shape[0] // 2, grad.shape[1] // 4

    def block(self, group, i):
        return self.grad.at[pl.ds(i * self.rows, self.rows), aligned(group, self.wide, 128)]

    def depart(self):
        for i in range(2):
            to = self.others[i]
            for k, group in enumerate((to, self.others[2])):
                self.copies.remote(self.block(group, i), self.inbox.at[i, k], self.sem.at[i, k], to, self.s)

    def middle(self, rooms, load):
        for i in range(2):
            arrived(self.inbox.at[i, 1], self.sem.at[i, 1])
            local(self.inbox.at[i, 1], rooms[i], load.at[i])
        for i in range(2):
            arrived(rooms[i], load.at[i])
            to = self.others[1 - i]
            add_rows(self.block(to, i), rooms[i])
            self.copies.remote(self.block(to, i), self.inbox.at[i, 2], self.sem.at[i, 2], to, self.s)

    def final(self, rooms, load):
        for i in range(2):
            for k in range(2):
                arrived(self.inbox.at[i, 2 * k], self.sem.at[i, 2 * k])
                local(self.inbox.at[i, 2 * k], rooms[2 * i + k], load.at[2 * i + k])
        for i in range(2):
            for k in range(2):
                arrived(rooms[2 * i + k], load.at[2 * i + k])
            mine, first, second = self.block(self.g, i), rooms[2 * i], rooms[2 * i + 1]

            def read(at):
                return mine[at].astype(jnp.float32) + first[at].astype(jnp.float32) + second[at].astype(jnp.float32)

            def write(at, value):
                mine[at] = value.astype(jnp.bfloat16)

            pour(read, write, self.rows // 16)


def everyone_on_line(copies, src, dst, sem, g, s, to_rows):
    for d in range(1, 8):
        to = (s + d) % 8
        copies.remote(to_rows(to), dst.at[s], sem, g, to)


def mean_square(values):
    return jnp.mean(values * values, axis=-1, keepdims=True)


def pour(read, write, count):
    def piece(i, carry):
        at = aligned(i, 16, 16)
        write(at, read(at))
        return carry

    lax.fori_loop(0, count, piece, 0)


class LineScatter:
    def __init__(self, copies, part, rows, side, inbox, side_sem, line_sem, queue):
        self.copies, self.part, self.rows, self.queue = copies, part, rows, queue
        self.side, self.inbox, self.side_sem, self.line_sem = side, inbox, side_sem, line_sem
        self.g, self.s, _, _, self.z, self.c = where_am_i()

    def mine(self, chip):
        return self.part.at[aligned(2 * chip + self.c, self.rows, 16)]

    def begin(self):
        for chip in (3, 0, 2, 1):
            theirs = aligned(2 * chip + 1 - self.c, self.rows, 16)
            self.copies.remote(
                self.part.at[theirs], self.side.at[chip], self.side_sem.at[chip], self.g, self.s + 1 - 2 * self.c
            )

    def add_on(self, chip, way):
        own, side = self.mine(chip), self.side.at[chip]
        slot = chip - 1 if way == 0 else chip
        come = self.inbox.at[way, slot]
        arrived(side, self.side_sem.at[chip])
        arrived(come, self.line_sem.at[way, slot])

        def three(at):
            return own[at].astype(jnp.float32) + side[at].astype(jnp.float32) + come[at].astype(jnp.float32)

        def write(at, value):
            own[at] = value.astype(jnp.bfloat16)

        pour(three, write, self.rows // 16)

    def push(self, chip, way, when):
        slot = chip - 1 if way == 0 else chip
        to = (self.s + 2) % 8 if way == 0 else (self.s + 6) % 8
        return self.copies.remote(
            self.mine(chip), self.inbox.at[way, slot], self.line_sem.at[way, slot], self.g, to, when
        )

    def pass_on(self, chip, way):
        end = self.z == (0 if way == 0 else 3)
        own, side = self.mine(chip), self.side.at[chip]

        def two(at):
            return own[at].astype(jnp.float32) + side[at].astype(jnp.float32)

        def write(at, value):
            own[at] = value.astype(jnp.bfloat16)

        @pl.when(end)
        def _():
            arrived(side, self.side_sem.at[chip])
            pour(two, write, self.rows // 16)

        if way in self.queue:
            copies, entry = self.queue.pop(way)
            copies.settle(entry)
        self.queue[way] = (self.copies, self.push(chip, way, end))

    def start(self, i):
        self.pass_on(3 - i, 0)
        self.pass_on(i, 1)

    def hop(self, i):
        z = self.z
        for inner in (1, 2):

            @pl.when(z == inner)
            def _():
                near = inner == 1
                if i < 2:
                    self.add_on(3 - i if near else i, 0 if near else 1)
                else:
                    self.add_on(0 if near else 3, 1 if near else 0)

        for inner in (1, 2):
            near = inner == 1
            if i < 2:
                self.push(3 - i if near else i, 0 if near else 1, z == inner)
            else:
                self.push(0 if near else 3, 1 if near else 0, z == inner)

    def receive(self):
        z = self.z
        arrived(self.side.at[z], self.side_sem.at[z])
        left, right = jnp.maximum(z - 1, 0), jnp.minimum(z, 2)
        arrived(self.inbox.at[0, left], self.line_sem.at[0, left], z > 0)
        arrived(self.inbox.at[1, right], self.line_sem.at[1, right], z < 3)

    def total(self, at):
        z = self.z
        value = self.mine(z)[at].astype(jnp.float32) + self.side[z, at].astype(jnp.float32)
        from_left = self.inbox[0, jnp.maximum(z - 1, 0), at].astype(jnp.float32)
        from_right = self.inbox[1, jnp.minimum(z, 2), at].astype(jnp.float32)
        return value + jnp.where(z > 0, from_left, 0.0) + jnp.where(z < 3, from_right, 0.0)


def silu(values):
    return values / (1.0 + jnp.exp(-values))


def decay_table(rate, length):
    offset = lax.broadcasted_iota(jnp.int32, (length, length), 0) - lax.broadcasted_iota(jnp.int32, (length, length), 1)
    steps = jnp.maximum(offset, 0).astype(jnp.float32)
    return jnp.where(offset >= 0, jnp.exp(-rate * steps), 0.0)


def live_rows(first, count, length):
    return ((first + lax.broadcasted_iota(jnp.int32, (count, 1), 0)) < length).astype(jnp.float32)


def slope(values):
    sigma = 1.0 / (1.0 + jnp.exp(-values))
    return sigma * (1.0 + values * (1.0 - sigma))


def turned_table(rate, length):
    offset = lax.broadcasted_iota(jnp.int32, (length, length), 1) - lax.broadcasted_iota(jnp.int32, (length, length), 0)
    steps = jnp.maximum(offset, 0).astype(jnp.float32)
    return jnp.where(offset >= 0, jnp.exp(-rate * steps), 0.0)


def columns_of(out, tiles, b, rows):
    for owner in range(8):
        out[pl.ds(owner * rows, rows)] = jnp.broadcast_to(tiles[b, owner, :1], (128, 128)).T[:rows]


def turn(dst, read, count, columns):
    def block(i, carry):
        dst[pl.ds(0, columns), aligned(i, 128, 128)] = read(aligned(i, 128, 128)).T
        return carry

    lax.fori_loop(0, count, block, 0)


def tiles_of(width, body):
    def tile(i, carry):
        body(aligned(i, 256, 256), i)
        return carry

    lax.fori_loop(0, width // 256, tile, 0)


def layer_part(
    lengths, decay, x, cot, wq, wk, wv, wu, wo, w1, w2, w3,
    out_all, grad_all, fq, fk, fv, fu, fo, ff_, fs, ft,
    n1_all, dm_all, n2_all, da_all, q_all, k_all, v_all, u_all, o_all, f_all, s_all, t_all, pre_all, in_f, in_t, in_o, in_h, x_f, y_f,
    send, load, own, hop_n, side_n, hop_d, side_d, z_head, z_out, z_ff, xy_head, xy_out, xy_ff, spread_f, join_f,
    out, grad_x, out_sem, n1, dm, n2, da, h, a_v, b_v, w_v, wa_v, wo_v, p_v, turned, part, side, inbox, side_sem, line_sem,
    side_m, inbox_m, side_sem_m, line_sem_m, table, squares, inbox_sq, scale, scale_in, sq_sem, sc_sem, column,
    mix, mix_in, mix_sem, inverse, mixed, pre, pre_sem, go_v, grads_h,
    xy_f, xy_t, xy_o, xy_h, z_f, z_t, z_o, z_h,
):
    g, s, y, x_, z, c = where_am_i()
    others = across(y, x_)
    plane = [(o, 2 * z + e) for o in others for e in range(2)]
    rows, width = x.shape[1], x.shape[2]
    length = 8 * rows
    tokens = 2 * length
    depth, wide = wq.shape
    head = q_all.shape[1] // 2
    hidden = f_all.shape[0]
    quarter = hidden // 2
    half = length // 2
    target = g // 2
    mine = aligned(g % 2, head, head)
    here = c == target
    order = [(z + d) % 4 for d in (0, 1, 3, 2)]
    spare = Spare(send)
    copies, later, turned_out, bulk, last = [Copies(spare) for _ in range(5)]
    early, sums = [[Copies(spare) for _ in range(2)] for _ in range(2)]
    gather_n = Gather(copies, n1_all, rows, hop_n, side_n)
    gather_d = Gather(later, dm_all, rows, hop_d, side_d)
    gather_m = Gather(later, n2_all, rows, hop_n, side_n)
    gather_a = Gather(last, da_all, rows, hop_d, side_d)
    heads = list(zip((wq, wk, wv, wu), (q_all, k_all, v_all, u_all)))
    w1_f, w2_f, w3_f = [w_v.at[pl.ds(n * hidden, hidden)] for n in range(3)]
    w1_in, w2_in = [w_v.at[pl.ds(n * depth, depth), pl.ds(512, 2 * hidden)] for n in range(2)]
    w1_t, w2_t = [w_v.at[pl.ds(0, 2 * hidden), pl.ds(n * depth, depth)] for n in range(2)]
    low_v = p_v.at[2, pl.ds(0, length), pl.ds(0, 2 * head)]

    def at_b(b):
        return pl.ds(b * length, length)

    def dz(n, at):
        return p_v.at[n // 2, at, pl.ds((n % 2) * 2 * head, 2 * head)]

    def nat_v(at):
        return p_v.at[2, at, pl.ds(0, 2 * head)]

    local(w1, w1_in, load.at[0])
    local(w2, w2_in, load.at[1])
    greet(line_partners(g, s) + plane)

    def send_heads(n):
        src, dst = heads[n]
        for d in (2, 1, 3, 0):
            to = (z + d) % 4
            a, b = src.at[:, aligned(to, head, head)], dst.at[aligned(s, depth, 16), mine]
            if d:
                copies.remote(a, b, z_head.at[n, z], g, 2 * to + target)
            else:
                copies.remote(a, b, z_head.at[n, z], g, 2 * to + target, c != target)
                local(a, b, z_head.at[n, z], here)

    def pass_heads(n):
        dst = heads[n][1]
        for zs in order:
            block = dst.at[aligned(zs, 2 * depth, 16), mine]
            arrived(block, z_head.at[n, zs], here)
            for r, o in enumerate(others[:2]):
                copies.remote(block, block, xy_head.at[n, r, zs], o, s, here)

    def relay_heads(n):
        dst = heads[n][1]
        for zs in order:
            for r, when in ((0, here), (1, jnp.logical_not(here))):
                lanes = aligned(others[r] % 2, head, head)
                arrived(dst.at[aligned(zs, 2 * depth, 16), lanes], xy_head.at[n, r, zs], when)
                part_ = dst.at[aligned(2 * zs + r, depth, 16), lanes]
                copies.remote(part_, part_, xy_head.at[n, 2, zs], others[1 - r], s, when)

    def send_out():
        for i in range(2):
            to = 2 * c + i
            a = wo.at[pl.ds(i * head, head)]
            b = o_all.at[aligned(z % 2, head, head), aligned(g, wide, 128)]
            self_ = jnp.logical_and(to == z, c == z // 2)
            copies.remote(a, b, z_out.at[z % 2], g, 2 * to + z // 2, jnp.logical_not(self_))
            local(a, b, z_out.at[z % 2], self_)

    def pass_out():
        for j in range(2):
            arrived(o_all.at[pl.ds(j * head, head), aligned(g, wide, 128)], z_out.at[j])
        block = o_all.at[:, aligned(g, wide, 128)]
        for r, o in enumerate(others[:2]):
            copies.remote(block, block, xy_out.at[r], o, s)

    def relay_out():
        for r in range(2):
            lanes = aligned(others[r], wide, 128)
            arrived(o_all.at[:, lanes], xy_out.at[r])
            part_ = o_all.at[pl.ds(r * head, head), lanes]
            copies.remote(part_, part_, xy_out.at[2], others[1 - r], s)

    def spread_ff():
        for n, src in enumerate((w1_t, w2_t)):
            for r, o in enumerate(others):
                turned_out.remote(src.at[aligned(o, quarter, 16)], x_f.at[n, g], spread_f.at[n], o, s)
            local(src.at[aligned(g, quarter, 16)], x_f.at[n, g], spread_f.at[n])

    def ff_block(n, group, zs):
        return (f_all, s_all)[n].at[aligned(group % 2, quarter, 16), aligned(zs, 2 * depth, 128)]

    def send_ff(n):
        arrived(x_f.at[n], spread_f.at[n])
        b = (f_all, s_all)[n].at[aligned(g % 2, quarter, 16), aligned(s, depth, 128)]
        for d in (2, 1, 3, 0):
            to = (z + d) % 4
            a = x_f.at[n, to]
            if d:
                later.remote(a, b, z_ff.at[n, z], g, 2 * to + target)
            else:
                later.remote(a, b, z_ff.at[n, z], g, 2 * to + target, c != target)
                local(a, b, z_ff.at[n, z], here)

    def pass_ff(n):
        for zs in order:
            block = ff_block(n, g, zs)
            arrived(block, z_ff.at[n, zs], here)
            for r, o in enumerate(others[:2]):
                later.remote(block, block, xy_ff.at[n, r, zs], o, s, here)

    def relay_ff(n):
        for zs in order:
            for r, when in ((0, here), (1, jnp.logical_not(here))):
                arrived(ff_block(n, others[r], zs), xy_ff.at[n, r, zs], when)
                part_ = (f_all, s_all)[n].at[aligned(others[r] % 2, quarter, 16), aligned(2 * zs + r, depth, 128)]
                later.remote(part_, part_, xy_ff.at[n, 2, zs], others[1 - r], s, when)

    def send_third():
        block = t_all.at[:, aligned(g, wide, 128)]
        for r, o in enumerate(others[:2]):
            later.remote(w3, block, xy_ff.at[2, r, 0], o, s)
        local(w3, block, z_ff.at[2, 0])

    def relay_third():
        for r in range(2):
            lanes = aligned(others[r], wide, 128)
            arrived(t_all.at[:, lanes], xy_ff.at[2, r, 0])
            part_ = t_all.at[pl.ds(r * quarter, quarter), lanes]
            later.remote(part_, part_, xy_ff.at[2, 2, 0], others[1 - r], s)

    send_heads(0)
    send_heads(1)
    for b in range(2):

        def norm(at):
            v = x[b, at].astype(jnp.float32)
            return v * lax.rsqrt(mean_square(v) + EPS)

        def keep(at, value):
            n1[b, at] = value.astype(jnp.bfloat16)

        pour(norm, keep, rows // 16)
        first = s * rows

        def masked(i, carry):
            at = aligned(i, 16, 16)
            live = live_rows(first + i * 16, 16, lengths[0, b])
            dm[b, at] = (cot[b, at].astype(jnp.float32) * live).astype(jnp.bfloat16)
            return carry

        lax.fori_loop(0, rows // 16, masked, 0)
    for n, (src, dst) in enumerate(((w1_in, w1_t), (w2_in, w2_t))):
        arrived(src, load.at[n])
        dst[...] = src[...].T
    spread_ff()
    pass_heads(0)
    send_heads(2)
    pass_heads(1)
    send_heads(3)
    for b in range(2):
        gather_n.begin(n1.at[b], own.at[0, b], b)
    pass_heads(2)
    relay_heads(0)
    pass_heads(3)
    send_out()
    relay_heads(1)
    gather_n.step(0, 1)
    gather_n.step(1, 1)
    pass_out()
    relay_heads(2)
    gather_n.step(0, 2)
    gather_n.step(1, 2)
    relay_heads(3)
    relay_out()
    gather_n.step(0, 3)
    send_ff(0)
    send_ff(1)
    send_third()
    over = others[2]
    for n, (_, dst) in enumerate(heads):
        for zs in range(4):
            block = dst.at[pl.ds(zs * 2 * depth, 2 * depth), aligned(over % 2, head, head)]
            arrived(block, xy_head.at[n, 2, zs], over // 2 == c)
    arrived(o_all.at[:, aligned(over, wide, 128)], xy_out.at[2])
    for n, (_, dst) in enumerate(heads):
        local(dst, wa_v.at[n], load.at[n])
    local(o_all, wo_v, load.at[4])
    gather_n.finish(own.at[0, 0], 0)
    local(n1_all.at[0], a_v.at[at_b(0)], load.at[5])
    for j in range(2):
        table[j] = decay_table(decay[4 * (2 * c + j) + z], length)
    for n in range(4):
        arrived(wa_v.at[n], load.at[n])
    arrived(wo_v, load.at[4])

    def scatters_of(copies, first, queue):
        kept = (side, inbox, side_sem, line_sem) if first else (side_m, inbox_m, side_sem_m, line_sem_m)
        return [LineScatter(copies[b], part.at[b], rows, *[k.at[b] for k in kept], queue) for b in range(2)]

    scatters = scatters_of(early, True, {})
    for b in range(2):
        if b == 1:
            gather_n.step(1, 3)
            gather_n.finish(own.at[0, 1], 1)
            local(n1_all.at[1], a_v.at[at_b(1)], load.at[6])
        arrived(a_v.at[at_b(b)], load.at[5 + b])
        if b == 1:
            for j in range(2):
                arrived(pre.at[j], pre_sem.at[j])

        def project(i, carry):
            at = aligned(i, half, 16)
            from_ = aligned(2 * b + i, half, 16)
            for n in range(4):
                value = product(a_v[from_], wa_v[n])
                for j in range(2):
                    pre[j, n, at] = value[:, j * head : (j + 1) * head]
            return carry

        lax.fori_loop(0, 2, project, 0)
        if b == 1:
            scatters[0].start(1)
        live = live_rows(0, length, lengths[0, b])
        square = 0.0
        for j in range(2):
            q = silu(pre[j, 0]).astype(jnp.bfloat16)
            k = (silu(pre[j, 1]) * live).astype(jnp.bfloat16)
            v = (silu(pre[j, 2]) * live).astype(jnp.bfloat16)
            scores = (product_right(q, k) * table[j]).astype(jnp.bfloat16)
            attended = product(scores, v)
            pre[j, 4] = attended
            gated = silu(pre[j, 3]) * attended
            square = square + jnp.sum(gated * gated, axis=-1, keepdims=True)
            low_v[:, pl.ds(j * head, head)] = gated.astype(jnp.bfloat16)
            local(pre.at[j], pre_all.at[b, j], pre_sem.at[j])
        row = jnp.broadcast_to(square, (length, 128)).T[:8]
        for to in range(8):
            squares[b, to, :, :rows] = row[:, to * rows : (to + 1) * rows]
        everyone_on_line(later, squares, inbox_sq.at[b], sq_sem.at[b], g, s, lambda to: squares.at[b, to])
        local(squares.at[b, s], inbox_sq.at[b, s], sq_sem.at[b])

        def out_part(i, carry):
            at = aligned(i, 256, 256)
            part[b, :, at] = product(low_v[...], wo_v[:, at]).astype(jnp.bfloat16)
            return carry

        lax.fori_loop(0, width // 256, out_part, 0)
        scatters[b].begin()
        if b == 0:
            scatters[0].start(0)

    def hidden_state(b):
        arrived(inbox_sq.at[b], sq_sem.at[b])
        total = inbox_sq[b, 0]
        for d in range(1, 8):
            total = total + inbox_sq[b, d]
        row = lax.rsqrt(total / width + EPS)
        scale[b] = row
        column[b] = jnp.broadcast_to(row[:1], (128, 128)).T
        scatter = scatters[b]
        scatter.receive()

        def finish(i, carry):
            piece = aligned(i, 16, 16)
            at = aligned(b * (rows // 16) + i, 16, 16)
            a = scatter.total(piece) * column[b, piece, :1]
            value = x[b, piece].astype(jnp.float32) + a
            h[at] = value
            n2[b, piece] = (value * lax.rsqrt(mean_square(value) + EPS)).astype(jnp.bfloat16)
            return carry

        lax.fori_loop(0, rows // 16, finish, 0)
        gather_m.begin(n2.at[b], own.at[2, b], b)

    gather_d.begin(dm.at[0], own.at[1, 0], 0)
    scatters[0].hop(0)
    relay_third()
    scatters[0].start(2)
    scatters[0].hop(1)
    pass_ff(0)
    scatters[1].start(0)
    scatters[0].hop(2)
    pass_ff(1)
    gather_d.step(0, 1)
    hidden_state(0)
    scatters[1].start(1)
    scatters[1].hop(0)
    gather_d.step(0, 2)
    scatters[1].start(2)
    scatters[1].hop(1)
    gather_m.step(0, 1)
    scatters[1].hop(2)
    relay_ff(0)
    gather_d.step(0, 3)
    gather_m.step(0, 2)
    gather_d.begin(dm.at[1], own.at[1, 1], 1)
    hidden_state(1)
    gather_m.step(0, 3)
    relay_ff(1)
    gather_d.finish(own.at[1, 0], 0)
    local(dm_all.at[0], b_v.at[at_b(0)], load.at[2])
    gather_m.finish(own.at[2, 0], 0)
    local(n2_all.at[0], a_v.at[at_b(0)], load.at[0])
    gather_d.step(1, 1, True)
    gather_m.step(1, 1, True)
    turned_out.finish()
    for n, (dst, room) in enumerate(((f_all, w1_f), (s_all, w2_f), (t_all, w3_f))):
        if n < 2:
            for zs in range(4):
                arrived(ff_block(n, over, zs), xy_ff.at[n, 2, zs], over // 2 == c)
        else:
            arrived(dst.at[:, aligned(over, wide, 128)], xy_ff.at[2, 2, 0])
        if n == 2:
            arrived(dst.at[:, aligned(g, wide, 128)], z_ff.at[2, 0])
        local(dst, room, load.at[4 + n])
    for b in range(2):
        early[b].finish()

    def feed_forward(b):
        def tile(i, carry):
            at = aligned(b * 2 + i, half, 16)
            first = product_right(a_v[at], w1_f[...])
            second = product_right(a_v[at], w2_f[...])
            back = product_right(b_v[at], w3_f[...])
            p_v[0, at] = (back * second).astype(jnp.bfloat16)
            p_v[1, at] = (back * first).astype(jnp.bfloat16)
            p_v[2, at] = (first * second).astype(jnp.bfloat16)
            return carry

        lax.fori_loop(0, 2, tile, 0)

    def norm_part(b):
        def body(at, i):
            value = product(p_v[0, at_b(b)], w1_f[:, at]) + product(p_v[1, at_b(b)], w2_f[:, at])
            part[b, :, at] = value.astype(jnp.bfloat16)

        tiles_of(width, body)

    def mixed_part(b):
        def body(at, i):
            part[b, :, at] = product(p_v[2, at_b(b)], w3_f[:, at]).astype(jnp.bfloat16)

        tiles_of(width, body)

    half_w = width // 2
    groups_f = [GroupSum(bulk, w_v.at[pl.ds(n * hidden, hidden)], in_f.at[n], xy_f.at[n]) for n in range(2)]
    groups_t = ColumnSum(bulk, w_v.at[pl.ds(2 * hidden, hidden)], in_t, xy_t)

    def rooms_ff(ref):
        return ref.at[pl.ds(0, hidden), pl.ds(0, half_w)], ref.at[pl.ds(0, quarter), pl.ds(half_w, half_w)]

    def spread_place(i):
        return pl.ds(pl.multiple_of((i % 2) * half_w + (i // 2) * 256, 256), 256)

    def weight_part(n, operand):
        turn(turned, lambda t: p_v[n, t], tokens // 128, hidden)

        def body(at, i):
            place = spread_place(i) if n < 2 else at
            w_v[pl.ds(n * hidden, hidden), place] = product(turned[...], operand[:, at]).astype(jnp.bfloat16)

        tiles_of(width, body)
        if n < 2:
            groups_f[n].depart()
        else:
            groups_t.depart()

    def hidden_gradient(b):
        scatter = second[b]
        scatter.receive()

        def finish(i, carry):
            piece = aligned(i, 16, 16)
            at = aligned(b * (rows // 16) + i, 16, 16)
            value = h[at]
            scale_h = lax.rsqrt(mean_square(value) + EPS)
            normed = value * scale_h
            grad = scatter.total(piece)
            along = jnp.mean(normed * grad, axis=-1, keepdims=True)
            live = live_rows(s * rows + i * 16, 16, lengths[0, b])
            upstream = cot[b, piece].astype(jnp.float32) * live
            grad_hidden = upstream + scale_h * (grad - normed * along)
            grad_x[at] = grad_hidden
            low = grad_hidden.astype(jnp.bfloat16)
            da[b, piece] = low
            dot = jnp.mean(low.astype(jnp.float32) * (value - x[b, piece].astype(jnp.float32)), axis=-1, keepdims=True)
            column[b, piece] = jnp.broadcast_to(dot, (16, 128))
            return carry

        lax.fori_loop(0, rows // 16, finish, 0)
        gather_a.begin(da.at[b], own.at[3, b], b)
        mix[b, :, :rows] = column[b].T[:8, :rows]
        for d in range(1, 8):
            last.remote(mix.at[b], mix_in.at[b, s], mix_sem.at[b], g, (s + d) % 8)
        local(mix.at[b], mix_in.at[b, s], mix_sem.at[b])

    second = scatters_of(early, True, {})
    for n in (0, 4, 5, 2, 6):
        ref = {0: a_v.at[at_b(0)], 2: b_v.at[at_b(0)], 4: w1_f, 5: w2_f, 6: w3_f}[n]
        arrived(ref, load.at[n])
    feed_forward(0)
    gather_m.step(1, 2, True)
    gather_d.step(1, 2, True)
    norm_part(0)
    second[0].begin()
    second[0].start(0)
    for k in (1, 2):
        gather_d.step(1, k, False)
        gather_m.step(1, k, False)
    gather_m.step(1, 3)
    gather_d.step(1, 3)
    gather_d.finish(own.at[1, 1], 1)
    local(dm_all.at[1], b_v.at[at_b(1)], load.at[3])
    gather_m.finish(own.at[2, 1], 1)
    local(n2_all.at[1], a_v.at[at_b(1)], load.at[1])
    for b in range(2):
        for d in range(1, 8):
            later.remote(scale.at[b], scale_in.at[b, s], sc_sem.at[b], g, (s + d) % 8)
        local(scale.at[b], scale_in.at[b, s], sc_sem.at[b])
    second[0].start(1)
    second[0].hop(0)
    arrived(a_v.at[at_b(1)], load.at[1])
    arrived(b_v.at[at_b(1)], load.at[3])
    feed_forward(1)
    second[0].start(2)
    second[0].hop(1)
    second[0].hop(2)
    norm_part(1)
    def load_pre(b, j):
        local(pre_all.at[b, j], pre.at[j], pre_sem.at[j])

    def attention_back(b):
        gather_a.finish(own.at[3, b], b)
        local(da_all.at[b], a_v.at[at_b(b)], load.at[b])
        arrived(mix_in.at[b], mix_sem.at[b])
        columns_of(mixed, mix_in, b, rows)
        live = live_rows(0, length, lengths[0, b])
        arrived(a_v.at[at_b(b)], load.at[b])
        for j in range(2):
            arrived(pre.at[j], pre_sem.at[j])
            lanes = pl.ds(j * head, head)
            error = product_right(a_v[at_b(b)], wo_v[pl.ds(j * head, head)])
            q_pre, k_pre, v_pre, u_pre, o = [pre[j, n] for n in range(5)]
            sigma = 1.0 / (1.0 + jnp.exp(-u_pre))
            u = u_pre * sigma
            scale_g = inverse[at_b(b), :1]
            nat = u * o * scale_g
            nat_v(at_b(b))[:, lanes] = nat.astype(jnp.bfloat16)
            dg = scale_g * (error - nat * mixed[:, :1])
            dz(3, at_b(b))[:, lanes] = (dg * o * (sigma * (1.0 + u_pre * (1.0 - sigma)))).astype(jnp.bfloat16)
            do = (dg * u).astype(jnp.bfloat16)
            q = silu(q_pre).astype(jnp.bfloat16)
            k = (silu(k_pre) * live).astype(jnp.bfloat16)
            v = (silu(v_pre) * live).astype(jnp.bfloat16)
            scores = (product_right(k, q) * table[j]).astype(jnp.bfloat16)
            dv = product(scores, do)
            d_scores = (product_right(v, do) * table[j]).astype(jnp.bfloat16)
            dk = product(d_scores, q)
            dq = product_left(d_scores, k)
            dz(0, at_b(b))[:, lanes] = (dq * slope(pre[j, 0])).astype(jnp.bfloat16)
            dz(1, at_b(b))[:, lanes] = (dk * live * slope(pre[j, 1])).astype(jnp.bfloat16)
            dz(2, at_b(b))[:, lanes] = (dv * live * slope(pre[j, 2])).astype(jnp.bfloat16)
            if b == 0:
                load_pre(1, j)

    def first_part(b):
        def body(at, i):
            value = product_right(dz(0, at_b(b))[...], wa_v[0, at])
            for n in range(1, 4):
                value = value + product_right(dz(n, at_b(b))[...], wa_v[n, at])
            part[b, :, at] = value.astype(jnp.bfloat16)

        tiles_of(width, body)

    second[1].begin()
    second[1].start(0)
    hidden_gradient(0)
    weight_part(0, a_v)
    second[1].start(1)
    second[1].hop(0)
    gather_a.step(0, 1)
    third = scatters_of(sums, False, {})
    early[0].finish()
    mixed_part(0)
    third[0].begin()
    third[0].start(0)
    second[1].start(2)
    second[1].hop(1)
    second[1].hop(2)
    third[0].start(1)
    third[0].hop(0)
    gather_a.step(0, 2)
    weight_part(1, a_v)
    hidden_gradient(1)
    third[0].start(2)
    third[0].hop(1)
    groups_f[0].middle(*rooms_ff(a_v), load.at[pl.ds(13, 2)])
    gather_a.step(0, 3)
    third[0].hop(2)
    early[1].finish()
    mixed_part(1)
    third[1].begin()
    third[1].start(0)
    for j in range(2):
        table[j] = turned_table(decay[4 * (2 * c + j) + z], length)
    for b in range(2):
        arrived(scale_in.at[b], sc_sem.at[b])
        columns_of(inverse.at[at_b(b)], scale_in, b, rows)

    for j in range(2):
        arrived(pre.at[j], pre_sem.at[j])
        load_pre(0, j)
    gather_a.step(1, 1)
    third[1].start(1)
    third[1].hop(0)
    weight_part(2, b_v)
    gather_a.step(1, 2)
    third[1].start(2)
    third[1].hop(1)
    third[1].hop(2)
    groups_f[1].middle(*rooms_ff(b_v), load.at[pl.ds(13, 2)])
    for b in range(2):
        local(n1_all.at[b], b_v.at[at_b(b)], load.at[2 + b])
    later.finish()
    attention_back(0)
    gather_a.step(1, 3)
    def sum_ff(n):
        small = w_v.at[pl.ds(n * hidden, quarter), pl.ds(half_w, half_w)]
        groups_f[n].settle()
        total = w_v.at[pl.ds(n * hidden, quarter), pl.ds(0, half_w)]
        groups_f[n].final(total, small, load.at[pl.ds(13, 2)])
        for d in (2, 1, 3, 0):
            chip = (z + d) % 4
            src = total.at[:, aligned(chip, depth, 128)]
            if d:
                last.remote(src, y_f.at[n, z], z_f.at[n, z], g, 2 * chip + c)
            else:
                local(src, y_f.at[n, z], z_f.at[n, z])

    def join_ff(n, result):
        for r, o in enumerate(others + (g,)):
            arrived(y_f.at[n, o], z_f.at[n, o])
            dst = result.at[aligned(g, quarter, 16)]
            if r < 3:
                last.remote(y_f.at[n, o], dst, join_f.at[n], o, s)
            else:
                local(y_f.at[n, o], dst, join_f.at[n])

    def rooms_column(rows):
        return [b_v.at[pl.ds(0, rows), pl.ds(i * wide, wide)] for i in range(4)]

    def sum_third():
        groups_t.final(rooms_column(quarter), load.at[pl.ds(13, 4)])
        local(w_v.at[pl.ds(2 * hidden, hidden), aligned(g, wide, 128)], ft, z_t)

    groups_h = [GroupSum(last, grads_h.at[n], in_h.at[n], xy_h.at[n]) for n in range(4)]
    groups_o = ColumnSum(last, go_v, in_o, xy_o)

    def room_h(first, count):
        return w_v.at[pl.ds(first * head, count * head), pl.ds(half_w, half_w)]

    def middle_head(n):
        groups_h[n].middle(room_h(3 * (n % 2), 2), room_h(3 * (n % 2) + 2, 1), load.at[pl.ds(18, 2)])

    def head_part(n):
        turn(turned, lambda t: dz(n, t)[...], tokens // 128, 2 * head)

        def body(at, i):
            grads_h[n, :, spread_place(i)] = product(turned[pl.ds(0, 2 * head)], b_v[:, at]).astype(jnp.bfloat16)

        tiles_of(width, body)

    def out_weight():
        turn(turned, lambda t: nat_v(t)[...], tokens // 128, 2 * head)

        def body(at, i):
            go_v[:, at] = product(turned[pl.ds(0, 2 * head)], a_v[:, at]).astype(jnp.bfloat16)

        tiles_of(width, body)

    def sum_head(n, result):
        total = room_h(6 + n, 1)
        groups_h[n].final(total, room_h(10, 1), load.at[pl.ds(18, 2)])
        for d in (2, 1, 3, 0):
            chip = (z + d) % 4
            src = total.at[:, aligned(chip, depth, 128)]
            dst = result.at[aligned(z, head, head)]
            if d:
                last.remote(src, dst, z_h.at[n], g, 2 * chip + c)
            else:
                local(src, dst, z_h.at[n])

    def sum_out():
        groups_o.final(rooms_column(head), load.at[pl.ds(13, 4)])
        mine_o = go_v.at[:, aligned(g, wide, 128)]
        for j in range(2):
            to = 2 * (2 * c + j) + z // 2
            src = mine_o.at[pl.ds(j * head, head)]
            dst = fo.at[aligned(z % 2, head, head)]
            last.remote(src, dst, z_o.at[z % 2], g, to, to != s)
            local(src, dst, z_o.at[z % 2], to == s)

    sum_ff(0)
    attention_back(1)
    for b in range(2):
        arrived(b_v.at[at_b(b)], load.at[2 + b])
    head_part(0)
    groups_h[0].depart()
    for b in range(2):
        third[b].receive()
        scatter = third[b]

        def result(i, carry):
            piece = aligned(i, 16, 16)
            at = aligned(b * (rows // 16) + i, 16, 16)
            out[at] = (h[at] + scatter.total(piece)).astype(jnp.bfloat16)
            return carry

        lax.fori_loop(0, rows // 16, result, 0)
    local(out, out_all, out_sem.at[2])
    for b in range(2):
        sums[b].finish()
    fourth = scatters_of(early, True, {})
    first_part(0)
    fourth[0].begin()
    fourth[0].start(0)
    head_part(1)
    groups_h[1].depart()
    sum_ff(1)
    groups_t.middle(
        [w_v.at[pl.ds(0, quarter), pl.ds(half_w + k * wide, wide)] for k in range(2)], load.at[pl.ds(13, 2)]
    )
    first_part(1)
    fourth[0].start(1)
    fourth[0].hop(0)
    fourth[1].begin()
    head_part(2)
    groups_h[2].depart()
    middle_head(0)
    head_part(3)
    groups_h[3].depart()
    middle_head(1)
    fourth[0].start(2)
    fourth[0].hop(1)
    out_weight()
    groups_o.depart()
    middle_head(2)
    fourth[0].hop(2)
    fourth[1].start(0)
    middle_head(3)
    sum_head(0, fq)
    fourth[1].start(1)
    fourth[1].hop(0)
    groups_o.middle(rooms_column(head), load.at[pl.ds(13, 2)])
    sum_head(1, fk)
    join_ff(0, ff_)
    join_ff(1, fs)
    fourth[1].start(2)
    fourth[1].hop(1)
    sum_head(2, fv)
    fourth[1].hop(2)
    sum_head(3, fu)
    sum_out()
    sum_third()
    for b in range(2):
        fourth[b].receive()
        scatter = fourth[b]

        def finish_x(i, carry):
            piece = aligned(i, 16, 16)
            at = aligned(b * (rows // 16) + i, 16, 16)
            v = x[b, piece].astype(jnp.float32)
            scale_x = lax.rsqrt(mean_square(v) + EPS)
            normed = v * scale_x
            grad = scatter.total(piece)
            along = jnp.mean(normed * grad, axis=-1, keepdims=True)
            grad_x[at] = grad_x[at] + scale_x * (grad - normed * along)
            return carry

        lax.fori_loop(0, rows // 16, finish_x, 0)
        block = pl.ds(b * rows, rows)
        local(grad_x.at[block], grad_all.at[block], out_sem.at[b])


    arrived(out, out_sem.at[2])
    for b in range(2):
        arrived(grad_x.at[pl.ds(b * rows, rows)], out_sem.at[b])
    for n, result in enumerate((ff_, fs)):
        arrived(result, join_f.at[n])
    arrived(ft, z_t)
    for j in range(2):
        arrived(fo.at[pl.ds(0, head)], z_o.at[j])
    for n, result in enumerate((fq, fk, fv, fu)):
        arrived(result, z_h.at[n])
    for b in range(2):
        early[b].finish()
    bulk.finish()
    last.finish()
    copies.finish()


def call(kernel, number, ins, outs, scratch, name):
    return pl.pallas_call(
        kernel,
        out_shape=[shape for shape, _ in outs],
        in_specs=[spec for _, spec in ins],
        out_specs=[spec for _, spec in outs],
        scratch_shapes=scratch,
        compiler_params=pltpu.CompilerParams(
            collective_id=number, has_side_effects=True, vmem_limit_bytes=64 * 2**20 - 2**17
        ),
        name=name,
    )(*[value for value, _ in ins])


def finish_arrays(count, turned_count, *refs):
    ins, outs, held, done = refs[:count], refs[count : 2 * count], refs[2 * count : 3 * count], refs[3 * count : 4 * count]
    in_sem, out_sem = refs[4 * count :]
    for i in range(count):
        local(ins[i], held[i], in_sem.at[i])
    for i in range(count):
        arrived(held[i], in_sem.at[i])
        if i < 2:
            local(held[i], outs[i], out_sem.at[i])
            continue
        if i < 2 + turned_count:
            done[i][...] = held[i][...].T.astype(jnp.float32)
        else:

            def write(at, value):
                done[i][at] = value

            pour(lambda at: held[i][at].astype(jnp.float32), write, held[i].shape[0] // 16)
        local(done[i], outs[i], out_sem.at[i])
    for i in range(count):
        arrived(outs[i], out_sem.at[i])


def finished(out, grad_x, turned, straight):
    arrays = [out, grad_x] + turned + straight
    shapes = [jax.ShapeDtypeStruct(v.shape, v.dtype) for v in (out, grad_x)]
    shapes += [wide_array(*v.shape[::-1]) for v in turned] + [wide_array(*v.shape) for v in straight]
    count = len(arrays)
    small = jax.ShapeDtypeStruct((8, 128), jnp.float32)
    done = [small, small] + shapes[2:]
    return pl.pallas_call(
        functools.partial(finish_arrays, count, len(turned)),
        out_shape=shapes,
        in_specs=[ANY] * count,
        out_specs=[ANY] * count,
        scratch_shapes=[pltpu.VMEM(v.shape, v.dtype) for v in arrays] + [pltpu.VMEM(v.shape, v.dtype) for v in done]
        + [dma(count), dma(count)],
        compiler_params=pltpu.CompilerParams(vmem_limit_bytes=62 * 2**20),
        name="finish_arrays",
    )(*arrays)


def low_array(*shape):
    return jax.ShapeDtypeStruct(shape, jnp.bfloat16)


def wide_array(*shape):
    return jax.ShapeDtypeStruct(shape, jnp.float32)


def dma(*shape):
    return pltpu.SemaphoreType.DMA(shape)


def scatter_scratch(rows, width):
    return [
        pltpu.VMEM((2, 4, rows, width), jnp.bfloat16),
        pltpu.VMEM((2, 2, 3, rows, width), jnp.bfloat16),
        dma(2, 4),
        dma(2, 2, 3),
    ]


def line_shards(
    tokens, cotangent, lengths, decay_rate,
    w_query, w_key, w_value, w_gate, w_out, w_first, w_second, w_third,
):
    bf16, f32 = jnp.bfloat16, jnp.float32
    rows, width = tokens.shape[2], tokens.shape[3]
    depth, wide = w_query.shape
    head = width // decay_rate.shape[0]
    hidden = w_third.shape[0]
    length = 8 * rows
    x_low = tokens[:, 0]
    in_smem = pl.BlockSpec(memory_space=pltpu.SMEM)
    gathered = low_array(2, length, width)
    out, grad_x, fq, fk, fv, fu, fo, ff, fs, ft = call(
        layer_part,
        0,
        [(lengths.T, in_smem), (decay_rate, in_smem), (x_low, VMEM), (cotangent[:, 0], VMEM)]
        + [(v, ANY) for v in (w_query, w_key, w_value, w_gate, w_out, w_first, w_second, w_third)],
        [(low_array(2 * rows, width), ANY), (wide_array(2 * rows, width), ANY)]
        + [(low_array(wide, depth), ANY)] * 4 + [(low_array(depth, wide), ANY)]
        + [(low_array(2 * hidden, depth), ANY)] * 2 + [(low_array(hidden, wide), ANY)]
        + [(gathered, ANY)] * 4
        + [(low_array(width, 2 * head), ANY)] * 4
        + [(low_array(2 * head, width), ANY)]
        + [(low_array(hidden, width), ANY)] * 3
        + [(wide_array(2, 2, 5, length, head), ANY)]
        + [(low_array(2, 5 * hidden // 2, width // 2), ANY), (low_array(2, 3, hidden // 2, wide), ANY), (low_array(2, 3, head, wide), ANY),
           (low_array(4, 5 * head, width // 2), ANY)]
        + [(low_array(2, 4, hidden // 2, depth), ANY)] * 2,
        [dma(100), dma(26), dma(4, 2)] + [dma(2, 2, 3), dma(2, 7)] * 2
        + [dma(4, 4), dma(2), dma(3, 4), dma(4, 3, 4), dma(3), dma(3, 3, 4), dma(2), dma(2)]
        + [pltpu.VMEM((2 * rows, width), bf16), pltpu.VMEM((2 * rows, width), f32), dma(3)]
        + [pltpu.VMEM((2, rows, width), bf16)] * 4
        + [pltpu.VMEM((2 * rows, width), f32),
           pltpu.VMEM((2 * length, width), bf16), pltpu.VMEM((2 * length, width), bf16), pltpu.VMEM((3 * hidden, width), bf16),
           pltpu.VMEM((4, width, 2 * head), bf16), pltpu.VMEM((2 * head, width), bf16),
           pltpu.VMEM((3, 2 * length, hidden), bf16), pltpu.VMEM((hidden, 2 * length), bf16),
           pltpu.VMEM((2, length, width), bf16)]
        + scatter_scratch(rows, width) + scatter_scratch(rows, width)
        + [pltpu.VMEM((2, length, length), f32), pltpu.VMEM((2, 8, 8, 128), f32), pltpu.VMEM((2, 8, 8, 128), f32),
           pltpu.VMEM((2, 8, 128), f32), pltpu.VMEM((2, 8, 8, 128), f32), dma(2), dma(2), pltpu.VMEM((2, 128, 128), f32),
           pltpu.VMEM((2, 8, 128), f32), pltpu.VMEM((2, 8, 8, 128), f32), dma(2),
           pltpu.VMEM((2 * length, 128), f32), pltpu.VMEM((length, 128), f32),
           pltpu.VMEM((2, 5, length, head), f32), dma(2),
           pltpu.VMEM((2 * head, width), bf16), pltpu.VMEM((4, 2 * head, width), bf16),
           dma(2, 4), dma(2, 3), dma(2, 3), dma(4, 4), dma(2, 4), dma(), dma(2), dma(4)],
        "layer_part",
    )[:10]
    results = finished(out, grad_x, [ff, fs, fq, fk, fv, fu], [ft, fo])
    out, grad_x, ff, fs, fq, fk, fv, fu, ft, fo = results
    return (out.reshape(2, 1, rows, width), grad_x.reshape(2, 1, rows, width), fq, fk, fv, fu, fo, ff, fs, ft)


def solution(mesh):
    in_specs = (
        P(None, "grp", "seq", None),
        P(None, "grp", "seq", None),
        P(None, "grp"),
        P(),
        P("seq", "grp"),
        P("seq", "grp"),
        P("seq", "grp"),
        P("seq", "grp"),
        P("seq", "grp"),
        P("seq", "grp"),
        P("seq", "grp"),
        P("seq", "grp"),
    )
    out_specs = (
        P(None, "grp", "seq", None),
        P(None, "grp", "seq", None),
        P("seq", "grp"),
        P("seq", "grp"),
        P("seq", "grp"),
        P("seq", "grp"),
        P("seq", "grp"),
        P("seq", "grp"),
        P("seq", "grp"),
        P("seq", "grp"),
    )
    fast = mesh.shape["grp"] == 4 and mesh.shape["seq"] == 8
    return jax.shard_map(line_shards if fast else shards, mesh=mesh, in_specs=in_specs, out_specs=out_specs, check_vma=False)
```
